32 devices in a mesh: expert: 16 (over z, y, core), etp: 2 (over x).
Axes of the slice: x: 2, y: 2, z: 4, core: 2. Of those that a mesh axis runs over, the one named last changes fastest.
Arguments:
- tokens: bfloat16 [2048, 2048], P('expert', 'etp'), may hold values from -6 to 6
- out_grad: bfloat16 [2048, 2048], P('expert', 'etp'), may hold values from -12 to 12
- routes: int32 [2048, 8], P('expert'), may hold values from 0 to 15, all different within a row; in each aligned block of 128 rows (0 to 127, 128 to 255, ...) at most 72 rows name the same one
- combine: float32 [2048, 8], P('expert'), may hold values from 0.02 to 0.5
- w_gate: bfloat16 [16, 768, 2048], P('expert', 'etp'), may hold values from -0.125 to 0.125
- w_up: bfloat16 [16, 768, 2048], P('expert', 'etp'), may hold values from -0.125 to 0.125
- w_down: bfloat16 [16, 768, 2048], P('expert', 'etp'), may hold values from -0.21875 to 0.21875
Outputs:
- grad_tokens: bfloat16 [2048, 2048], P('expert', 'etp')
- grad_gate: bfloat16 [16, 768, 2048], P('expert', 'etp')
- grad_up: bfloat16 [16, 768, 2048], P('expert', 'etp')
- grad_down: bfloat16 [16, 768, 2048], P('expert', 'etp')
The draws below stay inside these ranges and needn't reach their ends.
Inputs may be any that keep to these rules, and one draw needn't show every extreme that they name: `routes`: each row names 8 different experts. Within each aligned block of 128 rows (the rows of one index of expert) no expert is named by more than 72 rows, and in some block one expert is named by exactly 72 rows.
All inputs are finite; a program needn't handle non-finite values.
Results may differ from the reference program's by a relative error of at most 0.0064.
Values may be sent and summed in bfloat16 or wider, within the bound.
No kernel may reach another device: no remote copies, remote signals or barrier semaphores. Data moves between devices by JAX's collectives and lax.ppermute only.
A program may use at most 128 MiB of HBM per device.

```python
import math
import jax
import jax.numpy as jnp
import numpy as np
from jax import lax

D = 2048
H = 768
TOP = 8
TOK_DEV = 128
EXPERTS = 16
CAP = 72
TOKENS = 2048
N_EXPERT = 16


def level_of(rng, dims, cuts, smallest, largest):
    def one(dim, parts):
        draws = jax.random.uniform(jax.random.fold_in(jax.random.fold_in(rng, 6), dim), (parts,), jnp.float32, smallest / len(cuts), largest / len(cuts))
        return jnp.repeat(jnp.exp(draws), dims[dim] // parts).reshape((-1,) + (1,) * (len(dims) - dim - 1))

    loudness = one(*cuts[0])
    for cut in cuts[1:]:
        loudness = loudness * one(*cut)
    return loudness


def assign_block(stream_key, own, number, rows, amount, top, bound, lean):
    ranking = jax.random.permutation(stream_key, amount)
    heavy_load, ordinary = shares(amount, rows * top, bound, lean, True), shares(amount, rows * top, bound, lean, False)
    places = jnp.arange(amount)

    def named(tallies, rotation):
        used = int((tallies > 0).sum())
        fixed = max(1, used // 4)
        passed = fixed + (places - fixed + rotation * (used - fixed)) % max(1, amount - fixed)
        return jnp.zeros((amount,), jnp.int32).at[ranking[jnp.where(places < fixed, places, passed)]].set(jnp.asarray(tallies, jnp.int32))

    tallies = jnp.where(number % 4 == 0, named(heavy_load, number // 4), named(ordinary, number - number // 4 - 1))
    mixed = jax.random.permutation(jax.random.fold_in(own, 3), amount)
    donor, receiver = mixed[0:amount // 2 * 2:2], mixed[1:amount // 2 * 2:2]
    slack = jnp.minimum(tallies[donor] - 1, bound - tallies[receiver]) // 2
    slack = jnp.where((donor == ranking[0]) | (receiver == ranking[0]) | (tallies[receiver] == 0), 0, jnp.maximum(slack, 0))
    passed = jax.random.randint(jax.random.fold_in(own, 4), (amount // 2,), 0, 1 << 20) % (slack + 1)
    tallies = tallies.at[donor].add(-passed).at[receiver].add(passed)
    members = jnp.searchsorted(jnp.cumsum(tallies), jnp.arange(rows * top), side="right").astype(jnp.int32)
    table = members.reshape(top, rows).T
    table = table[jax.random.permutation(jax.random.fold_in(own, 1), rows)]
    rotation = jax.random.randint(jax.random.fold_in(own, 2), (rows, 1), 0, top)
    return jnp.take_along_axis(table, (jnp.arange(top)[None, :] + rotation) % top, axis=1)


def shares(count, total, bound, lean, full):
    loads = [(1 << 20) // math.isqrt(standing ** lean) + 1 for standing in range(1, count + 1)]
    largest = bound if full else min(bound, max(-(-total // count), total * loads[0] // sum(loads)))
    least = 1 if total - largest >= count - 1 else 0
    holding, surplus = [largest] + [least] * (count - 1), total - largest - least * (count - 1)
    while surplus > 0:
        candidates = [i for i in range(1, count) if holding[i] < largest] or [i for i in range(1, count) if holding[i] < bound]
        whole, left = sum([loads[i] for i in candidates]), surplus
        for i in candidates:
            addition = min(bound - holding[i], max(1, left * loads[i] // whole), surplus)
            holding[i] = holding[i] + addition
            surplus = surplus - addition
    return np.array(holding)


def gaussian(key, dims, deviation, limit, pieces=(), held_as=jnp.bfloat16):
    drawn = jax.random.normal(key, dims, jnp.float32) * deviation
    if len(pieces) > 0:
        drawn = level_of(key, dims, pieces, -0.22, 0.18) * drawn
    return jnp.clip(drawn, min=-limit, max=limit).astype(held_as)


def setup_inputs(seed: int = 0) -> dict:
    arg_keys = jax.random.split(jax.random.key(seed), 8)
    tokens = gaussian(arg_keys[0], (TOKENS, D), 1.0, 6.0, ((0, 16), (1, 2)))
    out_grad = gaussian(arg_keys[1], (TOKENS, D), 2.0, 12.0, ((0, 16), (1, 2)))
    routes_keys = jax.random.split(jax.random.fold_in(arg_keys[2], 1), TOKENS // TOK_DEV)
    routes_turns = jax.random.permutation(jax.random.fold_in(arg_keys[2], 3), TOKENS // TOK_DEV)
    routes = jax.vmap(lambda own, number: assign_block(jax.random.fold_in(arg_keys[2], 2), own, number, TOK_DEV, EXPERTS, TOP, CAP, 1))(routes_keys, routes_turns).reshape((TOKENS, TOP))
    combine = jnp.clip(jnp.exp(math.log(0.5) - 3.218876 * jax.random.uniform(arg_keys[3], (TOKENS, TOP), jnp.float32) ** level_of(arg_keys[3], (TOKENS, TOP), ((0, 16),), -0.2, 0.2)), 0.02, 0.5)
    w_gate = gaussian(arg_keys[4], (EXPERTS, H, D), D ** -0.5, 0.125, ((0, 16), (1, 2)))
    w_up = gaussian(arg_keys[5], (EXPERTS, H, D), D ** -0.5, 0.125, ((0, 16), (1, 2)))
    w_down = gaussian(arg_keys[6], (EXPERTS, H, D), H ** -0.5, 0.21875, ((0, 16), (1, 2)))
    return dict(tokens=tokens, out_grad=out_grad, routes=routes, combine=combine, w_gate=w_gate, w_up=w_up, w_down=w_down)


def routing_table(routes):
    blocks = routes.reshape(N_EXPERT, TOK_DEV * TOP)
    labels = jnp.arange(EXPERTS, dtype=jnp.int32)

    def place(block_routes):
        one_hot = (block_routes[:, None] == labels[None, :]).astype(jnp.int32)
        earlier = jnp.cumsum(one_hot, axis=0) - one_hot
        return jnp.sum(earlier * one_hot, axis=1).astype(jnp.int32)

    position = jax.vmap(place)(blocks)
    anchor = jnp.arange(N_EXPERT, dtype=jnp.int32)[:, None]
    slot = blocks * (N_EXPERT * CAP) + anchor * CAP + position
    filler = TOKENS * TOP
    table = jnp.full((EXPERTS * N_EXPERT * CAP,), filler, jnp.int32)
    table = table.at[slot.reshape(-1)].set(jnp.arange(filler, dtype=jnp.int32))
    return table.reshape(EXPERTS, N_EXPERT * CAP)


def reference(tokens, out_grad, routes, combine, w_gate, w_up, w_down):
    table = routing_table(routes)
    filler = TOKENS * TOP
    weights_flat = combine.reshape(-1)

    def expert_step(grad_total, operands):
        rows, gate_w, up_w, down_w = operands
        is_live = rows < filler
        safe_rows = jnp.minimum(rows, filler - 1)
        token_of = safe_rows // TOP
        rows_x = tokens[token_of] * is_live[:, None].astype(tokens.dtype)
        scale = weights_flat[safe_rows] * is_live.astype(weights_flat.dtype)
        rows_g = (scale[:, None] * out_grad[token_of].astype(jnp.float32)).astype(jnp.bfloat16)
        gate = jnp.dot(rows_x, gate_w.T, preferred_element_type=jnp.float32)
        up = jnp.dot(rows_x, up_w.T, preferred_element_type=jnp.float32)
        hidden_grad = jnp.dot(rows_g, down_w.T, preferred_element_type=jnp.float32)
        sigma = jax.nn.sigmoid(gate)
        silu = gate * sigma
        acts = (silu * up).astype(jnp.bfloat16)
        grad_down = jnp.dot(acts.T, rows_g, preferred_element_type=jnp.float32).astype(jnp.bfloat16)
        gate_term = (hidden_grad * up * sigma * (1.0 + gate * (1.0 - sigma))).astype(jnp.bfloat16)
        up_term = (hidden_grad * silu).astype(jnp.bfloat16)
        grad_gate = jnp.dot(gate_term.T, rows_x, preferred_element_type=jnp.float32).astype(jnp.bfloat16)
        grad_up = jnp.dot(up_term.T, rows_x, preferred_element_type=jnp.float32).astype(jnp.bfloat16)
        slot_grads = (jnp.dot(gate_term, gate_w, preferred_element_type=jnp.float32)
                      + jnp.dot(up_term, up_w, preferred_element_type=jnp.float32)).astype(jnp.bfloat16)
        target = jnp.where(is_live, token_of, TOKENS)
        grad_total = grad_total.at[target].add(slot_grads.astype(jnp.float32), mode="drop")
        return grad_total, (grad_gate, grad_up, grad_down)

    start_total = jnp.zeros((TOKENS, D), jnp.float32)
    grad_total, (grad_gate, grad_up, grad_down) = lax.scan(expert_step, start_total, (table, w_gate, w_up, w_down))
    return grad_total.astype(jnp.bfloat16), grad_gate, grad_up, grad_down
```

```python
import functools

import jax
import jax.numpy as jnp
from jax import lax
from jax.experimental import pallas as pl
from jax.experimental.pallas import tpu as pltpu
from jax.sharding import PartitionSpec as P

CONTRACT_LAST = (((1,), (1,)), ((), ()))
CONTRACT_FIRST = (((0,), (0,)), ((), ()))


def pack_rows(token_rows, grad_rows, token_of, scale, is_live):
    mask = is_live[:, None].astype(token_rows.dtype)
    inputs_sent = token_rows[token_of] * mask
    grads_sent = (scale[:, None] * grad_rows[token_of].astype(jnp.float32)).astype(jnp.bfloat16)
    return (inputs_sent, grads_sent)


def pair_positions(routed_flat, experts):
    pair_total = routed_flat.shape[0]
    span = 128
    groups = pair_total // span
    labels = jnp.arange(experts, dtype=jnp.int32)
    one_hot = (routed_flat[:, None] == labels[None, :]).astype(jnp.bfloat16)
    grouped = one_hot.reshape(groups, span, experts)
    row_ids = jnp.arange(span, dtype=jnp.int32)
    lower = (row_ids[None, :] < row_ids[:, None]).astype(jnp.bfloat16)
    within = jnp.einsum("ij,bje->bie", lower, grouped, preferred_element_type=jnp.float32)
    group_sums = jnp.sum(grouped.astype(jnp.float32), axis=1)
    group_before = jnp.cumsum(group_sums, axis=0) - group_sums
    earlier = within + group_before[:, None, :]
    counted = jnp.sum(earlier * grouped.astype(jnp.float32), axis=2)
    return counted.reshape(pair_total).astype(jnp.int32)


def exchange_body(tokens, out_grad, routes, combine, w_gate, w_up, w_down):
    experts = lax.axis_size("expert")
    tok_rows = tokens.shape[0]
    col_width = tokens.shape[1]
    choose_count = routes.shape[1]
    per_pair = tok_rows * choose_count // experts
    capacity = per_pair + per_pair // 8
    routed_flat = routes.reshape(-1)
    pair_total = routed_flat.shape[0]
    position = pair_positions(routed_flat, experts)
    target = routed_flat * capacity + position
    anchor = jnp.full((experts * capacity,), pair_total, jnp.int32)
    anchor = anchor.at[target].set(jnp.arange(pair_total, dtype=jnp.int32))
    is_live = anchor < pair_total
    safe_anchor = jnp.minimum(anchor, pair_total - 1)
    token_of = safe_anchor // choose_count
    scale = combine.reshape(-1)[safe_anchor] * is_live.astype(jnp.float32)
    full_tokens, full_grads = (
        lax.all_gather(tokens, "etp", axis=1, tiled=True),
        lax.all_gather(out_grad, "etp", axis=1, tiled=True),
    )
    inputs_sent, grads_sent = pack_rows(full_tokens, full_grads, token_of, scale, is_live)
    rows_x, rows_g = (
        lax.all_to_all(inputs_sent, "expert", split_axis=0, concat_axis=0, tiled=True),
        lax.all_to_all(grads_sent, "expert", split_axis=0, concat_axis=0, tiled=True),
    )
    gate_w = w_gate[0]
    up_w = w_up[0]
    down_w = w_down[0]
    gate = lax.dot_general(rows_x, gate_w, CONTRACT_LAST, preferred_element_type=jnp.float32)
    up = lax.dot_general(rows_x, up_w, CONTRACT_LAST, preferred_element_type=jnp.float32)
    hidden_grad = lax.dot_general(rows_g, down_w, CONTRACT_LAST, preferred_element_type=jnp.float32)
    sigma = jax.nn.sigmoid(gate)
    silu = gate * sigma
    acts = (silu * up).astype(jnp.bfloat16)
    grad_down = lax.dot_general(acts, rows_g, CONTRACT_FIRST, preferred_element_type=jnp.float32)
    gate_term = (hidden_grad * up * sigma * (1.0 + gate * (1.0 - sigma))).astype(jnp.bfloat16)
    up_term = (hidden_grad * silu).astype(jnp.bfloat16)
    grad_gate = lax.dot_general(
        gate_term, rows_x, CONTRACT_FIRST, preferred_element_type=jnp.float32
    )
    grad_up = lax.dot_general(up_term, rows_x, CONTRACT_FIRST, preferred_element_type=jnp.float32)
    swapped_gate, swapped_up = (
        lax.all_to_all(gate_w, "etp", split_axis=1, concat_axis=0, tiled=True),
        lax.all_to_all(up_w, "etp", split_axis=1, concat_axis=0, tiled=True),
    )
    running = jnp.dot(
        lax.all_gather(gate_term, "etp", axis=1, tiled=True),
        swapped_gate,
        preferred_element_type=jnp.float32,
    )
    slot_grads = running + jnp.dot(
        lax.all_gather(up_term, "etp", axis=1, tiled=True),
        swapped_up,
        preferred_element_type=jnp.float32,
    )
    slot_grads = slot_grads.astype(jnp.bfloat16)
    returned = lax.all_to_all(slot_grads, "expert", split_axis=0, concat_axis=0, tiled=True)
    picked = returned[target].astype(jnp.float32).reshape(tok_rows, choose_count, col_width)
    grad_tokens = jnp.sum(picked, axis=1).astype(jnp.bfloat16)
    return (
        grad_tokens,
        grad_gate.astype(jnp.bfloat16)[None],
        grad_up.astype(jnp.bfloat16)[None],
        grad_down.astype(jnp.bfloat16)[None],
    )


def expert_kernel(me_ref, info_ref, x_ref, g_ref, wg_ref, wu_ref, wd_ref,
                  part_ref, rx_ref, rg_ref, act_ref, gt_ref, ut_ref):
    me = me_ref[0]
    blocks, halves, rows, width = x_ref.shape
    top = info_ref.shape[1] // 2
    span = blocks * rows
    slots = rx_ref.shape[0]
    named, weights = [], []
    for b in range(blocks):
        hit = info_ref[b, :top, :] == me.astype(jnp.float32)
        named.append(jnp.sum(hit.astype(jnp.float32), axis=0, keepdims=True))
        weights.append(jnp.sum(jnp.where(hit, info_ref[b, top:, :], 0.0), axis=0, keepdims=True))
    named = jnp.concatenate(named, axis=1)
    weights = jnp.concatenate(weights, axis=1)
    earlier = (
        lax.broadcasted_iota(jnp.int32, (span, span), 0)
        < lax.broadcasted_iota(jnp.int32, (span, span), 1)
    ).astype(jnp.bfloat16)
    counted = jnp.dot(
        jnp.broadcast_to(named, (16, span)).astype(jnp.bfloat16),
        earlier,
        preferred_element_type=jnp.float32,
    )[:1]
    slot_of = jnp.where(named > 0.0, counted.astype(jnp.int32), -1)
    chosen = slot_of == lax.broadcasted_iota(jnp.int32, (slots, span), 0)
    pick = chosen.astype(jnp.bfloat16)
    scale = jnp.sum(jnp.where(chosen, weights, 0.0), axis=1, keepdims=True)

    gate = up = hidden_grad = 0.0
    for h in range(halves):
        cols = slice(h * width, (h + 1) * width)
        x = x_ref[:, h].reshape(span, width)
        rx = jnp.dot(pick, x, preferred_element_type=jnp.float32).astype(jnp.bfloat16)
        rx_ref[:, cols] = rx
        gate += lax.dot_general(rx, wg_ref[:, cols], CONTRACT_LAST, preferred_element_type=jnp.float32)
        up += lax.dot_general(rx, wu_ref[:, cols], CONTRACT_LAST, preferred_element_type=jnp.float32)
        g = g_ref[:, h].reshape(span, width)
        rg = (scale * jnp.dot(pick, g, preferred_element_type=jnp.float32)).astype(jnp.bfloat16)
        rg_ref[:, cols] = rg
        hidden_grad += lax.dot_general(rg, wd_ref[:, cols], CONTRACT_LAST, preferred_element_type=jnp.float32)

    sigma = 1.0 / (1.0 + jnp.exp(-gate))
    silu = gate * sigma
    act_ref[...] = (silu * up).astype(jnp.bfloat16)
    gate_term = (hidden_grad * up * sigma * (1.0 + gate * (1.0 - sigma))).astype(jnp.bfloat16)
    up_term = (hidden_grad * silu).astype(jnp.bfloat16)
    gt_ref[...] = gate_term
    ut_ref[...] = up_term
    for h in range(halves):
        cols = slice(h * width, (h + 1) * width)
        slot = jnp.dot(gate_term, wg_ref[:, cols], preferred_element_type=jnp.float32)
        slot += jnp.dot(up_term, wu_ref[:, cols], preferred_element_type=jnp.float32)
        back = lax.dot_general(
            pick, slot.astype(jnp.bfloat16), CONTRACT_FIRST, preferred_element_type=jnp.float32
        )
        part_ref[:, h] = back.astype(jnp.bfloat16).reshape(blocks, rows, width)


def run_experts(me, info, x, g, gate_w, up_w, down_w, per_step, slots):
    blocks, halves, rows, width = x.shape
    hidden, features = gate_w.shape
    steps = blocks // per_step
    flops = 2 * steps * slots * features * (hidden * 5 + per_step * rows * 3)
    moved = 2 * (x.size * 3 + 3 * gate_w.size + steps * slots * (2 * features + 3 * hidden))
    whole = pl.BlockSpec((hidden, features), lambda i, me: (0, 0))
    token_blocks = pl.BlockSpec((per_step, halves, rows, width), lambda i, me: (i, 0, 0, 0))
    return pl.pallas_call(
        expert_kernel,
        grid_spec=pltpu.PrefetchScalarGridSpec(
            num_scalar_prefetch=1,
            grid=(steps,),
            in_specs=[
                pl.BlockSpec((per_step,) + info.shape[1:], lambda i, me: (i, 0, 0)),
                token_blocks,
                token_blocks,
                whole,
                whole,
                whole,
            ],
            out_specs=[
                token_blocks,
                pl.BlockSpec((slots, features), lambda i, me: (i, 0)),
                pl.BlockSpec((slots, features), lambda i, me: (i, 0)),
                pl.BlockSpec((slots, hidden), lambda i, me: (i, 0)),
                pl.BlockSpec((slots, hidden), lambda i, me: (i, 0)),
                pl.BlockSpec((slots, hidden), lambda i, me: (i, 0)),
            ],
        ),
        out_shape=[
            jax.ShapeDtypeStruct(x.shape, jnp.bfloat16),
            jax.ShapeDtypeStruct((steps * slots, features), jnp.bfloat16),
            jax.ShapeDtypeStruct((steps * slots, features), jnp.bfloat16),
            jax.ShapeDtypeStruct((steps * slots, hidden), jnp.bfloat16),
            jax.ShapeDtypeStruct((steps * slots, hidden), jnp.bfloat16),
            jax.ShapeDtypeStruct((steps * slots, hidden), jnp.bfloat16),
        ],
        compiler_params=pltpu.CompilerParams(vmem_limit_bytes=56 * 1024 * 1024),
        cost_estimate=pl.CostEstimate(flops=flops, bytes_accessed=moved, transcendentals=steps * slots * hidden),
        name="experts",
    )(me, info, x, g, gate_w, up_w, down_w)


def gather_body(per_step, tokens, out_grad, routes, combine, w_gate, w_up, w_down):
    experts = lax.axis_size("expert")
    halves = lax.axis_size("etp")
    rows, width = tokens.shape
    top = routes.shape[1]
    per_pair = rows * top // experts
    capacity = per_pair + per_pair // 8
    slots = -(-per_step * capacity // 16) * 16
    me = lax.axis_index("expert").astype(jnp.int32).reshape(1)
    info = jnp.concatenate([routes.astype(jnp.float32), combine], axis=1).T
    info = lax.all_gather(info, "expert", axis=0)
    x = lax.all_gather(tokens, ("expert", "etp"), axis=0).reshape(experts, halves, rows, width)
    g = lax.all_gather(out_grad, ("expert", "etp"), axis=0).reshape(experts, halves, rows, width)
    part, rows_x, rows_g, acts, gate_term, up_term = run_experts(
        me, info, x, g, w_gate[0], w_up[0], w_down[0], per_step, slots
    )
    part = part.reshape(experts * halves * rows, width)
    grad_tokens = lax.psum_scatter(part, ("expert", "etp"), scatter_dimension=0, tiled=True)
    grad_down = lax.dot_general(acts, rows_g, CONTRACT_FIRST, preferred_element_type=jnp.float32)
    grad_gate = lax.dot_general(gate_term, rows_x, CONTRACT_FIRST, preferred_element_type=jnp.float32)
    grad_up = lax.dot_general(up_term, rows_x, CONTRACT_FIRST, preferred_element_type=jnp.float32)
    return (
        grad_tokens,
        grad_gate.astype(jnp.bfloat16)[None],
        grad_up.astype(jnp.bfloat16)[None],
        grad_down.astype(jnp.bfloat16)[None],
    )


def solution(mesh):
    experts = mesh.shape["expert"]

    def body(tokens, out_grad, routes, combine, w_gate, w_up, w_down):
        rows, top = routes.shape
        if top * 4 >= experts and experts % 4 == 0:
            run = functools.partial(gather_body, experts // 4)
        else:
            run = exchange_body
        return run(tokens, out_grad, routes, combine, w_gate, w_up, w_down)

    placed = (
        P("expert", "etp"),
        P("expert", "etp"),
        P("expert", None),
        P("expert", None),
        P("expert", "etp", None),
        P("expert", "etp", None),
        P("expert", "etp", None),
    )
    return jax.shard_map(
        body,
        mesh=mesh,
        in_specs=placed,
        out_specs=(
            P("expert", "etp"),
            P("expert", "etp", None),
            P("expert", "etp", None),
            P("expert", "etp", None),
        ),
        check_vma=False,
    )
```

```python
import functools

import jax
import jax.numpy as jnp
from jax import lax
from jax.experimental import pallas as pl
from jax.experimental.pallas import tpu as pltpu
from jax.sharding import PartitionSpec as P

CONTRACT_LAST = (((1,), (1,)), ((), ()))
CONTRACT_FIRST = (((0,), (0,)), ((), ()))
INFO_ROWS = 16


def pack_rows(token_rows, grad_rows, token_of, scale, is_live):
    mask = is_live[:, None].astype(token_rows.dtype)
    inputs_sent = token_rows[token_of] * mask
    grads_sent = (scale[:, None] * grad_rows[token_of].astype(jnp.float32)).astype(jnp.bfloat16)
    return (inputs_sent, grads_sent)


def pair_positions(routed_flat, experts):
    pair_total = routed_flat.shape[0]
    span = 128
    groups = pair_total // span
    labels = jnp.arange(experts, dtype=jnp.int32)
    one_hot = (routed_flat[:, None] == labels[None, :]).astype(jnp.bfloat16)
    grouped = one_hot.reshape(groups, span, experts)
    row_ids = jnp.arange(span, dtype=jnp.int32)
    lower = (row_ids[None, :] < row_ids[:, None]).astype(jnp.bfloat16)
    within = jnp.einsum("ij,bje->bie", lower, grouped, preferred_element_type=jnp.float32)
    group_sums = jnp.sum(grouped.astype(jnp.float32), axis=1)
    group_before = jnp.cumsum(group_sums, axis=0) - group_sums
    earlier = within + group_before[:, None, :]
    counted = jnp.sum(earlier * grouped.astype(jnp.float32), axis=2)
    return counted.reshape(pair_total).astype(jnp.int32)


def exchange_body(tokens, out_grad, routes, combine, w_gate, w_up, w_down):
    experts = lax.axis_size("expert")
    tok_rows = tokens.shape[0]
    col_width = tokens.shape[1]
    choose_count = routes.shape[1]
    per_pair = tok_rows * choose_count // experts
    capacity = per_pair + per_pair // 8
    routed_flat = routes.reshape(-1)
    pair_total = routed_flat.shape[0]
    position = pair_positions(routed_flat, experts)
    target = routed_flat * capacity + position
    anchor = jnp.full((experts * capacity,), pair_total, jnp.int32)
    anchor = anchor.at[target].set(jnp.arange(pair_total, dtype=jnp.int32))
    is_live = anchor < pair_total
    safe_anchor = jnp.minimum(anchor, pair_total - 1)
    token_of = safe_anchor // choose_count
    scale = combine.reshape(-1)[safe_anchor] * is_live.astype(jnp.float32)
    full_tokens, full_grads = (
        lax.all_gather(tokens, "etp", axis=1, tiled=True),
        lax.all_gather(out_grad, "etp", axis=1, tiled=True),
    )
    inputs_sent, grads_sent = pack_rows(full_tokens, full_grads, token_of, scale, is_live)
    rows_x, rows_g = (
        lax.all_to_all(inputs_sent, "expert", split_axis=0, concat_axis=0, tiled=True),
        lax.all_to_all(grads_sent, "expert", split_axis=0, concat_axis=0, tiled=True),
    )
    gate_w = w_gate[0]
    up_w = w_up[0]
    down_w = w_down[0]
    gate = lax.dot_general(rows_x, gate_w, CONTRACT_LAST, preferred_element_type=jnp.float32)
    up = lax.dot_general(rows_x, up_w, CONTRACT_LAST, preferred_element_type=jnp.float32)
    hidden_grad = lax.dot_general(rows_g, down_w, CONTRACT_LAST, preferred_element_type=jnp.float32)
    sigma = jax.nn.sigmoid(gate)
    silu = gate * sigma
    acts = (silu * up).astype(jnp.bfloat16)
    grad_down = lax.dot_general(acts, rows_g, CONTRACT_FIRST, preferred_element_type=jnp.float32)
    gate_term = (hidden_grad * up * sigma * (1.0 + gate * (1.0 - sigma))).astype(jnp.bfloat16)
    up_term = (hidden_grad * silu).astype(jnp.bfloat16)
    grad_gate = lax.dot_general(
        gate_term, rows_x, CONTRACT_FIRST, preferred_element_type=jnp.float32
    )
    grad_up = lax.dot_general(up_term, rows_x, CONTRACT_FIRST, preferred_element_type=jnp.float32)
    swapped_gate, swapped_up = (
        lax.all_to_all(gate_w, "etp", split_axis=1, concat_axis=0, tiled=True),
        lax.all_to_all(up_w, "etp", split_axis=1, concat_axis=0, tiled=True),
    )
    running = jnp.dot(
        lax.all_gather(gate_term, "etp", axis=1, tiled=True),
        swapped_gate,
        preferred_element_type=jnp.float32,
    )
    slot_grads = running + jnp.dot(
        lax.all_gather(up_term, "etp", axis=1, tiled=True),
        swapped_up,
        preferred_element_type=jnp.float32,
    )
    slot_grads = slot_grads.astype(jnp.bfloat16)
    returned = lax.all_to_all(slot_grads, "expert", split_axis=0, concat_axis=0, tiled=True)
    picked = returned[target].astype(jnp.float32).reshape(tok_rows, choose_count, col_width)
    grad_tokens = jnp.sum(picked, axis=1).astype(jnp.bfloat16)
    return (
        grad_tokens,
        grad_gate.astype(jnp.bfloat16)[None],
        grad_up.astype(jnp.bfloat16)[None],
        grad_down.astype(jnp.bfloat16)[None],
    )


def pack_kernel(tokens_ref, grads_ref, routes_ref, combine_ref, out_ref):
    rows = tokens_ref.shape[0]
    out_ref[:rows] = tokens_ref[...]
    out_ref[rows:2 * rows] = grads_ref[...]
    top = routes_ref.shape[1]
    routes = routes_ref[...].astype(jnp.float32).T
    weights = combine_ref[...].T
    high = weights.astype(jnp.bfloat16).astype(jnp.float32)
    middle = (weights - high).astype(jnp.bfloat16).astype(jnp.float32)
    low = weights - high - middle
    blank = jnp.zeros((INFO_ROWS - 4, rows), jnp.float32)
    for k in range(top):
        own = slice(k, k + 1)
        column = jnp.concatenate([routes[own], high[own], middle[own], low[own], blank], axis=0)
        out_ref[2 * rows:, k * rows:(k + 1) * rows] = column.astype(jnp.bfloat16)


def pack_share(tokens, out_grad, routes, combine):
    rows, width = tokens.shape
    return pl.pallas_call(
        pack_kernel,
        out_shape=jax.ShapeDtypeStruct((2 * rows + INFO_ROWS, width), jnp.bfloat16),
        name="pack",
    )(tokens, out_grad, routes, combine)


def expert_kernel(chained, top, rows, place_ref, *refs):
    shares, refs = refs[:8], refs[8:]
    wg_ref, wu_ref, wd_ref = refs[:3]
    refs = refs[3 + (5 if chained else 0):]
    near_ref, far_ref, rx_ref, rg_ref, act_ref, gt_ref, ut_ref = refs
    me = place_ref[0].astype(jnp.float32)
    own_half = place_ref[1]
    width = shares[0].shape[1]
    blocks = 4
    span = blocks * rows
    slots = rx_ref.shape[0]
    named, weights = [], []
    for b in range(blocks):
        hits, weight = 0.0, 0.0
        for k in range(top):
            info = shares[2 * b][2 * rows:, k * rows:(k + 1) * rows].astype(jnp.float32)
            hit = info[0:1] == me
            hits += hit.astype(jnp.float32)
            weight += jnp.where(hit, info[1:2] + info[2:3] + info[3:4], 0.0)
        named.append(hits)
        weights.append(weight)
    named = jnp.concatenate(named, axis=1)
    weights = jnp.concatenate(weights, axis=1)
    earlier = (
        lax.broadcasted_iota(jnp.int32, (span, span), 0)
        < lax.broadcasted_iota(jnp.int32, (span, span), 1)
    ).astype(jnp.bfloat16)
    counted = jnp.dot(
        jnp.broadcast_to(named, (16, span)).astype(jnp.bfloat16),
        earlier,
        preferred_element_type=jnp.float32,
    )[:1]
    slot_of = jnp.where(named > 0.0, counted.astype(jnp.int32), -1)
    chosen = slot_of == lax.broadcasted_iota(jnp.int32, (slots, span), 0)
    pick = chosen.astype(jnp.bfloat16)
    scale = jnp.sum(jnp.where(chosen, weights, 0.0), axis=1, keepdims=True)

    gate = up = hidden_grad = 0.0
    for h in range(2):
        start = pl.multiple_of((own_half if h == 0 else 1 - own_half) * width, width)
        cols = pl.ds(start, width)
        x = jnp.concatenate([shares[2 * b + h][:rows] for b in range(blocks)], axis=0)
        rx = jnp.dot(pick, x, preferred_element_type=jnp.float32).astype(jnp.bfloat16)
        rx_ref[:, cols] = rx
        gate += lax.dot_general(rx, wg_ref[:, cols], CONTRACT_LAST, preferred_element_type=jnp.float32)
        up += lax.dot_general(rx, wu_ref[:, cols], CONTRACT_LAST, preferred_element_type=jnp.float32)
        g = jnp.concatenate([shares[2 * b + h][rows:2 * rows] for b in range(blocks)], axis=0)
        rg = (scale * jnp.dot(pick, g, preferred_element_type=jnp.float32)).astype(jnp.bfloat16)
        rg_ref[:, cols] = rg
        hidden_grad += lax.dot_general(rg, wd_ref[:, cols], CONTRACT_LAST, preferred_element_type=jnp.float32)

    sigma = 1.0 / (1.0 + jnp.exp(-gate))
    silu = gate * sigma
    act_ref[...] = (silu * up).astype(jnp.bfloat16)
    gate_term = (hidden_grad * up * sigma * (1.0 + gate * (1.0 - sigma))).astype(jnp.bfloat16)
    up_term = (hidden_grad * silu).astype(jnp.bfloat16)
    gt_ref[...] = gate_term
    ut_ref[...] = up_term
    for h in range(2):
        start = pl.multiple_of((own_half if h == 0 else 1 - own_half) * width, width)
        cols = pl.ds(start, width)
        slot = jnp.dot(gate_term, wg_ref[:, cols], preferred_element_type=jnp.float32)
        slot += jnp.dot(up_term, wu_ref[:, cols], preferred_element_type=jnp.float32)
        back = lax.dot_general(
            pick, slot.astype(jnp.bfloat16), CONTRACT_FIRST, preferred_element_type=jnp.float32
        ).astype(jnp.bfloat16)
        for b in range(blocks):
            target = near_ref if b < 2 else far_ref
            target[b % 2, h] = back[b * rows:(b + 1) * rows]


def run_experts(index, chunks, place, shares, weights, kept, top, rows, slots):
    width = shares[0].shape[1]
    hidden, features = weights[0].shape
    vmem = pl.BlockSpec(memory_space=pltpu.VMEM)
    part = jax.ShapeDtypeStruct((2, 2, rows, width), jnp.bfloat16)
    wide = jax.ShapeDtypeStruct((chunks * slots, features), jnp.bfloat16)
    narrow = jax.ShapeDtypeStruct((chunks * slots, hidden), jnp.bfloat16)
    wide_block = pl.BlockSpec((slots, features), lambda i: (index, 0))
    narrow_block = pl.BlockSpec((slots, hidden), lambda i: (index, 0))
    part_block = pl.BlockSpec(part.shape, lambda i: (0, 0, 0, 0))
    first_kept = 1 + len(shares) + 3
    return pl.pallas_call(
        functools.partial(expert_kernel, kept is not None, top, rows),
        grid=(1,),
        in_specs=[pl.BlockSpec(memory_space=pltpu.SMEM)]
        + [pl.BlockSpec(s.shape, lambda i: (0, 0)) for s in shares]
        + [pl.BlockSpec((hidden, features), lambda i: (0, 0))] * 3
        + [pl.BlockSpec(memory_space=pl.ANY)] * (0 if kept is None else 5),
        out_specs=[part_block] * 2 + [wide_block] * 2 + [narrow_block] * 3,
        out_shape=[part, part, wide, wide, narrow, narrow, narrow],
        input_output_aliases={} if kept is None else {first_kept + i: 2 + i for i in range(5)},
        compiler_params=pltpu.CompilerParams(vmem_limit_bytes=56 * 1024 * 1024),
        cost_estimate=pl.CostEstimate(
            flops=2 * slots * features * (hidden * 5 + 4 * rows * 3),
            bytes_accessed=2 * (8 * shares[0].size + 3 * hidden * features + slots * (2 * features + 3 * hidden)),
            transcendentals=slots * hidden,
        ),
        name="experts",
    )(place, *shares, *weights, *(kept or ()))


def ring_order(length):
    return list(range(0, min(1, length))) + list(range(1, length, 2)) + list(range(2, length, 2))[::-1]


def gather_body(tokens, out_grad, routes, combine, w_gate, w_up, w_down):
    experts = lax.axis_size("expert")
    chunks = experts // 4
    rows, width = tokens.shape
    top = routes.shape[1]
    per_pair = rows * top // experts
    capacity = per_pair + per_pair // 8
    slots = -(-4 * capacity // 16) * 16
    order = ring_order(chunks)
    ahead = [
        (order[i] * 4 + r, order[(i + 1) % chunks] * 4 + r) for i in range(chunks) for r in range(4)
    ]

    def to_ring(value):
        return lax.ppermute(value, "expert", ahead)

    def to_side(value):
        return lax.ppermute(value, "expert", [(e, e ^ 2) for e in range(experts)])

    def to_core(value):
        return lax.ppermute(value, "expert", [(e, e ^ 1) for e in range(experts)])

    def to_half(value):
        return lax.ppermute(value, "etp", [(0, 1), (1, 0)])

    place = jnp.stack([lax.axis_index("expert"), lax.axis_index("etp")]).astype(jnp.int32)
    weights = (w_gate[0], w_up[0], w_down[0])
    share = pack_share(tokens, out_grad, routes, combine)
    kept = None
    running = None
    for c in range(chunks):
        if c > 0:
            share = to_ring(share)
        across, aside = to_half(share), to_side(share)
        both = to_half(aside) if c % 2 == 0 else to_side(across)
        near = [share, across, aside, both]
        far = [to_core(s) for s in near]
        near_part, far_part, *kept = run_experts(
            c, chunks, place, near + far, weights, kept, top, rows, slots
        )
        mine = near_part.astype(jnp.float32) + to_core(far_part).astype(jnp.float32)
        if c % 2 == 0:
            mine = mine[0] + to_side(mine[1].astype(jnp.bfloat16)).astype(jnp.float32)
            mine = mine[0] + to_half(mine[1].astype(jnp.bfloat16)).astype(jnp.float32)
        else:
            mine = mine[:, 0] + to_half(mine[:, 1].astype(jnp.bfloat16)).astype(jnp.float32)
            mine = mine[0] + to_side(mine[1].astype(jnp.bfloat16)).astype(jnp.float32)
        if c == 0:
            own = mine
        else:
            running = mine if c == 1 else mine + running.astype(jnp.float32)
            running = to_ring(running.astype(jnp.bfloat16))
    grad_tokens = (own if running is None else own + running.astype(jnp.float32)).astype(jnp.bfloat16)
    rows_x, rows_g, acts, gate_term, up_term = kept
    grad_down = lax.dot_general(acts, rows_g, CONTRACT_FIRST, preferred_element_type=jnp.float32)
    grad_gate = lax.dot_general(gate_term, rows_x, CONTRACT_FIRST, preferred_element_type=jnp.float32)
    grad_up = lax.dot_general(up_term, rows_x, CONTRACT_FIRST, preferred_element_type=jnp.float32)
    return (
        grad_tokens,
        grad_gate.astype(jnp.bfloat16)[None],
        grad_up.astype(jnp.bfloat16)[None],
        grad_down.astype(jnp.bfloat16)[None],
    )


def solution(mesh):
    experts = mesh.shape["expert"]

    def body(tokens, out_grad, routes, combine, w_gate, w_up, w_down):
        rows, width = tokens.shape
        top = routes.shape[1]
        gathers = top * 4 >= experts and experts % 4 == 0 and mesh.shape["etp"] == 2
        run = gather_body if gathers and top * rows <= width else exchange_body
        return run(tokens, out_grad, routes, combine, w_gate, w_up, w_down)

    placed = (
        P("expert", "etp"),
        P("expert", "etp"),
        P("expert", None),
        P("expert", None),
        P("expert", "etp", None),
        P("expert", "etp", None),
        P("expert", "etp", None),
    )
    return jax.shard_map(
        body,
        mesh=mesh,
        in_specs=placed,
        out_specs=(
            P("expert", "etp"),
            P("expert", "etp", None),
            P("expert", "etp", None),
            P("expert", "etp", None),
        ),
        check_vma=False,
    )
```

```python
import functools

import jax
import jax.numpy as jnp
from jax import lax
from jax.experimental import pallas as pl
from jax.experimental.pallas import tpu as pltpu
from jax.sharding import PartitionSpec as P

CONTRACT_LAST = (((1,), (1,)), ((), ()))
CONTRACT_FIRST = (((0,), (0,)), ((), ()))
INFO_ROWS = 16


def pack_rows(token_rows, grad_rows, token_of, scale, is_live):
    mask = is_live[:, None].astype(token_rows.dtype)
    inputs_sent = token_rows[token_of] * mask
    grads_sent = (scale[:, None] * grad_rows[token_of].astype(jnp.float32)).astype(jnp.bfloat16)
    return (inputs_sent, grads_sent)


def pair_positions(routed_flat, experts):
    pair_total = routed_flat.shape[0]
    span = 128
    groups = pair_total // span
    labels = jnp.arange(experts, dtype=jnp.int32)
    one_hot = (routed_flat[:, None] == labels[None, :]).astype(jnp.bfloat16)
    grouped = one_hot.reshape(groups, span, experts)
    row_ids = jnp.arange(span, dtype=jnp.int32)
    lower = (row_ids[None, :] < row_ids[:, None]).astype(jnp.bfloat16)
    within = jnp.einsum("ij,bje->bie", lower, grouped, preferred_element_type=jnp.float32)
    group_sums = jnp.sum(grouped.astype(jnp.float32), axis=1)
    group_before = jnp.cumsum(group_sums, axis=0) - group_sums
    earlier = within + group_before[:, None, :]
    counted = jnp.sum(earlier * grouped.astype(jnp.float32), axis=2)
    return counted.reshape(pair_total).astype(jnp.int32)


def exchange_body(tokens, out_grad, routes, combine, w_gate, w_up, w_down):
    experts = lax.axis_size("expert")
    tok_rows = tokens.shape[0]
    col_width = tokens.shape[1]
    choose_count = routes.shape[1]
    per_pair = tok_rows * choose_count // experts
    capacity = per_pair + per_pair // 8
    routed_flat = routes.reshape(-1)
    pair_total = routed_flat.shape[0]
    position = pair_positions(routed_flat, experts)
    target = routed_flat * capacity + position
    anchor = jnp.full((experts * capacity,), pair_total, jnp.int32)
    anchor = anchor.at[target].set(jnp.arange(pair_total, dtype=jnp.int32))
    is_live = anchor < pair_total
    safe_anchor = jnp.minimum(anchor, pair_total - 1)
    token_of = safe_anchor // choose_count
    scale = combine.reshape(-1)[safe_anchor] * is_live.astype(jnp.float32)
    full_tokens, full_grads = (
        lax.all_gather(tokens, "etp", axis=1, tiled=True),
        lax.all_gather(out_grad, "etp", axis=1, tiled=True),
    )
    inputs_sent, grads_sent = pack_rows(full_tokens, full_grads, token_of, scale, is_live)
    rows_x, rows_g = (
        lax.all_to_all(inputs_sent, "expert", split_axis=0, concat_axis=0, tiled=True),
        lax.all_to_all(grads_sent, "expert", split_axis=0, concat_axis=0, tiled=True),
    )
    gate_w = w_gate[0]
    up_w = w_up[0]
    down_w = w_down[0]
    gate = lax.dot_general(rows_x, gate_w, CONTRACT_LAST, preferred_element_type=jnp.float32)
    up = lax.dot_general(rows_x, up_w, CONTRACT_LAST, preferred_element_type=jnp.float32)
    hidden_grad = lax.dot_general(rows_g, down_w, CONTRACT_LAST, preferred_element_type=jnp.float32)
    sigma = jax.nn.sigmoid(gate)
    silu = gate * sigma
    acts = (silu * up).astype(jnp.bfloat16)
    grad_down = lax.dot_general(acts, rows_g, CONTRACT_FIRST, preferred_element_type=jnp.float32)
    gate_term = (hidden_grad * up * sigma * (1.0 + gate * (1.0 - sigma))).astype(jnp.bfloat16)
    up_term = (hidden_grad * silu).astype(jnp.bfloat16)
    grad_gate = lax.dot_general(
        gate_term, rows_x, CONTRACT_FIRST, preferred_element_type=jnp.float32
    )
    grad_up = lax.dot_general(up_term, rows_x, CONTRACT_FIRST, preferred_element_type=jnp.float32)
    swapped_gate, swapped_up = (
        lax.all_to_all(gate_w, "etp", split_axis=1, concat_axis=0, tiled=True),
        lax.all_to_all(up_w, "etp", split_axis=1, concat_axis=0, tiled=True),
    )
    running = jnp.dot(
        lax.all_gather(gate_term, "etp", axis=1, tiled=True),
        swapped_gate,
        preferred_element_type=jnp.float32,
    )
    slot_grads = running + jnp.dot(
        lax.all_gather(up_term, "etp", axis=1, tiled=True),
        swapped_up,
        preferred_element_type=jnp.float32,
    )
    slot_grads = slot_grads.astype(jnp.bfloat16)
    returned = lax.all_to_all(slot_grads, "expert", split_axis=0, concat_axis=0, tiled=True)
    picked = returned[target].astype(jnp.float32).reshape(tok_rows, choose_count, col_width)
    grad_tokens = jnp.sum(picked, axis=1).astype(jnp.bfloat16)
    return (
        grad_tokens,
        grad_gate.astype(jnp.bfloat16)[None],
        grad_up.astype(jnp.bfloat16)[None],
        grad_down.astype(jnp.bfloat16)[None],
    )


def pack_kernel(tokens_ref, grads_ref, routes_ref, combine_ref, out_ref, info_ref, sems):
    rows = tokens_ref.shape[0]
    moves = [
        pltpu.make_async_copy(tokens_ref, out_ref.at[pl.ds(0, rows)], sems.at[0]),
        pltpu.make_async_copy(grads_ref, out_ref.at[pl.ds(rows, rows)], sems.at[1]),
        pltpu.make_async_copy(info_ref, out_ref.at[pl.ds(2 * rows, INFO_ROWS)], sems.at[2]),
    ]
    moves[0].start()
    moves[1].start()
    top = routes_ref.shape[0]
    routes = routes_ref[...].astype(jnp.float32)
    weights = combine_ref[...]
    high = weights.astype(jnp.bfloat16).astype(jnp.float32)
    middle = (weights - high).astype(jnp.bfloat16).astype(jnp.float32)
    low = weights - high - middle
    blank = jnp.zeros((INFO_ROWS - 4, rows), jnp.float32)
    info_ref[...] = jnp.zeros(info_ref.shape, info_ref.dtype)
    for k in range(top):
        own = slice(k, k + 1)
        column = jnp.concatenate([routes[own], high[own], middle[own], low[own], blank], axis=0)
        info_ref[:, k * rows:(k + 1) * rows] = column.astype(jnp.bfloat16)
    moves[2].start()
    for move in moves:
        move.wait()


def pack_share(tokens, out_grad, routes, combine):
    rows, width = tokens.shape
    anywhere = pl.BlockSpec(memory_space=pl.ANY)
    vmem = pl.BlockSpec(memory_space=pltpu.VMEM)
    return pl.pallas_call(
        pack_kernel,
        in_specs=[anywhere, anywhere, vmem, vmem],
        out_specs=anywhere,
        out_shape=jax.ShapeDtypeStruct((2 * rows + INFO_ROWS, width), jnp.bfloat16),
        scratch_shapes=[pltpu.VMEM((INFO_ROWS, width), jnp.bfloat16), pltpu.SemaphoreType.DMA((3,))],
        cost_estimate=pl.CostEstimate(flops=0, bytes_accessed=8 * rows * width, transcendentals=0),
        name="pack",
    )(tokens, out_grad, routes.T, combine.T)


def expert_kernel(index, chained, top, place_ref, *refs):
    shares, weight_refs = refs[:8], refs[8:11]
    refs = refs[11 + (5 if chained else 0):]
    near_ref, far_ref = refs[:2]
    kept_refs = refs[2:7]
    x_buf, g_buf, info_buf, wg_ref, wu_ref, wd_ref, rx_ref, rg_ref, act_ref, gt_ref, ut_ref, slot_ref, back_ref = refs[7:20]
    in_sems, weight_sems, kept_sems, out_sems = refs[20:]
    me = place_ref[0].astype(jnp.float32)
    own_half = place_ref[1]
    core = place_ref[2]
    other = 1 - core
    halves, blocks, rows, width = x_buf.shape
    slots = rx_ref.shape[0]
    pairs = blocks // 2
    pair_slots = slots // pairs

    spots = [(0, 0), (core, other), (other, core), (1, 1),
             (0, 2), (other, 2 + core), (core, 2 + other), (1, 3)]
    info_moves = [
        pltpu.make_async_copy(
            shares[s].at[pl.ds(2 * rows, INFO_ROWS)], info_buf.at[b], in_sems.at[16 + b]
        )
        for b, s in enumerate((0, 3, 4, 7))
    ]
    x_moves = [
        pltpu.make_async_copy(shares[s].at[pl.ds(0, rows)], x_buf.at[spots[s]], in_sems.at[s])
        for s in range(8)
    ]
    g_moves = [
        pltpu.make_async_copy(shares[s].at[pl.ds(rows, rows)], g_buf.at[spots[s]], in_sems.at[8 + s])
        for s in range(8)
    ]
    weight_moves = [
        pltpu.make_async_copy(source, target, weight_sems.at[i])
        for i, (source, target) in enumerate(zip(weight_refs, (wg_ref, wu_ref, wd_ref)))
    ]
    kept_moves = [
        pltpu.make_async_copy(
            source, target.at[pl.ds(index * slots, slots)], kept_sems.at[i]
        )
        for i, (source, target) in enumerate(zip((rx_ref, rg_ref, act_ref, gt_ref, ut_ref), kept_refs))
    ]
    out_moves = [
        pltpu.make_async_copy(
            back_ref.at[spots[s]], (near_ref if s < 4 else far_ref).at[s % 4], out_sems.at[s]
        )
        for s in range(8)
    ]
    for move in info_moves + x_moves + weight_moves[:2] + g_moves + weight_moves[2:]:
        move.start()

    for move in info_moves:
        move.wait()
    earlier = (
        lax.broadcasted_iota(jnp.int32, (2 * rows, 2 * rows), 0)
        < lax.broadcasted_iota(jnp.int32, (2 * rows, 2 * rows), 1)
    ).astype(jnp.bfloat16)
    picks, scales = [], []
    for p in range(pairs):
        named, weights = [], []
        for b in (2 * p, 2 * p + 1):
            hits, weight = 0.0, 0.0
            for k in range(top):
                info = info_buf[b, :, k * rows:(k + 1) * rows].astype(jnp.float32)
                hit = info[0:1] == me
                hits += hit.astype(jnp.float32)
                weight += jnp.where(hit, info[1:2] + info[2:3] + info[3:4], 0.0)
            named.append(hits)
            weights.append(weight)
        named = jnp.concatenate(named, axis=1)
        weights = jnp.concatenate(weights, axis=1)
        counted = jnp.dot(
            jnp.broadcast_to(named, (16, 2 * rows)).astype(jnp.bfloat16),
            earlier,
            preferred_element_type=jnp.float32,
        )[:1]
        slot_of = jnp.where(named > 0.0, counted.astype(jnp.int32), -1)
        chosen = slot_of == lax.broadcasted_iota(jnp.int32, (pair_slots, 2 * rows), 0)
        picks.append(chosen.astype(jnp.bfloat16))
        scales.append(jnp.sum(jnp.where(chosen, weights, 0.0), axis=1, keepdims=True))

    def columns(h):
        return pl.ds(pl.multiple_of((own_half if h == 0 else 1 - own_half) * width, width), width)

    def slot_rows(p):
        return slice(p * pair_slots, (p + 1) * pair_slots)

    for move in x_moves:
        move.wait()
    for h in range(halves):
        for p in range(pairs):
            x = x_buf[h, 2 * p:2 * p + 2].reshape(2 * rows, width)
            picked = jnp.dot(picks[p], x, preferred_element_type=jnp.float32)
            rx_ref[slot_rows(p), columns(h)] = picked.astype(jnp.bfloat16)
    kept_moves[0].start()
    weight_moves[0].wait()
    gate = lax.dot_general(rx_ref[...], wg_ref[...], CONTRACT_LAST, preferred_element_type=jnp.float32)
    weight_moves[1].wait()
    up = lax.dot_general(rx_ref[...], wu_ref[...], CONTRACT_LAST, preferred_element_type=jnp.float32)
    sigma = 1.0 / (1.0 + jnp.exp(-gate))
    silu = gate * sigma
    act_ref[...] = (silu * up).astype(jnp.bfloat16)
    kept_moves[2].start()

    for move in g_moves:
        move.wait()
    for h in range(halves):
        for p in range(pairs):
            g = g_buf[h, 2 * p:2 * p + 2].reshape(2 * rows, width)
            picked = jnp.dot(picks[p], g, preferred_element_type=jnp.float32)
            rg_ref[slot_rows(p), columns(h)] = (scales[p] * picked).astype(jnp.bfloat16)
    kept_moves[1].start()
    weight_moves[2].wait()
    hidden_grad = lax.dot_general(rg_ref[...], wd_ref[...], CONTRACT_LAST, preferred_element_type=jnp.float32)
    gt_ref[...] = (hidden_grad * up * sigma * (1.0 + gate * (1.0 - sigma))).astype(jnp.bfloat16)
    ut_ref[...] = (hidden_grad * silu).astype(jnp.bfloat16)
    kept_moves[3].start()
    kept_moves[4].start()

    slot = jnp.dot(gt_ref[...], wg_ref[...], preferred_element_type=jnp.float32)
    slot += jnp.dot(ut_ref[...], wu_ref[...], preferred_element_type=jnp.float32)
    slot_ref[...] = slot.astype(jnp.bfloat16)
    for p in reversed(range(pairs)):
        for h in range(halves):
            back = lax.dot_general(
                picks[p], slot_ref[slot_rows(p), columns(h)], CONTRACT_FIRST,
                preferred_element_type=jnp.float32,
            )
            back_ref[h, 2 * p:2 * p + 2] = back.astype(jnp.bfloat16).reshape(2, rows, width)
        for s in range(4 * p, 4 * p + 4):
            out_moves[s].start()
    for move in kept_moves + out_moves:
        move.wait()


def run_experts(index, chunks, place, shares, weights, kept, top, rows, slots):
    width = shares[0].shape[1]
    hidden, features = weights[0].shape
    anywhere = pl.BlockSpec(memory_space=pl.ANY)
    part = jax.ShapeDtypeStruct((4, rows, width), jnp.bfloat16)
    wide = jax.ShapeDtypeStruct((chunks * slots, features), jnp.bfloat16)
    narrow = jax.ShapeDtypeStruct((chunks * slots, hidden), jnp.bfloat16)
    held = pltpu.VMEM((2, 4, rows, width), jnp.bfloat16)
    first_kept = 1 + len(shares) + 3
    return pl.pallas_call(
        functools.partial(expert_kernel, index, kept is not None, top),
        in_specs=[pl.BlockSpec(memory_space=pltpu.SMEM)] + [anywhere] * (11 if kept is None else 16),
        out_specs=[anywhere] * 7,
        out_shape=[part, part, wide, wide, narrow, narrow, narrow],
        scratch_shapes=[held, held, pltpu.VMEM((4, INFO_ROWS, width), jnp.bfloat16)]
        + [pltpu.VMEM((hidden, features), jnp.bfloat16)] * 3
        + [pltpu.VMEM((slots, features), jnp.bfloat16)] * 2
        + [pltpu.VMEM((slots, hidden), jnp.bfloat16)] * 3
        + [pltpu.VMEM((slots, features), jnp.bfloat16), held]
        + [pltpu.SemaphoreType.DMA((n,)) for n in (20, 3, 5, 8)],
        input_output_aliases={} if kept is None else {first_kept + i: 2 + i for i in range(5)},
        compiler_params=pltpu.CompilerParams(vmem_limit_bytes=32 * 1024 * 1024),
        cost_estimate=pl.CostEstimate(
            flops=2 * slots * features * (hidden * 5 + 2 * rows * 3),
            bytes_accessed=2 * (8 * shares[0].size + 3 * hidden * features + slots * (2 * features + 3 * hidden)),
            transcendentals=slots * hidden,
        ),
        name="experts",
    )(place, *shares, *weights, *(kept or ()))


def ring_order(length):
    return list(range(0, min(1, length))) + list(range(1, length, 2)) + list(range(2, length, 2))[::-1]


def gather_body(tokens, out_grad, routes, combine, w_gate, w_up, w_down):
    experts = lax.axis_size("expert")
    chunks = experts // 4
    rows, width = tokens.shape
    top = routes.shape[1]
    per_pair = rows * top // experts
    capacity = per_pair + per_pair // 8
    slots = 2 * (-(-2 * capacity // 16) * 16)
    order = ring_order(chunks)
    after = {order[i]: order[(i + 1) % chunks] for i in range(chunks)}
    devices = [(e, h) for e in range(experts) for h in range(2)]

    def permute(value, target):
        pairs = [(e * 2 + h, target(e, h)[0] * 2 + target(e, h)[1]) for e, h in devices]
        return lax.ppermute(value, ("expert", "etp"), pairs)

    def to_ring(value):
        return permute(value, lambda e, h: (after[e // 4] * 4 + e % 4, h))

    def to_core(value):
        return permute(value, lambda e, h: (e ^ 1, h))

    def to_first(value):
        return permute(value, lambda e, h: (e, h ^ 1) if e % 2 else (e ^ 2, h))

    def to_second(value):
        return permute(value, lambda e, h: (e ^ 2, h) if e % 2 else (e, h ^ 1))

    me = lax.axis_index("expert")
    place = jnp.stack([me, lax.axis_index("etp"), me % 2]).astype(jnp.int32)
    weights = (w_gate[0], w_up[0], w_down[0])
    share = pack_share(tokens, out_grad, routes, combine)
    kept = None
    running = None
    for c in range(chunks):
        first, second = to_first(share), to_second(share)
        if c + 1 < chunks:
            following = to_ring(share)
            first, second, following = lax.optimization_barrier((first, second, following))
        else:
            following = None
        near = [share, first, second, to_second(first)]
        far = [to_core(s) for s in near]
        share = following
        near_part, far_part, *kept = run_experts(
            c, chunks, place, near + far, weights, kept, top, rows, slots
        )
        mine = near_part.astype(jnp.float32) + to_core(far_part).astype(jnp.float32)
        mine = mine[:2] + to_second(mine[2:].astype(jnp.bfloat16)).astype(jnp.float32)
        mine = mine[0] + to_first(mine[1].astype(jnp.bfloat16)).astype(jnp.float32)
        if c == 0:
            own = mine
        else:
            running = mine if c == 1 else mine + running.astype(jnp.float32)
            running = to_ring(running.astype(jnp.bfloat16))
    grad_tokens = (own if running is None else own + running.astype(jnp.float32)).astype(jnp.bfloat16)
    rows_x, rows_g, acts, gate_term, up_term = kept
    grad_down = lax.dot_general(acts, rows_g, CONTRACT_FIRST, preferred_element_type=jnp.float32)
    grad_gate = lax.dot_general(gate_term, rows_x, CONTRACT_FIRST, preferred_element_type=jnp.float32)
    grad_up = lax.dot_general(up_term, rows_x, CONTRACT_FIRST, preferred_element_type=jnp.float32)
    return (
        grad_tokens,
        grad_gate.astype(jnp.bfloat16)[None],
        grad_up.astype(jnp.bfloat16)[None],
        grad_down.astype(jnp.bfloat16)[None],
    )


def solution(mesh):
    experts = mesh.shape["expert"]

    def body(tokens, out_grad, routes, combine, w_gate, w_up, w_down):
        rows, width = tokens.shape
        top = routes.shape[1]
        gathers = top * 4 >= experts and experts % 4 == 0 and mesh.shape["etp"] == 2
        run = gather_body if gathers and top * rows <= width else exchange_body
        return run(tokens, out_grad, routes, combine, w_gate, w_up, w_down)

    placed = (
        P("expert", "etp"),
        P("expert", "etp"),
        P("expert", None),
        P("expert", None),
        P("expert", "etp", None),
        P("expert", "etp", None),
        P("expert", "etp", None),
    )
    return jax.shard_map(
        body,
        mesh=mesh,
        in_specs=placed,
        out_specs=(
            P("expert", "etp"),
            P("expert", "etp", None),
            P("expert", "etp", None),
            P("expert", "etp", None),
        ),
        check_vma=False,
    )
```

```python
import functools

import jax
import jax.numpy as jnp
from jax import lax
from jax.experimental import pallas as pl
from jax.experimental.pallas import tpu as pltpu
from jax.sharding import PartitionSpec as P

CONTRACT_LAST = (((1,), (1,)), ((), ()))
CONTRACT_FIRST = (((0,), (0,)), ((), ()))
INFO_ROWS = 16
VMEM_LIMIT = 24 * 1024 * 1024


def pack_rows(token_rows, grad_rows, token_of, scale, is_live):
    mask = is_live[:, None].astype(token_rows.dtype)
    inputs_sent = token_rows[token_of] * mask
    grads_sent = (scale[:, None] * grad_rows[token_of].astype(jnp.float32)).astype(jnp.bfloat16)
    return (inputs_sent, grads_sent)


def pair_positions(routed_flat, experts):
    pair_total = routed_flat.shape[0]
    span = 128
    groups = pair_total // span
    labels = jnp.arange(experts, dtype=jnp.int32)
    one_hot = (routed_flat[:, None] == labels[None, :]).astype(jnp.bfloat16)
    grouped = one_hot.reshape(groups, span, experts)
    row_ids = jnp.arange(span, dtype=jnp.int32)
    lower = (row_ids[None, :] < row_ids[:, None]).astype(jnp.bfloat16)
    within = jnp.einsum("ij,bje->bie", lower, grouped, preferred_element_type=jnp.float32)
    group_sums = jnp.sum(grouped.astype(jnp.float32), axis=1)
    group_before = jnp.cumsum(group_sums, axis=0) - group_sums
    earlier = within + group_before[:, None, :]
    counted = jnp.sum(earlier * grouped.astype(jnp.float32), axis=2)
    return counted.reshape(pair_total).astype(jnp.int32)


def exchange_body(tokens, out_grad, routes, combine, w_gate, w_up, w_down):
    experts = lax.axis_size("expert")
    tok_rows = tokens.shape[0]
    col_width = tokens.shape[1]
    choose_count = routes.shape[1]
    per_pair = tok_rows * choose_count // experts
    capacity = per_pair + per_pair // 8
    routed_flat = routes.reshape(-1)
    pair_total = routed_flat.shape[0]
    position = pair_positions(routed_flat, experts)
    target = routed_flat * capacity + position
    anchor = jnp.full((experts * capacity,), pair_total, jnp.int32)
    anchor = anchor.at[target].set(jnp.arange(pair_total, dtype=jnp.int32))
    is_live = anchor < pair_total
    safe_anchor = jnp.minimum(anchor, pair_total - 1)
    token_of = safe_anchor // choose_count
    scale = combine.reshape(-1)[safe_anchor] * is_live.astype(jnp.float32)
    full_tokens, full_grads = (
        lax.all_gather(tokens, "etp", axis=1, tiled=True),
        lax.all_gather(out_grad, "etp", axis=1, tiled=True),
    )
    inputs_sent, grads_sent = pack_rows(full_tokens, full_grads, token_of, scale, is_live)
    rows_x, rows_g = (
        lax.all_to_all(inputs_sent, "expert", split_axis=0, concat_axis=0, tiled=True),
        lax.all_to_all(grads_sent, "expert", split_axis=0, concat_axis=0, tiled=True),
    )
    gate_w = w_gate[0]
    up_w = w_up[0]
    down_w = w_down[0]
    gate = lax.dot_general(rows_x, gate_w, CONTRACT_LAST, preferred_element_type=jnp.float32)
    up = lax.dot_general(rows_x, up_w, CONTRACT_LAST, preferred_element_type=jnp.float32)
    hidden_grad = lax.dot_general(rows_g, down_w, CONTRACT_LAST, preferred_element_type=jnp.float32)
    sigma = jax.nn.sigmoid(gate)
    silu = gate * sigma
    acts = (silu * up).astype(jnp.bfloat16)
    grad_down = lax.dot_general(acts, rows_g, CONTRACT_FIRST, preferred_element_type=jnp.float32)
    gate_term = (hidden_grad * up * sigma * (1.0 + gate * (1.0 - sigma))).astype(jnp.bfloat16)
    up_term = (hidden_grad * silu).astype(jnp.bfloat16)
    grad_gate = lax.dot_general(
        gate_term, rows_x, CONTRACT_FIRST, preferred_element_type=jnp.float32
    )
    grad_up = lax.dot_general(up_term, rows_x, CONTRACT_FIRST, preferred_element_type=jnp.float32)
    swapped_gate, swapped_up = (
        lax.all_to_all(gate_w, "etp", split_axis=1, concat_axis=0, tiled=True),
        lax.all_to_all(up_w, "etp", split_axis=1, concat_axis=0, tiled=True),
    )
    running = jnp.dot(
        lax.all_gather(gate_term, "etp", axis=1, tiled=True),
        swapped_gate,
        preferred_element_type=jnp.float32,
    )
    slot_grads = running + jnp.dot(
        lax.all_gather(up_term, "etp", axis=1, tiled=True),
        swapped_up,
        preferred_element_type=jnp.float32,
    )
    slot_grads = slot_grads.astype(jnp.bfloat16)
    returned = lax.all_to_all(slot_grads, "expert", split_axis=0, concat_axis=0, tiled=True)
    picked = returned[target].astype(jnp.float32).reshape(tok_rows, choose_count, col_width)
    grad_tokens = jnp.sum(picked, axis=1).astype(jnp.bfloat16)
    return (
        grad_tokens,
        grad_gate.astype(jnp.bfloat16)[None],
        grad_up.astype(jnp.bfloat16)[None],
        grad_down.astype(jnp.bfloat16)[None],
    )


def pack_kernel(tokens_ref, grads_ref, routes_ref, combine_ref, out_ref):
    rows = tokens_ref.shape[0]
    out_ref[:rows] = tokens_ref[...]
    out_ref[rows:2 * rows] = grads_ref[...]
    top = routes_ref.shape[0]
    routes = routes_ref[...].astype(jnp.float32)
    weights = combine_ref[...]
    high = weights.astype(jnp.bfloat16).astype(jnp.float32)
    middle = (weights - high).astype(jnp.bfloat16).astype(jnp.float32)
    low = weights - high - middle
    blank = jnp.zeros((INFO_ROWS - 4, rows), jnp.float32)
    for k in range(top):
        own = slice(k, k + 1)
        column = jnp.concatenate([routes[own], high[own], middle[own], low[own], blank], axis=0)
        out_ref[2 * rows:, k * rows:(k + 1) * rows] = column.astype(jnp.bfloat16)


def pack_share(tokens, out_grad, routes, combine):
    rows, width = tokens.shape
    vmem = pl.BlockSpec(memory_space=pltpu.VMEM)
    return pl.pallas_call(
        pack_kernel,
        in_specs=[vmem] * 4,
        out_specs=vmem,
        out_shape=jax.ShapeDtypeStruct((2 * rows + INFO_ROWS, width), jnp.bfloat16),
        cost_estimate=pl.CostEstimate(flops=0, bytes_accessed=8 * rows * width, transcendentals=0),
        name="pack",
    )(tokens, out_grad, routes.T, combine.T)


def expert_kernel(index, chained, top, rows, place_ref, *refs):
    pair_refs = refs[:4]
    wg_ref, wu_ref, wd_ref = refs[4:7]
    refs = refs[7 + (5 if chained else 0):]
    near_ref, far_ref = refs[:2]
    kept_refs = refs[2:7]
    rx_ref, rg_ref, act_ref, gt_ref, ut_ref, slot_ref, sems = refs[7:]
    me = place_ref[0].astype(jnp.float32)
    own_half = place_ref[1]
    core = place_ref[2]
    slots = rx_ref.shape[0]
    width = near_ref.shape[2]
    pair_slots = slots // 2
    kept_moves = [
        pltpu.make_async_copy(source, target.at[pl.ds(index * slots, slots)], sems.at[i])
        for i, (source, target) in enumerate(zip((rx_ref, rg_ref, act_ref, gt_ref, ut_ref), kept_refs))
    ]

    def columns(h):
        return pl.ds(pl.multiple_of((own_half if h == 0 else 1 - own_half) * width, width), width)

    def slot_rows(p):
        return slice(p * pair_slots, (p + 1) * pair_slots)

    def swapped(p):
        return core == 1 if p == 0 else core == 0

    def gathered(p, h, part):
        here = pl.ds(part * rows, rows)
        first, second = pair_refs[2 * p], pair_refs[2 * p + 1]
        if h == 0:
            inner = jnp.where(swapped(p), second[0, here], first[1, here])
            return jnp.concatenate([first[0, here], inner], axis=0)
        inner = jnp.where(swapped(p), first[1, here], second[0, here])
        return jnp.concatenate([inner, second[1, here]], axis=0)

    earlier = (
        lax.broadcasted_iota(jnp.int32, (2 * rows, 2 * rows), 0)
        < lax.broadcasted_iota(jnp.int32, (2 * rows, 2 * rows), 1)
    ).astype(jnp.bfloat16)
    picks, scales = [], []
    for p in range(2):
        named, weights = [], []
        for pair_ref, s in ((pair_refs[2 * p], 0), (pair_refs[2 * p + 1], 1)):
            hits, weight = 0.0, 0.0
            for k in range(top):
                info = pair_ref[s, pl.ds(2 * rows, INFO_ROWS), k * rows:(k + 1) * rows].astype(jnp.float32)
                hit = info[0:1] == me
                hits += hit.astype(jnp.float32)
                weight += jnp.where(hit, info[1:2] + info[2:3] + info[3:4], 0.0)
            named.append(hits)
            weights.append(weight)
        named = jnp.concatenate(named, axis=1)
        weights = jnp.concatenate(weights, axis=1)
        counted = jnp.dot(
            jnp.broadcast_to(named, (16, 2 * rows)).astype(jnp.bfloat16),
            earlier,
            preferred_element_type=jnp.float32,
        )[:1]
        slot_of = jnp.where(named > 0.0, counted.astype(jnp.int32), -1)
        chosen = slot_of == lax.broadcasted_iota(jnp.int32, (pair_slots, 2 * rows), 0)
        picks.append(chosen.astype(jnp.bfloat16))
        scales.append(jnp.sum(jnp.where(chosen, weights, 0.0), axis=1, keepdims=True))

    for h in range(2):
        for p in range(2):
            picked = jnp.dot(picks[p], gathered(p, h, 0), preferred_element_type=jnp.float32)
            rx_ref[slot_rows(p), columns(h)] = picked.astype(jnp.bfloat16)
    kept_moves[0].start()
    for h in range(2):
        for p in range(2):
            picked = jnp.dot(picks[p], gathered(p, h, 1), preferred_element_type=jnp.float32)
            rg_ref[slot_rows(p), columns(h)] = (scales[p] * picked).astype(jnp.bfloat16)
    kept_moves[1].start()
    gate = lax.dot_general(rx_ref[...], wg_ref[...], CONTRACT_LAST, preferred_element_type=jnp.float32)
    up = lax.dot_general(rx_ref[...], wu_ref[...], CONTRACT_LAST, preferred_element_type=jnp.float32)
    hidden_grad = lax.dot_general(rg_ref[...], wd_ref[...], CONTRACT_LAST, preferred_element_type=jnp.float32)
    sigma = 1.0 / (1.0 + jnp.exp(-gate))
    silu = gate * sigma
    act_ref[...] = (silu * up).astype(jnp.bfloat16)
    gt_ref[...] = (hidden_grad * up * sigma * (1.0 + gate * (1.0 - sigma))).astype(jnp.bfloat16)
    ut_ref[...] = (hidden_grad * silu).astype(jnp.bfloat16)
    for move in kept_moves[2:]:
        move.start()

    slot = jnp.dot(gt_ref[...], wg_ref[...], preferred_element_type=jnp.float32)
    slot += jnp.dot(ut_ref[...], wu_ref[...], preferred_element_type=jnp.float32)
    slot_ref[...] = slot.astype(jnp.bfloat16)
    for p, out_ref in enumerate((near_ref, far_ref)):
        backs = []
        for h in range(2):
            back = lax.dot_general(
                picks[p], slot_ref[slot_rows(p), columns(h)], CONTRACT_FIRST,
                preferred_element_type=jnp.float32,
            ).astype(jnp.bfloat16)
            backs.append(back)
        out_ref[0] = backs[0][:rows]
        out_ref[1] = jnp.where(swapped(p), backs[1][:rows], backs[0][rows:])
        out_ref[2] = jnp.where(swapped(p), backs[0][rows:], backs[1][:rows])
        out_ref[3] = backs[1][rows:]
    for move in kept_moves:
        move.wait()


def run_experts(index, chunks, place, pairs, weights, kept, top, rows, slots):
    width = pairs[0].shape[2]
    hidden, features = weights[0].shape
    anywhere = pl.BlockSpec(memory_space=pl.ANY)
    vmem = pl.BlockSpec(memory_space=pltpu.VMEM)
    part = jax.ShapeDtypeStruct((4, rows, width), jnp.bfloat16)
    wide = jax.ShapeDtypeStruct((chunks * slots, features), jnp.bfloat16)
    narrow = jax.ShapeDtypeStruct((chunks * slots, hidden), jnp.bfloat16)
    first_kept = 1 + len(pairs) + 3
    return pl.pallas_call(
        functools.partial(expert_kernel, index, kept is not None, top, rows),
        in_specs=[pl.BlockSpec(memory_space=pltpu.SMEM)] + [vmem] * 7 + [anywhere] * (0 if kept is None else 5),
        out_specs=[vmem] * 2 + [anywhere] * 5,
        out_shape=[part, part, wide, wide, narrow, narrow, narrow],
        scratch_shapes=[pltpu.VMEM((slots, features), jnp.bfloat16)] * 2
        + [pltpu.VMEM((slots, hidden), jnp.bfloat16)] * 3
        + [pltpu.VMEM((slots, features), jnp.bfloat16), pltpu.SemaphoreType.DMA((5,))],
        input_output_aliases={} if kept is None else {first_kept + i: 2 + i for i in range(5)},
        compiler_params=pltpu.CompilerParams(vmem_limit_bytes=VMEM_LIMIT),
        cost_estimate=pl.CostEstimate(
            flops=2 * slots * features * (hidden * 5 + 2 * rows * 3),
            bytes_accessed=2 * (4 * pairs[0].size + 3 * hidden * features + slots * (2 * features + 3 * hidden)),
            transcendentals=slots * hidden,
        ),
        name="experts",
    )(place, *pairs, *weights, *(kept or ()))


def ring_order(length):
    return list(range(0, min(1, length))) + list(range(1, length, 2)) + list(range(2, length, 2))[::-1]


def gather_body(tokens, out_grad, routes, combine, w_gate, w_up, w_down):
    experts = lax.axis_size("expert")
    chunks = experts // 4
    rows, width = tokens.shape
    top = routes.shape[1]
    per_pair = rows * top // experts
    capacity = per_pair + per_pair // 8
    slots = 2 * (-(-2 * capacity // 16) * 16)
    order = ring_order(chunks)
    after = {order[i]: order[(i + 1) % chunks] for i in range(chunks)}
    devices = [(e, h) for e in range(experts) for h in range(2)]

    def permute(value, target):
        pairs = [(e * 2 + h, target(e, h)[0] * 2 + target(e, h)[1]) for e, h in devices]
        return lax.ppermute(value, ("expert", "etp"), pairs)

    def to_ring(value):
        return permute(value, lambda e, h: (after[e // 4] * 4 + e % 4, h))

    def to_core(value):
        return permute(value, lambda e, h: (e ^ 1, h))

    def to_first(value):
        return permute(value, lambda e, h: (e, h ^ 1) if e % 2 else (e ^ 2, h))

    def to_second(value):
        return permute(value, lambda e, h: (e ^ 2, h) if e % 2 else (e, h ^ 1))

    me = lax.axis_index("expert")
    place = jnp.stack([me, lax.axis_index("etp"), me % 2]).astype(jnp.int32)
    weights = (w_gate[0], w_up[0], w_down[0])
    share = pack_share(tokens, out_grad, routes, combine)
    together = lax.optimization_barrier
    kept = None
    sums, sends, running = [], [], None
    first, second, following = together((to_first(share), to_second(share), to_ring(share)))
    pair, share = jnp.stack([share, first]), following
    for c in range(chunks):
        moved = to_second(first if c == 0 else pair)
        if c + 1 < chunks:
            following = to_ring(share) if c + 2 < chunks else None
            moved, first, following = together((moved, to_first(share), following))
        second = jnp.stack([second, moved]) if c == 0 else moved
        ready = [pair, second, to_core(pair), to_core(second)]
        if c + 1 < chunks:
            pair = jnp.stack([share, first])
            pair, share, sends, *ready = together((pair, following, sends, *ready))
        near_part, far_part, *kept = run_experts(
            c, chunks, place, ready, weights, kept, top, rows, slots
        )
        for i in range(len(sums)):
            if sums[i].ndim == 3:
                sums[i] = sums[i] + to_second(sends[i]).astype(jnp.float32)
                sums[i], sends[i] = sums[i][0], sums[i][1].astype(jnp.bfloat16)
            elif sends[i] is not None:
                sums[i], sends[i] = sums[i] + to_first(sends[i]).astype(jnp.float32), None
        mine = near_part.astype(jnp.float32) + to_core(far_part).astype(jnp.float32)
        sums.append(mine[:2])
        sends.append(mine[2:].astype(jnp.bfloat16))
    for c in range(chunks):
        if sums[c].ndim == 3:
            sums[c] = sums[c] + to_second(sends[c]).astype(jnp.float32)
            sums[c], sends[c] = sums[c][0], sums[c][1].astype(jnp.bfloat16)
        if sends[c] is not None:
            sums[c] = sums[c] + to_first(sends[c]).astype(jnp.float32)
        if c > 0:
            running = sums[c] if c == 1 else sums[c] + running.astype(jnp.float32)
            running = to_ring(running.astype(jnp.bfloat16))
    own = sums[0]
    grad_tokens = (own if running is None else own + running.astype(jnp.float32)).astype(jnp.bfloat16)
    rows_x, rows_g, acts, gate_term, up_term = kept
    grad_down = lax.dot_general(acts, rows_g, CONTRACT_FIRST, preferred_element_type=jnp.float32)
    grad_gate = lax.dot_general(gate_term, rows_x, CONTRACT_FIRST, preferred_element_type=jnp.float32)
    grad_up = lax.dot_general(up_term, rows_x, CONTRACT_FIRST, preferred_element_type=jnp.float32)
    return (
        grad_tokens,
        grad_gate.astype(jnp.bfloat16)[None],
        grad_up.astype(jnp.bfloat16)[None],
        grad_down.astype(jnp.bfloat16)[None],
    )


def solution(mesh):
    experts = mesh.shape["expert"]

    def body(tokens, out_grad, routes, combine, w_gate, w_up, w_down):
        rows, width = tokens.shape
        top = routes.shape[1]
        gathers = top * 4 >= experts and experts % 4 == 0 and mesh.shape["etp"] == 2
        run = gather_body if gathers and top * rows <= width else exchange_body
        return run(tokens, out_grad, routes, combine, w_gate, w_up, w_down)

    placed = (
        P("expert", "etp"),
        P("expert", "etp"),
        P("expert", None),
        P("expert", None),
        P("expert", "etp", None),
        P("expert", "etp", None),
        P("expert", "etp", None),
    )
    return jax.shard_map(
        body,
        mesh=mesh,
        in_specs=placed,
        out_specs=(
            P("expert", "etp"),
            P("expert", "etp", None),
            P("expert", "etp", None),
            P("expert", "etp", None),
        ),
        check_vma=False,
    )
```

```python
import functools

import jax
import jax.numpy as jnp
from jax import lax
from jax.experimental import pallas as pl
from jax.experimental.pallas import tpu as pltpu
from jax.sharding import PartitionSpec as P

CONTRACT_LAST = (((1,), (1,)), ((), ()))
CONTRACT_FIRST = (((0,), (0,)), ((), ()))
INFO_ROWS = 16
VMEM_LIMIT = 16 * 1024 * 1024


def pack_rows(token_rows, grad_rows, token_of, scale, is_live):
    mask = is_live[:, None].astype(token_rows.dtype)
    inputs_sent = token_rows[token_of] * mask
    grads_sent = (scale[:, None] * grad_rows[token_of].astype(jnp.float32)).astype(jnp.bfloat16)
    return (inputs_sent, grads_sent)


def pair_positions(routed_flat, experts):
    pair_total = routed_flat.shape[0]
    span = 128
    groups = pair_total // span
    labels = jnp.arange(experts, dtype=jnp.int32)
    one_hot = (routed_flat[:, None] == labels[None, :]).astype(jnp.bfloat16)
    grouped = one_hot.reshape(groups, span, experts)
    row_ids = jnp.arange(span, dtype=jnp.int32)
    lower = (row_ids[None, :] < row_ids[:, None]).astype(jnp.bfloat16)
    within = jnp.einsum("ij,bje->bie", lower, grouped, preferred_element_type=jnp.float32)
    group_sums = jnp.sum(grouped.astype(jnp.float32), axis=1)
    group_before = jnp.cumsum(group_sums, axis=0) - group_sums
    earlier = within + group_before[:, None, :]
    counted = jnp.sum(earlier * grouped.astype(jnp.float32), axis=2)
    return counted.reshape(pair_total).astype(jnp.int32)


def exchange_body(tokens, out_grad, routes, combine, w_gate, w_up, w_down):
    experts = lax.axis_size("expert")
    tok_rows = tokens.shape[0]
    col_width = tokens.shape[1]
    choose_count = routes.shape[1]
    per_pair = tok_rows * choose_count // experts
    capacity = per_pair + per_pair // 8
    routed_flat = routes.reshape(-1)
    pair_total = routed_flat.shape[0]
    position = pair_positions(routed_flat, experts)
    target = routed_flat * capacity + position
    anchor = jnp.full((experts * capacity,), pair_total, jnp.int32)
    anchor = anchor.at[target].set(jnp.arange(pair_total, dtype=jnp.int32))
    is_live = anchor < pair_total
    safe_anchor = jnp.minimum(anchor, pair_total - 1)
    token_of = safe_anchor // choose_count
    scale = combine.reshape(-1)[safe_anchor] * is_live.astype(jnp.float32)
    full_tokens, full_grads = (
        lax.all_gather(tokens, "etp", axis=1, tiled=True),
        lax.all_gather(out_grad, "etp", axis=1, tiled=True),
    )
    inputs_sent, grads_sent = pack_rows(full_tokens, full_grads, token_of, scale, is_live)
    rows_x, rows_g = (
        lax.all_to_all(inputs_sent, "expert", split_axis=0, concat_axis=0, tiled=True),
        lax.all_to_all(grads_sent, "expert", split_axis=0, concat_axis=0, tiled=True),
    )
    gate_w = w_gate[0]
    up_w = w_up[0]
    down_w = w_down[0]
    gate = lax.dot_general(rows_x, gate_w, CONTRACT_LAST, preferred_element_type=jnp.float32)
    up = lax.dot_general(rows_x, up_w, CONTRACT_LAST, preferred_element_type=jnp.float32)
    hidden_grad = lax.dot_general(rows_g, down_w, CONTRACT_LAST, preferred_element_type=jnp.float32)
    sigma = jax.nn.sigmoid(gate)
    silu = gate * sigma
    acts = (silu * up).astype(jnp.bfloat16)
    grad_down = lax.dot_general(acts, rows_g, CONTRACT_FIRST, preferred_element_type=jnp.float32)
    gate_term = (hidden_grad * up * sigma * (1.0 + gate * (1.0 - sigma))).astype(jnp.bfloat16)
    up_term = (hidden_grad * silu).astype(jnp.bfloat16)
    grad_gate = lax.dot_general(
        gate_term, rows_x, CONTRACT_FIRST, preferred_element_type=jnp.float32
    )
    grad_up = lax.dot_general(up_term, rows_x, CONTRACT_FIRST, preferred_element_type=jnp.float32)
    swapped_gate, swapped_up = (
        lax.all_to_all(gate_w, "etp", split_axis=1, concat_axis=0, tiled=True),
        lax.all_to_all(up_w, "etp", split_axis=1, concat_axis=0, tiled=True),
    )
    running = jnp.dot(
        lax.all_gather(gate_term, "etp", axis=1, tiled=True),
        swapped_gate,
        preferred_element_type=jnp.float32,
    )
    slot_grads = running + jnp.dot(
        lax.all_gather(up_term, "etp", axis=1, tiled=True),
        swapped_up,
        preferred_element_type=jnp.float32,
    )
    slot_grads = slot_grads.astype(jnp.bfloat16)
    returned = lax.all_to_all(slot_grads, "expert", split_axis=0, concat_axis=0, tiled=True)
    picked = returned[target].astype(jnp.float32).reshape(tok_rows, choose_count, col_width)
    grad_tokens = jnp.sum(picked, axis=1).astype(jnp.bfloat16)
    return (
        grad_tokens,
        grad_gate.astype(jnp.bfloat16)[None],
        grad_up.astype(jnp.bfloat16)[None],
        grad_down.astype(jnp.bfloat16)[None],
    )


def pack_kernel(tokens_ref, grads_ref, routes_ref, combine_ref, out_ref):
    rows = tokens_ref.shape[0]
    out_ref[:rows] = tokens_ref[...]
    out_ref[rows:2 * rows] = grads_ref[...]
    top = routes_ref.shape[0]
    routes = routes_ref[...].astype(jnp.float32)
    weights = combine_ref[...]
    high = weights.astype(jnp.bfloat16).astype(jnp.float32)
    middle = (weights - high).astype(jnp.bfloat16).astype(jnp.float32)
    low = weights - high - middle
    blank = jnp.zeros((INFO_ROWS - 4, rows), jnp.float32)
    for k in range(top):
        own = slice(k, k + 1)
        column = jnp.concatenate([routes[own], high[own], middle[own], low[own], blank], axis=0)
        out_ref[2 * rows:, k * rows:(k + 1) * rows] = column.astype(jnp.bfloat16)


def pack_share(tokens, out_grad, routes, combine):
    rows, width = tokens.shape
    vmem = pl.BlockSpec(memory_space=pltpu.VMEM)
    return pl.pallas_call(
        pack_kernel,
        in_specs=[vmem] * 4,
        out_specs=vmem,
        out_shape=jax.ShapeDtypeStruct((2 * rows + INFO_ROWS, width), jnp.bfloat16),
        cost_estimate=pl.CostEstimate(flops=0, bytes_accessed=8 * rows * width, transcendentals=0),
        name="pack",
    )(tokens, out_grad, routes.T, combine.T)


def expert_kernel(index, chained, top, rows, place_ref, *refs):
    shares = refs[:4], refs[4:8]
    wg_ref, wu_ref, wd_ref = refs[8:11]
    refs = refs[11 + (5 if chained else 0):]
    near_ref, far_ref = refs[:2]
    kept_refs = refs[2:7]
    rx_ref, rg_ref, act_ref, gt_ref, ut_ref, slot_ref, sems = refs[7:]
    me = place_ref[0].astype(jnp.float32)
    own_half = place_ref[1]
    core = place_ref[2]
    slots = rx_ref.shape[0]
    width = near_ref.shape[2]
    pair_slots = slots // 2
    kept_moves = [
        pltpu.make_async_copy(source, target.at[pl.ds(index * slots, slots)], sems.at[i])
        for i, (source, target) in enumerate(zip((rx_ref, rg_ref, act_ref, gt_ref, ut_ref), kept_refs))
    ]

    def columns(h):
        return pl.ds(pl.multiple_of((own_half if h == 0 else 1 - own_half) * width, width), width)

    def slot_rows(p):
        return slice(p * pair_slots, (p + 1) * pair_slots)

    def swapped(p):
        return core == 1 if p == 0 else core == 0

    def gathered(p, h, part):
        own, first, second, both = [ref[pl.ds(part * rows, rows)] for ref in shares[p]]
        if h == 0:
            return jnp.concatenate([own, jnp.where(swapped(p), second, first)], axis=0)
        return jnp.concatenate([jnp.where(swapped(p), first, second), both], axis=0)

    earlier = (
        lax.broadcasted_iota(jnp.int32, (2 * rows, 2 * rows), 0)
        < lax.broadcasted_iota(jnp.int32, (2 * rows, 2 * rows), 1)
    ).astype(jnp.bfloat16)
    picks, scales = [], []
    for p in range(2):
        named, weights = [], []
        for share_ref in (shares[p][0], shares[p][3]):
            hits, weight = 0.0, 0.0
            for k in range(top):
                info = share_ref[pl.ds(2 * rows, INFO_ROWS), k * rows:(k + 1) * rows].astype(jnp.float32)
                hit = info[0:1] == me
                hits += hit.astype(jnp.float32)
                weight += jnp.where(hit, info[1:2] + info[2:3] + info[3:4], 0.0)
            named.append(hits)
            weights.append(weight)
        named = jnp.concatenate(named, axis=1)
        weights = jnp.concatenate(weights, axis=1)
        counted = jnp.dot(
            jnp.broadcast_to(named, (16, 2 * rows)).astype(jnp.bfloat16),
            earlier,
            preferred_element_type=jnp.float32,
        )[:1]
        slot_of = jnp.where(named > 0.0, counted.astype(jnp.int32), -1)
        chosen = slot_of == lax.broadcasted_iota(jnp.int32, (pair_slots, 2 * rows), 0)
        picks.append(chosen.astype(jnp.bfloat16))
        scales.append(jnp.sum(jnp.where(chosen, weights, 0.0), axis=1, keepdims=True))

    for h in range(2):
        for p in range(2):
            picked = jnp.dot(picks[p], gathered(p, h, 0), preferred_element_type=jnp.float32)
            rx_ref[slot_rows(p), columns(h)] = picked.astype(jnp.bfloat16)
    kept_moves[0].start()
    for h in range(2):
        for p in range(2):
            picked = jnp.dot(picks[p], gathered(p, h, 1), preferred_element_type=jnp.float32)
            rg_ref[slot_rows(p), columns(h)] = (scales[p] * picked).astype(jnp.bfloat16)
    kept_moves[1].start()
    gate = lax.dot_general(rx_ref[...], wg_ref[...], CONTRACT_LAST, preferred_element_type=jnp.float32)
    up = lax.dot_general(rx_ref[...], wu_ref[...], CONTRACT_LAST, preferred_element_type=jnp.float32)
    hidden_grad = lax.dot_general(rg_ref[...], wd_ref[...], CONTRACT_LAST, preferred_element_type=jnp.float32)
    sigma = 1.0 / (1.0 + jnp.exp(-gate))
    silu = gate * sigma
    act_ref[...] = (silu * up).astype(jnp.bfloat16)
    gt_ref[...] = (hidden_grad * up * sigma * (1.0 + gate * (1.0 - sigma))).astype(jnp.bfloat16)
    ut_ref[...] = (hidden_grad * silu).astype(jnp.bfloat16)
    for move in kept_moves[2:]:
        move.start()

    slot = jnp.dot(gt_ref[...], wg_ref[...], preferred_element_type=jnp.float32)
    slot += jnp.dot(ut_ref[...], wu_ref[...], preferred_element_type=jnp.float32)
    slot_ref[...] = slot.astype(jnp.bfloat16)
    for p, out_ref in enumerate((near_ref, far_ref)):
        backs = []
        for h in range(2):
            back = lax.dot_general(
                picks[p], slot_ref[slot_rows(p), columns(h)], CONTRACT_FIRST,
                preferred_element_type=jnp.float32,
            ).astype(jnp.bfloat16)
            backs.append(back)
        out_ref[0] = backs[0][:rows]
        out_ref[1] = jnp.where(swapped(p), backs[1][:rows], backs[0][rows:])
        out_ref[2] = jnp.where(swapped(p), backs[0][rows:], backs[1][:rows])
        out_ref[3] = backs[1][rows:]
    for move in kept_moves:
        move.wait()


def run_experts(index, chunks, place, shares, weights, kept, top, rows, slots):
    width = shares[0].shape[1]
    hidden, features = weights[0].shape
    anywhere = pl.BlockSpec(memory_space=pl.ANY)
    vmem = pl.BlockSpec(memory_space=pltpu.VMEM)
    part = jax.ShapeDtypeStruct((4, rows, width), jnp.bfloat16)
    wide = jax.ShapeDtypeStruct((chunks * slots, features), jnp.bfloat16)
    narrow = jax.ShapeDtypeStruct((chunks * slots, hidden), jnp.bfloat16)
    first_kept = 1 + len(shares) + 3
    return pl.pallas_call(
        functools.partial(expert_kernel, index, kept is not None, top, rows),
        in_specs=[pl.BlockSpec(memory_space=pltpu.SMEM)] + [vmem] * 11 + [anywhere] * (0 if kept is None else 5),
        out_specs=[vmem] * 2 + [anywhere] * 5,
        out_shape=[part, part, wide, wide, narrow, narrow, narrow],
        scratch_shapes=[pltpu.VMEM((slots, features), jnp.bfloat16)] * 2
        + [pltpu.VMEM((slots, hidden), jnp.bfloat16)] * 3
        + [pltpu.VMEM((slots, features), jnp.bfloat16), pltpu.SemaphoreType.DMA((5,))],
        input_output_aliases={} if kept is None else {first_kept + i: 2 + i for i in range(5)},
        compiler_params=pltpu.CompilerParams(vmem_limit_bytes=VMEM_LIMIT),
        cost_estimate=pl.CostEstimate(
            flops=4 * slots * features * (hidden * 5 + 2 * rows * 3),
            bytes_accessed=2 * (8 * shares[0].size + 3 * hidden * features + slots * (2 * features + 3 * hidden)),
            transcendentals=slots * hidden,
        ),
        name="experts",
    )(place, *shares, *weights, *(kept or ()))


def ring_order(length):
    return list(range(0, min(1, length))) + list(range(1, length, 2)) + list(range(2, length, 2))[::-1]


def gather_body(tokens, out_grad, routes, combine, w_gate, w_up, w_down):
    experts = lax.axis_size("expert")
    chunks = experts // 4
    rows, width = tokens.shape
    top = routes.shape[1]
    per_pair = rows * top // experts
    capacity = per_pair + per_pair // 8
    slots = 2 * (-(-2 * capacity // 16) * 16)
    order = ring_order(chunks)
    after = {order[i]: order[(i + 1) % chunks] for i in range(chunks)}
    devices = [(e, h) for e in range(experts) for h in range(2)]

    def permute(value, target):
        pairs = [(e * 2 + h, target(e, h)[0] * 2 + target(e, h)[1]) for e, h in devices]
        return lax.ppermute(value, ("expert", "etp"), pairs)

    def to_ring(value):
        return permute(value, lambda e, h: (after[e // 4] * 4 + e % 4, h))

    def to_core(value):
        return permute(value, lambda e, h: (e ^ 1, h))

    def to_first(value):
        return permute(value, lambda e, h: (e, h ^ 1) if e % 2 else (e ^ 2, h))

    def to_second(value):
        return permute(value, lambda e, h: (e ^ 2, h) if e % 2 else (e, h ^ 1))

    me = lax.axis_index("expert")
    place = jnp.stack([me, lax.axis_index("etp"), me % 2]).astype(jnp.int32)
    weights = (w_gate[0], w_up[0], w_down[0])
    share = pack_share(tokens, out_grad, routes, combine)
    def crossed_sums(near_part, far_part, beside=()):
        mine = near_part.astype(jnp.float32) + to_core(far_part).astype(jnp.float32)
        mine, send = mine[:2], mine[2:].astype(jnp.bfloat16)
        send, beside = lax.optimization_barrier((send, beside))
        mine = mine + to_second(send).astype(jnp.float32)
        return mine[0], mine[1].astype(jnp.bfloat16), beside

    ring_sends = [("s", 1)] + [(kind, c) for c in range(2, chunks) for kind in ("s", "f")]
    ring_sends = [key for key in ring_sends if key[1] < chunks]
    plane_sends = [("f", 0), ("a", 0), ("f", 1), ("b", 0)] + [(kind, c) for c in range(1, chunks) for kind in ("a", "b")]
    plane_sends = [key for key in plane_sends if key[1] < chunks]
    have, crossed, fresh = {("s", 0): share}, {}, [("s", 0)]
    kept, done, parts = None, 0, None
    sums, sends = [], []
    while done < chunks:
        came = {}
        planned = [key for key in plane_sends if (("f" if key[0] == "b" else "s"), key[1]) in have][:2]
        for kind, c in planned:
            source = have["f" if kind == "b" else "s", c]
            came[kind, c] = to_first(source) if kind == "f" else to_second(source)
            plane_sends.remove((kind, c))
        if ring_sends and (ring_sends[0][0], ring_sends[0][1] - 1) in have:
            kind, c = ring_sends.pop(0)
            came[kind, c] = to_ring(have[kind, c - 1])
        swaps = {key: to_core(have[key]) for key in fresh}
        for i in range(len(sums)):
            if sends[i] is not None:
                sums[i], sends[i] = sums[i] + to_first(sends[i]).astype(jnp.float32), None
        if parts is not None:
            mine, send, _ = crossed_sums(*parts)
            sums.append(mine)
            sends.append(send)
            parts = None
        members = [(kind, done) for kind in "sfab"]
        near = [have[key] for key in members if key in have]
        far = [crossed.get(key, swaps.get(key) if done + 1 == chunks else None) for key in members]
        if len(near) == 4 and all(value is not None for value in far):
            near_part, far_part, *kept = run_experts(
                done, chunks, place, near + far, weights, kept, top, rows, slots
            )
            parts = near_part, far_part
            done += 1
        if done < chunks:
            came, swaps, sends, parts = lax.optimization_barrier((came, swaps, sends, parts))
        fresh = list(came)
        have.update(came)
        crossed.update(swaps)
    mine, send, sends = crossed_sums(*parts, sends)
    sums.append(mine)
    sends.append(send)
    running = None
    for c in range(chunks):
        if sends[c] is not None:
            sums[c] = sums[c] + to_first(sends[c]).astype(jnp.float32)
        if c > 0:
            running = sums[c] if c == 1 else sums[c] + running.astype(jnp.float32)
            running = to_ring(running.astype(jnp.bfloat16))
    own = sums[0]
    grad_tokens = (own if running is None else own + running.astype(jnp.float32)).astype(jnp.bfloat16)
    rows_x, rows_g, acts, gate_term, up_term = kept
    grad_down = lax.dot_general(acts, rows_g, CONTRACT_FIRST, preferred_element_type=jnp.float32)
    grad_gate = lax.dot_general(gate_term, rows_x, CONTRACT_FIRST, preferred_element_type=jnp.float32)
    grad_up = lax.dot_general(up_term, rows_x, CONTRACT_FIRST, preferred_element_type=jnp.float32)
    return (
        grad_tokens,
        grad_gate.astype(jnp.bfloat16)[None],
        grad_up.astype(jnp.bfloat16)[None],
        grad_down.astype(jnp.bfloat16)[None],
    )


def solution(mesh):
    experts = mesh.shape["expert"]

    def body(tokens, out_grad, routes, combine, w_gate, w_up, w_down):
        rows, width = tokens.shape
        top = routes.shape[1]
        gathers = top * 4 >= experts and experts % 4 == 0 and mesh.shape["etp"] == 2
        run = gather_body if gathers and top * rows <= width else exchange_body
        return run(tokens, out_grad, routes, combine, w_gate, w_up, w_down)

    placed = (
        P("expert", "etp"),
        P("expert", "etp"),
        P("expert", None),
        P("expert", None),
        P("expert", "etp", None),
        P("expert", "etp", None),
        P("expert", "etp", None),
    )
    return jax.shard_map(
        body,
        mesh=mesh,
        in_specs=placed,
        out_specs=(
            P("expert", "etp"),
            P("expert", "etp", None),
            P("expert", "etp", None),
            P("expert", "etp", None),
        ),
        check_vma=False,
    )
```

```python
import functools

import jax
import jax.numpy as jnp
from jax import lax
from jax.experimental import pallas as pl
from jax.experimental.pallas import tpu as pltpu
from jax.sharding import PartitionSpec as P

CONTRACT_LAST = (((1,), (1,)), ((), ()))
CONTRACT_FIRST = (((0,), (0,)), ((), ()))
INFO_ROWS = 16
VMEM_LIMIT = 16 * 1024 * 1024


def pack_rows(token_rows, grad_rows, token_of, scale, is_live):
    mask = is_live[:, None].astype(token_rows.dtype)
    inputs_sent = token_rows[token_of] * mask
    grads_sent = (scale[:, None] * grad_rows[token_of].astype(jnp.float32)).astype(jnp.bfloat16)
    return (inputs_sent, grads_sent)


def pair_positions(routed_flat, experts):
    pair_total = routed_flat.shape[0]
    span = 128
    groups = pair_total // span
    labels = jnp.arange(experts, dtype=jnp.int32)
    one_hot = (routed_flat[:, None] == labels[None, :]).astype(jnp.bfloat16)
    grouped = one_hot.reshape(groups, span, experts)
    row_ids = jnp.arange(span, dtype=jnp.int32)
    lower = (row_ids[None, :] < row_ids[:, None]).astype(jnp.bfloat16)
    within = jnp.einsum("ij,bje->bie", lower, grouped, preferred_element_type=jnp.float32)
    group_sums = jnp.sum(grouped.astype(jnp.float32), axis=1)
    group_before = jnp.cumsum(group_sums, axis=0) - group_sums
    earlier = within + group_before[:, None, :]
    counted = jnp.sum(earlier * grouped.astype(jnp.float32), axis=2)
    return counted.reshape(pair_total).astype(jnp.int32)


def exchange_body(tokens, out_grad, routes, combine, w_gate, w_up, w_down):
    experts = lax.axis_size("expert")
    tok_rows = tokens.shape[0]
    col_width = tokens.shape[1]
    choose_count = routes.shape[1]
    per_pair = tok_rows * choose_count // experts
    capacity = per_pair + per_pair // 8
    routed_flat = routes.reshape(-1)
    pair_total = routed_flat.shape[0]
    position = pair_positions(routed_flat, experts)
    target = routed_flat * capacity + position
    anchor = jnp.full((experts * capacity,), pair_total, jnp.int32)
    anchor = anchor.at[target].set(jnp.arange(pair_total, dtype=jnp.int32))
    is_live = anchor < pair_total
    safe_anchor = jnp.minimum(anchor, pair_total - 1)
    token_of = safe_anchor // choose_count
    scale = combine.reshape(-1)[safe_anchor] * is_live.astype(jnp.float32)
    full_tokens, full_grads = (
        lax.all_gather(tokens, "etp", axis=1, tiled=True),
        lax.all_gather(out_grad, "etp", axis=1, tiled=True),
    )
    inputs_sent, grads_sent = pack_rows(full_tokens, full_grads, token_of, scale, is_live)
    rows_x, rows_g = (
        lax.all_to_all(inputs_sent, "expert", split_axis=0, concat_axis=0, tiled=True),
        lax.all_to_all(grads_sent, "expert", split_axis=0, concat_axis=0, tiled=True),
    )
    gate_w = w_gate[0]
    up_w = w_up[0]
    down_w = w_down[0]
    gate = lax.dot_general(rows_x, gate_w, CONTRACT_LAST, preferred_element_type=jnp.float32)
    up = lax.dot_general(rows_x, up_w, CONTRACT_LAST, preferred_element_type=jnp.float32)
    hidden_grad = lax.dot_general(rows_g, down_w, CONTRACT_LAST, preferred_element_type=jnp.float32)
    sigma = jax.nn.sigmoid(gate)
    silu = gate * sigma
    acts = (silu * up).astype(jnp.bfloat16)
    grad_down = lax.dot_general(acts, rows_g, CONTRACT_FIRST, preferred_element_type=jnp.float32)
    gate_term = (hidden_grad * up * sigma * (1.0 + gate * (1.0 - sigma))).astype(jnp.bfloat16)
    up_term = (hidden_grad * silu).astype(jnp.bfloat16)
    grad_gate = lax.dot_general(
        gate_term, rows_x, CONTRACT_FIRST, preferred_element_type=jnp.float32
    )
    grad_up = lax.dot_general(up_term, rows_x, CONTRACT_FIRST, preferred_element_type=jnp.float32)
    swapped_gate, swapped_up = (
        lax.all_to_all(gate_w, "etp", split_axis=1, concat_axis=0, tiled=True),
        lax.all_to_all(up_w, "etp", split_axis=1, concat_axis=0, tiled=True),
    )
    running = jnp.dot(
        lax.all_gather(gate_term, "etp", axis=1, tiled=True),
        swapped_gate,
        preferred_element_type=jnp.float32,
    )
    slot_grads = running + jnp.dot(
        lax.all_gather(up_term, "etp", axis=1, tiled=True),
        swapped_up,
        preferred_element_type=jnp.float32,
    )
    slot_grads = slot_grads.astype(jnp.bfloat16)
    returned = lax.all_to_all(slot_grads, "expert", split_axis=0, concat_axis=0, tiled=True)
    picked = returned[target].astype(jnp.float32).reshape(tok_rows, choose_count, col_width)
    grad_tokens = jnp.sum(picked, axis=1).astype(jnp.bfloat16)
    return (
        grad_tokens,
        grad_gate.astype(jnp.bfloat16)[None],
        grad_up.astype(jnp.bfloat16)[None],
        grad_down.astype(jnp.bfloat16)[None],
    )


def pack_kernel(tokens_ref, grads_ref, routes_ref, combine_ref, out_ref):
    rows = tokens_ref.shape[0]
    out_ref[:rows] = tokens_ref[...]
    out_ref[rows:2 * rows] = grads_ref[...]
    top = routes_ref.shape[0]
    routes = routes_ref[...].astype(jnp.float32)
    weights = combine_ref[...]
    high = weights.astype(jnp.bfloat16).astype(jnp.float32)
    middle = (weights - high).astype(jnp.bfloat16).astype(jnp.float32)
    low = weights - high - middle
    blank = jnp.zeros((INFO_ROWS - 4, rows), jnp.float32)
    for k in range(top):
        own = slice(k, k + 1)
        column = jnp.concatenate([routes[own], high[own], middle[own], low[own], blank], axis=0)
        out_ref[2 * rows:, k * rows:(k + 1) * rows] = column.astype(jnp.bfloat16)


def pack_share(tokens, out_grad, routes, combine):
    rows, width = tokens.shape
    vmem = pl.BlockSpec(memory_space=pltpu.VMEM)
    return pl.pallas_call(
        pack_kernel,
        in_specs=[vmem] * 4,
        out_specs=vmem,
        out_shape=jax.ShapeDtypeStruct((2 * rows + INFO_ROWS, width), jnp.bfloat16),
        cost_estimate=pl.CostEstimate(flops=0, bytes_accessed=8 * rows * width, transcendentals=0),
        name="pack",
    )(tokens, out_grad, routes.T, combine.T)


def load_kernel(*refs):
    count = (len(refs) - 1) // 2
    moves = [pltpu.make_async_copy(refs[i], refs[count + i], refs[-1].at[i]) for i in range(count)]
    for move in moves:
        move.start()
    for move in moves:
        move.wait()


def load_weights(weights):
    return pl.pallas_call(
        load_kernel,
        in_specs=[pl.BlockSpec(memory_space=pltpu.HBM)] * len(weights),
        out_specs=[pl.BlockSpec(memory_space=pltpu.VMEM)] * len(weights),
        out_shape=[jax.ShapeDtypeStruct(w.shape, w.dtype) for w in weights],
        scratch_shapes=[pltpu.SemaphoreType.DMA((len(weights),))],
        name="load",
    )(*weights)


def pick_kernel(top, rows, place_ref, *refs):
    shares, (mine_ref, theirs_ref, picks_ref) = refs[:4], refs[4:]
    me, own_half, core = place_ref[0], place_ref[1], place_ref[2]
    pair_slots, width = mine_ref.shape[1], shares[0].shape[1]
    earlier = (
        lax.broadcasted_iota(jnp.int32, (2 * rows, 2 * rows), 0)
        < lax.broadcasted_iota(jnp.int32, (2 * rows, 2 * rows), 1)
    ).astype(jnp.bfloat16)
    infos = [
        [share_ref[pl.ds(2 * rows, INFO_ROWS), k * rows:(k + 1) * rows].astype(jnp.float32) for k in range(top)]
        for share_ref in (shares[0], shares[3])
    ]
    picks, scales = [], []
    for expert in (me, me + 1 - 2 * core):
        named, weights = [], []
        for block in infos:
            hits, weight = 0.0, 0.0
            for info in block:
                hit = info[0:1] == expert.astype(jnp.float32)
                hits += hit.astype(jnp.float32)
                weight += jnp.where(hit, info[1:2] + info[2:3] + info[3:4], 0.0)
            named.append(hits)
            weights.append(weight)
        named = jnp.concatenate(named, axis=1)
        weights = jnp.concatenate(weights, axis=1)
        counted = jnp.dot(
            jnp.broadcast_to(named, (16, 2 * rows)).astype(jnp.bfloat16),
            earlier,
            preferred_element_type=jnp.float32,
        )[:1]
        slot_of = jnp.where(named > 0.0, counted.astype(jnp.int32), -1)
        chosen = slot_of == lax.broadcasted_iota(jnp.int32, (pair_slots, 2 * rows), 0)
        picks.append(chosen.astype(jnp.bfloat16))
        scales.append(jnp.sum(jnp.where(chosen, weights, 0.0), axis=1, keepdims=True))
    picks = jnp.concatenate(picks, axis=0)
    scales = jnp.concatenate(scales, axis=0)
    picks_ref[...] = picks
    for h in range(2):
        cols = pl.ds(pl.multiple_of((own_half if h == 0 else 1 - own_half) * width, width), width)
        for part in range(2):
            own, first, second, both = [ref[pl.ds(part * rows, rows)] for ref in shares]
            if h == 0:
                held = jnp.concatenate([own, jnp.where(core == 1, second, first)], axis=0)
            else:
                held = jnp.concatenate([jnp.where(core == 1, first, second), both], axis=0)
            picked = jnp.dot(picks, held, preferred_element_type=jnp.float32)
            if part == 1:
                picked = scales * picked
            picked = picked.astype(jnp.bfloat16)
            mine_ref[part, :, cols] = picked[:pair_slots]
            theirs_ref[part, :, cols] = picked[pair_slots:]


def expert_kernel(index, chained, mine_ref, theirs_ref, wg_ref, wu_ref, wd_ref, *refs):
    near_ref, far_ref, *kept_refs = refs[5 if chained else 0:][:7]
    act_ref, gt_ref, ut_ref, sems = refs[-4:]
    pair_slots = mine_ref.shape[1]
    slots = 2 * pair_slots

    def kept_move(source, target, part, count, i):
        return pltpu.make_async_copy(
            source, kept_refs[target].at[pl.ds(index * slots + part * pair_slots, count)], sems.at[i]
        )

    moves = [
        kept_move(mine_ref.at[0], 0, 0, pair_slots, 0),
        kept_move(theirs_ref.at[0], 0, 1, pair_slots, 1),
        kept_move(mine_ref.at[1], 1, 0, pair_slots, 2),
        kept_move(theirs_ref.at[1], 1, 1, pair_slots, 3),
        kept_move(act_ref, 2, 0, slots, 4),
        kept_move(gt_ref, 3, 0, slots, 5),
        kept_move(ut_ref, 4, 0, slots, 6),
    ]
    for move in moves[:4]:
        move.start()
    rows_x = jnp.concatenate([mine_ref[0], theirs_ref[0]], axis=0)
    rows_g = jnp.concatenate([mine_ref[1], theirs_ref[1]], axis=0)
    gate = lax.dot_general(rows_x, wg_ref[...], CONTRACT_LAST, preferred_element_type=jnp.float32)
    up = lax.dot_general(rows_x, wu_ref[...], CONTRACT_LAST, preferred_element_type=jnp.float32)
    hidden_grad = lax.dot_general(rows_g, wd_ref[...], CONTRACT_LAST, preferred_element_type=jnp.float32)
    sigma = 1.0 / (1.0 + jnp.exp(-gate))
    silu = gate * sigma
    act_ref[...] = (silu * up).astype(jnp.bfloat16)
    gt_ref[...] = (hidden_grad * up * sigma * (1.0 + gate * (1.0 - sigma))).astype(jnp.bfloat16)
    ut_ref[...] = (hidden_grad * silu).astype(jnp.bfloat16)
    for move in moves[4:]:
        move.start()
    slot = jnp.dot(gt_ref[...], wg_ref[...], preferred_element_type=jnp.float32)
    slot += jnp.dot(ut_ref[...], wu_ref[...], preferred_element_type=jnp.float32)
    far_ref[...] = slot[pair_slots:].astype(jnp.bfloat16)
    near_ref[...] = slot[:pair_slots].astype(jnp.bfloat16)
    for move in moves:
        move.wait()


def place_kernel(place_ref, picks_ref, near_ref, far_ref, keep_ref, send_ref):
    own_half, core = place_ref[1], place_ref[2]
    _, rows, width = keep_ref.shape
    pair_slots = near_ref.shape[0]
    backs = []
    for h in range(2):
        cols = pl.ds(pl.multiple_of((own_half if h == 0 else 1 - own_half) * width, width), width)
        slot = jnp.concatenate([near_ref[:, cols], far_ref[:, cols]], axis=0)
        backs.append(lax.dot_general(picks_ref[...], slot, CONTRACT_FIRST, preferred_element_type=jnp.float32))
    keep_ref[0] = backs[0][:rows]
    keep_ref[1] = jnp.where(core == 1, backs[1][:rows], backs[0][rows:])
    send_ref[0] = jnp.where(core == 1, backs[0][rows:], backs[1][:rows]).astype(jnp.bfloat16)
    send_ref[1] = backs[1][rows:].astype(jnp.bfloat16)


def pick_rows(place, shares, top, rows, pair_slots):
    width = shares[0].shape[1]
    vmem = pl.BlockSpec(memory_space=pltpu.VMEM)
    picked = jax.ShapeDtypeStruct((2, pair_slots, 2 * width), jnp.bfloat16)
    return pl.pallas_call(
        functools.partial(pick_kernel, top, rows),
        in_specs=[pl.BlockSpec(memory_space=pltpu.SMEM)] + [vmem] * 4,
        out_specs=[vmem] * 3,
        out_shape=[picked, picked, jax.ShapeDtypeStruct((2 * pair_slots, 2 * rows), jnp.bfloat16)],
        compiler_params=pltpu.CompilerParams(vmem_limit_bytes=VMEM_LIMIT),
        cost_estimate=pl.CostEstimate(
            flops=32 * pair_slots * 2 * rows * 2 * width,
            bytes_accessed=2 * (4 * shares[0].size + 8 * pair_slots * width),
            transcendentals=0,
        ),
        name="pick",
    )(place, *shares)


def run_experts(index, chunks, mine, theirs, weights, kept):
    _, pair_slots, features = mine.shape
    hidden = weights[0].shape[0]
    slots = 2 * pair_slots
    hbm = pl.BlockSpec(memory_space=pltpu.HBM)
    vmem = pl.BlockSpec(memory_space=pltpu.VMEM)
    part = jax.ShapeDtypeStruct((pair_slots, features), jnp.bfloat16)
    wide = jax.ShapeDtypeStruct((chunks * slots, features), jnp.bfloat16)
    narrow = jax.ShapeDtypeStruct((chunks * slots, hidden), jnp.bfloat16)
    return pl.pallas_call(
        functools.partial(expert_kernel, index, kept is not None),
        in_specs=[vmem] * 5 + [hbm] * (0 if kept is None else 5),
        out_specs=[vmem] * 2 + [hbm] * 5,
        out_shape=[part, part, wide, wide, narrow, narrow, narrow],
        scratch_shapes=[pltpu.VMEM((slots, hidden), jnp.bfloat16)] * 3 + [pltpu.SemaphoreType.DMA((7,))],
        input_output_aliases={} if kept is None else {5 + i: 2 + i for i in range(5)},
        compiler_params=pltpu.CompilerParams(vmem_limit_bytes=VMEM_LIMIT),
        cost_estimate=pl.CostEstimate(
            flops=20 * slots * features * hidden,
            bytes_accessed=2 * (3 * hidden * features + slots * (4 * features + 3 * hidden)),
            transcendentals=slots * hidden,
        ),
        name="experts",
    )(mine, theirs, *weights, *(kept or ()))


def place_rows(place, picks, near, far, rows, width):
    vmem = pl.BlockSpec(memory_space=pltpu.VMEM)
    return pl.pallas_call(
        place_kernel,
        in_specs=[pl.BlockSpec(memory_space=pltpu.SMEM)] + [vmem] * 3,
        out_specs=[vmem] * 2,
        out_shape=[
            jax.ShapeDtypeStruct((2, rows, width), jnp.float32),
            jax.ShapeDtypeStruct((2, rows, width), jnp.bfloat16),
        ],
        compiler_params=pltpu.CompilerParams(vmem_limit_bytes=VMEM_LIMIT),
        cost_estimate=pl.CostEstimate(
            flops=4 * picks.size * 2 * width, bytes_accessed=4 * near.size + 12 * rows * width, transcendentals=0
        ),
        name="place",
    )(place, picks, near, far)


def ring_order(length):
    return list(range(0, min(1, length))) + list(range(1, length, 2)) + list(range(2, length, 2))[::-1]


def gather_body(tokens, out_grad, routes, combine, w_gate, w_up, w_down):
    experts = lax.axis_size("expert")
    chunks = experts // 4
    rows, width = tokens.shape
    top = routes.shape[1]
    per_pair = rows * top // experts
    capacity = per_pair + per_pair // 8
    pair_slots = -(-2 * capacity // 16) * 16
    order = ring_order(chunks)
    after = {order[i]: order[(i + 1) % chunks] for i in range(chunks)}
    devices = [(e, h) for e in range(experts) for h in range(2)]

    def permute(value, target):
        pairs = [(e * 2 + h, target(e, h)[0] * 2 + target(e, h)[1]) for e, h in devices]
        return lax.ppermute(value, ("expert", "etp"), pairs)

    def to_ring(value):
        return permute(value, lambda e, h: (after[e // 4] * 4 + e % 4, h))

    def to_core(value):
        return permute(value, lambda e, h: (e ^ 1, h))

    def to_first(value):
        return permute(value, lambda e, h: (e, h ^ 1) if e % 2 else (e ^ 2, h))

    def to_second(value):
        return permute(value, lambda e, h: (e ^ 2, h) if e % 2 else (e, h ^ 1))

    me = lax.axis_index("expert")
    place = jnp.stack([me, lax.axis_index("etp"), me % 2]).astype(jnp.int32)
    share = pack_share(tokens, out_grad, routes, combine)
    weights = load_weights((w_gate[0], w_up[0], w_down[0]))

    def summed(picks, near, far, beside=()):
        keep, send = place_rows(place, picks, near, to_core(far), rows, width)
        send, beside = lax.optimization_barrier((send, beside))
        mine = keep + to_second(send).astype(jnp.float32)
        return mine[0], mine[1].astype(jnp.bfloat16), beside

    ring_sends = [("s", 1)] + [(kind, c) for c in range(2, chunks) for kind in ("s", "f")]
    ring_sends = [key for key in ring_sends if key[1] < chunks]
    plane_sends = [("f", 0), ("a", 0), ("f", 1), ("b", 0)] + [(kind, c) for c in range(1, chunks) for kind in ("a", "b")]
    plane_sends = [key for key in plane_sends if key[1] < chunks]
    have = {("s", 0): share}
    kept, parts, picked, done = None, None, None, 0
    sums, sends = [], []
    next_pick = 0
    while done < chunks:
        came = {}
        planned = [key for key in plane_sends if (("f" if key[0] == "b" else "s"), key[1]) in have][:2]
        for kind, c in planned:
            source = have["f" if kind == "b" else "s", c]
            came[kind, c] = to_first(source) if kind == "f" else to_second(source)
            plane_sends.remove((kind, c))
        if ring_sends and (ring_sends[0][0], ring_sends[0][1] - 1) in have:
            kind, c = ring_sends.pop(0)
            came[kind, c] = to_ring(have[kind, c - 1])
        for i in range(len(sums)):
            if sends[i] is not None:
                sums[i], sends[i] = sums[i] + to_first(sends[i]).astype(jnp.float32), None
        if parts is not None:
            mine, send, _ = summed(*parts)
            sums.append(mine)
            sends.append(send)
            parts = None
        arrived = [have.get((kind, next_pick)) for kind in "sfab"]
        last = next_pick + 1 == chunks
        if picked is not None:
            mine, theirs, picks = picked
            near, far, *kept = run_experts(done, chunks, mine, theirs, weights, kept)
            parts = picks, near, far
            picked = None
            done += 1
        if all(value is not None for value in arrived) and next_pick < chunks:
            mine, theirs, picks = pick_rows(place, arrived, top, rows, pair_slots)
            picked = mine, to_core(theirs), picks
            next_pick += 1
            if last:
                if parts is not None:
                    mine, send, _ = summed(*parts)
                    sums.append(mine)
                    sends.append(send)
                mine, theirs, picks = picked
                near, far, *kept = run_experts(done, chunks, mine, theirs, weights, kept)
                parts = picks, near, far
                done += 1
        if done < chunks:
            came, sends, parts, picked, weights = lax.optimization_barrier((came, sends, parts, picked, weights))
        have.update(came)
    mine, send, sends = summed(*parts, sends)
    sums.append(mine)
    sends.append(send)
    running = None
    for c in range(chunks):
        if sends[c] is not None:
            sums[c] = sums[c] + to_first(sends[c]).astype(jnp.float32)
        if c > 0:
            running = sums[c] if c == 1 else sums[c] + running.astype(jnp.float32)
            running = to_ring(running.astype(jnp.bfloat16))
    own = sums[0]
    grad_tokens = (own if running is None else own + running.astype(jnp.float32)).astype(jnp.bfloat16)
    rows_x, rows_g, acts, gate_term, up_term = kept
    grad_down = lax.dot_general(acts, rows_g, CONTRACT_FIRST, preferred_element_type=jnp.float32)
    grad_gate = lax.dot_general(gate_term, rows_x, CONTRACT_FIRST, preferred_element_type=jnp.float32)
    grad_up = lax.dot_general(up_term, rows_x, CONTRACT_FIRST, preferred_element_type=jnp.float32)
    return (
        grad_tokens,
        grad_gate.astype(jnp.bfloat16)[None],
        grad_up.astype(jnp.bfloat16)[None],
        grad_down.astype(jnp.bfloat16)[None],
    )


def solution(mesh):
    experts = mesh.shape["expert"]

    def body(tokens, out_grad, routes, combine, w_gate, w_up, w_down):
        rows, width = tokens.shape
        top = routes.shape[1]
        gathers = top * 4 >= experts and experts % 4 == 0 and mesh.shape["etp"] == 2
        run = gather_body if gathers and top * rows <= width else exchange_body
        return run(tokens, out_grad, routes, combine, w_gate, w_up, w_down)

    placed = (
        P("expert", "etp"),
        P("expert", "etp"),
        P("expert", None),
        P("expert", None),
        P("expert", "etp", None),
        P("expert", "etp", None),
        P("expert", "etp", None),
    )
    return jax.shard_map(
        body,
        mesh=mesh,
        in_specs=placed,
        out_specs=(
            P("expert", "etp"),
            P("expert", "etp", None),
            P("expert", "etp", None),
            P("expert", "etp", None),
        ),
        check_vma=False,
    )
```

```python
import functools

import jax
import jax.numpy as jnp
from jax import lax
from jax.experimental import pallas as pl
from jax.experimental.pallas import tpu as pltpu
from jax.sharding import PartitionSpec as P

CONTRACT_LAST = (((1,), (1,)), ((), ()))
CONTRACT_FIRST = (((0,), (0,)), ((), ()))
INFO_ROWS = 16
VMEM_LIMIT = 16 * 1024 * 1024


def pack_rows(token_rows, grad_rows, token_of, scale, is_live):
    mask = is_live[:, None].astype(token_rows.dtype)
    inputs_sent = token_rows[token_of] * mask
    grads_sent = (scale[:, None] * grad_rows[token_of].astype(jnp.float32)).astype(jnp.bfloat16)
    return (inputs_sent, grads_sent)


def pair_positions(routed_flat, experts):
    pair_total = routed_flat.shape[0]
    span = 128
    groups = pair_total // span
    labels = jnp.arange(experts, dtype=jnp.int32)
    one_hot = (routed_flat[:, None] == labels[None, :]).astype(jnp.bfloat16)
    grouped = one_hot.reshape(groups, span, experts)
    row_ids = jnp.arange(span, dtype=jnp.int32)
    lower = (row_ids[None, :] < row_ids[:, None]).astype(jnp.bfloat16)
    within = jnp.einsum("ij,bje->bie", lower, grouped, preferred_element_type=jnp.float32)
    group_sums = jnp.sum(grouped.astype(jnp.float32), axis=1)
    group_before = jnp.cumsum(group_sums, axis=0) - group_sums
    earlier = within + group_before[:, None, :]
    counted = jnp.sum(earlier * grouped.astype(jnp.float32), axis=2)
    return counted.reshape(pair_total).astype(jnp.int32)


def exchange_body(tokens, out_grad, routes, combine, w_gate, w_up, w_down):
    experts = lax.axis_size("expert")
    tok_rows = tokens.shape[0]
    col_width = tokens.shape[1]
    choose_count = routes.shape[1]
    per_pair = tok_rows * choose_count // experts
    capacity = per_pair + per_pair // 8
    routed_flat = routes.reshape(-1)
    pair_total = routed_flat.shape[0]
    position = pair_positions(routed_flat, experts)
    target = routed_flat * capacity + position
    anchor = jnp.full((experts * capacity,), pair_total, jnp.int32)
    anchor = anchor.at[target].set(jnp.arange(pair_total, dtype=jnp.int32))
    is_live = anchor < pair_total
    safe_anchor = jnp.minimum(anchor, pair_total - 1)
    token_of = safe_anchor // choose_count
    scale = combine.reshape(-1)[safe_anchor] * is_live.astype(jnp.float32)
    full_tokens, full_grads = (
        lax.all_gather(tokens, "etp", axis=1, tiled=True),
        lax.all_gather(out_grad, "etp", axis=1, tiled=True),
    )
    inputs_sent, grads_sent = pack_rows(full_tokens, full_grads, token_of, scale, is_live)
    rows_x, rows_g = (
        lax.all_to_all(inputs_sent, "expert", split_axis=0, concat_axis=0, tiled=True),
        lax.all_to_all(grads_sent, "expert", split_axis=0, concat_axis=0, tiled=True),
    )
    gate_w = w_gate[0]
    up_w = w_up[0]
    down_w = w_down[0]
    gate = lax.dot_general(rows_x, gate_w, CONTRACT_LAST, preferred_element_type=jnp.float32)
    up = lax.dot_general(rows_x, up_w, CONTRACT_LAST, preferred_element_type=jnp.float32)
    hidden_grad = lax.dot_general(rows_g, down_w, CONTRACT_LAST, preferred_element_type=jnp.float32)
    sigma = jax.nn.sigmoid(gate)
    silu = gate * sigma
    acts = (silu * up).astype(jnp.bfloat16)
    grad_down = lax.dot_general(acts, rows_g, CONTRACT_FIRST, preferred_element_type=jnp.float32)
    gate_term = (hidden_grad * up * sigma * (1.0 + gate * (1.0 - sigma))).astype(jnp.bfloat16)
    up_term = (hidden_grad * silu).astype(jnp.bfloat16)
    grad_gate = lax.dot_general(
        gate_term, rows_x, CONTRACT_FIRST, preferred_element_type=jnp.float32
    )
    grad_up = lax.dot_general(up_term, rows_x, CONTRACT_FIRST, preferred_element_type=jnp.float32)
    swapped_gate, swapped_up = (
        lax.all_to_all(gate_w, "etp", split_axis=1, concat_axis=0, tiled=True),
        lax.all_to_all(up_w, "etp", split_axis=1, concat_axis=0, tiled=True),
    )
    running = jnp.dot(
        lax.all_gather(gate_term, "etp", axis=1, tiled=True),
        swapped_gate,
        preferred_element_type=jnp.float32,
    )
    slot_grads = running + jnp.dot(
        lax.all_gather(up_term, "etp", axis=1, tiled=True),
        swapped_up,
        preferred_element_type=jnp.float32,
    )
    slot_grads = slot_grads.astype(jnp.bfloat16)
    returned = lax.all_to_all(slot_grads, "expert", split_axis=0, concat_axis=0, tiled=True)
    picked = returned[target].astype(jnp.float32).reshape(tok_rows, choose_count, col_width)
    grad_tokens = jnp.sum(picked, axis=1).astype(jnp.bfloat16)
    return (
        grad_tokens,
        grad_gate.astype(jnp.bfloat16)[None],
        grad_up.astype(jnp.bfloat16)[None],
        grad_down.astype(jnp.bfloat16)[None],
    )


def pack_kernel(tokens_ref, grads_ref, routes_ref, combine_ref, out_ref):
    rows = tokens_ref.shape[0]
    out_ref[:rows] = tokens_ref[...]
    out_ref[rows:2 * rows] = grads_ref[...]
    top = routes_ref.shape[0]
    routes = routes_ref[...].astype(jnp.float32)
    weights = combine_ref[...]
    high = weights.astype(jnp.bfloat16).astype(jnp.float32)
    middle = (weights - high).astype(jnp.bfloat16).astype(jnp.float32)
    low = weights - high - middle
    blank = jnp.zeros((INFO_ROWS - 4, rows), jnp.float32)
    for k in range(top):
        own = slice(k, k + 1)
        column = jnp.concatenate([routes[own], high[own], middle[own], low[own], blank], axis=0)
        out_ref[2 * rows:, k * rows:(k + 1) * rows] = column.astype(jnp.bfloat16)


def pack_share(tokens, out_grad, routes, combine):
    rows, width = tokens.shape
    vmem = pl.BlockSpec(memory_space=pltpu.VMEM)
    return pl.pallas_call(
        pack_kernel,
        in_specs=[vmem] * 4,
        out_specs=vmem,
        out_shape=jax.ShapeDtypeStruct((2 * rows + INFO_ROWS, width), jnp.bfloat16),
        cost_estimate=pl.CostEstimate(flops=0, bytes_accessed=8 * rows * width, transcendentals=0),
        name="pack",
    )(tokens, out_grad, routes.T, combine.T)


def load_kernel(*refs):
    count = (len(refs) - 1) // 2
    moves = [pltpu.make_async_copy(refs[i], refs[count + i], refs[-1].at[i]) for i in range(count)]
    for move in moves:
        move.start()
    for move in moves:
        move.wait()


def load_weights(weights):
    return pl.pallas_call(
        load_kernel,
        in_specs=[pl.BlockSpec(memory_space=pltpu.HBM)] * len(weights),
        out_specs=[pl.BlockSpec(memory_space=pltpu.VMEM)] * len(weights),
        out_shape=[jax.ShapeDtypeStruct(w.shape, w.dtype) for w in weights],
        scratch_shapes=[pltpu.SemaphoreType.DMA((len(weights),))],
        name="load",
    )(*weights)


def pick_kernel(top, rows, place_ref, *refs):
    shares, (mine_ref, theirs_ref, picks_ref) = refs[:4], refs[4:]
    me, own_half, core = place_ref[0], place_ref[1], place_ref[2]
    pair_slots, width = mine_ref.shape[1], shares[0].shape[1]
    earlier = (
        lax.broadcasted_iota(jnp.int32, (2 * rows, 2 * rows), 0)
        < lax.broadcasted_iota(jnp.int32, (2 * rows, 2 * rows), 1)
    ).astype(jnp.bfloat16)
    infos = [
        [share_ref[pl.ds(2 * rows, INFO_ROWS), k * rows:(k + 1) * rows].astype(jnp.float32) for k in range(top)]
        for share_ref in (shares[0], shares[3])
    ]
    picks, scales = [], []
    for expert in (me, me + 1 - 2 * core):
        named, weights = [], []
        for block in infos:
            hits, weight = 0.0, 0.0
            for info in block:
                hit = info[0:1] == expert.astype(jnp.float32)
                hits += hit.astype(jnp.float32)
                weight += jnp.where(hit, info[1:2] + info[2:3] + info[3:4], 0.0)
            named.append(hits)
            weights.append(weight)
        named = jnp.concatenate(named, axis=1)
        weights = jnp.concatenate(weights, axis=1)
        counted = jnp.dot(
            jnp.broadcast_to(named, (16, 2 * rows)).astype(jnp.bfloat16),
            earlier,
            preferred_element_type=jnp.float32,
        )[:1]
        slot_of = jnp.where(named > 0.0, counted.astype(jnp.int32), -1)
        chosen = slot_of == lax.broadcasted_iota(jnp.int32, (pair_slots, 2 * rows), 0)
        picks.append(chosen.astype(jnp.bfloat16))
        scales.append(jnp.sum(jnp.where(chosen, weights, 0.0), axis=1, keepdims=True))
    picks = jnp.concatenate(picks, axis=0)
    scales = jnp.concatenate(scales, axis=0)
    picks_ref[...] = picks
    for h in range(2):
        cols = pl.ds(pl.multiple_of((own_half if h == 0 else 1 - own_half) * width, width), width)
        for part in range(2):
            own, first, second, both = [ref[pl.ds(part * rows, rows)] for ref in shares]
            if h == 0:
                held = jnp.concatenate([own, jnp.where(core == 1, second, first)], axis=0)
            else:
                held = jnp.concatenate([jnp.where(core == 1, first, second), both], axis=0)
            picked = jnp.dot(picks, held, preferred_element_type=jnp.float32)
            if part == 1:
                picked = scales * picked
            picked = picked.astype(jnp.bfloat16)
            mine_ref[part, :, cols] = picked[:pair_slots]
            theirs_ref[part, :, cols] = picked[pair_slots:]


def expert_kernel(index, chained, mine_ref, theirs_ref, wg_ref, wu_ref, wd_ref, *refs):
    near_ref, far_ref, *kept_refs = refs[5 if chained else 0:][:7]
    act_ref, gt_ref, ut_ref, sems = refs[-4:]
    pair_slots = mine_ref.shape[1]
    slots = 2 * pair_slots

    def kept_move(source, target, part, count, i):
        return pltpu.make_async_copy(
            source, kept_refs[target].at[pl.ds(index * slots + part * pair_slots, count)], sems.at[i]
        )

    moves = [
        kept_move(mine_ref.at[0], 0, 0, pair_slots, 0),
        kept_move(theirs_ref.at[0], 0, 1, pair_slots, 1),
        kept_move(mine_ref.at[1], 1, 0, pair_slots, 2),
        kept_move(theirs_ref.at[1], 1, 1, pair_slots, 3),
        kept_move(act_ref, 2, 0, slots, 4),
        kept_move(gt_ref, 3, 0, slots, 5),
        kept_move(ut_ref, 4, 0, slots, 6),
    ]
    for move in moves[:4]:
        move.start()
    rows_x = jnp.concatenate([mine_ref[0], theirs_ref[0]], axis=0)
    rows_g = jnp.concatenate([mine_ref[1], theirs_ref[1]], axis=0)
    gate = lax.dot_general(rows_x, wg_ref[...], CONTRACT_LAST, preferred_element_type=jnp.float32)
    up = lax.dot_general(rows_x, wu_ref[...], CONTRACT_LAST, preferred_element_type=jnp.float32)
    hidden_grad = lax.dot_general(rows_g, wd_ref[...], CONTRACT_LAST, preferred_element_type=jnp.float32)
    sigma = 1.0 / (1.0 + jnp.exp(-gate))
    silu = gate * sigma
    act_ref[...] = (silu * up).astype(jnp.bfloat16)
    gt_ref[...] = (hidden_grad * up * sigma * (1.0 + gate * (1.0 - sigma))).astype(jnp.bfloat16)
    ut_ref[...] = (hidden_grad * silu).astype(jnp.bfloat16)
    for move in moves[4:]:
        move.start()
    slot = jnp.dot(gt_ref[...], wg_ref[...], preferred_element_type=jnp.float32)
    slot += jnp.dot(ut_ref[...], wu_ref[...], preferred_element_type=jnp.float32)
    far_ref[...] = slot[pair_slots:].astype(jnp.bfloat16)
    near_ref[...] = slot[:pair_slots].astype(jnp.bfloat16)
    for move in moves:
        move.wait()


def place_kernel(place_ref, picks_ref, near_ref, far_ref, keep_ref, send_ref):
    own_half, core = place_ref[1], place_ref[2]
    _, rows, width = keep_ref.shape
    pair_slots = near_ref.shape[0]
    backs = []
    for h in range(2):
        cols = pl.ds(pl.multiple_of((own_half if h == 0 else 1 - own_half) * width, width), width)
        slot = jnp.concatenate([near_ref[:, cols], far_ref[:, cols]], axis=0)
        backs.append(lax.dot_general(picks_ref[...], slot, CONTRACT_FIRST, preferred_element_type=jnp.float32))
    keep_ref[0] = backs[0][:rows]
    keep_ref[1] = jnp.where(core == 1, backs[1][:rows], backs[0][rows:])
    send_ref[0] = jnp.where(core == 1, backs[0][rows:], backs[1][:rows]).astype(jnp.bfloat16)
    send_ref[1] = backs[1][rows:].astype(jnp.bfloat16)


def pick_rows(place, shares, top, rows, pair_slots):
    width = shares[0].shape[1]
    vmem = pl.BlockSpec(memory_space=pltpu.VMEM)
    picked = jax.ShapeDtypeStruct((2, pair_slots, 2 * width), jnp.bfloat16)
    return pl.pallas_call(
        functools.partial(pick_kernel, top, rows),
        in_specs=[pl.BlockSpec(memory_space=pltpu.SMEM)] + [vmem] * 4,
        out_specs=[vmem] * 3,
        out_shape=[picked, picked, jax.ShapeDtypeStruct((2 * pair_slots, 2 * rows), jnp.bfloat16)],
        compiler_params=pltpu.CompilerParams(vmem_limit_bytes=VMEM_LIMIT),
        cost_estimate=pl.CostEstimate(
            flops=32 * pair_slots * 2 * rows * 2 * width,
            bytes_accessed=2 * (4 * shares[0].size + 8 * pair_slots * width),
            transcendentals=0,
        ),
        name="pick",
    )(place, *shares)


def run_experts(index, chunks, mine, theirs, weights, kept):
    _, pair_slots, features = mine.shape
    hidden = weights[0].shape[0]
    slots = 2 * pair_slots
    hbm = pl.BlockSpec(memory_space=pltpu.HBM)
    vmem = pl.BlockSpec(memory_space=pltpu.VMEM)
    part = jax.ShapeDtypeStruct((pair_slots, features), jnp.bfloat16)
    wide = jax.ShapeDtypeStruct((chunks * slots, features), jnp.bfloat16)
    narrow = jax.ShapeDtypeStruct((chunks * slots, hidden), jnp.bfloat16)
    return pl.pallas_call(
        functools.partial(expert_kernel, index, kept is not None),
        in_specs=[vmem] * 5 + [hbm] * (0 if kept is None else 5),
        out_specs=[vmem] * 2 + [hbm] * 5,
        out_shape=[part, part, wide, wide, narrow, narrow, narrow],
        scratch_shapes=[pltpu.VMEM((slots, hidden), jnp.bfloat16)] * 3 + [pltpu.SemaphoreType.DMA((7,))],
        input_output_aliases={} if kept is None else {5 + i: 2 + i for i in range(5)},
        compiler_params=pltpu.CompilerParams(vmem_limit_bytes=VMEM_LIMIT),
        cost_estimate=pl.CostEstimate(
            flops=20 * slots * features * hidden,
            bytes_accessed=2 * (3 * hidden * features + slots * (4 * features + 3 * hidden)),
            transcendentals=slots * hidden,
        ),
        name="experts",
    )(mine, theirs, *weights, *(kept or ()))


def place_rows(place, picks, near, far, rows, width):
    vmem = pl.BlockSpec(memory_space=pltpu.VMEM)
    return pl.pallas_call(
        place_kernel,
        in_specs=[pl.BlockSpec(memory_space=pltpu.SMEM)] + [vmem] * 3,
        out_specs=[vmem] * 2,
        out_shape=[
            jax.ShapeDtypeStruct((2, rows, width), jnp.float32),
            jax.ShapeDtypeStruct((2, rows, width), jnp.bfloat16),
        ],
        compiler_params=pltpu.CompilerParams(vmem_limit_bytes=VMEM_LIMIT),
        cost_estimate=pl.CostEstimate(
            flops=4 * picks.size * 2 * width, bytes_accessed=4 * near.size + 12 * rows * width, transcendentals=0
        ),
        name="place",
    )(place, picks, near, far)


def ring_order(length):
    return list(range(0, min(1, length))) + list(range(1, length, 2)) + list(range(2, length, 2))[::-1]


def gather_body(tokens, out_grad, routes, combine, w_gate, w_up, w_down):
    experts = lax.axis_size("expert")
    chunks = experts // 4
    rows, width = tokens.shape
    top = routes.shape[1]
    per_pair = rows * top // experts
    capacity = per_pair + per_pair // 8
    pair_slots = -(-2 * capacity // 16) * 16
    order = ring_order(chunks)
    after = {order[i]: order[(i + 1) % chunks] for i in range(chunks)}
    devices = [(e, h) for e in range(experts) for h in range(2)]

    def permute(value, target):
        pairs = [(e * 2 + h, target(e, h)[0] * 2 + target(e, h)[1]) for e, h in devices]
        return lax.ppermute(value, ("expert", "etp"), pairs)

    def to_ring(value):
        return permute(value, lambda e, h: (after[e // 4] * 4 + e % 4, h))

    def to_owner(value, back):
        owner = {order[i]: order[(i - back) % chunks] for i in range(chunks)}
        return permute(value, lambda e, h: (owner[e // 4] * 4 + e % 4, h))

    def to_core(value):
        return permute(value, lambda e, h: (e ^ 1, h))

    def to_first(value):
        return permute(value, lambda e, h: (e, h ^ 1) if e % 2 else (e ^ 2, h))

    def to_second(value):
        return permute(value, lambda e, h: (e ^ 2, h) if e % 2 else (e, h ^ 1))

    me = lax.axis_index("expert")
    place = jnp.stack([me, lax.axis_index("etp"), me % 2]).astype(jnp.int32)
    share = pack_share(tokens, out_grad, routes, combine)
    weights = load_weights((w_gate[0], w_up[0], w_down[0]))

    def tied(values, mark):
        return lax.optimization_barrier((values, mark))[0]

    def placed(picks, near, far):
        return place_rows(place, picks, near, to_core(far), rows, width)

    def added(keep, came):
        return keep + came.astype(jnp.float32)

    ring_sends = [("s", 1)] + [(kind, c) for c in range(2, chunks) for kind in ("s", "f")]
    ring_sends = [key for key in ring_sends if key[1] < chunks]
    plane_sends = [("f", 0), ("a", 0), ("f", 1), ("b", 0)] + [(kind, c) for c in range(1, chunks) for kind in ("a", "b")]
    plane_sends = [key for key in plane_sends if key[1] < chunks]
    have = {("s", 0): share}
    kept, picked, parts, waiting = None, None, None, None
    late, done = [], 0
    while plane_sends:
        came = {}
        planned = [key for key in plane_sends if (("f" if key[0] == "b" else "s"), key[1]) in have][:2]
        for kind, c in planned:
            source = have["f" if kind == "b" else "s", c]
            came[kind, c] = to_first(source) if kind == "f" else to_second(source)
            plane_sends.remove((kind, c))
        if ring_sends and (ring_sends[0][0], ring_sends[0][1] - 1) in have:
            kind, c = ring_sends.pop(0)
            came[kind, c] = to_ring(have[kind, c - 1])
        ready, waiting = waiting, placed(*parts) if parts is not None else None
        if ready is not None:
            keep, send = ready
            late.append((keep, to_second(send if waiting is None else tied(send, waiting[1]))))
        parts = None
        if picked is not None:
            mine, theirs, picks = picked
            near, far, *kept = run_experts(done, chunks, mine, to_core(theirs), weights, kept)
            parts, picked = (picks, near, far), None
            done += 1
        if plane_sends and all((kind, done) in have for kind in "sfab"):
            picked = pick_rows(place, [have.pop((kind, done)) for kind in "sfab"], top, rows, pair_slots)
        came, have, picked, parts, waiting, weights = lax.optimization_barrier(
            (came, have, picked, parts, waiting, weights)
        )
        have.update(came)
    mine, theirs, picks = pick_rows(place, [have[kind, done] for kind in "sfab"], top, rows, pair_slots)
    if waiting is not None:
        keep, send = waiting
        late.append((keep, to_second(tied(send, theirs))))
    if parts is not None:
        keep, send = placed(*tied(parts, theirs))
        late.append((keep, to_second(send)))
    near, far, *kept = run_experts(done, chunks, mine, to_core(theirs), weights, kept)
    keep, send = placed(picks, near, far)
    late.append((keep, to_second(send)))
    marks = ([near] * chunks + [send])[-(len(late) - 1):] + [None]
    grad_tokens = 0.0
    for c, ((keep, came), mark) in enumerate(zip(late, marks)):
        pair = added(keep, came if mark is None else tied(came, mark))
        total = added(pair[0], to_first(pair[1].astype(jnp.bfloat16)))
        grad_tokens += total if c == 0 else to_owner(total.astype(jnp.bfloat16), c).astype(jnp.float32)
    grad_tokens = grad_tokens.astype(jnp.bfloat16)
    rows_x, rows_g, acts, gate_term, up_term = kept
    grad_down = lax.dot_general(acts, rows_g, CONTRACT_FIRST, preferred_element_type=jnp.float32)
    grad_gate = lax.dot_general(gate_term, rows_x, CONTRACT_FIRST, preferred_element_type=jnp.float32)
    grad_up = lax.dot_general(up_term, rows_x, CONTRACT_FIRST, preferred_element_type=jnp.float32)
    return (
        grad_tokens,
        grad_gate.astype(jnp.bfloat16)[None],
        grad_up.astype(jnp.bfloat16)[None],
        grad_down.astype(jnp.bfloat16)[None],
    )


def solution(mesh):
    experts = mesh.shape["expert"]

    def body(tokens, out_grad, routes, combine, w_gate, w_up, w_down):
        rows, width = tokens.shape
        top = routes.shape[1]
        gathers = top * 4 >= experts and experts % 4 == 0 and mesh.shape["etp"] == 2
        run = gather_body if gathers and top * rows <= width else exchange_body
        return run(tokens, out_grad, routes, combine, w_gate, w_up, w_down)

    placed = (
        P("expert", "etp"),
        P("expert", "etp"),
        P("expert", None),
        P("expert", None),
        P("expert", "etp", None),
        P("expert", "etp", None),
        P("expert", "etp", None),
    )
    return jax.shard_map(
        body,
        mesh=mesh,
        in_specs=placed,
        out_specs=(
            P("expert", "etp"),
            P("expert", "etp", None),
            P("expert", "etp", None),
            P("expert", "etp", None),
        ),
        check_vma=False,
    )
```

```python
import functools

import jax
import jax.numpy as jnp
from jax import lax
from jax.experimental import pallas as pl
from jax.experimental.pallas import tpu as pltpu
from jax.sharding import PartitionSpec as P

CONTRACT_LAST = (((1,), (1,)), ((), ()))
CONTRACT_FIRST = (((0,), (0,)), ((), ()))
INFO_ROWS = 16
VMEM_LIMIT = 16 * 1024 * 1024


def pack_rows(token_rows, grad_rows, token_of, scale, is_live):
    mask = is_live[:, None].astype(token_rows.dtype)
    inputs_sent = token_rows[token_of] * mask
    grads_sent = (scale[:, None] * grad_rows[token_of].astype(jnp.float32)).astype(jnp.bfloat16)
    return (inputs_sent, grads_sent)


def pair_positions(routed_flat, experts):
    pair_total = routed_flat.shape[0]
    span = 128
    groups = pair_total // span
    labels = jnp.arange(experts, dtype=jnp.int32)
    one_hot = (routed_flat[:, None] == labels[None, :]).astype(jnp.bfloat16)
    grouped = one_hot.reshape(groups, span, experts)
    row_ids = jnp.arange(span, dtype=jnp.int32)
    lower = (row_ids[None, :] < row_ids[:, None]).astype(jnp.bfloat16)
    within = jnp.einsum("ij,bje->bie", lower, grouped, preferred_element_type=jnp.float32)
    group_sums = jnp.sum(grouped.astype(jnp.float32), axis=1)
    group_before = jnp.cumsum(group_sums, axis=0) - group_sums
    earlier = within + group_before[:, None, :]
    counted = jnp.sum(earlier * grouped.astype(jnp.float32), axis=2)
    return counted.reshape(pair_total).astype(jnp.int32)


def exchange_body(tokens, out_grad, routes, combine, w_gate, w_up, w_down):
    experts = lax.axis_size("expert")
    tok_rows = tokens.shape[0]
    col_width = tokens.shape[1]
    choose_count = routes.shape[1]
    per_pair = tok_rows * choose_count // experts
    capacity = per_pair + per_pair // 8
    routed_flat = routes.reshape(-1)
    pair_total = routed_flat.shape[0]
    position = pair_positions(routed_flat, experts)
    target = routed_flat * capacity + position
    anchor = jnp.full((experts * capacity,), pair_total, jnp.int32)
    anchor = anchor.at[target].set(jnp.arange(pair_total, dtype=jnp.int32))
    is_live = anchor < pair_total
    safe_anchor = jnp.minimum(anchor, pair_total - 1)
    token_of = safe_anchor // choose_count
    scale = combine.reshape(-1)[safe_anchor] * is_live.astype(jnp.float32)
    full_tokens, full_grads = (
        lax.all_gather(tokens, "etp", axis=1, tiled=True),
        lax.all_gather(out_grad, "etp", axis=1, tiled=True),
    )
    inputs_sent, grads_sent = pack_rows(full_tokens, full_grads, token_of, scale, is_live)
    rows_x, rows_g = (
        lax.all_to_all(inputs_sent, "expert", split_axis=0, concat_axis=0, tiled=True),
        lax.all_to_all(grads_sent, "expert", split_axis=0, concat_axis=0, tiled=True),
    )
    gate_w = w_gate[0]
    up_w = w_up[0]
    down_w = w_down[0]
    gate = lax.dot_general(rows_x, gate_w, CONTRACT_LAST, preferred_element_type=jnp.float32)
    up = lax.dot_general(rows_x, up_w, CONTRACT_LAST, preferred_element_type=jnp.float32)
    hidden_grad = lax.dot_general(rows_g, down_w, CONTRACT_LAST, preferred_element_type=jnp.float32)
    sigma = jax.nn.sigmoid(gate)
    silu = gate * sigma
    acts = (silu * up).astype(jnp.bfloat16)
    grad_down = lax.dot_general(acts, rows_g, CONTRACT_FIRST, preferred_element_type=jnp.float32)
    gate_term = (hidden_grad * up * sigma * (1.0 + gate * (1.0 - sigma))).astype(jnp.bfloat16)
    up_term = (hidden_grad * silu).astype(jnp.bfloat16)
    grad_gate = lax.dot_general(
        gate_term, rows_x, CONTRACT_FIRST, preferred_element_type=jnp.float32
    )
    grad_up = lax.dot_general(up_term, rows_x, CONTRACT_FIRST, preferred_element_type=jnp.float32)
    swapped_gate, swapped_up = (
        lax.all_to_all(gate_w, "etp", split_axis=1, concat_axis=0, tiled=True),
        lax.all_to_all(up_w, "etp", split_axis=1, concat_axis=0, tiled=True),
    )
    running = jnp.dot(
        lax.all_gather(gate_term, "etp", axis=1, tiled=True),
        swapped_gate,
        preferred_element_type=jnp.float32,
    )
    slot_grads = running + jnp.dot(
        lax.all_gather(up_term, "etp", axis=1, tiled=True),
        swapped_up,
        preferred_element_type=jnp.float32,
    )
    slot_grads = slot_grads.astype(jnp.bfloat16)
    returned = lax.all_to_all(slot_grads, "expert", split_axis=0, concat_axis=0, tiled=True)
    picked = returned[target].astype(jnp.float32).reshape(tok_rows, choose_count, col_width)
    grad_tokens = jnp.sum(picked, axis=1).astype(jnp.bfloat16)
    return (
        grad_tokens,
        grad_gate.astype(jnp.bfloat16)[None],
        grad_up.astype(jnp.bfloat16)[None],
        grad_down.astype(jnp.bfloat16)[None],
    )


def pack_kernel(tokens_ref, grads_ref, routes_ref, combine_ref, out_ref):
    rows = tokens_ref.shape[0]
    out_ref[:rows] = tokens_ref[...]
    out_ref[rows:2 * rows] = grads_ref[...]
    top = routes_ref.shape[0]
    routes = routes_ref[...].astype(jnp.float32)
    weights = combine_ref[...]
    high = weights.astype(jnp.bfloat16).astype(jnp.float32)
    middle = (weights - high).astype(jnp.bfloat16).astype(jnp.float32)
    low = weights - high - middle
    blank = jnp.zeros((INFO_ROWS - 4, rows), jnp.float32)
    for k in range(top):
        own = slice(k, k + 1)
        column = jnp.concatenate([routes[own], high[own], middle[own], low[own], blank], axis=0)
        out_ref[2 * rows:, k * rows:(k + 1) * rows] = column.astype(jnp.bfloat16)


def pack_share(tokens, out_grad, routes, combine):
    rows, width = tokens.shape
    vmem = pl.BlockSpec(memory_space=pltpu.VMEM)
    return pl.pallas_call(
        pack_kernel,
        in_specs=[vmem] * 4,
        out_specs=vmem,
        out_shape=jax.ShapeDtypeStruct((2 * rows + INFO_ROWS, width), jnp.bfloat16),
        cost_estimate=pl.CostEstimate(flops=0, bytes_accessed=8 * rows * width, transcendentals=0),
        name="pack",
    )(tokens, out_grad, routes.T, combine.T)


def load_kernel(*refs):
    count = (len(refs) - 1) // 2
    moves = [pltpu.make_async_copy(refs[i], refs[count + i], refs[-1].at[i]) for i in range(count)]
    for move in moves:
        move.start()
    for move in moves:
        move.wait()


def load_weights(weights):
    return pl.pallas_call(
        load_kernel,
        in_specs=[pl.BlockSpec(memory_space=pltpu.HBM)] * len(weights),
        out_specs=[pl.BlockSpec(memory_space=pltpu.VMEM)] * len(weights),
        out_shape=[jax.ShapeDtypeStruct(w.shape, w.dtype) for w in weights],
        scratch_shapes=[pltpu.SemaphoreType.DMA((len(weights),))],
        name="load",
    )(*weights)


def pick_kernel(top, rows, place_ref, *refs):
    shares, (mine_ref, theirs_ref, picks_ref) = refs[:4], refs[4:]
    me, own_half, core = place_ref[0], place_ref[1], place_ref[2]
    pair_slots, width = mine_ref.shape[1], shares[0].shape[1]
    earlier = (
        lax.broadcasted_iota(jnp.int32, (2 * rows, 2 * rows), 0)
        < lax.broadcasted_iota(jnp.int32, (2 * rows, 2 * rows), 1)
    ).astype(jnp.bfloat16)
    infos = [
        [share_ref[pl.ds(2 * rows, INFO_ROWS), k * rows:(k + 1) * rows].astype(jnp.float32) for k in range(top)]
        for share_ref in (shares[0], shares[3])
    ]
    picks, scales = [], []
    for expert in (me, me + 1 - 2 * core):
        named, weights = [], []
        for block in infos:
            hits, weight = 0.0, 0.0
            for info in block:
                hit = info[0:1] == expert.astype(jnp.float32)
                hits += hit.astype(jnp.float32)
                weight += jnp.where(hit, info[1:2] + info[2:3] + info[3:4], 0.0)
            named.append(hits)
            weights.append(weight)
        named = jnp.concatenate(named, axis=1)
        weights = jnp.concatenate(weights, axis=1)
        counted = jnp.dot(
            jnp.broadcast_to(named, (16, 2 * rows)).astype(jnp.bfloat16),
            earlier,
            preferred_element_type=jnp.float32,
        )[:1]
        slot_of = jnp.where(named > 0.0, counted.astype(jnp.int32), -1)
        chosen = slot_of == lax.broadcasted_iota(jnp.int32, (pair_slots, 2 * rows), 0)
        picks.append(chosen.astype(jnp.bfloat16))
        scales.append(jnp.sum(jnp.where(chosen, weights, 0.0), axis=1, keepdims=True))
    picks = jnp.concatenate(picks, axis=0)
    scales = jnp.concatenate(scales, axis=0)
    picks_ref[...] = picks
    for h in range(2):
        cols = pl.ds(pl.multiple_of((own_half if h == 0 else 1 - own_half) * width, width), width)
        for part in range(2):
            own, first, second, both = [ref[pl.ds(part * rows, rows)] for ref in shares]
            if h == 0:
                held = jnp.concatenate([own, jnp.where(core == 1, second, first)], axis=0)
            else:
                held = jnp.concatenate([jnp.where(core == 1, first, second), both], axis=0)
            picked = jnp.dot(picks, held, preferred_element_type=jnp.float32)
            if part == 1:
                picked = scales * picked
            picked = picked.astype(jnp.bfloat16)
            mine_ref[part, :, cols] = picked[:pair_slots]
            theirs_ref[part, :, cols] = picked[pair_slots:]


def expert_kernel(index, chained, mine_ref, theirs_ref, wg_ref, wu_ref, wd_ref, *refs):
    near_ref, far_ref, *kept_refs = refs[5 if chained else 0:][:7]
    act_ref, gt_ref, ut_ref, sems = refs[-4:]
    pair_slots = mine_ref.shape[1]
    slots = 2 * pair_slots

    def kept_move(source, target, part, count, i):
        return pltpu.make_async_copy(
            source, kept_refs[target].at[pl.ds(index * slots + part * pair_slots, count)], sems.at[i]
        )

    moves = [
        kept_move(mine_ref.at[0], 0, 0, pair_slots, 0),
        kept_move(theirs_ref.at[0], 0, 1, pair_slots, 1),
        kept_move(mine_ref.at[1], 1, 0, pair_slots, 2),
        kept_move(theirs_ref.at[1], 1, 1, pair_slots, 3),
        kept_move(act_ref, 2, 0, slots, 4),
        kept_move(gt_ref, 3, 0, slots, 5),
        kept_move(ut_ref, 4, 0, slots, 6),
    ]
    for move in moves[:4]:
        move.start()
    rows_x = jnp.concatenate([mine_ref[0], theirs_ref[0]], axis=0)
    rows_g = jnp.concatenate([mine_ref[1], theirs_ref[1]], axis=0)
    gate = lax.dot_general(rows_x, wg_ref[...], CONTRACT_LAST, preferred_element_type=jnp.float32)
    up = lax.dot_general(rows_x, wu_ref[...], CONTRACT_LAST, preferred_element_type=jnp.float32)
    hidden_grad = lax.dot_general(rows_g, wd_ref[...], CONTRACT_LAST, preferred_element_type=jnp.float32)
    sigma = 1.0 / (1.0 + jnp.exp(-gate))
    silu = gate * sigma
    act_ref[...] = (silu * up).astype(jnp.bfloat16)
    gt_ref[...] = (hidden_grad * up * sigma * (1.0 + gate * (1.0 - sigma))).astype(jnp.bfloat16)
    ut_ref[...] = (hidden_grad * silu).astype(jnp.bfloat16)
    for move in moves[4:]:
        move.start()
    slot = jnp.dot(gt_ref[...], wg_ref[...], preferred_element_type=jnp.float32)
    slot += jnp.dot(ut_ref[...], wu_ref[...], preferred_element_type=jnp.float32)
    far_ref[...] = slot[pair_slots:].astype(jnp.bfloat16)
    near_ref[...] = slot[:pair_slots].astype(jnp.bfloat16)
    for move in moves:
        move.wait()


def place_kernel(place_ref, picks_ref, near_ref, far_ref, keep_ref, send_ref):
    own_half, core = place_ref[1], place_ref[2]
    _, rows, width = keep_ref.shape
    pair_slots = near_ref.shape[0]
    backs = []
    for h in range(2):
        cols = pl.ds(pl.multiple_of((own_half if h == 0 else 1 - own_half) * width, width), width)
        slot = jnp.concatenate([near_ref[:, cols], far_ref[:, cols]], axis=0)
        backs.append(lax.dot_general(picks_ref[...], slot, CONTRACT_FIRST, preferred_element_type=jnp.float32))
    keep_ref[0] = backs[0][:rows]
    keep_ref[1] = jnp.where(core == 1, backs[1][:rows], backs[0][rows:])
    send_ref[0] = jnp.where(core == 1, backs[0][rows:], backs[1][:rows]).astype(jnp.bfloat16)
    send_ref[1] = backs[1][rows:].astype(jnp.bfloat16)


def pick_rows(place, shares, top, rows, pair_slots):
    width = shares[0].shape[1]
    vmem = pl.BlockSpec(memory_space=pltpu.VMEM)
    picked = jax.ShapeDtypeStruct((2, pair_slots, 2 * width), jnp.bfloat16)
    return pl.pallas_call(
        functools.partial(pick_kernel, top, rows),
        in_specs=[pl.BlockSpec(memory_space=pltpu.SMEM)] + [vmem] * 4,
        out_specs=[vmem] * 3,
        out_shape=[picked, picked, jax.ShapeDtypeStruct((2 * pair_slots, 2 * rows), jnp.bfloat16)],
        compiler_params=pltpu.CompilerParams(vmem_limit_bytes=VMEM_LIMIT),
        cost_estimate=pl.CostEstimate(
            flops=32 * pair_slots * 2 * rows * 2 * width,
            bytes_accessed=2 * (4 * shares[0].size + 8 * pair_slots * width),
            transcendentals=0,
        ),
        name="pick",
    )(place, *shares)


def run_experts(index, chunks, mine, theirs, weights, kept):
    _, pair_slots, features = mine.shape
    hidden = weights[0].shape[0]
    slots = 2 * pair_slots
    hbm = pl.BlockSpec(memory_space=pltpu.HBM)
    vmem = pl.BlockSpec(memory_space=pltpu.VMEM)
    part = jax.ShapeDtypeStruct((pair_slots, features), jnp.bfloat16)
    wide = jax.ShapeDtypeStruct((chunks * slots, features), jnp.bfloat16)
    narrow = jax.ShapeDtypeStruct((chunks * slots, hidden), jnp.bfloat16)
    return pl.pallas_call(
        functools.partial(expert_kernel, index, kept is not None),
        in_specs=[vmem] * 5 + [hbm] * (0 if kept is None else 5),
        out_specs=[vmem] * 2 + [hbm] * 5,
        out_shape=[part, part, wide, wide, narrow, narrow, narrow],
        scratch_shapes=[pltpu.VMEM((slots, hidden), jnp.bfloat16)] * 3 + [pltpu.SemaphoreType.DMA((7,))],
        input_output_aliases={} if kept is None else {5 + i: 2 + i for i in range(5)},
        compiler_params=pltpu.CompilerParams(vmem_limit_bytes=VMEM_LIMIT),
        cost_estimate=pl.CostEstimate(
            flops=20 * slots * features * hidden,
            bytes_accessed=2 * (3 * hidden * features + slots * (4 * features + 3 * hidden)),
            transcendentals=slots * hidden,
        ),
        name="experts",
    )(mine, theirs, *weights, *(kept or ()))


def place_rows(place, picks, near, far, rows, width):
    vmem = pl.BlockSpec(memory_space=pltpu.VMEM)
    return pl.pallas_call(
        place_kernel,
        in_specs=[pl.BlockSpec(memory_space=pltpu.SMEM)] + [vmem] * 3,
        out_specs=[vmem] * 2,
        out_shape=[
            jax.ShapeDtypeStruct((2, rows, width), jnp.float32),
            jax.ShapeDtypeStruct((2, rows, width), jnp.bfloat16),
        ],
        compiler_params=pltpu.CompilerParams(vmem_limit_bytes=VMEM_LIMIT),
        cost_estimate=pl.CostEstimate(
            flops=4 * picks.size * 2 * width, bytes_accessed=4 * near.size + 12 * rows * width, transcendentals=0
        ),
        name="place",
    )(place, picks, near, far)


def ring_order(length):
    return list(range(0, min(1, length))) + list(range(1, length, 2)) + list(range(2, length, 2))[::-1]


def gather_body(tokens, out_grad, routes, combine, w_gate, w_up, w_down):
    experts = lax.axis_size("expert")
    chunks = experts // 4
    rows, width = tokens.shape
    top = routes.shape[1]
    per_pair = rows * top // experts
    capacity = per_pair + per_pair // 8
    pair_slots = -(-2 * capacity // 16) * 16
    order = ring_order(chunks)
    after = {order[i]: order[(i + 1) % chunks] for i in range(chunks)}
    devices = [(e, h) for e in range(experts) for h in range(2)]

    def permute(value, target):
        pairs = [(e * 2 + h, target(e, h)[0] * 2 + target(e, h)[1]) for e, h in devices]
        return lax.ppermute(value, ("expert", "etp"), pairs)

    def to_ring(value):
        return permute(value, lambda e, h: (after[e // 4] * 4 + e % 4, h))

    def to_core(value):
        return permute(value, lambda e, h: (e ^ 1, h))

    def to_first(value):
        return permute(value, lambda e, h: (e, h ^ 1) if e % 2 else (e ^ 2, h))

    def to_second(value):
        return permute(value, lambda e, h: (e ^ 2, h) if e % 2 else (e, h ^ 1))

    me = lax.axis_index("expert")
    place = jnp.stack([me, lax.axis_index("etp"), me % 2]).astype(jnp.int32)
    share = pack_share(tokens, out_grad, routes, combine)
    weights = load_weights((w_gate[0], w_up[0], w_down[0]))

    def tied(values, mark):
        return lax.optimization_barrier((values, mark))[0]

    def placed(picks, near, far):
        return place_rows(place, picks, near, to_core(far), rows, width)

    def added(keep, came):
        return keep + came.astype(jnp.float32)

    ring_sends = [("s", 1)] + [(kind, c) for c in range(2, chunks) for kind in ("s", "f")]
    ring_sends = [key for key in ring_sends if key[1] < chunks]
    plane_sends = [("f", 0), ("a", 0), ("f", 1), ("b", 0)] + [(kind, c) for c in range(1, chunks) for kind in ("a", "b")]
    plane_sends = [key for key in plane_sends if key[1] < chunks]
    have = {("s", 0): share}
    kept, picked, parts, waiting = None, None, None, None
    late, done = [], 0
    while plane_sends:
        came = {}
        planned = [key for key in plane_sends if (("f" if key[0] == "b" else "s"), key[1]) in have][:2]
        for kind, c in planned:
            source = have["f" if kind == "b" else "s", c]
            came[kind, c] = to_first(source) if kind == "f" else to_second(source)
            plane_sends.remove((kind, c))
        if ring_sends and (ring_sends[0][0], ring_sends[0][1] - 1) in have:
            kind, c = ring_sends.pop(0)
            came[kind, c] = to_ring(have[kind, c - 1])
        ready, waiting = waiting, placed(*parts) if parts is not None else None
        if ready is not None:
            keep, send = ready
            late.append((keep, to_second(send if waiting is None else tied(send, waiting[1]))))
        parts = None
        if picked is not None:
            mine, theirs, picks = picked
            near, far, *kept = run_experts(done, chunks, mine, to_core(theirs), weights, kept)
            parts, picked = (picks, near, far), None
            done += 1
        if plane_sends and all((kind, done) in have for kind in "sfab"):
            picked = pick_rows(place, [have.pop((kind, done)) for kind in "sfab"], top, rows, pair_slots)
        came, have, picked, parts, waiting, weights = lax.optimization_barrier(
            (came, have, picked, parts, waiting, weights)
        )
        have.update(came)
    mine, theirs, picks = pick_rows(place, [have[kind, done] for kind in "sfab"], top, rows, pair_slots)
    if waiting is not None:
        keep, send = waiting
        late.append((keep, to_second(tied(send, theirs))))
    if parts is not None:
        keep, send = placed(*tied(parts, theirs))
        late.append((keep, to_second(send)))
    near, far, *kept = run_experts(done, chunks, mine, to_core(theirs), weights, kept)
    keep, send = placed(picks, near, far)
    late.append((keep, to_second(send)))
    running = None
    for c in range(1, chunks):
        keep, came = late[c]
        if c + 1 < chunks:
            came = tied(came, near if c + 2 < chunks else send)
        pair = added(keep, came)
        came = to_first(pair[1].astype(jnp.bfloat16))
        total = added(pair[0], came if c + 1 == chunks else tied(came, send))
        running = (total if running is None else added(total, running)).astype(jnp.bfloat16)
        if c + 1 < chunks:
            running = to_ring(running)
    keep, came = late[0]
    pair = added(keep, came if running is None else tied(came, near))
    came = pair[1].astype(jnp.bfloat16)
    own = added(pair[0], to_first(came if running is None else tied(came, running)))
    grad_tokens = (own if running is None else added(own, to_ring(running))).astype(jnp.bfloat16)
    kept = tied(kept, send)
    rows_x, rows_g, acts, gate_term, up_term = kept
    grad_down = lax.dot_general(acts, rows_g, CONTRACT_FIRST, preferred_element_type=jnp.float32)
    grad_gate = lax.dot_general(gate_term, rows_x, CONTRACT_FIRST, preferred_element_type=jnp.float32)
    grad_up = lax.dot_general(up_term, rows_x, CONTRACT_FIRST, preferred_element_type=jnp.float32)
    return (
        grad_tokens,
        grad_gate.astype(jnp.bfloat16)[None],
        grad_up.astype(jnp.bfloat16)[None],
        grad_down.astype(jnp.bfloat16)[None],
    )


def solution(mesh):
    experts = mesh.shape["expert"]

    def body(tokens, out_grad, routes, combine, w_gate, w_up, w_down):
        rows, width = tokens.shape
        top = routes.shape[1]
        gathers = top * 4 >= experts and experts % 4 == 0 and mesh.shape["etp"] == 2
        run = gather_body if gathers and top * rows <= width else exchange_body
        return run(tokens, out_grad, routes, combine, w_gate, w_up, w_down)

    placed = (
        P("expert", "etp"),
        P("expert", "etp"),
        P("expert", None),
        P("expert", None),
        P("expert", "etp", None),
        P("expert", "etp", None),
        P("expert", "etp", None),
    )
    return jax.shard_map(
        body,
        mesh=mesh,
        in_specs=placed,
        out_specs=(
            P("expert", "etp"),
            P("expert", "etp", None),
            P("expert", "etp", None),
            P("expert", "etp", None),
        ),
        check_vma=False,
    )
```

```python
import functools

import jax
import jax.numpy as jnp
from jax import lax
from jax.experimental import pallas as pl
from jax.experimental.pallas import tpu as pltpu
from jax.sharding import PartitionSpec as P

CONTRACT_LAST = (((1,), (1,)), ((), ()))
CONTRACT_FIRST = (((0,), (0,)), ((), ()))
INFO_ROWS = 16
VMEM_LIMIT = 16 * 1024 * 1024


def pack_rows(token_rows, grad_rows, token_of, scale, is_live):
    mask = is_live[:, None].astype(token_rows.dtype)
    inputs_sent = token_rows[token_of] * mask
    grads_sent = (scale[:, None] * grad_rows[token_of].astype(jnp.float32)).astype(jnp.bfloat16)
    return (inputs_sent, grads_sent)


def pair_positions(routed_flat, experts):
    pair_total = routed_flat.shape[0]
    span = 128
    groups = pair_total // span
    labels = jnp.arange(experts, dtype=jnp.int32)
    one_hot = (routed_flat[:, None] == labels[None, :]).astype(jnp.bfloat16)
    grouped = one_hot.reshape(groups, span, experts)
    row_ids = jnp.arange(span, dtype=jnp.int32)
    lower = (row_ids[None, :] < row_ids[:, None]).astype(jnp.bfloat16)
    within = jnp.einsum("ij,bje->bie", lower, grouped, preferred_element_type=jnp.float32)
    group_sums = jnp.sum(grouped.astype(jnp.float32), axis=1)
    group_before = jnp.cumsum(group_sums, axis=0) - group_sums
    earlier = within + group_before[:, None, :]
    counted = jnp.sum(earlier * grouped.astype(jnp.float32), axis=2)
    return counted.reshape(pair_total).astype(jnp.int32)


def exchange_body(tokens, out_grad, routes, combine, w_gate, w_up, w_down):
    experts = lax.axis_size("expert")
    tok_rows = tokens.shape[0]
    col_width = tokens.shape[1]
    choose_count = routes.shape[1]
    per_pair = tok_rows * choose_count // experts
    capacity = per_pair + per_pair // 8
    routed_flat = routes.reshape(-1)
    pair_total = routed_flat.shape[0]
    position = pair_positions(routed_flat, experts)
    target = routed_flat * capacity + position
    anchor = jnp.full((experts * capacity,), pair_total, jnp.int32)
    anchor = anchor.at[target].set(jnp.arange(pair_total, dtype=jnp.int32))
    is_live = anchor < pair_total
    safe_anchor = jnp.minimum(anchor, pair_total - 1)
    token_of = safe_anchor // choose_count
    scale = combine.reshape(-1)[safe_anchor] * is_live.astype(jnp.float32)
    full_tokens, full_grads = (
        lax.all_gather(tokens, "etp", axis=1, tiled=True),
        lax.all_gather(out_grad, "etp", axis=1, tiled=True),
    )
    inputs_sent, grads_sent = pack_rows(full_tokens, full_grads, token_of, scale, is_live)
    rows_x, rows_g = (
        lax.all_to_all(inputs_sent, "expert", split_axis=0, concat_axis=0, tiled=True),
        lax.all_to_all(grads_sent, "expert", split_axis=0, concat_axis=0, tiled=True),
    )
    gate_w = w_gate[0]
    up_w = w_up[0]
    down_w = w_down[0]
    gate = lax.dot_general(rows_x, gate_w, CONTRACT_LAST, preferred_element_type=jnp.float32)
    up = lax.dot_general(rows_x, up_w, CONTRACT_LAST, preferred_element_type=jnp.float32)
    hidden_grad = lax.dot_general(rows_g, down_w, CONTRACT_LAST, preferred_element_type=jnp.float32)
    sigma = jax.nn.sigmoid(gate)
    silu = gate * sigma
    acts = (silu * up).astype(jnp.bfloat16)
    grad_down = lax.dot_general(acts, rows_g, CONTRACT_FIRST, preferred_element_type=jnp.float32)
    gate_term = (hidden_grad * up * sigma * (1.0 + gate * (1.0 - sigma))).astype(jnp.bfloat16)
    up_term = (hidden_grad * silu).astype(jnp.bfloat16)
    grad_gate = lax.dot_general(
        gate_term, rows_x, CONTRACT_FIRST, preferred_element_type=jnp.float32
    )
    grad_up = lax.dot_general(up_term, rows_x, CONTRACT_FIRST, preferred_element_type=jnp.float32)
    swapped_gate, swapped_up = (
        lax.all_to_all(gate_w, "etp", split_axis=1, concat_axis=0, tiled=True),
        lax.all_to_all(up_w, "etp", split_axis=1, concat_axis=0, tiled=True),
    )
    running = jnp.dot(
        lax.all_gather(gate_term, "etp", axis=1, tiled=True),
        swapped_gate,
        preferred_element_type=jnp.float32,
    )
    slot_grads = running + jnp.dot(
        lax.all_gather(up_term, "etp", axis=1, tiled=True),
        swapped_up,
        preferred_element_type=jnp.float32,
    )
    slot_grads = slot_grads.astype(jnp.bfloat16)
    returned = lax.all_to_all(slot_grads, "expert", split_axis=0, concat_axis=0, tiled=True)
    picked = returned[target].astype(jnp.float32).reshape(tok_rows, choose_count, col_width)
    grad_tokens = jnp.sum(picked, axis=1).astype(jnp.bfloat16)
    return (
        grad_tokens,
        grad_gate.astype(jnp.bfloat16)[None],
        grad_up.astype(jnp.bfloat16)[None],
        grad_down.astype(jnp.bfloat16)[None],
    )


def pack_kernel(tokens_ref, grads_ref, routes_ref, combine_ref, out_ref):
    rows = tokens_ref.shape[0]
    out_ref[:rows] = tokens_ref[...]
    out_ref[rows:2 * rows] = grads_ref[...]
    top = routes_ref.shape[0]
    routes = routes_ref[...].astype(jnp.float32)
    weights = combine_ref[...]
    high = weights.astype(jnp.bfloat16).astype(jnp.float32)
    middle = (weights - high).astype(jnp.bfloat16).astype(jnp.float32)
    low = weights - high - middle
    blank = jnp.zeros((INFO_ROWS - 4, rows), jnp.float32)
    for k in range(top):
        own = slice(k, k + 1)
        column = jnp.concatenate([routes[own], high[own], middle[own], low[own], blank], axis=0)
        out_ref[2 * rows:, k * rows:(k + 1) * rows] = column.astype(jnp.bfloat16)


def pack_share(tokens, out_grad, routes, combine):
    rows, width = tokens.shape
    vmem = pl.BlockSpec(memory_space=pltpu.VMEM)
    return pl.pallas_call(
        pack_kernel,
        in_specs=[vmem] * 4,
        out_specs=vmem,
        out_shape=jax.ShapeDtypeStruct((2 * rows + INFO_ROWS, width), jnp.bfloat16),
        name="pack",
    )(tokens, out_grad, routes.T, combine.T)


def load_kernel(*refs):
    count = (len(refs) - 1) // 2
    moves = [pltpu.make_async_copy(refs[i], refs[count + i], refs[-1].at[i]) for i in range(count)]
    for move in moves:
        move.start()
    for move in moves:
        move.wait()


def load_weights(weights):
    return pl.pallas_call(
        load_kernel,
        in_specs=[pl.BlockSpec(memory_space=pltpu.HBM)] * len(weights),
        out_specs=[pl.BlockSpec(memory_space=pltpu.VMEM)] * len(weights),
        out_shape=[jax.ShapeDtypeStruct(w.shape, w.dtype) for w in weights],
        scratch_shapes=[pltpu.SemaphoreType.DMA((len(weights),))],
        name="load",
    )(*weights)


def pick_kernel(top, rows, place_ref, *refs):
    shares, (mine_ref, theirs_ref, picks_ref) = refs[:4], refs[4:]
    me, own_half, core = place_ref[0], place_ref[1], place_ref[2]
    pair_slots, width = mine_ref.shape[1], shares[0].shape[1]
    earlier = (
        lax.broadcasted_iota(jnp.int32, (2 * rows, 2 * rows), 0)
        < lax.broadcasted_iota(jnp.int32, (2 * rows, 2 * rows), 1)
    ).astype(jnp.bfloat16)
    infos = [
        [share_ref[pl.ds(2 * rows, INFO_ROWS), k * rows:(k + 1) * rows].astype(jnp.float32) for k in range(top)]
        for share_ref in (shares[0], shares[3])
    ]
    picks, scales = [], []
    for expert in (me, me + 1 - 2 * core):
        named, weights = [], []
        for block in infos:
            hits, weight = 0.0, 0.0
            for info in block:
                hit = info[0:1] == expert.astype(jnp.float32)
                hits += hit.astype(jnp.float32)
                weight += jnp.where(hit, info[1:2] + info[2:3] + info[3:4], 0.0)
            named.append(hits)
            weights.append(weight)
        named = jnp.concatenate(named, axis=1)
        weights = jnp.concatenate(weights, axis=1)
        counted = jnp.dot(
            jnp.broadcast_to(named, (16, 2 * rows)).astype(jnp.bfloat16),
            earlier,
            preferred_element_type=jnp.float32,
        )[:1]
        slot_of = jnp.where(named > 0.0, counted.astype(jnp.int32), -1)
        chosen = slot_of == lax.broadcasted_iota(jnp.int32, (pair_slots, 2 * rows), 0)
        picks.append(chosen.astype(jnp.bfloat16))
        scales.append(jnp.sum(jnp.where(chosen, weights, 0.0), axis=1, keepdims=True))
    picks = jnp.concatenate(picks, axis=0)
    scales = jnp.concatenate(scales, axis=0)
    picks_ref[...] = picks
    for h in range(2):
        cols = pl.ds(pl.multiple_of((own_half if h == 0 else 1 - own_half) * width, width), width)
        for part in range(2):
            own, first, second, both = [ref[pl.ds(part * rows, rows)] for ref in shares]
            if h == 0:
                held = jnp.concatenate([own, jnp.where(core == 1, second, first)], axis=0)
            else:
                held = jnp.concatenate([jnp.where(core == 1, first, second), both], axis=0)
            picked = jnp.dot(picks, held, preferred_element_type=jnp.float32)
            if part == 1:
                picked = scales * picked
            picked = picked.astype(jnp.bfloat16)
            mine_ref[part, :, cols] = picked[:pair_slots]
            theirs_ref[part, :, cols] = picked[pair_slots:]


def expert_kernel(index, chained, mine_ref, theirs_ref, wg_ref, wu_ref, wd_ref, *refs):
    near_ref, far_ref, *kept_refs = refs[5 if chained else 0:][:7]
    act_ref, gt_ref, ut_ref, sems = refs[-4:]
    pair_slots = mine_ref.shape[1]
    slots = 2 * pair_slots

    def kept_move(source, target, part, count, i):
        return pltpu.make_async_copy(
            source, kept_refs[target].at[pl.ds(index * slots + part * pair_slots, count)], sems.at[i]
        )

    moves = [
        kept_move(mine_ref.at[0], 0, 0, pair_slots, 0),
        kept_move(theirs_ref.at[0], 0, 1, pair_slots, 1),
        kept_move(mine_ref.at[1], 1, 0, pair_slots, 2),
        kept_move(theirs_ref.at[1], 1, 1, pair_slots, 3),
        kept_move(act_ref, 2, 0, slots, 4),
        kept_move(gt_ref, 3, 0, slots, 5),
        kept_move(ut_ref, 4, 0, slots, 6),
    ]
    for move in moves[:4]:
        move.start()
    rows_x = jnp.concatenate([mine_ref[0], theirs_ref[0]], axis=0)
    rows_g = jnp.concatenate([mine_ref[1], theirs_ref[1]], axis=0)
    gate = lax.dot_general(rows_x, wg_ref[...], CONTRACT_LAST, preferred_element_type=jnp.float32)
    up = lax.dot_general(rows_x, wu_ref[...], CONTRACT_LAST, preferred_element_type=jnp.float32)
    hidden_grad = lax.dot_general(rows_g, wd_ref[...], CONTRACT_LAST, preferred_element_type=jnp.float32)
    sigma = 1.0 / (1.0 + jnp.exp(-gate))
    silu = gate * sigma
    act_ref[...] = (silu * up).astype(jnp.bfloat16)
    gt_ref[...] = (hidden_grad * up * sigma * (1.0 + gate * (1.0 - sigma))).astype(jnp.bfloat16)
    ut_ref[...] = (hidden_grad * silu).astype(jnp.bfloat16)
    for move in moves[4:]:
        move.start()
    slot = jnp.dot(gt_ref[...], wg_ref[...], preferred_element_type=jnp.float32)
    slot += jnp.dot(ut_ref[...], wu_ref[...], preferred_element_type=jnp.float32)
    far_ref[...] = slot[pair_slots:].astype(jnp.bfloat16)
    near_ref[...] = slot[:pair_slots].astype(jnp.bfloat16)
    for move in moves:
        move.wait()


def place_kernel(place_ref, picks_ref, near_ref, far_ref, keep_ref, send_ref):
    own_half, core = place_ref[1], place_ref[2]
    _, rows, width = keep_ref.shape
    pair_slots = near_ref.shape[0]
    backs = []
    for h in range(2):
        cols = pl.ds(pl.multiple_of((own_half if h == 0 else 1 - own_half) * width, width), width)
        slot = jnp.concatenate([near_ref[:, cols], far_ref[:, cols]], axis=0)
        backs.append(lax.dot_general(picks_ref[...], slot, CONTRACT_FIRST, preferred_element_type=jnp.float32))
    keep_ref[0] = backs[0][:rows]
    keep_ref[1] = jnp.where(core == 1, backs[1][:rows], backs[0][rows:])
    send_ref[0] = jnp.where(core == 1, backs[0][rows:], backs[1][:rows]).astype(jnp.bfloat16)
    send_ref[1] = backs[1][rows:].astype(jnp.bfloat16)


def pick_rows(place, shares, top, rows, pair_slots):
    width = shares[0].shape[1]
    vmem = pl.BlockSpec(memory_space=pltpu.VMEM)
    picked = jax.ShapeDtypeStruct((2, pair_slots, 2 * width), jnp.bfloat16)
    return pl.pallas_call(
        functools.partial(pick_kernel, top, rows),
        in_specs=[pl.BlockSpec(memory_space=pltpu.SMEM)] + [vmem] * 4,
        out_specs=[vmem] * 3,
        out_shape=[picked, picked, jax.ShapeDtypeStruct((2 * pair_slots, 2 * rows), jnp.bfloat16)],
        compiler_params=pltpu.CompilerParams(vmem_limit_bytes=VMEM_LIMIT),
        name="pick",
    )(place, *shares)


def run_experts(index, chunks, mine, theirs, weights, kept):
    _, pair_slots, features = mine.shape
    hidden = weights[0].shape[0]
    slots = 2 * pair_slots
    hbm = pl.BlockSpec(memory_space=pltpu.HBM)
    vmem = pl.BlockSpec(memory_space=pltpu.VMEM)
    part = jax.ShapeDtypeStruct((pair_slots, features), jnp.bfloat16)
    wide = jax.ShapeDtypeStruct((chunks * slots, features), jnp.bfloat16)
    narrow = jax.ShapeDtypeStruct((chunks * slots, hidden), jnp.bfloat16)
    return pl.pallas_call(
        functools.partial(expert_kernel, index, kept is not None),
        in_specs=[vmem] * 5 + [hbm] * (0 if kept is None else 5),
        out_specs=[vmem] * 2 + [hbm] * 5,
        out_shape=[part, part, wide, wide, narrow, narrow, narrow],
        scratch_shapes=[pltpu.VMEM((slots, hidden), jnp.bfloat16)] * 3 + [pltpu.SemaphoreType.DMA((7,))],
        input_output_aliases={} if kept is None else {5 + i: 2 + i for i in range(5)},
        compiler_params=pltpu.CompilerParams(vmem_limit_bytes=VMEM_LIMIT),
        name="experts",
    )(mine, theirs, *weights, *(kept or ()))


def place_rows(place, picks, near, far, rows, width):
    vmem = pl.BlockSpec(memory_space=pltpu.VMEM)
    return pl.pallas_call(
        place_kernel,
        in_specs=[pl.BlockSpec(memory_space=pltpu.SMEM)] + [vmem] * 3,
        out_specs=[vmem] * 2,
        out_shape=[
            jax.ShapeDtypeStruct((2, rows, width), jnp.float32),
            jax.ShapeDtypeStruct((2, rows, width), jnp.bfloat16),
        ],
        compiler_params=pltpu.CompilerParams(vmem_limit_bytes=VMEM_LIMIT),
        name="place",
    )(place, picks, near, far)


def ring_order(length):
    return list(range(0, min(1, length))) + list(range(1, length, 2)) + list(range(2, length, 2))[::-1]


def gather_body(tokens, out_grad, routes, combine, w_gate, w_up, w_down):
    experts = lax.axis_size("expert")
    chunks = experts // 4
    rows, width = tokens.shape
    top = routes.shape[1]
    per_pair = rows * top // experts
    capacity = per_pair + per_pair // 8
    pair_slots = -(-2 * capacity // 16) * 16
    order = ring_order(chunks)
    after = {order[i]: order[(i + 1) % chunks] for i in range(chunks)}
    devices = [(e, h) for e in range(experts) for h in range(2)]

    def permute(value, target):
        pairs = [(e * 2 + h, target(e, h)[0] * 2 + target(e, h)[1]) for e, h in devices]
        return lax.ppermute(value, ("expert", "etp"), pairs)

    def to_ring(value):
        return permute(value, lambda e, h: (after[e // 4] * 4 + e % 4, h))

    def to_core(value):
        return permute(value, lambda e, h: (e ^ 1, h))

    def to_first(value):
        return permute(value, lambda e, h: (e, h ^ 1) if e % 2 else (e ^ 2, h))

    def to_second(value):
        return permute(value, lambda e, h: (e ^ 2, h) if e % 2 else (e, h ^ 1))

    me = lax.axis_index("expert")
    place = jnp.stack([me, lax.axis_index("etp"), me % 2]).astype(jnp.int32)
    share = pack_share(tokens, out_grad, routes, combine)
    weights = load_weights((w_gate[0], w_up[0], w_down[0]))

    def tied(values, mark):
        return lax.optimization_barrier((values, mark))[0]

    def placed(picks, near, far):
        return place_rows(place, picks, near, to_core(far), rows, width)

    def added(keep, came):
        return keep + came.astype(jnp.float32)

    ring_sends = [("s", 1)] + [(kind, c) for c in range(2, chunks) for kind in ("f", "s")]
    ring_sends.sort(key=lambda key: key[1] * 2 - (key[0] == "s"))
    plane_sends = [("f", 0), ("a", 0), ("b", 0), ("f", 1), ("a", 1), ("b", 1)]
    plane_sends += [(kind, c) for c in range(2, chunks) for kind in ("a", "b")]
    ring_sends = [key for key in ring_sends if key[1] < chunks]
    plane_sends = [key for key in plane_sends if key[1] < chunks]

    def source_of(key, by_ring):
        kind, c = key
        return (kind, c - 1) if by_ring else ("f" if kind == "b" else "s", c)

    have = {("s", 0): share}
    kept, picked, parts, waiting = None, None, None, None
    late, done = [], 0
    while plane_sends:
        came = {}
        for key in [key for key in plane_sends if source_of(key, False) in have][:2]:
            value = have[source_of(key, False)]
            came[key] = to_first(value) if key[0] == "f" else to_second(value)
            plane_sends.remove(key)
        for key in [key for key in ring_sends if source_of(key, True) in have][:1]:
            came[key] = to_ring(have[source_of(key, True)])
            ring_sends.remove(key)
        ready, waiting, before = waiting, None, parts
        if picked is not None:
            mine, theirs, picks = picked
            near, far, *kept = run_experts(done, chunks, mine, to_core(theirs), weights, kept)
            parts, picked = (picks, near, far), None
            done += 1
        else:
            parts = None
        if before is not None:
            waiting = placed(*before)
        if plane_sends and all((kind, done) in have for kind in "sfab"):
            picked = pick_rows(place, [have[kind, done] for kind in "sfab"], top, rows, pair_slots)
        if ready is not None:
            late.append(ready)
        needed = {key: have[key] for key in have if key[1] >= done}
        came, have, picked, parts, waiting, late, weights = lax.optimization_barrier(
            (came, needed, picked, parts, waiting, late, weights)
        )
        have.update(came)
    mine, theirs, picks = pick_rows(place, [have[kind, done] for kind in "sfab"], top, rows, pair_slots)
    unsent, late = late, []
    if waiting is not None:
        keep, send = waiting
        late.append((keep, to_second(tied(send, theirs))))
    beside = theirs
    if parts is not None:
        keep, beside = placed(*tied(parts, theirs))
        late.append((keep, to_second(beside)))
    late = [(keep, to_second(tied(send, beside))) for keep, send in unsent] + late
    near, far, *kept = run_experts(done, chunks, mine, to_core(theirs), weights, kept)
    keep, send = placed(picks, near, far)
    late.append((keep, to_second(send)))
    running = None
    for c in range(1, chunks):
        keep, came = late[c]
        if c + 1 < chunks:
            came = tied(came, near if c == 1 else mark)
        pair = added(keep, came)
        came = to_first(pair[1].astype(jnp.bfloat16))
        total = added(pair[0], came if c + 1 == chunks else tied(came, send))
        running = (total if running is None else added(total, running)).astype(jnp.bfloat16)
        mark = running if c == 1 else mark
        if c + 1 < chunks:
            running = to_ring(running)
    keep, came = late[0]
    pair = added(keep, came if running is None else tied(came, mark))
    came = pair[1].astype(jnp.bfloat16)
    own = added(pair[0], to_first(came if running is None else tied(came, running)))
    grad_tokens = (own if running is None else added(own, to_ring(running))).astype(jnp.bfloat16)
    kept = tied(kept, send)
    rows_x, rows_g, acts, gate_term, up_term = kept
    grad_down = lax.dot_general(acts, rows_g, CONTRACT_FIRST, preferred_element_type=jnp.float32)
    grad_gate = lax.dot_general(gate_term, rows_x, CONTRACT_FIRST, preferred_element_type=jnp.float32)
    grad_up = lax.dot_general(up_term, rows_x, CONTRACT_FIRST, preferred_element_type=jnp.float32)
    return (
        grad_tokens,
        grad_gate.astype(jnp.bfloat16)[None],
        grad_up.astype(jnp.bfloat16)[None],
        grad_down.astype(jnp.bfloat16)[None],
    )


def solution(mesh):
    experts = mesh.shape["expert"]

    def body(tokens, out_grad, routes, combine, w_gate, w_up, w_down):
        rows, width = tokens.shape
        top = routes.shape[1]
        gathers = top * 4 >= experts and experts % 4 == 0 and mesh.shape["etp"] == 2
        run = gather_body if gathers and top * rows <= width else exchange_body
        return run(tokens, out_grad, routes, combine, w_gate, w_up, w_down)

    placed = (
        P("expert", "etp"),
        P("expert", "etp"),
        P("expert", None),
        P("expert", None),
        P("expert", "etp", None),
        P("expert", "etp", None),
        P("expert", "etp", None),
    )
    return jax.shard_map(
        body,
        mesh=mesh,
        in_specs=placed,
        out_specs=(
            P("expert", "etp"),
            P("expert", "etp", None),
            P("expert", "etp", None),
            P("expert", "etp", None),
        ),
        check_vma=False,
    )
```

```python
import functools

import jax
import jax.numpy as jnp
from jax import lax
from jax.experimental import pallas as pl
from jax.experimental.pallas import tpu as pltpu
from jax.sharding import PartitionSpec as P

CONTRACT_LAST = (((1,), (1,)), ((), ()))
CONTRACT_FIRST = (((0,), (0,)), ((), ()))
INFO_ROWS = 16
VMEM_LIMIT = 16 * 1024 * 1024


def pack_rows(token_rows, grad_rows, token_of, scale, is_live):
    mask = is_live[:, None].astype(token_rows.dtype)
    inputs_sent = token_rows[token_of] * mask
    grads_sent = (scale[:, None] * grad_rows[token_of].astype(jnp.float32)).astype(jnp.bfloat16)
    return (inputs_sent, grads_sent)


def pair_positions(routed_flat, experts):
    pair_total = routed_flat.shape[0]
    span = 128
    groups = pair_total // span
    labels = jnp.arange(experts, dtype=jnp.int32)
    one_hot = (routed_flat[:, None] == labels[None, :]).astype(jnp.bfloat16)
    grouped = one_hot.reshape(groups, span, experts)
    row_ids = jnp.arange(span, dtype=jnp.int32)
    lower = (row_ids[None, :] < row_ids[:, None]).astype(jnp.bfloat16)
    within = jnp.einsum("ij,bje->bie", lower, grouped, preferred_element_type=jnp.float32)
    group_sums = jnp.sum(grouped.astype(jnp.float32), axis=1)
    group_before = jnp.cumsum(group_sums, axis=0) - group_sums
    earlier = within + group_before[:, None, :]
    counted = jnp.sum(earlier * grouped.astype(jnp.float32), axis=2)
    return counted.reshape(pair_total).astype(jnp.int32)


def exchange_body(tokens, out_grad, routes, combine, w_gate, w_up, w_down):
    experts = lax.axis_size("expert")
    tok_rows = tokens.shape[0]
    col_width = tokens.shape[1]
    choose_count = routes.shape[1]
    per_pair = tok_rows * choose_count // experts
    capacity = per_pair + per_pair // 8
    routed_flat = routes.reshape(-1)
    pair_total = routed_flat.shape[0]
    position = pair_positions(routed_flat, experts)
    target = routed_flat * capacity + position
    anchor = jnp.full((experts * capacity,), pair_total, jnp.int32)
    anchor = anchor.at[target].set(jnp.arange(pair_total, dtype=jnp.int32))
    is_live = anchor < pair_total
    safe_anchor = jnp.minimum(anchor, pair_total - 1)
    token_of = safe_anchor // choose_count
    scale = combine.reshape(-1)[safe_anchor] * is_live.astype(jnp.float32)
    full_tokens, full_grads = (
        lax.all_gather(tokens, "etp", axis=1, tiled=True),
        lax.all_gather(out_grad, "etp", axis=1, tiled=True),
    )
    inputs_sent, grads_sent = pack_rows(full_tokens, full_grads, token_of, scale, is_live)
    rows_x, rows_g = (
        lax.all_to_all(inputs_sent, "expert", split_axis=0, concat_axis=0, tiled=True),
        lax.all_to_all(grads_sent, "expert", split_axis=0, concat_axis=0, tiled=True),
    )
    gate_w = w_gate[0]
    up_w = w_up[0]
    down_w = w_down[0]
    gate = lax.dot_general(rows_x, gate_w, CONTRACT_LAST, preferred_element_type=jnp.float32)
    up = lax.dot_general(rows_x, up_w, CONTRACT_LAST, preferred_element_type=jnp.float32)
    hidden_grad = lax.dot_general(rows_g, down_w, CONTRACT_LAST, preferred_element_type=jnp.float32)
    sigma = jax.nn.sigmoid(gate)
    silu = gate * sigma
    acts = (silu * up).astype(jnp.bfloat16)
    grad_down = lax.dot_general(acts, rows_g, CONTRACT_FIRST, preferred_element_type=jnp.float32)
    gate_term = (hidden_grad * up * sigma * (1.0 + gate * (1.0 - sigma))).astype(jnp.bfloat16)
    up_term = (hidden_grad * silu).astype(jnp.bfloat16)
    grad_gate = lax.dot_general(
        gate_term, rows_x, CONTRACT_FIRST, preferred_element_type=jnp.float32
    )
    grad_up = lax.dot_general(up_term, rows_x, CONTRACT_FIRST, preferred_element_type=jnp.float32)
    swapped_gate, swapped_up = (
        lax.all_to_all(gate_w, "etp", split_axis=1, concat_axis=0, tiled=True),
        lax.all_to_all(up_w, "etp", split_axis=1, concat_axis=0, tiled=True),
    )
    running = jnp.dot(
        lax.all_gather(gate_term, "etp", axis=1, tiled=True),
        swapped_gate,
        preferred_element_type=jnp.float32,
    )
    slot_grads = running + jnp.dot(
        lax.all_gather(up_term, "etp", axis=1, tiled=True),
        swapped_up,
        preferred_element_type=jnp.float32,
    )
    slot_grads = slot_grads.astype(jnp.bfloat16)
    returned = lax.all_to_all(slot_grads, "expert", split_axis=0, concat_axis=0, tiled=True)
    picked = returned[target].astype(jnp.float32).reshape(tok_rows, choose_count, col_width)
    grad_tokens = jnp.sum(picked, axis=1).astype(jnp.bfloat16)
    return (
        grad_tokens,
        grad_gate.astype(jnp.bfloat16)[None],
        grad_up.astype(jnp.bfloat16)[None],
        grad_down.astype(jnp.bfloat16)[None],
    )


def pack_kernel(tokens_ref, grads_ref, routes_ref, combine_ref, out_ref):
    rows = tokens_ref.shape[0]
    out_ref[:rows] = tokens_ref[...]
    out_ref[rows:2 * rows] = grads_ref[...]
    top = routes_ref.shape[0]
    routes = routes_ref[...].astype(jnp.float32)
    weights = combine_ref[...]
    high = weights.astype(jnp.bfloat16).astype(jnp.float32)
    middle = (weights - high).astype(jnp.bfloat16).astype(jnp.float32)
    low = weights - high - middle
    blank = jnp.zeros((INFO_ROWS - 4, rows), jnp.float32)
    for k in range(top):
        own = slice(k, k + 1)
        column = jnp.concatenate([routes[own], high[own], middle[own], low[own], blank], axis=0)
        out_ref[2 * rows:, k * rows:(k + 1) * rows] = column.astype(jnp.bfloat16)


def pack_share(tokens, out_grad, routes, combine):
    rows, width = tokens.shape
    vmem = pl.BlockSpec(memory_space=pltpu.VMEM)
    return pl.pallas_call(
        pack_kernel,
        in_specs=[vmem] * 4,
        out_specs=vmem,
        out_shape=jax.ShapeDtypeStruct((2 * rows + INFO_ROWS, width), jnp.bfloat16),
        name="pack",
    )(tokens, out_grad, routes.T, combine.T)


def load_kernel(*refs):
    count = (len(refs) - 1) // 2
    moves = [pltpu.make_async_copy(refs[i], refs[count + i], refs[-1].at[i]) for i in range(count)]
    for move in moves:
        move.start()
    for move in moves:
        move.wait()


def load_weights(weights):
    return pl.pallas_call(
        load_kernel,
        in_specs=[pl.BlockSpec(memory_space=pltpu.HBM)] * len(weights),
        out_specs=[pl.BlockSpec(memory_space=pltpu.VMEM)] * len(weights),
        out_shape=[jax.ShapeDtypeStruct(w.shape, w.dtype) for w in weights],
        scratch_shapes=[pltpu.SemaphoreType.DMA((len(weights),))],
        name="load",
    )(*weights)


def pick_kernel(top, rows, place_ref, *refs):
    shares, (mine_ref, theirs_ref, picks_ref) = refs[:4], refs[4:]
    me, own_half, core = place_ref[0], place_ref[1], place_ref[2]
    pair_slots, width = mine_ref.shape[1], shares[0].shape[1]
    earlier = (
        lax.broadcasted_iota(jnp.int32, (2 * rows, 2 * rows), 0)
        < lax.broadcasted_iota(jnp.int32, (2 * rows, 2 * rows), 1)
    ).astype(jnp.bfloat16)
    infos = [
        [share_ref[pl.ds(2 * rows, INFO_ROWS), k * rows:(k + 1) * rows].astype(jnp.float32) for k in range(top)]
        for share_ref in (shares[0], shares[3])
    ]
    picks, scales = [], []
    for expert in (me, me + 1 - 2 * core):
        named, weights = [], []
        for block in infos:
            hits, weight = 0.0, 0.0
            for info in block:
                hit = info[0:1] == expert.astype(jnp.float32)
                hits += hit.astype(jnp.float32)
                weight += jnp.where(hit, info[1:2] + info[2:3] + info[3:4], 0.0)
            named.append(hits)
            weights.append(weight)
        named = jnp.concatenate(named, axis=1)
        weights = jnp.concatenate(weights, axis=1)
        counted = jnp.dot(
            jnp.broadcast_to(named, (16, 2 * rows)).astype(jnp.bfloat16),
            earlier,
            preferred_element_type=jnp.float32,
        )[:1]
        slot_of = jnp.where(named > 0.0, counted.astype(jnp.int32), -1)
        chosen = slot_of == lax.broadcasted_iota(jnp.int32, (pair_slots, 2 * rows), 0)
        picks.append(chosen.astype(jnp.bfloat16))
        scales.append(jnp.sum(jnp.where(chosen, weights, 0.0), axis=1, keepdims=True))
    picks = jnp.concatenate(picks, axis=0)
    scales = jnp.concatenate(scales, axis=0)
    picks_ref[...] = picks
    for h in range(2):
        cols = pl.ds(pl.multiple_of((own_half if h == 0 else 1 - own_half) * width, width), width)
        for part in range(2):
            own, first, second, both = [ref[pl.ds(part * rows, rows)] for ref in shares]
            if h == 0:
                held = jnp.concatenate([own, jnp.where(core == 1, second, first)], axis=0)
            else:
                held = jnp.concatenate([jnp.where(core == 1, first, second), both], axis=0)
            picked = jnp.dot(picks, held, preferred_element_type=jnp.float32)
            if part == 1:
                picked = scales * picked
            picked = picked.astype(jnp.bfloat16)
            mine_ref[part, :, cols] = picked[:pair_slots]
            theirs_ref[part, :, cols] = picked[pair_slots:]


def expert_kernel(index, chained, mine_ref, theirs_ref, wg_ref, wu_ref, wd_ref, *refs):
    near_ref, far_ref, *kept_refs = refs[5 if chained else 0:][:7]
    act_ref, gt_ref, ut_ref, sems = refs[-4:]
    pair_slots = mine_ref.shape[1]
    slots = 2 * pair_slots

    def kept_move(source, target, part, count, i):
        return pltpu.make_async_copy(
            source, kept_refs[target].at[pl.ds(index * slots + part * pair_slots, count)], sems.at[i]
        )

    moves = [
        kept_move(mine_ref.at[0], 0, 0, pair_slots, 0),
        kept_move(theirs_ref.at[0], 0, 1, pair_slots, 1),
        kept_move(mine_ref.at[1], 1, 0, pair_slots, 2),
        kept_move(theirs_ref.at[1], 1, 1, pair_slots, 3),
        kept_move(act_ref, 2, 0, slots, 4),
        kept_move(gt_ref, 3, 0, slots, 5),
        kept_move(ut_ref, 4, 0, slots, 6),
    ]
    for move in moves[:4]:
        move.start()
    rows_x = jnp.concatenate([mine_ref[0], theirs_ref[0]], axis=0)
    rows_g = jnp.concatenate([mine_ref[1], theirs_ref[1]], axis=0)
    gate = lax.dot_general(rows_x, wg_ref[...], CONTRACT_LAST, preferred_element_type=jnp.float32)
    up = lax.dot_general(rows_x, wu_ref[...], CONTRACT_LAST, preferred_element_type=jnp.float32)
    hidden_grad = lax.dot_general(rows_g, wd_ref[...], CONTRACT_LAST, preferred_element_type=jnp.float32)
    sigma = 1.0 / (1.0 + jnp.exp(-gate))
    silu = gate * sigma
    act_ref[...] = (silu * up).astype(jnp.bfloat16)
    gt_ref[...] = (hidden_grad * up * sigma * (1.0 + gate * (1.0 - sigma))).astype(jnp.bfloat16)
    ut_ref[...] = (hidden_grad * silu).astype(jnp.bfloat16)
    for move in moves[4:]:
        move.start()
    slot = jnp.dot(gt_ref[...], wg_ref[...], preferred_element_type=jnp.float32)
    slot += jnp.dot(ut_ref[...], wu_ref[...], preferred_element_type=jnp.float32)
    far_ref[...] = slot[pair_slots:].astype(jnp.bfloat16)
    near_ref[...] = slot[:pair_slots].astype(jnp.bfloat16)
    for move in moves:
        move.wait()


def place_kernel(place_ref, picks_ref, near_ref, far_ref, keep_ref, send_ref):
    own_half, core = place_ref[1], place_ref[2]
    _, rows, width = keep_ref.shape
    pair_slots = near_ref.shape[0]
    backs = []
    for h in range(2):
        cols = pl.ds(pl.multiple_of((own_half if h == 0 else 1 - own_half) * width, width), width)
        slot = jnp.concatenate([near_ref[:, cols], far_ref[:, cols]], axis=0)
        backs.append(lax.dot_general(picks_ref[...], slot, CONTRACT_FIRST, preferred_element_type=jnp.float32))
    keep_ref[0] = backs[0][:rows]
    keep_ref[1] = jnp.where(core == 1, backs[1][:rows], backs[0][rows:])
    send_ref[0] = jnp.where(core == 1, backs[0][rows:], backs[1][:rows]).astype(jnp.bfloat16)
    send_ref[1] = backs[1][rows:].astype(jnp.bfloat16)


def pick_rows(place, shares, top, rows, pair_slots):
    width = shares[0].shape[1]
    vmem = pl.BlockSpec(memory_space=pltpu.VMEM)
    picked = jax.ShapeDtypeStruct((2, pair_slots, 2 * width), jnp.bfloat16)
    return pl.pallas_call(
        functools.partial(pick_kernel, top, rows),
        in_specs=[pl.BlockSpec(memory_space=pltpu.SMEM)] + [vmem] * 4,
        out_specs=[vmem] * 3,
        out_shape=[picked, picked, jax.ShapeDtypeStruct((2 * pair_slots, 2 * rows), jnp.bfloat16)],
        compiler_params=pltpu.CompilerParams(vmem_limit_bytes=VMEM_LIMIT),
        name="pick",
    )(place, *shares)


def run_experts(index, chunks, mine, theirs, weights, kept):
    _, pair_slots, features = mine.shape
    hidden = weights[0].shape[0]
    slots = 2 * pair_slots
    hbm = pl.BlockSpec(memory_space=pltpu.HBM)
    vmem = pl.BlockSpec(memory_space=pltpu.VMEM)
    part = jax.ShapeDtypeStruct((pair_slots, features), jnp.bfloat16)
    wide = jax.ShapeDtypeStruct((chunks * slots, features), jnp.bfloat16)
    narrow = jax.ShapeDtypeStruct((chunks * slots, hidden), jnp.bfloat16)
    return pl.pallas_call(
        functools.partial(expert_kernel, index, kept is not None),
        in_specs=[vmem] * 5 + [hbm] * (0 if kept is None else 5),
        out_specs=[vmem] * 2 + [hbm] * 5,
        out_shape=[part, part, wide, wide, narrow, narrow, narrow],
        scratch_shapes=[pltpu.VMEM((slots, hidden), jnp.bfloat16)] * 3 + [pltpu.SemaphoreType.DMA((7,))],
        input_output_aliases={} if kept is None else {5 + i: 2 + i for i in range(5)},
        compiler_params=pltpu.CompilerParams(vmem_limit_bytes=VMEM_LIMIT),
        name="experts",
    )(mine, theirs, *weights, *(kept or ()))


def place_rows(place, picks, near, far, rows, width):
    vmem = pl.BlockSpec(memory_space=pltpu.VMEM)
    return pl.pallas_call(
        place_kernel,
        in_specs=[pl.BlockSpec(memory_space=pltpu.SMEM)] + [vmem] * 3,
        out_specs=[vmem] * 2,
        out_shape=[
            jax.ShapeDtypeStruct((2, rows, width), jnp.float32),
            jax.ShapeDtypeStruct((2, rows, width), jnp.bfloat16),
        ],
        compiler_params=pltpu.CompilerParams(vmem_limit_bytes=VMEM_LIMIT),
        name="place",
    )(place, picks, near, far)


def ring_order(length):
    return list(range(0, min(1, length))) + list(range(1, length, 2)) + list(range(2, length, 2))[::-1]


def gather_body(tokens, out_grad, routes, combine, w_gate, w_up, w_down):
    experts = lax.axis_size("expert")
    chunks = experts // 4
    rows, width = tokens.shape
    top = routes.shape[1]
    per_pair = rows * top // experts
    capacity = per_pair + per_pair // 8
    pair_slots = -(-2 * capacity // 16) * 16
    order = ring_order(chunks)
    after = {order[i]: order[(i + 1) % chunks] for i in range(chunks)}
    devices = [(e, h) for e in range(experts) for h in range(2)]

    def permute(value, target):
        pairs = [(e * 2 + h, target(e, h)[0] * 2 + target(e, h)[1]) for e, h in devices]
        return lax.ppermute(value, ("expert", "etp"), pairs)

    def to_ring(value):
        return permute(value, lambda e, h: (after[e // 4] * 4 + e % 4, h))

    def to_core(value):
        return permute(value, lambda e, h: (e ^ 1, h))

    def to_first(value):
        return permute(value, lambda e, h: (e, h ^ 1) if e % 2 else (e ^ 2, h))

    def to_second(value):
        return permute(value, lambda e, h: (e ^ 2, h) if e % 2 else (e, h ^ 1))

    me = lax.axis_index("expert")
    place = jnp.stack([me, lax.axis_index("etp"), me % 2]).astype(jnp.int32)
    share = pack_share(tokens, out_grad, routes, combine)
    weights = load_weights((w_gate[0], w_up[0], w_down[0]))

    def tied(values, mark):
        return lax.optimization_barrier((values, mark))[0]

    def placed(picks, near, far):
        return place_rows(place, picks, near, to_core(far), rows, width)

    def added(keep, came):
        return keep + came.astype(jnp.float32)

    ring_sends = [("s", 1)] + [(kind, c) for c in range(2, chunks) for kind in ("f", "s")]
    ring_sends.sort(key=lambda key: key[1] * 2 - (key[0] == "s"))
    plane_sends = [("f", 0), ("a", 0), ("b", 0), ("f", 1), ("a", 1), ("b", 1)]
    plane_sends += [(kind, c) for c in range(2, chunks) for kind in ("a", "b")]
    ring_sends = [key for key in ring_sends if key[1] < chunks]
    plane_sends = [key for key in plane_sends if key[1] < chunks]

    def source_of(key, by_ring):
        kind, c = key
        return (kind, c - 1) if by_ring else ("f" if kind == "b" else "s", c)

    have = {("s", 0): share}
    kept, picked, parts, waiting = None, None, None, None
    late, done = [], 0
    while plane_sends:
        came = {}
        for key in [key for key in plane_sends if source_of(key, False) in have][:2]:
            value = have[source_of(key, False)]
            came[key] = to_first(value) if key[0] == "f" else to_second(value)
            plane_sends.remove(key)
        for key in [key for key in ring_sends if source_of(key, True) in have][:1]:
            came[key] = to_ring(have[source_of(key, True)])
            ring_sends.remove(key)
        ready, waiting = waiting, placed(*parts) if parts is not None else None
        parts = None
        if picked is not None:
            mine, theirs, picks = picked
            near, far, *kept = run_experts(done, chunks, mine, to_core(theirs), weights, kept)
            parts, picked = (picks, near, far), None
            done += 1
        if plane_sends and all((kind, done) in have for kind in "sfab"):
            picked = pick_rows(place, [have[kind, done] for kind in "sfab"], top, rows, pair_slots)
            if done == 0:
                mine, theirs, picks = picked
                near, far, *kept = run_experts(done, chunks, mine, to_core(theirs), weights, kept)
                parts, picked = (picks, near, far), None
                done += 1
        if ready is not None:
            keep, send = ready
            late.append((keep, to_second(send)))
        needed = {key: have[key] for key in have if key[1] >= done}
        order_of = sorted(came, key=lambda key: key[0] != "s")
        values, have, picked, parts, waiting, late, weights = lax.optimization_barrier(
            ([came[key] for key in order_of], needed, picked, parts, waiting, late, weights)
        )
        came = dict(zip(order_of, values))
        have.update(came)
    mine, theirs, picks = pick_rows(place, [have[kind, done] for kind in "sfab"], top, rows, pair_slots)
    if waiting is not None:
        keep, send = waiting
        late.append((keep, to_second(tied(send, theirs))))
    if parts is not None:
        keep, send = placed(*tied(parts, theirs))
        late.append((keep, to_second(send)))
    near, far, *kept = run_experts(done, chunks, mine, to_core(theirs), weights, kept)
    keep, send = placed(picks, near, far)
    late.append((keep, to_second(send)))
    running = None
    for c in range(1, chunks):
        keep, came = late[c]
        if c + 1 < chunks:
            came = tied(came, near if c == 1 else mark)
        pair = added(keep, came)
        came = to_first(pair[1].astype(jnp.bfloat16))
        total = added(pair[0], came if c + 1 == chunks else tied(came, send))
        running = (total if running is None else added(total, running)).astype(jnp.bfloat16)
        mark = running if c == 1 else mark
        if c + 1 < chunks:
            running = to_ring(running)
    keep, came = late[0]
    pair = added(keep, came if running is None else tied(came, mark))
    came = pair[1].astype(jnp.bfloat16)
    own = added(pair[0], to_first(came if running is None else tied(came, running)))
    grad_tokens = (own if running is None else added(own, to_ring(running))).astype(jnp.bfloat16)
    kept = tied(kept, send)
    rows_x, rows_g, acts, gate_term, up_term = kept
    grad_down = lax.dot_general(acts, rows_g, CONTRACT_FIRST, preferred_element_type=jnp.float32)
    grad_gate = lax.dot_general(gate_term, rows_x, CONTRACT_FIRST, preferred_element_type=jnp.float32)
    grad_up = lax.dot_general(up_term, rows_x, CONTRACT_FIRST, preferred_element_type=jnp.float32)
    return (
        grad_tokens,
        grad_gate.astype(jnp.bfloat16)[None],
        grad_up.astype(jnp.bfloat16)[None],
        grad_down.astype(jnp.bfloat16)[None],
    )


def solution(mesh):
    experts = mesh.shape["expert"]

    def body(tokens, out_grad, routes, combine, w_gate, w_up, w_down):
        rows, width = tokens.shape
        top = routes.shape[1]
        gathers = top * 4 >= experts and experts % 4 == 0 and mesh.shape["etp"] == 2
        run = gather_body if gathers and top * rows <= width else exchange_body
        return run(tokens, out_grad, routes, combine, w_gate, w_up, w_down)

    placed = (
        P("expert", "etp"),
        P("expert", "etp"),
        P("expert", None),
        P("expert", None),
        P("expert", "etp", None),
        P("expert", "etp", None),
        P("expert", "etp", None),
    )
    return jax.shard_map(
        body,
        mesh=mesh,
        in_specs=placed,
        out_specs=(
            P("expert", "etp"),
            P("expert", "etp", None),
            P("expert", "etp", None),
            P("expert", "etp", None),
        ),
        check_vma=False,
    )
```

```python
import functools

import jax
import jax.numpy as jnp
from jax import lax
from jax.experimental import pallas as pl
from jax.experimental.pallas import tpu as pltpu
from jax.sharding import PartitionSpec as P

CONTRACT_LAST = (((1,), (1,)), ((), ()))
CONTRACT_FIRST = (((0,), (0,)), ((), ()))
INFO_ROWS = 16
VMEM_LIMIT = 16 * 1024 * 1024


def pack_rows(token_rows, grad_rows, token_of, scale, is_live):
    mask = is_live[:, None].astype(token_rows.dtype)
    inputs_sent = token_rows[token_of] * mask
    grads_sent = (scale[:, None] * grad_rows[token_of].astype(jnp.float32)).astype(jnp.bfloat16)
    return (inputs_sent, grads_sent)


def pair_positions(routed_flat, experts):
    pair_total = routed_flat.shape[0]
    span = 128
    groups = pair_total // span
    labels = jnp.arange(experts, dtype=jnp.int32)
    one_hot = (routed_flat[:, None] == labels[None, :]).astype(jnp.bfloat16)
    grouped = one_hot.reshape(groups, span, experts)
    row_ids = jnp.arange(span, dtype=jnp.int32)
    lower = (row_ids[None, :] < row_ids[:, None]).astype(jnp.bfloat16)
    within = jnp.einsum("ij,bje->bie", lower, grouped, preferred_element_type=jnp.float32)
    group_sums = jnp.sum(grouped.astype(jnp.float32), axis=1)
    group_before = jnp.cumsum(group_sums, axis=0) - group_sums
    earlier = within + group_before[:, None, :]
    counted = jnp.sum(earlier * grouped.astype(jnp.float32), axis=2)
    return counted.reshape(pair_total).astype(jnp.int32)


def exchange_body(tokens, out_grad, routes, combine, w_gate, w_up, w_down):
    experts = lax.axis_size("expert")
    tok_rows = tokens.shape[0]
    col_width = tokens.shape[1]
    choose_count = routes.shape[1]
    per_pair = tok_rows * choose_count // experts
    capacity = per_pair + per_pair // 8
    routed_flat = routes.reshape(-1)
    pair_total = routed_flat.shape[0]
    position = pair_positions(routed_flat, experts)
    target = routed_flat * capacity + position
    anchor = jnp.full((experts * capacity,), pair_total, jnp.int32)
    anchor = anchor.at[target].set(jnp.arange(pair_total, dtype=jnp.int32))
    is_live = anchor < pair_total
    safe_anchor = jnp.minimum(anchor, pair_total - 1)
    token_of = safe_anchor // choose_count
    scale = combine.reshape(-1)[safe_anchor] * is_live.astype(jnp.float32)
    full_tokens, full_grads = (
        lax.all_gather(tokens, "etp", axis=1, tiled=True),
        lax.all_gather(out_grad, "etp", axis=1, tiled=True),
    )
    inputs_sent, grads_sent = pack_rows(full_tokens, full_grads, token_of, scale, is_live)
    rows_x, rows_g = (
        lax.all_to_all(inputs_sent, "expert", split_axis=0, concat_axis=0, tiled=True),
        lax.all_to_all(grads_sent, "expert", split_axis=0, concat_axis=0, tiled=True),
    )
    gate_w = w_gate[0]
    up_w = w_up[0]
    down_w = w_down[0]
    gate = lax.dot_general(rows_x, gate_w, CONTRACT_LAST, preferred_element_type=jnp.float32)
    up = lax.dot_general(rows_x, up_w, CONTRACT_LAST, preferred_element_type=jnp.float32)
    hidden_grad = lax.dot_general(rows_g, down_w, CONTRACT_LAST, preferred_element_type=jnp.float32)
    sigma = jax.nn.sigmoid(gate)
    silu = gate * sigma
    acts = (silu * up).astype(jnp.bfloat16)
    grad_down = lax.dot_general(acts, rows_g, CONTRACT_FIRST, preferred_element_type=jnp.float32)
    gate_term = (hidden_grad * up * sigma * (1.0 + gate * (1.0 - sigma))).astype(jnp.bfloat16)
    up_term = (hidden_grad * silu).astype(jnp.bfloat16)
    grad_gate = lax.dot_general(
        gate_term, rows_x, CONTRACT_FIRST, preferred_element_type=jnp.float32
    )
    grad_up = lax.dot_general(up_term, rows_x, CONTRACT_FIRST, preferred_element_type=jnp.float32)
    swapped_gate, swapped_up = (
        lax.all_to_all(gate_w, "etp", split_axis=1, concat_axis=0, tiled=True),
        lax.all_to_all(up_w, "etp", split_axis=1, concat_axis=0, tiled=True),
    )
    running = jnp.dot(
        lax.all_gather(gate_term, "etp", axis=1, tiled=True),
        swapped_gate,
        preferred_element_type=jnp.float32,
    )
    slot_grads = running + jnp.dot(
        lax.all_gather(up_term, "etp", axis=1, tiled=True),
        swapped_up,
        preferred_element_type=jnp.float32,
    )
    slot_grads = slot_grads.astype(jnp.bfloat16)
    returned = lax.all_to_all(slot_grads, "expert", split_axis=0, concat_axis=0, tiled=True)
    picked = returned[target].astype(jnp.float32).reshape(tok_rows, choose_count, col_width)
    grad_tokens = jnp.sum(picked, axis=1).astype(jnp.bfloat16)
    return (
        grad_tokens,
        grad_gate.astype(jnp.bfloat16)[None],
        grad_up.astype(jnp.bfloat16)[None],
        grad_down.astype(jnp.bfloat16)[None],
    )


def pack_kernel(tokens_ref, grads_ref, routes_ref, combine_ref, out_ref):
    rows = tokens_ref.shape[0]
    out_ref[:rows] = tokens_ref[...]
    out_ref[rows:2 * rows] = grads_ref[...]
    top = routes_ref.shape[0]
    routes = routes_ref[...].astype(jnp.float32)
    weights = combine_ref[...]
    high = weights.astype(jnp.bfloat16).astype(jnp.float32)
    middle = (weights - high).astype(jnp.bfloat16).astype(jnp.float32)
    low = weights - high - middle
    blank = jnp.zeros((INFO_ROWS - 4, rows), jnp.float32)
    for k in range(top):
        own = slice(k, k + 1)
        column = jnp.concatenate([routes[own], high[own], middle[own], low[own], blank], axis=0)
        out_ref[2 * rows:, k * rows:(k + 1) * rows] = column.astype(jnp.bfloat16)


def pack_share(tokens, out_grad, routes, combine):
    rows, width = tokens.shape
    vmem = pl.BlockSpec(memory_space=pltpu.VMEM)
    return pl.pallas_call(
        pack_kernel,
        in_specs=[vmem] * 4,
        out_specs=vmem,
        out_shape=jax.ShapeDtypeStruct((2 * rows + INFO_ROWS, width), jnp.bfloat16),
        name="pack",
    )(tokens, out_grad, routes.T, combine.T)


def load_kernel(*refs):
    count = (len(refs) - 1) // 2
    moves = [pltpu.make_async_copy(refs[i], refs[count + i], refs[-1].at[i]) for i in range(count)]
    for move in moves:
        move.start()
    for move in moves:
        move.wait()


def load_weights(weights):
    return pl.pallas_call(
        load_kernel,
        in_specs=[pl.BlockSpec(memory_space=pltpu.HBM)] * len(weights),
        out_specs=[pl.BlockSpec(memory_space=pltpu.VMEM)] * len(weights),
        out_shape=[jax.ShapeDtypeStruct(w.shape, w.dtype) for w in weights],
        scratch_shapes=[pltpu.SemaphoreType.DMA((len(weights),))],
        name="load",
    )(*weights)


def pick_kernel(top, rows, place_ref, *refs):
    shares, (mine_ref, theirs_ref, picks_ref) = refs[:4], refs[4:]
    me, own_half, core = place_ref[0], place_ref[1], place_ref[2]
    pair_slots, width = mine_ref.shape[1], shares[0].shape[1]
    earlier = (
        lax.broadcasted_iota(jnp.int32, (2 * rows, 2 * rows), 0)
        < lax.broadcasted_iota(jnp.int32, (2 * rows, 2 * rows), 1)
    ).astype(jnp.bfloat16)
    infos = [
        [share_ref[pl.ds(2 * rows, INFO_ROWS), k * rows:(k + 1) * rows].astype(jnp.float32) for k in range(top)]
        for share_ref in (shares[0], shares[3])
    ]
    picks, scales = [], []
    for expert in (me, me + 1 - 2 * core):
        named, weights = [], []
        for block in infos:
            hits, weight = 0.0, 0.0
            for info in block:
                hit = info[0:1] == expert.astype(jnp.float32)
                hits += hit.astype(jnp.float32)
                weight += jnp.where(hit, info[1:2] + info[2:3] + info[3:4], 0.0)
            named.append(hits)
            weights.append(weight)
        named = jnp.concatenate(named, axis=1)
        weights = jnp.concatenate(weights, axis=1)
        counted = jnp.dot(
            jnp.broadcast_to(named, (16, 2 * rows)).astype(jnp.bfloat16),
            earlier,
            preferred_element_type=jnp.float32,
        )[:1]
        slot_of = jnp.where(named > 0.0, counted.astype(jnp.int32), -1)
        chosen = slot_of == lax.broadcasted_iota(jnp.int32, (pair_slots, 2 * rows), 0)
        picks.append(chosen.astype(jnp.bfloat16))
        scales.append(jnp.sum(jnp.where(chosen, weights, 0.0), axis=1, keepdims=True))
    picks = jnp.concatenate(picks, axis=0)
    scales = jnp.concatenate(scales, axis=0)
    picks_ref[...] = picks
    for h in range(2):
        cols = pl.ds(pl.multiple_of((own_half if h == 0 else 1 - own_half) * width, width), width)
        for part in range(2):
            own, first, second, both = [ref[pl.ds(part * rows, rows)] for ref in shares]
            if h == 0:
                held = jnp.concatenate([own, jnp.where(core == 1, second, first)], axis=0)
            else:
                held = jnp.concatenate([jnp.where(core == 1, first, second), both], axis=0)
            picked = jnp.dot(picks, held, preferred_element_type=jnp.float32)
            if part == 1:
                picked = scales * picked
            picked = picked.astype(jnp.bfloat16)
            mine_ref[part, :, cols] = picked[:pair_slots]
            theirs_ref[part, :, cols] = picked[pair_slots:]


def expert_kernel(index, chained, mine_ref, theirs_ref, wg_ref, wu_ref, wd_ref, *refs):
    near_ref, far_ref, *kept_refs = refs[5 if chained else 0:][:7]
    act_ref, gt_ref, ut_ref, sems = refs[-4:]
    pair_slots = mine_ref.shape[1]
    slots = 2 * pair_slots

    def kept_move(source, target, part, count, i):
        return pltpu.make_async_copy(
            source, kept_refs[target].at[pl.ds(index * slots + part * pair_slots, count)], sems.at[i]
        )

    moves = [
        kept_move(mine_ref.at[0], 0, 0, pair_slots, 0),
        kept_move(theirs_ref.at[0], 0, 1, pair_slots, 1),
        kept_move(mine_ref.at[1], 1, 0, pair_slots, 2),
        kept_move(theirs_ref.at[1], 1, 1, pair_slots, 3),
        kept_move(act_ref, 2, 0, slots, 4),
        kept_move(gt_ref, 3, 0, slots, 5),
        kept_move(ut_ref, 4, 0, slots, 6),
    ]
    for move in moves[:4]:
        move.start()
    rows_x = jnp.concatenate([mine_ref[0], theirs_ref[0]], axis=0)
    rows_g = jnp.concatenate([mine_ref[1], theirs_ref[1]], axis=0)
    gate = lax.dot_general(rows_x, wg_ref[...], CONTRACT_LAST, preferred_element_type=jnp.float32)
    up = lax.dot_general(rows_x, wu_ref[...], CONTRACT_LAST, preferred_element_type=jnp.float32)
    hidden_grad = lax.dot_general(rows_g, wd_ref[...], CONTRACT_LAST, preferred_element_type=jnp.float32)
    sigma = 1.0 / (1.0 + jnp.exp(-gate))
    silu = gate * sigma
    act_ref[...] = (silu * up).astype(jnp.bfloat16)
    gt_ref[...] = (hidden_grad * up * sigma * (1.0 + gate * (1.0 - sigma))).astype(jnp.bfloat16)
    ut_ref[...] = (hidden_grad * silu).astype(jnp.bfloat16)
    for move in moves[4:]:
        move.start()
    slot = jnp.dot(gt_ref[...], wg_ref[...], preferred_element_type=jnp.float32)
    slot += jnp.dot(ut_ref[...], wu_ref[...], preferred_element_type=jnp.float32)
    far_ref[...] = slot[pair_slots:].astype(jnp.bfloat16)
    near_ref[...] = slot[:pair_slots].astype(jnp.bfloat16)
    for move in moves:
        move.wait()


def place_kernel(place_ref, picks_ref, near_ref, far_ref, keep_ref, send_ref):
    own_half, core = place_ref[1], place_ref[2]
    _, rows, width = keep_ref.shape
    pair_slots = near_ref.shape[0]
    backs = []
    for h in range(2):
        cols = pl.ds(pl.multiple_of((own_half if h == 0 else 1 - own_half) * width, width), width)
        slot = jnp.concatenate([near_ref[:, cols], far_ref[:, cols]], axis=0)
        backs.append(lax.dot_general(picks_ref[...], slot, CONTRACT_FIRST, preferred_element_type=jnp.float32))
    keep_ref[0] = backs[0][:rows]
    keep_ref[1] = jnp.where(core == 1, backs[1][:rows], backs[0][rows:])
    send_ref[0] = jnp.where(core == 1, backs[0][rows:], backs[1][:rows]).astype(jnp.bfloat16)
    send_ref[1] = backs[1][rows:].astype(jnp.bfloat16)


def pick_rows(place, shares, top, rows, pair_slots):
    width = shares[0].shape[1]
    vmem = pl.BlockSpec(memory_space=pltpu.VMEM)
    picked = jax.ShapeDtypeStruct((2, pair_slots, 2 * width), jnp.bfloat16)
    return pl.pallas_call(
        functools.partial(pick_kernel, top, rows),
        in_specs=[pl.BlockSpec(memory_space=pltpu.SMEM)] + [vmem] * 4,
        out_specs=[vmem] * 3,
        out_shape=[picked, picked, jax.ShapeDtypeStruct((2 * pair_slots, 2 * rows), jnp.bfloat16)],
        compiler_params=pltpu.CompilerParams(vmem_limit_bytes=VMEM_LIMIT),
        name="pick",
    )(place, *shares)


def run_experts(index, chunks, mine, theirs, weights, kept):
    _, pair_slots, features = mine.shape
    hidden = weights[0].shape[0]
    slots = 2 * pair_slots
    hbm = pl.BlockSpec(memory_space=pltpu.HBM)
    vmem = pl.BlockSpec(memory_space=pltpu.VMEM)
    part = jax.ShapeDtypeStruct((pair_slots, features), jnp.bfloat16)
    wide = jax.ShapeDtypeStruct((chunks * slots, features), jnp.bfloat16)
    narrow = jax.ShapeDtypeStruct((chunks * slots, hidden), jnp.bfloat16)
    return pl.pallas_call(
        functools.partial(expert_kernel, index, kept is not None),
        in_specs=[vmem] * 5 + [hbm] * (0 if kept is None else 5),
        out_specs=[vmem] * 2 + [hbm] * 5,
        out_shape=[part, part, wide, wide, narrow, narrow, narrow],
        scratch_shapes=[pltpu.VMEM((slots, hidden), jnp.bfloat16)] * 3 + [pltpu.SemaphoreType.DMA((7,))],
        input_output_aliases={} if kept is None else {5 + i: 2 + i for i in range(5)},
        compiler_params=pltpu.CompilerParams(vmem_limit_bytes=VMEM_LIMIT),
        name="experts",
    )(mine, theirs, *weights, *(kept or ()))


def place_rows(place, picks, near, far, rows, width):
    vmem = pl.BlockSpec(memory_space=pltpu.VMEM)
    return pl.pallas_call(
        place_kernel,
        in_specs=[pl.BlockSpec(memory_space=pltpu.SMEM)] + [vmem] * 3,
        out_specs=[vmem] * 2,
        out_shape=[
            jax.ShapeDtypeStruct((2, rows, width), jnp.float32),
            jax.ShapeDtypeStruct((2, rows, width), jnp.bfloat16),
        ],
        compiler_params=pltpu.CompilerParams(vmem_limit_bytes=VMEM_LIMIT),
        name="place",
    )(place, picks, near, far)


def ring_order(length):
    return list(range(0, min(1, length))) + list(range(1, length, 2)) + list(range(2, length, 2))[::-1]


def gather_body(tokens, out_grad, routes, combine, w_gate, w_up, w_down):
    experts = lax.axis_size("expert")
    chunks = experts // 4
    rows, width = tokens.shape
    top = routes.shape[1]
    per_pair = rows * top // experts
    capacity = per_pair + per_pair // 8
    pair_slots = -(-2 * capacity // 16) * 16
    order = ring_order(chunks)
    after = {order[i]: order[(i + 1) % chunks] for i in range(chunks)}
    devices = [(e, h) for e in range(experts) for h in range(2)]

    def permute(value, target):
        pairs = [(e * 2 + h, target(e, h)[0] * 2 + target(e, h)[1]) for e, h in devices]
        return lax.ppermute(value, ("expert", "etp"), pairs)

    def to_ring(value):
        return permute(value, lambda e, h: (after[e // 4] * 4 + e % 4, h))

    def to_core(value):
        return permute(value, lambda e, h: (e ^ 1, h))

    def to_first(value):
        return permute(value, lambda e, h: (e, h ^ 1) if e % 2 else (e ^ 2, h))

    def to_second(value):
        return permute(value, lambda e, h: (e ^ 2, h) if e % 2 else (e, h ^ 1))

    me = lax.axis_index("expert")
    place = jnp.stack([me, lax.axis_index("etp"), me % 2]).astype(jnp.int32)
    share = pack_share(tokens, out_grad, routes, combine)
    weights = load_weights((w_gate[0], w_up[0], w_down[0]))

    def tied(values, mark):
        return lax.optimization_barrier((values, mark))[0]

    def placed(picks, near, far):
        return place_rows(place, picks, near, to_core(far), rows, width)

    def added(keep, came):
        return keep + came.astype(jnp.float32)

    ring_sends = [("s", 1)] + [(kind, c) for c in range(2, chunks) for kind in ("f", "s")]
    ring_sends.sort(key=lambda key: key[1] * 2 - (key[0] == "s"))
    plane_sends = [("f", 0), ("a", 0), ("b", 0), ("f", 1), ("a", 1), ("b", 1)]
    plane_sends += [(kind, c) for c in range(2, chunks) for kind in ("a", "b")]
    ring_sends = [key for key in ring_sends if key[1] < chunks]
    plane_sends = [key for key in plane_sends if key[1] < chunks]

    def source_of(key, by_ring):
        kind, c = key
        return (kind, c - 1) if by_ring else ("f" if kind == "b" else "s", c)

    have = {("s", 0): share}
    kept, picked, parts, waiting = None, None, None, None
    late, done = [], 0
    while plane_sends:
        came = {}
        for key in [key for key in plane_sends if source_of(key, False) in have][:2]:
            value = have[source_of(key, False)]
            came[key] = to_first(value) if key[0] == "f" else to_second(value)
            plane_sends.remove(key)
        for key in [key for key in ring_sends if source_of(key, True) in have][:1]:
            came[key] = to_ring(have[source_of(key, True)])
            ring_sends.remove(key)
        ready, waiting, before = waiting, None, parts
        if picked is not None:
            mine, theirs, picks = picked
            near, far, *kept = run_experts(done, chunks, mine, to_core(theirs), weights, kept)
            parts, picked = (picks, near, far), None
            done += 1
        else:
            parts = None
        if before is not None:
            waiting = placed(*before)
        if plane_sends and all((kind, done) in have for kind in "sfab"):
            picked = pick_rows(place, [have[kind, done] for kind in "sfab"], top, rows, pair_slots)
        if ready is not None:
            late.append(ready)
        needed = {key: have[key] for key in have if key[1] >= done}
        listed = sorted(came, reverse=True)
        values, have, picked, parts, waiting, late, weights = lax.optimization_barrier(
            ([came[key] for key in listed], needed, picked, parts, waiting, late, weights)
        )
        came = dict(zip(listed, values))
        have.update(came)
    mine, theirs, picks = pick_rows(place, [have[kind, done] for kind in "sfab"], top, rows, pair_slots)
    unsent, late = late, []
    if waiting is not None:
        keep, send = waiting
        late.append((keep, to_second(tied(send, theirs))))
    if parts is not None:
        keep, send = placed(*tied(parts, theirs))
        late.append((keep, to_second(send)))
    near, far, *kept = run_experts(done, chunks, mine, to_core(theirs), weights, kept)
    keep, send = placed(picks, near, far)
    late.append((keep, to_second(send)))
    late = [(keep, to_second(tied(first, send))) for keep, first in unsent] + late
    marks = [send] * (chunks + 2)
    running = None
    for c in range(1, chunks):
        keep, came = late[c]
        if c + 1 < chunks:
            came = tied(came, near if c == 1 else marks[0])
        pair = added(keep, came)
        came = to_first(pair[1].astype(jnp.bfloat16))
        total = added(pair[0], came if c + 1 == chunks else tied(came, send))
        running = (total if running is None else added(total, running)).astype(jnp.bfloat16)
        marks[min(c - 1, 2)] = running
        if c + 1 < chunks:
            running = to_ring(running)
    keep, came = late[0]
    pair = added(keep, came)
    came = pair[1].astype(jnp.bfloat16)
    own = added(pair[0], to_first(came if running is None else tied(came, running)))
    grad_tokens = (own if running is None else added(own, to_ring(running))).astype(jnp.bfloat16)
    rows_x, rows_g, acts, gate_term, up_term = kept
    acts, gate_term, up_term = tied(acts, marks[0]), tied(gate_term, marks[1]), tied(up_term, marks[2])
    grad_down = lax.dot_general(acts, rows_g, CONTRACT_FIRST, preferred_element_type=jnp.float32)
    grad_gate = lax.dot_general(gate_term, rows_x, CONTRACT_FIRST, preferred_element_type=jnp.float32)
    grad_up = lax.dot_general(up_term, rows_x, CONTRACT_FIRST, preferred_element_type=jnp.float32)
    return (
        grad_tokens,
        grad_gate.astype(jnp.bfloat16)[None],
        grad_up.astype(jnp.bfloat16)[None],
        grad_down.astype(jnp.bfloat16)[None],
    )


def solution(mesh):
    experts = mesh.shape["expert"]

    def body(tokens, out_grad, routes, combine, w_gate, w_up, w_down):
        rows, width = tokens.shape
        top = routes.shape[1]
        gathers = top * 4 >= experts and experts % 4 == 0 and mesh.shape["etp"] == 2
        run = gather_body if gathers and top * rows <= width else exchange_body
        return run(tokens, out_grad, routes, combine, w_gate, w_up, w_down)

    placed = (
        P("expert", "etp"),
        P("expert", "etp"),
        P("expert", None),
        P("expert", None),
        P("expert", "etp", None),
        P("expert", "etp", None),
        P("expert", "etp", None),
    )
    return jax.shard_map(
        body,
        mesh=mesh,
        in_specs=placed,
        out_specs=(
            P("expert", "etp"),
            P("expert", "etp", None),
            P("expert", "etp", None),
            P("expert", "etp", None),
        ),
        check_vma=False,
    )
```

```python
import functools

import jax
import jax.numpy as jnp
from jax import lax
from jax.experimental import pallas as pl
from jax.experimental.pallas import tpu as pltpu
from jax.sharding import PartitionSpec as P

CONTRACT_LAST = (((1,), (1,)), ((), ()))
CONTRACT_FIRST = (((0,), (0,)), ((), ()))
INFO_ROWS = 16
VMEM_LIMIT = 8 * 1024 * 1024


def pack_rows(token_rows, grad_rows, token_of, scale, is_live):
    mask = is_live[:, None].astype(token_rows.dtype)
    inputs_sent = token_rows[token_of] * mask
    grads_sent = (scale[:, None] * grad_rows[token_of].astype(jnp.float32)).astype(jnp.bfloat16)
    return (inputs_sent, grads_sent)


def pair_positions(routed_flat, experts):
    pair_total = routed_flat.shape[0]
    span = 128
    groups = pair_total // span
    labels = jnp.arange(experts, dtype=jnp.int32)
    one_hot = (routed_flat[:, None] == labels[None, :]).astype(jnp.bfloat16)
    grouped = one_hot.reshape(groups, span, experts)
    row_ids = jnp.arange(span, dtype=jnp.int32)
    lower = (row_ids[None, :] < row_ids[:, None]).astype(jnp.bfloat16)
    within = jnp.einsum("ij,bje->bie", lower, grouped, preferred_element_type=jnp.float32)
    group_sums = jnp.sum(grouped.astype(jnp.float32), axis=1)
    group_before = jnp.cumsum(group_sums, axis=0) - group_sums
    earlier = within + group_before[:, None, :]
    counted = jnp.sum(earlier * grouped.astype(jnp.float32), axis=2)
    return counted.reshape(pair_total).astype(jnp.int32)


def exchange_body(tokens, out_grad, routes, combine, w_gate, w_up, w_down):
    experts = lax.axis_size("expert")
    tok_rows = tokens.shape[0]
    col_width = tokens.shape[1]
    choose_count = routes.shape[1]
    per_pair = tok_rows * choose_count // experts
    capacity = per_pair + per_pair // 8
    routed_flat = routes.reshape(-1)
    pair_total = routed_flat.shape[0]
    position = pair_positions(routed_flat, experts)
    target = routed_flat * capacity + position
    anchor = jnp.full((experts * capacity,), pair_total, jnp.int32)
    anchor = anchor.at[target].set(jnp.arange(pair_total, dtype=jnp.int32))
    is_live = anchor < pair_total
    safe_anchor = jnp.minimum(anchor, pair_total - 1)
    token_of = safe_anchor // choose_count
    scale = combine.reshape(-1)[safe_anchor] * is_live.astype(jnp.float32)
    full_tokens, full_grads = (
        lax.all_gather(tokens, "etp", axis=1, tiled=True),
        lax.all_gather(out_grad, "etp", axis=1, tiled=True),
    )
    inputs_sent, grads_sent = pack_rows(full_tokens, full_grads, token_of, scale, is_live)
    rows_x, rows_g = (
        lax.all_to_all(inputs_sent, "expert", split_axis=0, concat_axis=0, tiled=True),
        lax.all_to_all(grads_sent, "expert", split_axis=0, concat_axis=0, tiled=True),
    )
    gate_w = w_gate[0]
    up_w = w_up[0]
    down_w = w_down[0]
    gate = lax.dot_general(rows_x, gate_w, CONTRACT_LAST, preferred_element_type=jnp.float32)
    up = lax.dot_general(rows_x, up_w, CONTRACT_LAST, preferred_element_type=jnp.float32)
    hidden_grad = lax.dot_general(rows_g, down_w, CONTRACT_LAST, preferred_element_type=jnp.float32)
    sigma = jax.nn.sigmoid(gate)
    silu = gate * sigma
    acts = (silu * up).astype(jnp.bfloat16)
    grad_down = lax.dot_general(acts, rows_g, CONTRACT_FIRST, preferred_element_type=jnp.float32)
    gate_term = (hidden_grad * up * sigma * (1.0 + gate * (1.0 - sigma))).astype(jnp.bfloat16)
    up_term = (hidden_grad * silu).astype(jnp.bfloat16)
    grad_gate = lax.dot_general(
        gate_term, rows_x, CONTRACT_FIRST, preferred_element_type=jnp.float32
    )
    grad_up = lax.dot_general(up_term, rows_x, CONTRACT_FIRST, preferred_element_type=jnp.float32)
    swapped_gate, swapped_up = (
        lax.all_to_all(gate_w, "etp", split_axis=1, concat_axis=0, tiled=True),
        lax.all_to_all(up_w, "etp", split_axis=1, concat_axis=0, tiled=True),
    )
    running = jnp.dot(
        lax.all_gather(gate_term, "etp", axis=1, tiled=True),
        swapped_gate,
        preferred_element_type=jnp.float32,
    )
    slot_grads = running + jnp.dot(
        lax.all_gather(up_term, "etp", axis=1, tiled=True),
        swapped_up,
        preferred_element_type=jnp.float32,
    )
    slot_grads = slot_grads.astype(jnp.bfloat16)
    returned = lax.all_to_all(slot_grads, "expert", split_axis=0, concat_axis=0, tiled=True)
    picked = returned[target].astype(jnp.float32).reshape(tok_rows, choose_count, col_width)
    grad_tokens = jnp.sum(picked, axis=1).astype(jnp.bfloat16)
    return (
        grad_tokens,
        grad_gate.astype(jnp.bfloat16)[None],
        grad_up.astype(jnp.bfloat16)[None],
        grad_down.astype(jnp.bfloat16)[None],
    )


def pack_kernel(tokens_ref, grads_ref, routes_ref, combine_ref, out_ref):
    rows = tokens_ref.shape[0]
    out_ref[:rows] = tokens_ref[...]
    out_ref[rows:2 * rows] = grads_ref[...]
    top = routes_ref.shape[0]
    routes = routes_ref[...].astype(jnp.float32)
    weights = combine_ref[...]
    high = weights.astype(jnp.bfloat16).astype(jnp.float32)
    middle = (weights - high).astype(jnp.bfloat16).astype(jnp.float32)
    low = weights - high - middle
    blank = jnp.zeros((INFO_ROWS - 4, rows), jnp.float32)
    for k in range(top):
        own = slice(k, k + 1)
        column = jnp.concatenate([routes[own], high[own], middle[own], low[own], blank], axis=0)
        out_ref[2 * rows:, k * rows:(k + 1) * rows] = column.astype(jnp.bfloat16)


def pack_share(tokens, out_grad, routes, combine):
    rows, width = tokens.shape
    vmem = pl.BlockSpec(memory_space=pltpu.VMEM)
    return pl.pallas_call(
        pack_kernel,
        in_specs=[vmem] * 4,
        out_specs=vmem,
        out_shape=jax.ShapeDtypeStruct((2 * rows + INFO_ROWS, width), jnp.bfloat16),
        compiler_params=pltpu.CompilerParams(vmem_limit_bytes=VMEM_LIMIT),
        name="pack",
    )(tokens, out_grad, routes.T, combine.T)


def pick_kernel(top, rows, place_ref, *refs):
    shares, (mine_ref, theirs_ref, picks_ref) = refs[:4], refs[4:]
    me, own_half, core = place_ref[0], place_ref[1], place_ref[2]
    pair_slots, width = mine_ref.shape[1], shares[0].shape[1]
    earlier = (
        lax.broadcasted_iota(jnp.int32, (2 * rows, 2 * rows), 0)
        < lax.broadcasted_iota(jnp.int32, (2 * rows, 2 * rows), 1)
    ).astype(jnp.bfloat16)
    infos = [
        [share_ref[pl.ds(2 * rows, INFO_ROWS), k * rows:(k + 1) * rows].astype(jnp.float32) for k in range(top)]
        for share_ref in (shares[0], shares[3])
    ]
    picks, scales = [], []
    for expert in (me, me + 1 - 2 * core):
        named, weights = [], []
        for block in infos:
            hits, weight = 0.0, 0.0
            for info in block:
                hit = info[0:1] == expert.astype(jnp.float32)
                hits += hit.astype(jnp.float32)
                weight += jnp.where(hit, info[1:2] + info[2:3] + info[3:4], 0.0)
            named.append(hits)
            weights.append(weight)
        named = jnp.concatenate(named, axis=1)
        weights = jnp.concatenate(weights, axis=1)
        counted = jnp.dot(
            jnp.broadcast_to(named, (16, 2 * rows)).astype(jnp.bfloat16),
            earlier,
            preferred_element_type=jnp.float32,
        )[:1]
        slot_of = jnp.where(named > 0.0, counted.astype(jnp.int32), -1)
        chosen = slot_of == lax.broadcasted_iota(jnp.int32, (pair_slots, 2 * rows), 0)
        picks.append(chosen.astype(jnp.bfloat16))
        scales.append(jnp.sum(jnp.where(chosen, weights, 0.0), axis=1, keepdims=True))
    picks = jnp.concatenate(picks, axis=0)
    scales = jnp.concatenate(scales, axis=0)
    picks_ref[...] = picks
    for h in range(2):
        cols = pl.ds(pl.multiple_of((own_half if h == 0 else 1 - own_half) * width, width), width)
        for part in range(2):
            own, first, second, both = [ref[pl.ds(part * rows, rows)] for ref in shares]
            if h == 0:
                held = jnp.concatenate([own, jnp.where(core == 1, second, first)], axis=0)
            else:
                held = jnp.concatenate([jnp.where(core == 1, first, second), both], axis=0)
            picked = jnp.dot(picks, held, preferred_element_type=jnp.float32)
            if part == 1:
                picked = scales * picked
            picked = picked.astype(jnp.bfloat16)
            mine_ref[part, :, cols] = picked[:pair_slots]
            theirs_ref[part, :, cols] = picked[pair_slots:]


def expert_kernel(index, chained, mine_ref, theirs_ref, wg_ref, wu_ref, wd_ref, *refs):
    near_ref, far_ref, *kept_refs = refs[5 if chained else 0:][:7]
    act_ref, gt_ref, ut_ref, sems = refs[-4:]
    pair_slots = mine_ref.shape[1]
    slots = 2 * pair_slots

    def kept_move(source, target, part, count, i):
        return pltpu.make_async_copy(
            source, kept_refs[target].at[pl.ds(index * slots + part * pair_slots, count)], sems.at[i]
        )

    moves = [
        kept_move(mine_ref.at[0], 0, 0, pair_slots, 0),
        kept_move(theirs_ref.at[0], 0, 1, pair_slots, 1),
        kept_move(mine_ref.at[1], 1, 0, pair_slots, 2),
        kept_move(theirs_ref.at[1], 1, 1, pair_slots, 3),
        kept_move(act_ref, 2, 0, slots, 4),
        kept_move(gt_ref, 3, 0, slots, 5),
        kept_move(ut_ref, 4, 0, slots, 6),
    ]
    for move in moves[:4]:
        move.start()
    rows_x = jnp.concatenate([mine_ref[0], theirs_ref[0]], axis=0)
    rows_g = jnp.concatenate([mine_ref[1], theirs_ref[1]], axis=0)
    gate = lax.dot_general(rows_x, wg_ref[...], CONTRACT_LAST, preferred_element_type=jnp.float32)
    up = lax.dot_general(rows_x, wu_ref[...], CONTRACT_LAST, preferred_element_type=jnp.float32)
    hidden_grad = lax.dot_general(rows_g, wd_ref[...], CONTRACT_LAST, preferred_element_type=jnp.float32)
    sigma = 1.0 / (1.0 + jnp.exp(-gate))
    silu = gate * sigma
    act_ref[...] = (silu * up).astype(jnp.bfloat16)
    gt_ref[...] = (hidden_grad * up * sigma * (1.0 + gate * (1.0 - sigma))).astype(jnp.bfloat16)
    ut_ref[...] = (hidden_grad * silu).astype(jnp.bfloat16)
    for move in moves[4:]:
        move.start()
    slot = jnp.dot(gt_ref[...], wg_ref[...], preferred_element_type=jnp.float32)
    slot += jnp.dot(ut_ref[...], wu_ref[...], preferred_element_type=jnp.float32)
    far_ref[...] = slot[pair_slots:].astype(jnp.bfloat16)
    near_ref[...] = slot[:pair_slots].astype(jnp.bfloat16)
    for move in moves:
        move.wait()


def place_kernel(place_ref, picks_ref, near_ref, far_ref, keep_ref, send_ref):
    own_half, core = place_ref[1], place_ref[2]
    _, rows, width = keep_ref.shape
    pair_slots = near_ref.shape[0]
    backs = []
    for h in range(2):
        cols = pl.ds(pl.multiple_of((own_half if h == 0 else 1 - own_half) * width, width), width)
        slot = jnp.concatenate([near_ref[:, cols], far_ref[:, cols]], axis=0)
        backs.append(lax.dot_general(picks_ref[...], slot, CONTRACT_FIRST, preferred_element_type=jnp.float32))
    keep_ref[0] = backs[0][:rows]
    keep_ref[1] = jnp.where(core == 1, backs[1][:rows], backs[0][rows:])
    send_ref[0] = jnp.where(core == 1, backs[0][rows:], backs[1][:rows]).astype(jnp.bfloat16)
    send_ref[1] = backs[1][rows:].astype(jnp.bfloat16)


def pick_rows(place, shares, top, rows, pair_slots):
    width = shares[0].shape[1]
    vmem = pl.BlockSpec(memory_space=pltpu.VMEM)
    picked = jax.ShapeDtypeStruct((2, pair_slots, 2 * width), jnp.bfloat16)
    return pl.pallas_call(
        functools.partial(pick_kernel, top, rows),
        in_specs=[pl.BlockSpec(memory_space=pltpu.SMEM)] + [vmem] * 4,
        out_specs=[vmem] * 3,
        out_shape=[picked, picked, jax.ShapeDtypeStruct((2 * pair_slots, 2 * rows), jnp.bfloat16)],
        compiler_params=pltpu.CompilerParams(vmem_limit_bytes=VMEM_LIMIT),
        name="pick",
    )(place, *shares)


def run_experts(index, chunks, mine, theirs, weights, kept):
    _, pair_slots, features = mine.shape
    hidden = weights[0].shape[0]
    slots = 2 * pair_slots
    hbm = pl.BlockSpec(memory_space=pltpu.HBM)
    vmem = pl.BlockSpec(memory_space=pltpu.VMEM)
    part = jax.ShapeDtypeStruct((pair_slots, features), jnp.bfloat16)
    wide = jax.ShapeDtypeStruct((chunks * slots, features), jnp.bfloat16)
    narrow = jax.ShapeDtypeStruct((chunks * slots, hidden), jnp.bfloat16)
    return pl.pallas_call(
        functools.partial(expert_kernel, index, kept is not None),
        in_specs=[vmem] * 5 + [hbm] * (0 if kept is None else 5),
        out_specs=[vmem] * 2 + [hbm] * 5,
        out_shape=[part, part, wide, wide, narrow, narrow, narrow],
        scratch_shapes=[pltpu.VMEM((slots, hidden), jnp.bfloat16)] * 3 + [pltpu.SemaphoreType.DMA((7,))],
        input_output_aliases={} if kept is None else {5 + i: 2 + i for i in range(5)},
        compiler_params=pltpu.CompilerParams(vmem_limit_bytes=VMEM_LIMIT),
        name="experts",
    )(mine, theirs, *weights, *(kept or ()))


def place_rows(place, picks, near, far, rows, width):
    vmem = pl.BlockSpec(memory_space=pltpu.VMEM)
    return pl.pallas_call(
        place_kernel,
        in_specs=[pl.BlockSpec(memory_space=pltpu.SMEM)] + [vmem] * 3,
        out_specs=[vmem] * 2,
        out_shape=[
            jax.ShapeDtypeStruct((2, rows, width), jnp.float32),
            jax.ShapeDtypeStruct((2, rows, width), jnp.bfloat16),
        ],
        compiler_params=pltpu.CompilerParams(vmem_limit_bytes=VMEM_LIMIT),
        name="place",
    )(place, picks, near, far)


def ring_order(length):
    return list(range(0, min(1, length))) + list(range(1, length, 2)) + list(range(2, length, 2))[::-1]


def gather_body(tokens, out_grad, routes, combine, w_gate, w_up, w_down):
    experts = lax.axis_size("expert")
    chunks = experts // 4
    rows, width = tokens.shape
    top = routes.shape[1]
    per_pair = rows * top // experts
    capacity = per_pair + per_pair // 8
    pair_slots = -(-2 * capacity // 16) * 16
    order = ring_order(chunks)
    after = {order[i]: order[(i + 1) % chunks] for i in range(chunks)}
    devices = [(e, h) for e in range(experts) for h in range(2)]

    def permute(value, target):
        pairs = [(e * 2 + h, target(e, h)[0] * 2 + target(e, h)[1]) for e, h in devices]
        return lax.ppermute(value, ("expert", "etp"), pairs)

    def to_ring(value):
        return permute(value, lambda e, h: (after[e // 4] * 4 + e % 4, h))

    def to_core(value):
        return permute(value, lambda e, h: (e ^ 1, h))

    def to_first(value):
        return permute(value, lambda e, h: (e, h ^ 1) if e % 2 else (e ^ 2, h))

    def to_second(value):
        return permute(value, lambda e, h: (e ^ 2, h) if e % 2 else (e, h ^ 1))

    me = lax.axis_index("expert")
    place = jnp.stack([me, lax.axis_index("etp"), me % 2]).astype(jnp.int32)
    share = pack_share(tokens, out_grad, routes, combine)
    weights = (w_gate[0], w_up[0], w_down[0])

    def tied(values, mark):
        return lax.optimization_barrier((values, mark))[0]

    def placed(picks, near, far):
        return place_rows(place, picks, near, to_core(far), rows, width)

    def added(keep, came):
        return keep + came.astype(jnp.float32)

    ring_sends = [("s", 1)] + [(kind, c) for c in range(2, chunks) for kind in ("f", "s")]
    ring_sends.sort(key=lambda key: key[1] * 2 - (key[0] == "s"))
    plane_sends = [("f", 0), ("a", 0), ("b", 0), ("f", 1), ("a", 1), ("b", 1)]
    plane_sends += [(kind, c) for c in range(2, chunks) for kind in ("a", "b")]
    ring_sends = [key for key in ring_sends if key[1] < chunks]
    plane_sends = [key for key in plane_sends if key[1] < chunks]

    def source_of(key, by_ring):
        kind, c = key
        return (kind, c - 1) if by_ring else ("f" if kind == "b" else "s", c)

    have = {("s", 0): share}
    kept, picked, parts, waiting = None, None, None, None
    late, done = [], 0
    while plane_sends:
        came = {}
        for key in [key for key in plane_sends if source_of(key, False) in have][:2]:
            value = have[source_of(key, False)]
            came[key] = to_first(value) if key[0] == "f" else to_second(value)
            plane_sends.remove(key)
        for key in [key for key in ring_sends if source_of(key, True) in have][:1]:
            came[key] = to_ring(have[source_of(key, True)])
            ring_sends.remove(key)
        ready, waiting, before = waiting, None, parts
        if picked is not None:
            mine, theirs, picks = picked
            near, far, *kept = run_experts(done, chunks, mine, to_core(theirs), weights, kept)
            parts, picked = (picks, near, far), None
            done += 1
        else:
            parts = None
        if before is not None:
            waiting = placed(*before)
        if plane_sends and all((kind, done) in have for kind in "sfab"):
            picked = pick_rows(place, [have[kind, done] for kind in "sfab"], top, rows, pair_slots)
        if ready is not None:
            late.append(ready)
        needed = {key: have[key] for key in have if key[1] >= done}
        listed = sorted(came)
        held = (needed, picked, parts, waiting if plane_sends else None, late)
        values, (have, picked, parts, held, late) = lax.optimization_barrier(([came[key] for key in listed], held))
        waiting = held if plane_sends else waiting
        came = dict(zip(listed, values))
        have.update(came)
    mine, theirs, picks = pick_rows(place, [have[kind, done] for kind in "sfab"], top, rows, pair_slots)
    unsent, late, early = late, [], None
    if waiting is not None:
        keep, send = waiting
        came, parts = lax.optimization_barrier((to_second(send), parts))
        late.append((keep, came))
    if parts is not None:
        keep, send = placed(*tied(parts, theirs))
        late.append((keep, to_second(send)))
        mine = tied(mine, send)
    near, far, *kept = run_experts(done, chunks, mine, to_core(theirs), weights, kept)
    if len(unsent) == 1 and late:
        pair = added(*late[0])
        came, near, far = lax.optimization_barrier((to_first(pair[1].astype(jnp.bfloat16)), near, far))
        early = added(pair[0], came)
        if len(late) > 1:
            keep, came = late[1]
            came, near = lax.optimization_barrier((came, near))
            late[1] = keep, came
    keep, send = placed(picks, near, far)
    late.append((keep, to_second(send)))
    late = [(keep, to_second(tied(first, send))) for keep, first in unsent] + late
    marks = [send] * (chunks + 2)
    running = None
    for c in range(1, chunks):
        if c == 1 and early is not None:
            total = early
        else:
            keep, came = late[c]
            if c + 1 < chunks:
                came = tied(came, near if c == 1 else send)
            pair = added(keep, came)
            came = to_first(pair[1].astype(jnp.bfloat16))
            total = added(pair[0], came if c + 1 == chunks else tied(came, send))
        running = (total if running is None else added(total, running)).astype(jnp.bfloat16)
        if c > 1:
            marks[min(c - 1, 2)] = running
        if c + 1 < chunks:
            running = to_ring(running)
    keep, came = late[0]
    pair = added(keep, came)
    came = pair[1].astype(jnp.bfloat16)
    own = added(pair[0], to_first(came if running is None else tied(came, running)))
    grad_tokens = (own if running is None else added(own, to_ring(running))).astype(jnp.bfloat16)
    rows_x, rows_g, acts, gate_term, up_term = kept
    acts, gate_term, up_term = tied(acts, marks[0]), tied(gate_term, marks[1]), tied(up_term, marks[2])
    grad_down = lax.dot_general(acts, rows_g, CONTRACT_FIRST, preferred_element_type=jnp.float32)
    grad_gate = lax.dot_general(gate_term, rows_x, CONTRACT_FIRST, preferred_element_type=jnp.float32)
    grad_up = lax.dot_general(up_term, rows_x, CONTRACT_FIRST, preferred_element_type=jnp.float32)
    return (
        grad_tokens,
        grad_gate.astype(jnp.bfloat16)[None],
        grad_up.astype(jnp.bfloat16)[None],
        grad_down.astype(jnp.bfloat16)[None],
    )


def solution(mesh):
    experts = mesh.shape["expert"]

    def body(tokens, out_grad, routes, combine, w_gate, w_up, w_down):
        rows, width = tokens.shape
        top = routes.shape[1]
        gathers = top * 4 >= experts and experts % 4 == 0 and mesh.shape["etp"] == 2
        run = gather_body if gathers and top * rows <= width else exchange_body
        return run(tokens, out_grad, routes, combine, w_gate, w_up, w_down)

    placed = (
        P("expert", "etp"),
        P("expert", "etp"),
        P("expert", None),
        P("expert", None),
        P("expert", "etp", None),
        P("expert", "etp", None),
        P("expert", "etp", None),
    )
    return jax.shard_map(
        body,
        mesh=mesh,
        in_specs=placed,
        out_specs=(
            P("expert", "etp"),
            P("expert", "etp", None),
            P("expert", "etp", None),
            P("expert", "etp", None),
        ),
        check_vma=False,
    )
```

```python
import functools

import jax
import jax.numpy as jnp
from jax import lax
from jax.experimental import pallas as pl
from jax.experimental.pallas import tpu as pltpu
from jax.sharding import PartitionSpec as P

CONTRACT_LAST = (((1,), (1,)), ((), ()))
CONTRACT_FIRST = (((0,), (0,)), ((), ()))
INFO_ROWS = 16
VMEM_LIMIT = 16 * 1024 * 1024


def pack_rows(token_rows, grad_rows, token_of, scale, is_live):
    mask = is_live[:, None].astype(token_rows.dtype)
    inputs_sent = token_rows[token_of] * mask
    grads_sent = (scale[:, None] * grad_rows[token_of].astype(jnp.float32)).astype(jnp.bfloat16)
    return (inputs_sent, grads_sent)


def pair_positions(routed_flat, experts):
    pair_total = routed_flat.shape[0]
    span = 128
    groups = pair_total // span
    labels = jnp.arange(experts, dtype=jnp.int32)
    one_hot = (routed_flat[:, None] == labels[None, :]).astype(jnp.bfloat16)
    grouped = one_hot.reshape(groups, span, experts)
    row_ids = jnp.arange(span, dtype=jnp.int32)
    lower = (row_ids[None, :] < row_ids[:, None]).astype(jnp.bfloat16)
    within = jnp.einsum("ij,bje->bie", lower, grouped, preferred_element_type=jnp.float32)
    group_sums = jnp.sum(grouped.astype(jnp.float32), axis=1)
    group_before = jnp.cumsum(group_sums, axis=0) - group_sums
    earlier = within + group_before[:, None, :]
    counted = jnp.sum(earlier * grouped.astype(jnp.float32), axis=2)
    return counted.reshape(pair_total).astype(jnp.int32)


def exchange_body(tokens, out_grad, routes, combine, w_gate, w_up, w_down):
    experts = lax.axis_size("expert")
    tok_rows = tokens.shape[0]
    col_width = tokens.shape[1]
    choose_count = routes.shape[1]
    per_pair = tok_rows * choose_count // experts
    capacity = per_pair + per_pair // 8
    routed_flat = routes.reshape(-1)
    pair_total = routed_flat.shape[0]
    position = pair_positions(routed_flat, experts)
    target = routed_flat * capacity + position
    anchor = jnp.full((experts * capacity,), pair_total, jnp.int32)
    anchor = anchor.at[target].set(jnp.arange(pair_total, dtype=jnp.int32))
    is_live = anchor < pair_total
    safe_anchor = jnp.minimum(anchor, pair_total - 1)
    token_of = safe_anchor // choose_count
    scale = combine.reshape(-1)[safe_anchor] * is_live.astype(jnp.float32)
    full_tokens, full_grads = (
        lax.all_gather(tokens, "etp", axis=1, tiled=True),
        lax.all_gather(out_grad, "etp", axis=1, tiled=True),
    )
    inputs_sent, grads_sent = pack_rows(full_tokens, full_grads, token_of, scale, is_live)
    rows_x, rows_g = (
        lax.all_to_all(inputs_sent, "expert", split_axis=0, concat_axis=0, tiled=True),
        lax.all_to_all(grads_sent, "expert", split_axis=0, concat_axis=0, tiled=True),
    )
    gate_w = w_gate[0]
    up_w = w_up[0]
    down_w = w_down[0]
    gate = lax.dot_general(rows_x, gate_w, CONTRACT_LAST, preferred_element_type=jnp.float32)
    up = lax.dot_general(rows_x, up_w, CONTRACT_LAST, preferred_element_type=jnp.float32)
    hidden_grad = lax.dot_general(rows_g, down_w, CONTRACT_LAST, preferred_element_type=jnp.float32)
    sigma = jax.nn.sigmoid(gate)
    silu = gate * sigma
    acts = (silu * up).astype(jnp.bfloat16)
    grad_down = lax.dot_general(acts, rows_g, CONTRACT_FIRST, preferred_element_type=jnp.float32)
    gate_term = (hidden_grad * up * sigma * (1.0 + gate * (1.0 - sigma))).astype(jnp.bfloat16)
    up_term = (hidden_grad * silu).astype(jnp.bfloat16)
    grad_gate = lax.dot_general(
        gate_term, rows_x, CONTRACT_FIRST, preferred_element_type=jnp.float32
    )
    grad_up = lax.dot_general(up_term, rows_x, CONTRACT_FIRST, preferred_element_type=jnp.float32)
    swapped_gate, swapped_up = (
        lax.all_to_all(gate_w, "etp", split_axis=1, concat_axis=0, tiled=True),
        lax.all_to_all(up_w, "etp", split_axis=1, concat_axis=0, tiled=True),
    )
    running = jnp.dot(
        lax.all_gather(gate_term, "etp", axis=1, tiled=True),
        swapped_gate,
        preferred_element_type=jnp.float32,
    )
    slot_grads = running + jnp.dot(
        lax.all_gather(up_term, "etp", axis=1, tiled=True),
        swapped_up,
        preferred_element_type=jnp.float32,
    )
    slot_grads = slot_grads.astype(jnp.bfloat16)
    returned = lax.all_to_all(slot_grads, "expert", split_axis=0, concat_axis=0, tiled=True)
    picked = returned[target].astype(jnp.float32).reshape(tok_rows, choose_count, col_width)
    grad_tokens = jnp.sum(picked, axis=1).astype(jnp.bfloat16)
    return (
        grad_tokens,
        grad_gate.astype(jnp.bfloat16)[None],
        grad_up.astype(jnp.bfloat16)[None],
        grad_down.astype(jnp.bfloat16)[None],
    )


def pack_kernel(tokens_ref, grads_ref, routes_ref, combine_ref, out_ref):
    rows = tokens_ref.shape[0]
    out_ref[:rows] = tokens_ref[...]
    out_ref[rows:2 * rows] = grads_ref[...]
    top = routes_ref.shape[0]
    routes = routes_ref[...].astype(jnp.float32)
    weights = combine_ref[...]
    high = weights.astype(jnp.bfloat16).astype(jnp.float32)
    middle = (weights - high).astype(jnp.bfloat16).astype(jnp.float32)
    low = weights - high - middle
    blank = jnp.zeros((INFO_ROWS - 4, rows), jnp.float32)
    for k in range(top):
        own = slice(k, k + 1)
        column = jnp.concatenate([routes[own], high[own], middle[own], low[own], blank], axis=0)
        out_ref[2 * rows:, k * rows:(k + 1) * rows] = column.astype(jnp.bfloat16)


def pack_share(tokens, out_grad, routes, combine):
    rows, width = tokens.shape
    vmem = pl.BlockSpec(memory_space=pltpu.VMEM)
    return pl.pallas_call(
        pack_kernel,
        in_specs=[vmem] * 4,
        out_specs=vmem,
        out_shape=jax.ShapeDtypeStruct((2 * rows + INFO_ROWS, width), jnp.bfloat16),
        name="pack",
    )(tokens, out_grad, routes.T, combine.T)


def pick_kernel(top, rows, place_ref, *refs):
    shares, (mine_ref, theirs_ref, picks_ref) = refs[:4], refs[4:]
    me, own_half, core = place_ref[0], place_ref[1], place_ref[2]
    pair_slots, width = mine_ref.shape[1], shares[0].shape[1]
    earlier = (
        lax.broadcasted_iota(jnp.int32, (2 * rows, 2 * rows), 0)
        < lax.broadcasted_iota(jnp.int32, (2 * rows, 2 * rows), 1)
    ).astype(jnp.bfloat16)
    infos = [
        [share_ref[pl.ds(2 * rows, INFO_ROWS), k * rows:(k + 1) * rows].astype(jnp.float32) for k in range(top)]
        for share_ref in (shares[0], shares[3])
    ]
    picks, scales = [], []
    for expert in (me, me + 1 - 2 * core):
        named, weights = [], []
        for block in infos:
            hits, weight = 0.0, 0.0
            for info in block:
                hit = info[0:1] == expert.astype(jnp.float32)
                hits += hit.astype(jnp.float32)
                weight += jnp.where(hit, info[1:2] + info[2:3] + info[3:4], 0.0)
            named.append(hits)
            weights.append(weight)
        named = jnp.concatenate(named, axis=1)
        weights = jnp.concatenate(weights, axis=1)
        counted = jnp.dot(
            jnp.broadcast_to(named, (16, 2 * rows)).astype(jnp.bfloat16),
            earlier,
            preferred_element_type=jnp.float32,
        )[:1]
        slot_of = jnp.where(named > 0.0, counted.astype(jnp.int32), -1)
        chosen = slot_of == lax.broadcasted_iota(jnp.int32, (pair_slots, 2 * rows), 0)
        picks.append(chosen.astype(jnp.bfloat16))
        scales.append(jnp.sum(jnp.where(chosen, weights, 0.0), axis=1, keepdims=True))
    picks = jnp.concatenate(picks, axis=0)
    scales = jnp.concatenate(scales, axis=0)
    picks_ref[...] = picks
    for h in range(2):
        cols = pl.ds(pl.multiple_of((own_half if h == 0 else 1 - own_half) * width, width), width)
        for part in range(2):
            own, first, second, both = [ref[pl.ds(part * rows, rows)] for ref in shares]
            if h == 0:
                held = jnp.concatenate([own, jnp.where(core == 1, second, first)], axis=0)
            else:
                held = jnp.concatenate([jnp.where(core == 1, first, second), both], axis=0)
            picked = jnp.dot(picks, held, preferred_element_type=jnp.float32)
            if part == 1:
                picked = scales * picked
            picked = picked.astype(jnp.bfloat16)
            mine_ref[part, :, cols] = picked[:pair_slots]
            theirs_ref[part, :, cols] = picked[pair_slots:]


def expert_kernel(index, chained, mine_ref, theirs_ref, wg_ref, wu_ref, wd_ref, *refs):
    near_ref, far_ref, *kept_refs = refs[5 if chained else 0:][:7]
    act_ref, gt_ref, ut_ref, sems = refs[-4:]
    pair_slots = mine_ref.shape[1]
    slots = 2 * pair_slots

    def kept_move(source, target, part, count, i):
        return pltpu.make_async_copy(
            source, kept_refs[target].at[pl.ds(index * slots + part * pair_slots, count)], sems.at[i]
        )

    moves = [
        kept_move(mine_ref.at[0], 0, 0, pair_slots, 0),
        kept_move(theirs_ref.at[0], 0, 1, pair_slots, 1),
        kept_move(mine_ref.at[1], 1, 0, pair_slots, 2),
        kept_move(theirs_ref.at[1], 1, 1, pair_slots, 3),
        kept_move(act_ref, 2, 0, slots, 4),
        kept_move(gt_ref, 3, 0, slots, 5),
        kept_move(ut_ref, 4, 0, slots, 6),
    ]
    for move in moves[:4]:
        move.start()
    rows_x = jnp.concatenate([mine_ref[0], theirs_ref[0]], axis=0)
    rows_g = jnp.concatenate([mine_ref[1], theirs_ref[1]], axis=0)
    gate = lax.dot_general(rows_x, wg_ref[...], CONTRACT_LAST, preferred_element_type=jnp.float32)
    up = lax.dot_general(rows_x, wu_ref[...], CONTRACT_LAST, preferred_element_type=jnp.float32)
    hidden_grad = lax.dot_general(rows_g, wd_ref[...], CONTRACT_LAST, preferred_element_type=jnp.float32)
    sigma = 1.0 / (1.0 + jnp.exp(-gate))
    silu = gate * sigma
    act_ref[...] = (silu * up).astype(jnp.bfloat16)
    gt_ref[...] = (hidden_grad * up * sigma * (1.0 + gate * (1.0 - sigma))).astype(jnp.bfloat16)
    ut_ref[...] = (hidden_grad * silu).astype(jnp.bfloat16)
    for move in moves[4:]:
        move.start()
    slot = jnp.dot(gt_ref[...], wg_ref[...], preferred_element_type=jnp.float32)
    slot += jnp.dot(ut_ref[...], wu_ref[...], preferred_element_type=jnp.float32)
    far_ref[...] = slot[pair_slots:].astype(jnp.bfloat16)
    near_ref[...] = slot[:pair_slots].astype(jnp.bfloat16)
    for move in moves:
        move.wait()


def place_kernel(place_ref, picks_ref, near_ref, far_ref, keep_ref, send_ref):
    own_half, core = place_ref[1], place_ref[2]
    _, rows, width = keep_ref.shape
    pair_slots = near_ref.shape[0]
    backs = []
    for h in range(2):
        cols = pl.ds(pl.multiple_of((own_half if h == 0 else 1 - own_half) * width, width), width)
        slot = jnp.concatenate([near_ref[:, cols], far_ref[:, cols]], axis=0)
        backs.append(lax.dot_general(picks_ref[...], slot, CONTRACT_FIRST, preferred_element_type=jnp.float32))
    keep_ref[0] = backs[0][:rows]
    keep_ref[1] = jnp.where(core == 1, backs[1][:rows], backs[0][rows:])
    send_ref[0] = jnp.where(core == 1, backs[0][rows:], backs[1][:rows]).astype(jnp.bfloat16)
    send_ref[1] = backs[1][rows:].astype(jnp.bfloat16)


def pick_rows(place, shares, top, rows, pair_slots):
    width = shares[0].shape[1]
    vmem = pl.BlockSpec(memory_space=pltpu.VMEM)
    picked = jax.ShapeDtypeStruct((2, pair_slots, 2 * width), jnp.bfloat16)
    return pl.pallas_call(
        functools.partial(pick_kernel, top, rows),
        in_specs=[pl.BlockSpec(memory_space=pltpu.SMEM)] + [vmem] * 4,
        out_specs=[vmem] * 3,
        out_shape=[picked, picked, jax.ShapeDtypeStruct((2 * pair_slots, 2 * rows), jnp.bfloat16)],
        compiler_params=pltpu.CompilerParams(vmem_limit_bytes=VMEM_LIMIT),
        name="pick",
    )(place, *shares)


def run_experts(index, chunks, mine, theirs, weights, kept):
    _, pair_slots, features = mine.shape
    hidden = weights[0].shape[0]
    slots = 2 * pair_slots
    hbm = pl.BlockSpec(memory_space=pltpu.HBM)
    vmem = pl.BlockSpec(memory_space=pltpu.VMEM)
    part = jax.ShapeDtypeStruct((pair_slots, features), jnp.bfloat16)
    wide = jax.ShapeDtypeStruct((chunks * slots, features), jnp.bfloat16)
    narrow = jax.ShapeDtypeStruct((chunks * slots, hidden), jnp.bfloat16)
    return pl.pallas_call(
        functools.partial(expert_kernel, index, kept is not None),
        in_specs=[vmem] * 5 + [hbm] * (0 if kept is None else 5),
        out_specs=[vmem] * 2 + [hbm] * 5,
        out_shape=[part, part, wide, wide, narrow, narrow, narrow],
        scratch_shapes=[pltpu.VMEM((slots, hidden), jnp.bfloat16)] * 3 + [pltpu.SemaphoreType.DMA((7,))],
        input_output_aliases={} if kept is None else {5 + i: 2 + i for i in range(5)},
        compiler_params=pltpu.CompilerParams(vmem_limit_bytes=VMEM_LIMIT),
        name="experts",
    )(mine, theirs, *weights, *(kept or ()))


def place_rows(place, picks, near, far, rows, width):
    vmem = pl.BlockSpec(memory_space=pltpu.VMEM)
    return pl.pallas_call(
        place_kernel,
        in_specs=[pl.BlockSpec(memory_space=pltpu.SMEM)] + [vmem] * 3,
        out_specs=[vmem] * 2,
        out_shape=[
            jax.ShapeDtypeStruct((2, rows, width), jnp.float32),
            jax.ShapeDtypeStruct((2, rows, width), jnp.bfloat16),
        ],
        compiler_params=pltpu.CompilerParams(vmem_limit_bytes=VMEM_LIMIT),
        name="place",
    )(place, picks, near, far)


def ring_order(length):
    return list(range(0, min(1, length))) + list(range(1, length, 2)) + list(range(2, length, 2))[::-1]


def gather_body(tokens, out_grad, routes, combine, w_gate, w_up, w_down):
    experts = lax.axis_size("expert")
    chunks = experts // 4
    rows, width = tokens.shape
    top = routes.shape[1]
    per_pair = rows * top // experts
    capacity = per_pair + per_pair // 8
    pair_slots = -(-2 * capacity // 16) * 16
    order = ring_order(chunks)
    after = {order[i]: order[(i + 1) % chunks] for i in range(chunks)}
    devices = [(e, h) for e in range(experts) for h in range(2)]

    def permute(value, target):
        pairs = [(e * 2 + h, target(e, h)[0] * 2 + target(e, h)[1]) for e, h in devices]
        return lax.ppermute(value, ("expert", "etp"), pairs)

    def to_ring(value):
        return permute(value, lambda e, h: (after[e // 4] * 4 + e % 4, h))

    def to_core(value):
        return permute(value, lambda e, h: (e ^ 1, h))

    def to_first(value):
        return permute(value, lambda e, h: (e, h ^ 1) if e % 2 else (e ^ 2, h))

    def to_second(value):
        return permute(value, lambda e, h: (e ^ 2, h) if e % 2 else (e, h ^ 1))

    me = lax.axis_index("expert")
    place = jnp.stack([me, lax.axis_index("etp"), me % 2]).astype(jnp.int32)
    share = pack_share(tokens, out_grad, routes, combine)
    weights = (w_gate[0], w_up[0], w_down[0])

    def tied(values, mark):
        return lax.optimization_barrier((values, mark))[0]

    def placed(picks, near, far):
        return place_rows(place, picks, near, to_core(far), rows, width)

    def added(keep, came):
        return keep + came.astype(jnp.float32)

    waves = [
        ([("f", 0), ("a", 0)], ("s", 1)),
        ([("b", 0), ("f", 1)], ("s", 2)),
        ([("a", 1), ("b", 1), ("a", 2)], ("s", 3)),
        ([("a", 3), ("f", 3)], ("f", 2)),
        ([("b", 2), ("b", 3)], None),
    ]
    have = {("s", 0): share}
    kept, picked, parts = None, None, None
    late, last, done = [], [], 0
    for plane, ring in waves:
        came = {}
        for kind, c in plane:
            if c < chunks:
                value = have["f" if kind == "b" else "s", c]
                came[kind, c] = to_first(value) if kind == "f" else to_second(value)
        if ring is not None and ring[1] < chunks:
            came[ring] = to_ring(have[ring[0], ring[1] - 1])
        before, parts = parts, None
        if picked is not None:
            mine, theirs, picks = picked
            near, far, *kept = run_experts(done, chunks, mine, to_core(theirs), weights, kept)
            parts, picked = (picks, near, far), None
            done += 1
        if ring is None:
            have.update(came)
            break
        if all((kind, done) in have for kind in "sfab") and done + 1 < chunks:
            picked = pick_rows(place, [have[kind, done] for kind in "sfab"], top, rows, pair_slots)
        listed = sorted(came, reverse=False)
        values, picked, parts, weights = lax.optimization_barrier(
            ([came[key] for key in listed], picked, parts, weights)
        )
        have.update(zip(listed, values))
    mark = []
    if before is not None:
        keep, send = placed(*before)
        late.append((keep, to_second(send)))
        mark.append(send)
    if parts is not None:
        mark.append(parts[1])
    while done < chunks:
        shares = tied([have[kind, done] for kind in "sfab"], mark)
        mine, theirs, picks = pick_rows(place, shares, top, rows, pair_slots)
        if parts is not None:
            keep, send = placed(*parts)
            late.append((keep, to_second(send)))
            mine, parts = tied(mine, send), None
        near, far, *kept = run_experts(done, chunks, mine, to_core(theirs), weights, kept)
        last.append((picks, near, far))
        done += 1
    nears = [near for _, near, _ in last]
    near, send = nears[-1], nears[0]
    for picks, first, far in last:
        keep, send = placed(picks, tied(first, send), far)
        late.append((keep, to_second(send)))
    ties = [nears[0], send]
    marks = [send] * (chunks + 2)
    running = None
    for c in range(1, chunks):
        keep, came = late[c]
        if c + 1 < chunks:
            came = tied(came, ties[c - 1])
        pair = added(keep, came)
        came = to_first(pair[1].astype(jnp.bfloat16))
        total = added(pair[0], tied(came, send) if c == 1 else came)
        running = (total if running is None else added(total, running)).astype(jnp.bfloat16)
        if c > 1:
            marks[min(c - 1, 2)] = running
        if c + 1 < chunks:
            running = to_ring(running)
    keep, came = late[0]
    pair = added(keep, tied(came, send))
    came = pair[1].astype(jnp.bfloat16)
    own = added(pair[0], to_first(came if running is None else tied(came, running)))
    grad_tokens = (own if running is None else added(own, to_ring(running))).astype(jnp.bfloat16)
    rows_x, rows_g, acts, gate_term, up_term = kept
    acts, gate_term, up_term = tied(acts, marks[0]), tied(gate_term, marks[1]), tied(up_term, marks[2])
    grad_down = lax.dot_general(acts, rows_g, CONTRACT_FIRST, preferred_element_type=jnp.float32)
    grad_gate = lax.dot_general(gate_term, rows_x, CONTRACT_FIRST, preferred_element_type=jnp.float32)
    grad_up = lax.dot_general(up_term, rows_x, CONTRACT_FIRST, preferred_element_type=jnp.float32)
    return (
        grad_tokens,
        grad_gate.astype(jnp.bfloat16)[None],
        grad_up.astype(jnp.bfloat16)[None],
        grad_down.astype(jnp.bfloat16)[None],
    )


def solution(mesh):
    experts = mesh.shape["expert"]

    def body(tokens, out_grad, routes, combine, w_gate, w_up, w_down):
        rows, width = tokens.shape
        top = routes.shape[1]
        gathers = top * 4 >= experts and experts % 4 == 0 and experts <= 16 and mesh.shape["etp"] == 2
        run = gather_body if gathers and top * rows <= width else exchange_body
        return run(tokens, out_grad, routes, combine, w_gate, w_up, w_down)

    placed = (
        P("expert", "etp"),
        P("expert", "etp"),
        P("expert", None),
        P("expert", None),
        P("expert", "etp", None),
        P("expert", "etp", None),
        P("expert", "etp", None),
    )
    return jax.shard_map(
        body,
        mesh=mesh,
        in_specs=placed,
        out_specs=(
            P("expert", "etp"),
            P("expert", "etp", None),
            P("expert", "etp", None),
            P("expert", "etp", None),
        ),
        check_vma=False,
    )
```

```python
import functools

import jax
import jax.numpy as jnp
from jax import lax
from jax.experimental import pallas as pl
from jax.experimental.pallas import tpu as pltpu
from jax.sharding import PartitionSpec as P

CONTRACT_LAST = (((1,), (1,)), ((), ()))
CONTRACT_FIRST = (((0,), (0,)), ((), ()))
INFO_ROWS = 16
VMEM_LIMIT = 16 * 1024 * 1024


def pack_rows(token_rows, grad_rows, token_of, scale, is_live):
    mask = is_live[:, None].astype(token_rows.dtype)
    inputs_sent = token_rows[token_of] * mask
    grads_sent = (scale[:, None] * grad_rows[token_of].astype(jnp.float32)).astype(jnp.bfloat16)
    return (inputs_sent, grads_sent)


def pair_positions(routed_flat, experts):
    pair_total = routed_flat.shape[0]
    span = 128
    groups = pair_total // span
    labels = jnp.arange(experts, dtype=jnp.int32)
    one_hot = (routed_flat[:, None] == labels[None, :]).astype(jnp.bfloat16)
    grouped = one_hot.reshape(groups, span, experts)
    row_ids = jnp.arange(span, dtype=jnp.int32)
    lower = (row_ids[None, :] < row_ids[:, None]).astype(jnp.bfloat16)
    within = jnp.einsum("ij,bje->bie", lower, grouped, preferred_element_type=jnp.float32)
    group_sums = jnp.sum(grouped.astype(jnp.float32), axis=1)
    group_before = jnp.cumsum(group_sums, axis=0) - group_sums
    earlier = within + group_before[:, None, :]
    counted = jnp.sum(earlier * grouped.astype(jnp.float32), axis=2)
    return counted.reshape(pair_total).astype(jnp.int32)


def exchange_body(tokens, out_grad, routes, combine, w_gate, w_up, w_down):
    experts = lax.axis_size("expert")
    tok_rows = tokens.shape[0]
    col_width = tokens.shape[1]
    choose_count = routes.shape[1]
    per_pair = tok_rows * choose_count // experts
    capacity = per_pair + per_pair // 8
    routed_flat = routes.reshape(-1)
    pair_total = routed_flat.shape[0]
    position = pair_positions(routed_flat, experts)
    target = routed_flat * capacity + position
    anchor = jnp.full((experts * capacity,), pair_total, jnp.int32)
    anchor = anchor.at[target].set(jnp.arange(pair_total, dtype=jnp.int32))
    is_live = anchor < pair_total
    safe_anchor = jnp.minimum(anchor, pair_total - 1)
    token_of = safe_anchor // choose_count
    scale = combine.reshape(-1)[safe_anchor] * is_live.astype(jnp.float32)
    full_tokens, full_grads = (
        lax.all_gather(tokens, "etp", axis=1, tiled=True),
        lax.all_gather(out_grad, "etp", axis=1, tiled=True),
    )
    inputs_sent, grads_sent = pack_rows(full_tokens, full_grads, token_of, scale, is_live)
    rows_x, rows_g = (
        lax.all_to_all(inputs_sent, "expert", split_axis=0, concat_axis=0, tiled=True),
        lax.all_to_all(grads_sent, "expert", split_axis=0, concat_axis=0, tiled=True),
    )
    gate_w = w_gate[0]
    up_w = w_up[0]
    down_w = w_down[0]
    gate = lax.dot_general(rows_x, gate_w, CONTRACT_LAST, preferred_element_type=jnp.float32)
    up = lax.dot_general(rows_x, up_w, CONTRACT_LAST, preferred_element_type=jnp.float32)
    hidden_grad = lax.dot_general(rows_g, down_w, CONTRACT_LAST, preferred_element_type=jnp.float32)
    sigma = jax.nn.sigmoid(gate)
    silu = gate * sigma
    acts = (silu * up).astype(jnp.bfloat16)
    grad_down = lax.dot_general(acts, rows_g, CONTRACT_FIRST, preferred_element_type=jnp.float32)
    gate_term = (hidden_grad * up * sigma * (1.0 + gate * (1.0 - sigma))).astype(jnp.bfloat16)
    up_term = (hidden_grad * silu).astype(jnp.bfloat16)
    grad_gate = lax.dot_general(
        gate_term, rows_x, CONTRACT_FIRST, preferred_element_type=jnp.float32
    )
    grad_up = lax.dot_general(up_term, rows_x, CONTRACT_FIRST, preferred_element_type=jnp.float32)
    swapped_gate, swapped_up = (
        lax.all_to_all(gate_w, "etp", split_axis=1, concat_axis=0, tiled=True),
        lax.all_to_all(up_w, "etp", split_axis=1, concat_axis=0, tiled=True),
    )
    running = jnp.dot(
        lax.all_gather(gate_term, "etp", axis=1, tiled=True),
        swapped_gate,
        preferred_element_type=jnp.float32,
    )
    slot_grads = running + jnp.dot(
        lax.all_gather(up_term, "etp", axis=1, tiled=True),
        swapped_up,
        preferred_element_type=jnp.float32,
    )
    slot_grads = slot_grads.astype(jnp.bfloat16)
    returned = lax.all_to_all(slot_grads, "expert", split_axis=0, concat_axis=0, tiled=True)
    picked = returned[target].astype(jnp.float32).reshape(tok_rows, choose_count, col_width)
    grad_tokens = jnp.sum(picked, axis=1).astype(jnp.bfloat16)
    return (
        grad_tokens,
        grad_gate.astype(jnp.bfloat16)[None],
        grad_up.astype(jnp.bfloat16)[None],
        grad_down.astype(jnp.bfloat16)[None],
    )


def pack_kernel(tokens_ref, grads_ref, routes_ref, combine_ref, out_ref):
    rows = tokens_ref.shape[0]
    out_ref[:rows] = tokens_ref[...]
    out_ref[rows:2 * rows] = grads_ref[...]
    top = routes_ref.shape[0]
    routes = routes_ref[...].astype(jnp.float32)
    weights = combine_ref[...]
    high = weights.astype(jnp.bfloat16).astype(jnp.float32)
    middle = (weights - high).astype(jnp.bfloat16).astype(jnp.float32)
    low = weights - high - middle
    blank = jnp.zeros((INFO_ROWS - 4, rows), jnp.float32)
    for k in range(top):
        own = slice(k, k + 1)
        column = jnp.concatenate([routes[own], high[own], middle[own], low[own], blank], axis=0)
        out_ref[2 * rows:, k * rows:(k + 1) * rows] = column.astype(jnp.bfloat16)


def pack_share(tokens, out_grad, routes, combine):
    rows, width = tokens.shape
    vmem = pl.BlockSpec(memory_space=pltpu.VMEM)
    return pl.pallas_call(
        pack_kernel,
        in_specs=[vmem] * 4,
        out_specs=vmem,
        out_shape=jax.ShapeDtypeStruct((2 * rows + INFO_ROWS, width), jnp.bfloat16),
        name="pack",
    )(tokens, out_grad, routes.T, combine.T)


def pick_kernel(top, rows, place_ref, *refs):
    shares, (mine_ref, theirs_ref, picks_ref) = refs[:4], refs[4:]
    me, own_half, core = place_ref[0], place_ref[1], place_ref[2]
    pair_slots, width = mine_ref.shape[1], shares[0].shape[1]
    earlier = (
        lax.broadcasted_iota(jnp.int32, (2 * rows, 2 * rows), 0)
        < lax.broadcasted_iota(jnp.int32, (2 * rows, 2 * rows), 1)
    ).astype(jnp.bfloat16)
    infos = [
        [share_ref[pl.ds(2 * rows, INFO_ROWS), k * rows:(k + 1) * rows].astype(jnp.float32) for k in range(top)]
        for share_ref in (shares[0], shares[3])
    ]
    picks, scales = [], []
    for expert in (me, me + 1 - 2 * core):
        named, weights = [], []
        for block in infos:
            hits, weight = 0.0, 0.0
            for info in block:
                hit = info[0:1] == expert.astype(jnp.float32)
                hits += hit.astype(jnp.float32)
                weight += jnp.where(hit, info[1:2] + info[2:3] + info[3:4], 0.0)
            named.append(hits)
            weights.append(weight)
        named = jnp.concatenate(named, axis=1)
        weights = jnp.concatenate(weights, axis=1)
        counted = jnp.dot(
            jnp.broadcast_to(named, (16, 2 * rows)).astype(jnp.bfloat16),
            earlier,
            preferred_element_type=jnp.float32,
        )[:1]
        slot_of = jnp.where(named > 0.0, counted.astype(jnp.int32), -1)
        chosen = slot_of == lax.broadcasted_iota(jnp.int32, (pair_slots, 2 * rows), 0)
        picks.append(chosen.astype(jnp.bfloat16))
        scales.append(jnp.sum(jnp.where(chosen, weights, 0.0), axis=1, keepdims=True))
    picks = jnp.concatenate(picks, axis=0)
    scales = jnp.concatenate(scales, axis=0)
    picks_ref[...] = picks
    for h in range(2):
        cols = pl.ds(pl.multiple_of((own_half if h == 0 else 1 - own_half) * width, width), width)
        for part in range(2):
            own, first, second, both = [ref[pl.ds(part * rows, rows)] for ref in shares]
            if h == 0:
                held = jnp.concatenate([own, jnp.where(core == 1, second, first)], axis=0)
            else:
                held = jnp.concatenate([jnp.where(core == 1, first, second), both], axis=0)
            picked = jnp.dot(picks, held, preferred_element_type=jnp.float32)
            if part == 1:
                picked = scales * picked
            picked = picked.astype(jnp.bfloat16)
            mine_ref[part, :, cols] = picked[:pair_slots]
            theirs_ref[part, :, cols] = picked[pair_slots:]


def expert_kernel(index, chained, mine_ref, theirs_ref, wg_ref, wu_ref, wd_ref, *refs):
    near_ref, far_ref, *kept_refs = refs[5 if chained else 0:][:7]
    act_ref, gt_ref, ut_ref, sems = refs[-4:]
    pair_slots = mine_ref.shape[1]
    slots = 2 * pair_slots

    def kept_move(source, target, part, count, i):
        return pltpu.make_async_copy(
            source, kept_refs[target].at[pl.ds(index * slots + part * pair_slots, count)], sems.at[i]
        )

    moves = [
        kept_move(mine_ref.at[0], 0, 0, pair_slots, 0),
        kept_move(theirs_ref.at[0], 0, 1, pair_slots, 1),
        kept_move(mine_ref.at[1], 1, 0, pair_slots, 2),
        kept_move(theirs_ref.at[1], 1, 1, pair_slots, 3),
        kept_move(act_ref, 2, 0, slots, 4),
        kept_move(gt_ref, 3, 0, slots, 5),
        kept_move(ut_ref, 4, 0, slots, 6),
    ]
    for move in moves[:4]:
        move.start()
    rows_x = jnp.concatenate([mine_ref[0], theirs_ref[0]], axis=0)
    rows_g = jnp.concatenate([mine_ref[1], theirs_ref[1]], axis=0)
    gate = lax.dot_general(rows_x, wg_ref[...], CONTRACT_LAST, preferred_element_type=jnp.float32)
    up = lax.dot_general(rows_x, wu_ref[...], CONTRACT_LAST, preferred_element_type=jnp.float32)
    hidden_grad = lax.dot_general(rows_g, wd_ref[...], CONTRACT_LAST, preferred_element_type=jnp.float32)
    sigma = 1.0 / (1.0 + jnp.exp(-gate))
    silu = gate * sigma
    act_ref[...] = (silu * up).astype(jnp.bfloat16)
    gt_ref[...] = (hidden_grad * up * sigma * (1.0 + gate * (1.0 - sigma))).astype(jnp.bfloat16)
    ut_ref[...] = (hidden_grad * silu).astype(jnp.bfloat16)
    for move in moves[4:]:
        move.start()
    slot = jnp.dot(gt_ref[...], wg_ref[...], preferred_element_type=jnp.float32)
    slot += jnp.dot(ut_ref[...], wu_ref[...], preferred_element_type=jnp.float32)
    far_ref[...] = slot[pair_slots:].astype(jnp.bfloat16)
    near_ref[...] = slot[:pair_slots].astype(jnp.bfloat16)
    for move in moves:
        move.wait()


def place_kernel(place_ref, picks_ref, near_ref, far_ref, keep_ref, send_ref):
    own_half, core = place_ref[1], place_ref[2]
    _, rows, width = keep_ref.shape
    pair_slots = near_ref.shape[0]
    backs = []
    for h in range(2):
        cols = pl.ds(pl.multiple_of((own_half if h == 0 else 1 - own_half) * width, width), width)
        slot = jnp.concatenate([near_ref[:, cols], far_ref[:, cols]], axis=0)
        backs.append(lax.dot_general(picks_ref[...], slot, CONTRACT_FIRST, preferred_element_type=jnp.float32))
    keep_ref[0] = backs[0][:rows]
    keep_ref[1] = jnp.where(core == 1, backs[1][:rows], backs[0][rows:])
    send_ref[0] = jnp.where(core == 1, backs[0][rows:], backs[1][:rows]).astype(jnp.bfloat16)
    send_ref[1] = backs[1][rows:].astype(jnp.bfloat16)


def pick_rows(place, shares, top, rows, pair_slots):
    width = shares[0].shape[1]
    vmem = pl.BlockSpec(memory_space=pltpu.VMEM)
    picked = jax.ShapeDtypeStruct((2, pair_slots, 2 * width), jnp.bfloat16)
    return pl.pallas_call(
        functools.partial(pick_kernel, top, rows),
        in_specs=[pl.BlockSpec(memory_space=pltpu.SMEM)] + [vmem] * 4,
        out_specs=[vmem] * 3,
        out_shape=[picked, picked, jax.ShapeDtypeStruct((2 * pair_slots, 2 * rows), jnp.bfloat16)],
        compiler_params=pltpu.CompilerParams(vmem_limit_bytes=VMEM_LIMIT),
        name="pick",
    )(place, *shares)


def run_experts(index, chunks, mine, theirs, weights, kept):
    _, pair_slots, features = mine.shape
    hidden = weights[0].shape[0]
    slots = 2 * pair_slots
    hbm = pl.BlockSpec(memory_space=pltpu.HBM)
    vmem = pl.BlockSpec(memory_space=pltpu.VMEM)
    part = jax.ShapeDtypeStruct((pair_slots, features), jnp.bfloat16)
    wide = jax.ShapeDtypeStruct((chunks * slots, features), jnp.bfloat16)
    narrow = jax.ShapeDtypeStruct((chunks * slots, hidden), jnp.bfloat16)
    return pl.pallas_call(
        functools.partial(expert_kernel, index, kept is not None),
        in_specs=[vmem] * 5 + [hbm] * (0 if kept is None else 5),
        out_specs=[vmem] * 2 + [hbm] * 5,
        out_shape=[part, part, wide, wide, narrow, narrow, narrow],
        scratch_shapes=[pltpu.VMEM((slots, hidden), jnp.bfloat16)] * 3 + [pltpu.SemaphoreType.DMA((7,))],
        input_output_aliases={} if kept is None else {5 + i: 2 + i for i in range(5)},
        compiler_params=pltpu.CompilerParams(vmem_limit_bytes=VMEM_LIMIT),
        name="experts",
    )(mine, theirs, *weights, *(kept or ()))


def place_rows(place, picks, near, far, rows, width):
    vmem = pl.BlockSpec(memory_space=pltpu.VMEM)
    return pl.pallas_call(
        place_kernel,
        in_specs=[pl.BlockSpec(memory_space=pltpu.SMEM)] + [vmem] * 3,
        out_specs=[vmem] * 2,
        out_shape=[
            jax.ShapeDtypeStruct((2, rows, width), jnp.float32),
            jax.ShapeDtypeStruct((2, rows, width), jnp.bfloat16),
        ],
        compiler_params=pltpu.CompilerParams(vmem_limit_bytes=VMEM_LIMIT),
        name="place",
    )(place, picks, near, far)


def ring_order(length):
    return list(range(0, min(1, length))) + list(range(1, length, 2)) + list(range(2, length, 2))[::-1]


def gather_body(tokens, out_grad, routes, combine, w_gate, w_up, w_down):
    experts = lax.axis_size("expert")
    chunks = experts // 4
    rows, width = tokens.shape
    top = routes.shape[1]
    per_pair = rows * top // experts
    capacity = per_pair + per_pair // 8
    pair_slots = -(-2 * capacity // 16) * 16
    order = ring_order(chunks)
    after = {order[i]: order[(i + 1) % chunks] for i in range(chunks)}
    devices = [(e, h) for e in range(experts) for h in range(2)]

    def permute(value, target):
        pairs = [(e * 2 + h, target(e, h)[0] * 2 + target(e, h)[1]) for e, h in devices]
        return lax.ppermute(value, ("expert", "etp"), pairs)

    def to_ring(value):
        return permute(value, lambda e, h: (after[e // 4] * 4 + e % 4, h))

    def to_core(value):
        return permute(value, lambda e, h: (e ^ 1, h))

    def to_first(value):
        return permute(value, lambda e, h: (e, h ^ 1) if e % 2 else (e ^ 2, h))

    def to_second(value):
        return permute(value, lambda e, h: (e ^ 2, h) if e % 2 else (e, h ^ 1))

    me = lax.axis_index("expert")
    place = jnp.stack([me, lax.axis_index("etp"), me % 2]).astype(jnp.int32)
    share = pack_share(tokens, out_grad, routes, combine)
    weights = (w_gate[0], w_up[0], w_down[0])

    def tied(values, mark):
        return lax.optimization_barrier((values, mark))[0]

    def placed(picks, near, far):
        return place_rows(place, picks, near, to_core(far), rows, width)

    def added(keep, came):
        return keep + came.astype(jnp.float32)

    waves = [
        ([("f", 0), ("a", 0)], ("s", 1)),
        ([("b", 0), ("f", 1)], ("s", 2)),
        ([("a", 1), ("b", 1), ("a", 2)], ("s", 3)),
        ([("a", 3), ("f", 3)], ("f", 2)),
        ([("b", 2), ("b", 3)], None),
    ]
    have = {("s", 0): share}
    kept, picked, parts = None, None, None
    late, last, done = [], [], 0
    for plane, ring in waves:
        came = {}
        for kind, c in plane:
            if c < chunks:
                value = have["f" if kind == "b" else "s", c]
                came[kind, c] = to_first(value) if kind == "f" else to_second(value)
        if ring is not None and ring[1] < chunks:
            came[ring] = to_ring(have[ring[0], ring[1] - 1])
        before, parts = parts, None
        if picked is not None:
            mine, theirs, picks = picked
            near, far, *kept = run_experts(done, chunks, mine, to_core(theirs), weights, kept)
            parts, picked = (picks, near, far), None
            done += 1
        if ring is None:
            have.update(came)
            break
        if all((kind, done) in have for kind in "sfab") and done + 1 < chunks:
            picked = pick_rows(place, [have[kind, done] for kind in "sfab"], top, rows, pair_slots)
        listed = sorted(came, reverse=False)
        values, picked, parts, weights = lax.optimization_barrier(
            ([came[key] for key in listed], picked, parts, weights)
        )
        have.update(zip(listed, values))
    mark = []
    if before is not None:
        keep, send = placed(*before)
        late.append((keep, to_second(send)))
        mark.append(send)
    if parts is not None:
        mark.append(parts[1])
    crossed = None
    if parts is not None:
        picks, near, far = parts
        crossed = to_core(far)
    while done < chunks:
        shares = tied([have[kind, done] for kind in "sfab"], mark)
        rows_of = pick_rows(place, shares, top, rows, pair_slots)
        last.append(rows_of)
        mark = [crossed]
        done += 1
    if crossed is not None:
        keep, send = place_rows(place, picks, near, crossed, rows, width)
        late.append((keep, to_second(send)))
    done -= len(last)
    for i, (mine, theirs, picks) in enumerate(last):
        mine = tied(mine, send) if i == 0 else mine
        near, far, *kept = run_experts(done, chunks, mine, to_core(theirs), weights, kept)
        last[i] = picks, near, far
        done += 1
    nears = [near for _, near, _ in last]
    near, send = nears[-1], nears[0]
    for picks, first, far in last:
        keep, send = placed(picks, tied(first, send), far)
        late.append((keep, to_second(send)))
    ties = [nears[0], send]
    marks = [send] * (chunks + 2)
    running = None
    for c in range(1, chunks):
        keep, came = late[c]
        came = tied(came, ties[c - 1] if c + 1 < chunks else previous)
        pair = added(keep, came)
        came = to_first(pair[1].astype(jnp.bfloat16))
        total = added(pair[0], tied(came, send) if c == 1 else came)
        running = (total if running is None else added(total, running)).astype(jnp.bfloat16)
        previous = running
        if c > 1:
            marks[min(c - 1, 2)] = running
        if c + 1 < chunks:
            running = to_ring(running)
    keep, came = late[0]
    pair = added(keep, tied(came, send))
    came = pair[1].astype(jnp.bfloat16)
    own = added(pair[0], to_first(came if running is None else tied(came, running)))
    grad_tokens = (own if running is None else added(own, to_ring(running))).astype(jnp.bfloat16)
    rows_x, rows_g, acts, gate_term, up_term = kept
    acts, gate_term, up_term = tied(acts, marks[0]), tied(gate_term, marks[1]), tied(up_term, marks[2])
    grad_down = lax.dot_general(acts, rows_g, CONTRACT_FIRST, preferred_element_type=jnp.float32)
    grad_gate = lax.dot_general(gate_term, rows_x, CONTRACT_FIRST, preferred_element_type=jnp.float32)
    grad_up = lax.dot_general(up_term, rows_x, CONTRACT_FIRST, preferred_element_type=jnp.float32)
    return (
        grad_tokens,
        grad_gate.astype(jnp.bfloat16)[None],
        grad_up.astype(jnp.bfloat16)[None],
        grad_down.astype(jnp.bfloat16)[None],
    )


def solution(mesh):
    experts = mesh.shape["expert"]

    def body(tokens, out_grad, routes, combine, w_gate, w_up, w_down):
        rows, width = tokens.shape
        top = routes.shape[1]
        gathers = top * 4 >= experts and experts % 4 == 0 and experts <= 16 and mesh.shape["etp"] == 2
        run = gather_body if gathers and top * rows <= width else exchange_body
        return run(tokens, out_grad, routes, combine, w_gate, w_up, w_down)

    placed = (
        P("expert", "etp"),
        P("expert", "etp"),
        P("expert", None),
        P("expert", None),
        P("expert", "etp", None),
        P("expert", "etp", None),
        P("expert", "etp", None),
    )
    return jax.shard_map(
        body,
        mesh=mesh,
        in_specs=placed,
        out_specs=(
            P("expert", "etp"),
            P("expert", "etp", None),
            P("expert", "etp", None),
            P("expert", "etp", None),
        ),
        check_vma=False,
    )
```

```python
import functools

import jax
import jax.numpy as jnp
from jax import lax
from jax.experimental import pallas as pl
from jax.experimental.pallas import tpu as pltpu
from jax.sharding import PartitionSpec as P

CONTRACT_LAST = (((1,), (1,)), ((), ()))
CONTRACT_FIRST = (((0,), (0,)), ((), ()))
INFO_ROWS = 16
VMEM_LIMIT = 16 * 1024 * 1024


def pack_rows(token_rows, grad_rows, token_of, scale, is_live):
    mask = is_live[:, None].astype(token_rows.dtype)
    inputs_sent = token_rows[token_of] * mask
    grads_sent = (scale[:, None] * grad_rows[token_of].astype(jnp.float32)).astype(jnp.bfloat16)
    return (inputs_sent, grads_sent)


def pair_positions(routed_flat, experts):
    pair_total = routed_flat.shape[0]
    span = 128
    groups = pair_total // span
    labels = jnp.arange(experts, dtype=jnp.int32)
    one_hot = (routed_flat[:, None] == labels[None, :]).astype(jnp.bfloat16)
    grouped = one_hot.reshape(groups, span, experts)
    row_ids = jnp.arange(span, dtype=jnp.int32)
    lower = (row_ids[None, :] < row_ids[:, None]).astype(jnp.bfloat16)
    within = jnp.einsum("ij,bje->bie", lower, grouped, preferred_element_type=jnp.float32)
    group_sums = jnp.sum(grouped.astype(jnp.float32), axis=1)
    group_before = jnp.cumsum(group_sums, axis=0) - group_sums
    earlier = within + group_before[:, None, :]
    counted = jnp.sum(earlier * grouped.astype(jnp.float32), axis=2)
    return counted.reshape(pair_total).astype(jnp.int32)


def exchange_body(tokens, out_grad, routes, combine, w_gate, w_up, w_down):
    experts = lax.axis_size("expert")
    tok_rows = tokens.shape[0]
    col_width = tokens.shape[1]
    choose_count = routes.shape[1]
    per_pair = tok_rows * choose_count // experts
    capacity = per_pair + per_pair // 8
    routed_flat = routes.reshape(-1)
    pair_total = routed_flat.shape[0]
    position = pair_positions(routed_flat, experts)
    target = routed_flat * capacity + position
    anchor = jnp.full((experts * capacity,), pair_total, jnp.int32)
    anchor = anchor.at[target].set(jnp.arange(pair_total, dtype=jnp.int32))
    is_live = anchor < pair_total
    safe_anchor = jnp.minimum(anchor, pair_total - 1)
    token_of = safe_anchor // choose_count
    scale = combine.reshape(-1)[safe_anchor] * is_live.astype(jnp.float32)
    full_tokens, full_grads = (
        lax.all_gather(tokens, "etp", axis=1, tiled=True),
        lax.all_gather(out_grad, "etp", axis=1, tiled=True),
    )
    inputs_sent, grads_sent = pack_rows(full_tokens, full_grads, token_of, scale, is_live)
    rows_x, rows_g = (
        lax.all_to_all(inputs_sent, "expert", split_axis=0, concat_axis=0, tiled=True),
        lax.all_to_all(grads_sent, "expert", split_axis=0, concat_axis=0, tiled=True),
    )
    gate_w = w_gate[0]
    up_w = w_up[0]
    down_w = w_down[0]
    gate = lax.dot_general(rows_x, gate_w, CONTRACT_LAST, preferred_element_type=jnp.float32)
    up = lax.dot_general(rows_x, up_w, CONTRACT_LAST, preferred_element_type=jnp.float32)
    hidden_grad = lax.dot_general(rows_g, down_w, CONTRACT_LAST, preferred_element_type=jnp.float32)
    sigma = jax.nn.sigmoid(gate)
    silu = gate * sigma
    acts = (silu * up).astype(jnp.bfloat16)
    grad_down = lax.dot_general(acts, rows_g, CONTRACT_FIRST, preferred_element_type=jnp.float32)
    gate_term = (hidden_grad * up * sigma * (1.0 + gate * (1.0 - sigma))).astype(jnp.bfloat16)
    up_term = (hidden_grad * silu).astype(jnp.bfloat16)
    grad_gate = lax.dot_general(
        gate_term, rows_x, CONTRACT_FIRST, preferred_element_type=jnp.float32
    )
    grad_up = lax.dot_general(up_term, rows_x, CONTRACT_FIRST, preferred_element_type=jnp.float32)
    swapped_gate, swapped_up = (
        lax.all_to_all(gate_w, "etp", split_axis=1, concat_axis=0, tiled=True),
        lax.all_to_all(up_w, "etp", split_axis=1, concat_axis=0, tiled=True),
    )
    running = jnp.dot(
        lax.all_gather(gate_term, "etp", axis=1, tiled=True),
        swapped_gate,
        preferred_element_type=jnp.float32,
    )
    slot_grads = running + jnp.dot(
        lax.all_gather(up_term, "etp", axis=1, tiled=True),
        swapped_up,
        preferred_element_type=jnp.float32,
    )
    slot_grads = slot_grads.astype(jnp.bfloat16)
    returned = lax.all_to_all(slot_grads, "expert", split_axis=0, concat_axis=0, tiled=True)
    picked = returned[target].astype(jnp.float32).reshape(tok_rows, choose_count, col_width)
    grad_tokens = jnp.sum(picked, axis=1).astype(jnp.bfloat16)
    return (
        grad_tokens,
        grad_gate.astype(jnp.bfloat16)[None],
        grad_up.astype(jnp.bfloat16)[None],
        grad_down.astype(jnp.bfloat16)[None],
    )


def pack_kernel(tokens_ref, grads_ref, routes_ref, combine_ref, out_ref):
    rows = tokens_ref.shape[0]
    out_ref[:rows] = tokens_ref[...]
    out_ref[rows:2 * rows] = grads_ref[...]
    top = routes_ref.shape[0]
    routes = routes_ref[...].astype(jnp.float32)
    weights = combine_ref[...]
    high = weights.astype(jnp.bfloat16).astype(jnp.float32)
    middle = (weights - high).astype(jnp.bfloat16).astype(jnp.float32)
    low = weights - high - middle
    blank = jnp.zeros((INFO_ROWS - 4, rows), jnp.float32)
    for k in range(top):
        own = slice(k, k + 1)
        column = jnp.concatenate([routes[own], high[own], middle[own], low[own], blank], axis=0)
        out_ref[2 * rows:, k * rows:(k + 1) * rows] = column.astype(jnp.bfloat16)


def pack_share(tokens, out_grad, routes, combine):
    rows, width = tokens.shape
    vmem = pl.BlockSpec(memory_space=pltpu.VMEM)
    return pl.pallas_call(
        pack_kernel,
        in_specs=[vmem] * 4,
        out_specs=vmem,
        out_shape=jax.ShapeDtypeStruct((2 * rows + INFO_ROWS, width), jnp.bfloat16),
        name="pack",
    )(tokens, out_grad, routes.T, combine.T)


def pick_kernel(top, rows, place_ref, *refs):
    shares, (mine_ref, theirs_ref, picks_ref) = refs[:4], refs[4:]
    me, own_half, core = place_ref[0], place_ref[1], place_ref[2]
    pair_slots, width = mine_ref.shape[1], shares[0].shape[1]
    earlier = (
        lax.broadcasted_iota(jnp.int32, (2 * rows, 2 * rows), 0)
        < lax.broadcasted_iota(jnp.int32, (2 * rows, 2 * rows), 1)
    ).astype(jnp.bfloat16)
    infos = [
        [share_ref[pl.ds(2 * rows, INFO_ROWS), k * rows:(k + 1) * rows].astype(jnp.float32) for k in range(top)]
        for share_ref in (shares[0], shares[3])
    ]
    picks, scales = [], []
    for expert in (me, me + 1 - 2 * core):
        named, weights = [], []
        for block in infos:
            hits, weight = 0.0, 0.0
            for info in block:
                hit = info[0:1] == expert.astype(jnp.float32)
                hits += hit.astype(jnp.float32)
                weight += jnp.where(hit, info[1:2] + info[2:3] + info[3:4], 0.0)
            named.append(hits)
            weights.append(weight)
        named = jnp.concatenate(named, axis=1)
        weights = jnp.concatenate(weights, axis=1)
        counted = jnp.dot(
            jnp.broadcast_to(named, (16, 2 * rows)).astype(jnp.bfloat16),
            earlier,
            preferred_element_type=jnp.float32,
        )[:1]
        slot_of = jnp.where(named > 0.0, counted.astype(jnp.int32), -1)
        chosen = slot_of == lax.broadcasted_iota(jnp.int32, (pair_slots, 2 * rows), 0)
        picks.append(chosen.astype(jnp.bfloat16))
        scales.append(jnp.sum(jnp.where(chosen, weights, 0.0), axis=1, keepdims=True))
    picks = jnp.concatenate(picks, axis=0)
    scales = jnp.concatenate(scales, axis=0)
    picks_ref[...] = picks
    for h in range(2):
        cols = pl.ds(pl.multiple_of((own_half if h == 0 else 1 - own_half) * width, width), width)
        for part in range(2):
            own, first, second, both = [ref[pl.ds(part * rows, rows)] for ref in shares]
            if h == 0:
                held = jnp.concatenate([own, jnp.where(core == 1, second, first)], axis=0)
            else:
                held = jnp.concatenate([jnp.where(core == 1, first, second), both], axis=0)
            picked = jnp.dot(picks, held, preferred_element_type=jnp.float32)
            if part == 1:
                picked = scales * picked
            picked = picked.astype(jnp.bfloat16)
            mine_ref[part, :, cols] = picked[:pair_slots]
            theirs_ref[part, :, cols] = picked[pair_slots:]


def expert_kernel(index, chained, mine_ref, theirs_ref, wg_ref, wu_ref, wd_ref, *refs):
    near_ref, far_ref, *kept_refs = refs[5 if chained else 0:][:7]
    act_ref, gt_ref, ut_ref, sems = refs[-4:]
    pair_slots = mine_ref.shape[1]
    slots = 2 * pair_slots

    def kept_move(source, target, part, count, i):
        return pltpu.make_async_copy(
            source, kept_refs[target].at[pl.ds(index * slots + part * pair_slots, count)], sems.at[i]
        )

    moves = [
        kept_move(mine_ref.at[0], 0, 0, pair_slots, 0),
        kept_move(theirs_ref.at[0], 0, 1, pair_slots, 1),
        kept_move(mine_ref.at[1], 1, 0, pair_slots, 2),
        kept_move(theirs_ref.at[1], 1, 1, pair_slots, 3),
        kept_move(act_ref, 2, 0, slots, 4),
        kept_move(gt_ref, 3, 0, slots, 5),
        kept_move(ut_ref, 4, 0, slots, 6),
    ]
    for move in moves[:4]:
        move.start()
    rows_x = jnp.concatenate([mine_ref[0], theirs_ref[0]], axis=0)
    rows_g = jnp.concatenate([mine_ref[1], theirs_ref[1]], axis=0)
    gate = lax.dot_general(rows_x, wg_ref[...], CONTRACT_LAST, preferred_element_type=jnp.float32)
    up = lax.dot_general(rows_x, wu_ref[...], CONTRACT_LAST, preferred_element_type=jnp.float32)
    hidden_grad = lax.dot_general(rows_g, wd_ref[...], CONTRACT_LAST, preferred_element_type=jnp.float32)
    sigma = 1.0 / (1.0 + jnp.exp(-gate))
    silu = gate * sigma
    act_ref[...] = (silu * up).astype(jnp.bfloat16)
    gt_ref[...] = (hidden_grad * up * sigma * (1.0 + gate * (1.0 - sigma))).astype(jnp.bfloat16)
    ut_ref[...] = (hidden_grad * silu).astype(jnp.bfloat16)
    for move in moves[4:]:
        move.start()
    slot = jnp.dot(gt_ref[...], wg_ref[...], preferred_element_type=jnp.float32)
    slot += jnp.dot(ut_ref[...], wu_ref[...], preferred_element_type=jnp.float32)
    far_ref[...] = slot[pair_slots:].astype(jnp.bfloat16)
    near_ref[...] = slot[:pair_slots].astype(jnp.bfloat16)
    for move in moves:
        move.wait()


def place_kernel(place_ref, picks_ref, near_ref, far_ref, keep_ref, send_ref):
    own_half, core = place_ref[1], place_ref[2]
    _, rows, width = keep_ref.shape
    pair_slots = near_ref.shape[0]
    backs = []
    for h in range(2):
        cols = pl.ds(pl.multiple_of((own_half if h == 0 else 1 - own_half) * width, width), width)
        slot = jnp.concatenate([near_ref[:, cols], far_ref[:, cols]], axis=0)
        backs.append(lax.dot_general(picks_ref[...], slot, CONTRACT_FIRST, preferred_element_type=jnp.float32))
    keep_ref[0] = backs[0][:rows]
    keep_ref[1] = jnp.where(core == 1, backs[1][:rows], backs[0][rows:])
    send_ref[0] = jnp.where(core == 1, backs[0][rows:], backs[1][:rows]).astype(jnp.bfloat16)
    send_ref[1] = backs[1][rows:].astype(jnp.bfloat16)


def pick_rows(place, shares, top, rows, pair_slots):
    width = shares[0].shape[1]
    vmem = pl.BlockSpec(memory_space=pltpu.VMEM)
    picked = jax.ShapeDtypeStruct((2, pair_slots, 2 * width), jnp.bfloat16)
    return pl.pallas_call(
        functools.partial(pick_kernel, top, rows),
        in_specs=[pl.BlockSpec(memory_space=pltpu.SMEM)] + [vmem] * 4,
        out_specs=[vmem] * 3,
        out_shape=[picked, picked, jax.ShapeDtypeStruct((2 * pair_slots, 2 * rows), jnp.bfloat16)],
        compiler_params=pltpu.CompilerParams(vmem_limit_bytes=VMEM_LIMIT),
        name="pick",
    )(place, *shares)


def run_experts(index, chunks, mine, theirs, weights, kept):
    _, pair_slots, features = mine.shape
    hidden = weights[0].shape[0]
    slots = 2 * pair_slots
    hbm = pl.BlockSpec(memory_space=pltpu.HBM)
    vmem = pl.BlockSpec(memory_space=pltpu.VMEM)
    part = jax.ShapeDtypeStruct((pair_slots, features), jnp.bfloat16)
    wide = jax.ShapeDtypeStruct((chunks * slots, features), jnp.bfloat16)
    narrow = jax.ShapeDtypeStruct((chunks * slots, hidden), jnp.bfloat16)
    return pl.pallas_call(
        functools.partial(expert_kernel, index, kept is not None),
        in_specs=[vmem] * 5 + [hbm] * (0 if kept is None else 5),
        out_specs=[vmem] * 2 + [hbm] * 5,
        out_shape=[part, part, wide, wide, narrow, narrow, narrow],
        scratch_shapes=[pltpu.VMEM((slots, hidden), jnp.bfloat16)] * 3 + [pltpu.SemaphoreType.DMA((7,))],
        input_output_aliases={} if kept is None else {5 + i: 2 + i for i in range(5)},
        compiler_params=pltpu.CompilerParams(vmem_limit_bytes=VMEM_LIMIT),
        name="experts",
    )(mine, theirs, *weights, *(kept or ()))


def place_rows(place, picks, near, far, rows, width):
    vmem = pl.BlockSpec(memory_space=pltpu.VMEM)
    return pl.pallas_call(
        place_kernel,
        in_specs=[pl.BlockSpec(memory_space=pltpu.SMEM)] + [vmem] * 3,
        out_specs=[vmem] * 2,
        out_shape=[
            jax.ShapeDtypeStruct((2, rows, width), jnp.float32),
            jax.ShapeDtypeStruct((2, rows, width), jnp.bfloat16),
        ],
        compiler_params=pltpu.CompilerParams(vmem_limit_bytes=VMEM_LIMIT),
        name="place",
    )(place, picks, near, far)


def ring_order(length):
    return list(range(0, min(1, length))) + list(range(1, length, 2)) + list(range(2, length, 2))[::-1]


def gather_body(tokens, out_grad, routes, combine, w_gate, w_up, w_down):
    experts = lax.axis_size("expert")
    chunks = experts // 4
    rows, width = tokens.shape
    top = routes.shape[1]
    per_pair = rows * top // experts
    capacity = per_pair + per_pair // 8
    pair_slots = -(-2 * capacity // 16) * 16
    order = ring_order(chunks)
    after = {order[i]: order[(i + 1) % chunks] for i in range(chunks)}
    devices = [(e, h) for e in range(experts) for h in range(2)]

    def permute(value, target):
        pairs = [(e * 2 + h, target(e, h)[0] * 2 + target(e, h)[1]) for e, h in devices]
        return lax.ppermute(value, ("expert", "etp"), pairs)

    def to_ring(value):
        return permute(value, lambda e, h: (after[e // 4] * 4 + e % 4, h))

    def to_core(value):
        return permute(value, lambda e, h: (e ^ 1, h))

    def to_first(value):
        return permute(value, lambda e, h: (e, h ^ 1) if e % 2 else (e ^ 2, h))

    def to_second(value):
        return permute(value, lambda e, h: (e ^ 2, h) if e % 2 else (e, h ^ 1))

    me = lax.axis_index("expert")
    place = jnp.stack([me, lax.axis_index("etp"), me % 2]).astype(jnp.int32)
    share = pack_share(tokens, out_grad, routes, combine)
    weights = (w_gate[0], w_up[0], w_down[0])

    def tied(values, mark):
        return lax.optimization_barrier((values, mark))[0]

    def placed(picks, near, far):
        return place_rows(place, picks, near, to_core(far), rows, width)

    def added(keep, came):
        return keep + came.astype(jnp.float32)

    waves = [
        ([("f", 0), ("a", 0)], ("s", 1)),
        ([("b", 0), ("f", 1)], ("s", 2)),
        ([("a", 1), ("b", 1), ("a", 2)], ("s", 3)),
        ([("a", 3), ("f", 3)], ("f", 2)),
        ([("b", 2), ("b", 3)], None),
    ]
    have = {("s", 0): share}
    kept, picked, parts = None, None, None
    late, last, done = [], [], 0
    for plane, ring in waves:
        came = {}
        for kind, c in plane:
            if c < chunks:
                value = have["f" if kind == "b" else "s", c]
                came[kind, c] = to_first(value) if kind == "f" else to_second(value)
        if ring is not None and ring[1] < chunks:
            came[ring] = to_ring(have[ring[0], ring[1] - 1])
        before, parts = parts, None
        if picked is not None:
            mine, theirs, picks = picked
            near, far, *kept = run_experts(done, chunks, mine, to_core(theirs), weights, kept)
            parts, picked = (picks, near, far), None
            done += 1
        if ring is None:
            have.update(came)
            break
        if all((kind, done) in have for kind in "sfab") and done + 1 < chunks:
            picked = pick_rows(place, [have[kind, done] for kind in "sfab"], top, rows, pair_slots)
        listed = sorted(came, reverse=False)
        values, picked, parts, weights = lax.optimization_barrier(
            ([came[key] for key in listed], picked, parts, weights)
        )
        have.update(zip(listed, values))
    mark = []
    if before is not None:
        keep, send = placed(*before)
        late.append((keep, to_second(send)))
        mark.append(send)
    if parts is not None:
        mark.append(parts[1])
    crossed = None
    if parts is not None:
        picks, near, far = parts
        crossed = to_core(far)
    while done < chunks:
        shares = tied([have[kind, done] for kind in "sfab"], mark)
        rows_of = pick_rows(place, shares, top, rows, pair_slots)
        last.append(rows_of)
        mark = [crossed]
        done += 1
    if crossed is not None:
        keep, send = place_rows(place, picks, near, crossed, rows, width)
        late.append((keep, to_second(send)))
    done -= len(last)
    for i, (mine, theirs, picks) in enumerate(last):
        mine = tied(mine, send) if i == 0 else mine
        near, far, *kept = run_experts(done, chunks, mine, to_core(theirs), weights, kept)
        last[i] = picks, near, far
        done += 1
    nears = [near for _, near, _ in last]
    near, send = nears[-1], nears[0]
    for picks, first, far in last:
        keep, send = placed(picks, tied(first, send), far)
        late.append((keep, to_second(send)))
    ties = [nears[0], send]
    marks = [send] * (chunks + 2)
    running = None
    for c in range(1, chunks):
        keep, came = late[c]
        came = tied(came, ties[c - 1] if c + 1 < chunks else previous)
        pair = added(keep, came)
        came = to_first(pair[1].astype(jnp.bfloat16))
        total = added(pair[0], tied(came, send) if c == 1 else came)
        running = (total if running is None else added(total, running)).astype(jnp.bfloat16)
        previous = running
        if c > 1:
            marks[min(c - 1, 2)] = running
        if c + 1 < chunks:
            running = to_ring(running)
    keep, came = late[0]
    pair = added(keep, tied(came, near))
    came = pair[1].astype(jnp.bfloat16)
    own = added(pair[0], to_first(came if running is None else tied(came, running)))
    grad_tokens = (own if running is None else added(own, to_ring(running))).astype(jnp.bfloat16)
    rows_x, rows_g, acts, gate_term, up_term = kept
    acts, gate_term, up_term = tied(acts, marks[0]), tied(gate_term, marks[1]), tied(up_term, marks[2])
    grad_down = lax.dot_general(acts, rows_g, CONTRACT_FIRST, preferred_element_type=jnp.float32)
    grad_gate = lax.dot_general(gate_term, rows_x, CONTRACT_FIRST, preferred_element_type=jnp.float32)
    grad_up = lax.dot_general(up_term, rows_x, CONTRACT_FIRST, preferred_element_type=jnp.float32)
    return (
        grad_tokens,
        grad_gate.astype(jnp.bfloat16)[None],
        grad_up.astype(jnp.bfloat16)[None],
        grad_down.astype(jnp.bfloat16)[None],
    )


def solution(mesh):
    experts = mesh.shape["expert"]

    def body(tokens, out_grad, routes, combine, w_gate, w_up, w_down):
        rows, width = tokens.shape
        top = routes.shape[1]
        gathers = top * 4 >= experts and experts % 4 == 0 and experts <= 16 and mesh.shape["etp"] == 2
        run = gather_body if gathers and top * rows <= width else exchange_body
        return run(tokens, out_grad, routes, combine, w_gate, w_up, w_down)

    placed = (
        P("expert", "etp"),
        P("expert", "etp"),
        P("expert", None),
        P("expert", None),
        P("expert", "etp", None),
        P("expert", "etp", None),
        P("expert", "etp", None),
    )
    return jax.shard_map(
        body,
        mesh=mesh,
        in_specs=placed,
        out_specs=(
            P("expert", "etp"),
            P("expert", "etp", None),
            P("expert", "etp", None),
            P("expert", "etp", None),
        ),
        check_vma=False,
    )
```

```python
import functools

import jax
import jax.numpy as jnp
from jax import lax
from jax.experimental import pallas as pl
from jax.experimental.pallas import tpu as pltpu
from jax.sharding import PartitionSpec as P

CONTRACT_LAST = (((1,), (1,)), ((), ()))
CONTRACT_FIRST = (((0,), (0,)), ((), ()))
INFO_ROWS = 16
VMEM_LIMIT = 16 * 1024 * 1024


def pack_rows(token_rows, grad_rows, token_of, scale, is_live):
    mask = is_live[:, None].astype(token_rows.dtype)
    inputs_sent = token_rows[token_of] * mask
    grads_sent = (scale[:, None] * grad_rows[token_of].astype(jnp.float32)).astype(jnp.bfloat16)
    return (inputs_sent, grads_sent)


def pair_positions(routed_flat, experts):
    pair_total = routed_flat.shape[0]
    span = 128
    groups = pair_total // span
    labels = jnp.arange(experts, dtype=jnp.int32)
    one_hot = (routed_flat[:, None] == labels[None, :]).astype(jnp.bfloat16)
    grouped = one_hot.reshape(groups, span, experts)
    row_ids = jnp.arange(span, dtype=jnp.int32)
    lower = (row_ids[None, :] < row_ids[:, None]).astype(jnp.bfloat16)
    within = jnp.einsum("ij,bje->bie", lower, grouped, preferred_element_type=jnp.float32)
    group_sums = jnp.sum(grouped.astype(jnp.float32), axis=1)
    group_before = jnp.cumsum(group_sums, axis=0) - group_sums
    earlier = within + group_before[:, None, :]
    counted = jnp.sum(earlier * grouped.astype(jnp.float32), axis=2)
    return counted.reshape(pair_total).astype(jnp.int32)


def exchange_body(tokens, out_grad, routes, combine, w_gate, w_up, w_down):
    experts = lax.axis_size("expert")
    tok_rows = tokens.shape[0]
    col_width = tokens.shape[1]
    choose_count = routes.shape[1]
    per_pair = tok_rows * choose_count // experts
    capacity = per_pair + per_pair // 8
    routed_flat = routes.reshape(-1)
    pair_total = routed_flat.shape[0]
    position = pair_positions(routed_flat, experts)
    target = routed_flat * capacity + position
    anchor = jnp.full((experts * capacity,), pair_total, jnp.int32)
    anchor = anchor.at[target].set(jnp.arange(pair_total, dtype=jnp.int32))
    is_live = anchor < pair_total
    safe_anchor = jnp.minimum(anchor, pair_total - 1)
    token_of = safe_anchor // choose_count
    scale = combine.reshape(-1)[safe_anchor] * is_live.astype(jnp.float32)
    full_tokens, full_grads = (
        lax.all_gather(tokens, "etp", axis=1, tiled=True),
        lax.all_gather(out_grad, "etp", axis=1, tiled=True),
    )
    inputs_sent, grads_sent = pack_rows(full_tokens, full_grads, token_of, scale, is_live)
    rows_x, rows_g = (
        lax.all_to_all(inputs_sent, "expert", split_axis=0, concat_axis=0, tiled=True),
        lax.all_to_all(grads_sent, "expert", split_axis=0, concat_axis=0, tiled=True),
    )
    gate_w = w_gate[0]
    up_w = w_up[0]
    down_w = w_down[0]
    gate = lax.dot_general(rows_x, gate_w, CONTRACT_LAST, preferred_element_type=jnp.float32)
    up = lax.dot_general(rows_x, up_w, CONTRACT_LAST, preferred_element_type=jnp.float32)
    hidden_grad = lax.dot_general(rows_g, down_w, CONTRACT_LAST, preferred_element_type=jnp.float32)
    sigma = jax.nn.sigmoid(gate)
    silu = gate * sigma
    acts = (silu * up).astype(jnp.bfloat16)
    grad_down = lax.dot_general(acts, rows_g, CONTRACT_FIRST, preferred_element_type=jnp.float32)
    gate_term = (hidden_grad * up * sigma * (1.0 + gate * (1.0 - sigma))).astype(jnp.bfloat16)
    up_term = (hidden_grad * silu).astype(jnp.bfloat16)
    grad_gate = lax.dot_general(
        gate_term, rows_x, CONTRACT_FIRST, preferred_element_type=jnp.float32
    )
    grad_up = lax.dot_general(up_term, rows_x, CONTRACT_FIRST, preferred_element_type=jnp.float32)
    swapped_gate, swapped_up = (
        lax.all_to_all(gate_w, "etp", split_axis=1, concat_axis=0, tiled=True),
        lax.all_to_all(up_w, "etp", split_axis=1, concat_axis=0, tiled=True),
    )
    running = jnp.dot(
        lax.all_gather(gate_term, "etp", axis=1, tiled=True),
        swapped_gate,
        preferred_element_type=jnp.float32,
    )
    slot_grads = running + jnp.dot(
        lax.all_gather(up_term, "etp", axis=1, tiled=True),
        swapped_up,
        preferred_element_type=jnp.float32,
    )
    slot_grads = slot_grads.astype(jnp.bfloat16)
    returned = lax.all_to_all(slot_grads, "expert", split_axis=0, concat_axis=0, tiled=True)
    picked = returned[target].astype(jnp.float32).reshape(tok_rows, choose_count, col_width)
    grad_tokens = jnp.sum(picked, axis=1).astype(jnp.bfloat16)
    return (
        grad_tokens,
        grad_gate.astype(jnp.bfloat16)[None],
        grad_up.astype(jnp.bfloat16)[None],
        grad_down.astype(jnp.bfloat16)[None],
    )


def pack_kernel(tokens_ref, grads_ref, routes_ref, combine_ref, out_ref):
    rows = tokens_ref.shape[0]
    out_ref[:rows] = tokens_ref[...]
    out_ref[rows:2 * rows] = grads_ref[...]
    top = routes_ref.shape[0]
    routes = routes_ref[...].astype(jnp.float32)
    weights = combine_ref[...]
    high = weights.astype(jnp.bfloat16).astype(jnp.float32)
    middle = (weights - high).astype(jnp.bfloat16).astype(jnp.float32)
    low = weights - high - middle
    blank = jnp.zeros((INFO_ROWS - 4, rows), jnp.float32)
    for k in range(top):
        own = slice(k, k + 1)
        column = jnp.concatenate([routes[own], high[own], middle[own], low[own], blank], axis=0)
        out_ref[2 * rows:, k * rows:(k + 1) * rows] = column.astype(jnp.bfloat16)


def pack_share(tokens, out_grad, routes, combine):
    rows, width = tokens.shape
    vmem = pl.BlockSpec(memory_space=pltpu.VMEM)
    return pl.pallas_call(
        pack_kernel,
        in_specs=[vmem] * 4,
        out_specs=vmem,
        out_shape=jax.ShapeDtypeStruct((2 * rows + INFO_ROWS, width), jnp.bfloat16),
        name="pack",
    )(tokens, out_grad, routes.T, combine.T)


def pick_kernel(top, rows, place_ref, *refs):
    shares, (mine_ref, theirs_ref, picks_ref) = refs[:4], refs[4:]
    me, own_half, core = place_ref[0], place_ref[1], place_ref[2]
    pair_slots, width = mine_ref.shape[1], shares[0].shape[1]
    earlier = (
        lax.broadcasted_iota(jnp.int32, (2 * rows, 2 * rows), 0)
        < lax.broadcasted_iota(jnp.int32, (2 * rows, 2 * rows), 1)
    ).astype(jnp.bfloat16)
    infos = [
        [share_ref[pl.ds(2 * rows, INFO_ROWS), k * rows:(k + 1) * rows].astype(jnp.float32) for k in range(top)]
        for share_ref in (shares[0], shares[3])
    ]
    picks, scales = [], []
    for expert in (me, me + 1 - 2 * core):
        named, weights = [], []
        for block in infos:
            hits, weight = 0.0, 0.0
            for info in block:
                hit = info[0:1] == expert.astype(jnp.float32)
                hits += hit.astype(jnp.float32)
                weight += jnp.where(hit, info[1:2] + info[2:3] + info[3:4], 0.0)
            named.append(hits)
            weights.append(weight)
        named = jnp.concatenate(named, axis=1)
        weights = jnp.concatenate(weights, axis=1)
        counted = jnp.dot(
            jnp.broadcast_to(named, (16, 2 * rows)).astype(jnp.bfloat16),
            earlier,
            preferred_element_type=jnp.float32,
        )[:1]
        slot_of = jnp.where(named > 0.0, counted.astype(jnp.int32), -1)
        chosen = slot_of == lax.broadcasted_iota(jnp.int32, (pair_slots, 2 * rows), 0)
        picks.append(chosen.astype(jnp.bfloat16))
        scales.append(jnp.sum(jnp.where(chosen, weights, 0.0), axis=1, keepdims=True))
    picks = jnp.concatenate(picks, axis=0)
    scales = jnp.concatenate(scales, axis=0)
    picks_ref[...] = picks
    for h in range(2):
        cols = pl.ds(pl.multiple_of((own_half if h == 0 else 1 - own_half) * width, width), width)
        for part in range(2):
            own, first, second, both = [ref[pl.ds(part * rows, rows)] for ref in shares]
            if h == 0:
                held = jnp.concatenate([own, jnp.where(core == 1, second, first)], axis=0)
            else:
                held = jnp.concatenate([jnp.where(core == 1, first, second), both], axis=0)
            picked = jnp.dot(picks, held, preferred_element_type=jnp.float32)
            if part == 1:
                picked = scales * picked
            picked = picked.astype(jnp.bfloat16)
            mine_ref[part, :, cols] = picked[:pair_slots]
            theirs_ref[part, :, cols] = picked[pair_slots:]


def expert_kernel(index, chained, mine_ref, theirs_ref, wg_ref, wu_ref, wd_ref, *refs):
    near_ref, far_ref, *kept_refs = refs[5 if chained else 0:][:7]
    act_ref, gt_ref, ut_ref, sems = refs[-4:]
    pair_slots = mine_ref.shape[1]
    slots = 2 * pair_slots

    def kept_move(source, target, part, count, i):
        return pltpu.make_async_copy(
            source, kept_refs[target].at[pl.ds(index * slots + part * pair_slots, count)], sems.at[i]
        )

    moves = [
        kept_move(mine_ref.at[0], 0, 0, pair_slots, 0),
        kept_move(theirs_ref.at[0], 0, 1, pair_slots, 1),
        kept_move(mine_ref.at[1], 1, 0, pair_slots, 2),
        kept_move(theirs_ref.at[1], 1, 1, pair_slots, 3),
        kept_move(act_ref, 2, 0, slots, 4),
        kept_move(gt_ref, 3, 0, slots, 5),
        kept_move(ut_ref, 4, 0, slots, 6),
    ]
    for move in moves[:4]:
        move.start()
    rows_x = jnp.concatenate([mine_ref[0], theirs_ref[0]], axis=0)
    rows_g = jnp.concatenate([mine_ref[1], theirs_ref[1]], axis=0)
    gate = lax.dot_general(rows_x, wg_ref[...], CONTRACT_LAST, preferred_element_type=jnp.float32)
    up = lax.dot_general(rows_x, wu_ref[...], CONTRACT_LAST, preferred_element_type=jnp.float32)
    hidden_grad = lax.dot_general(rows_g, wd_ref[...], CONTRACT_LAST, preferred_element_type=jnp.float32)
    sigma = 1.0 / (1.0 + jnp.exp(-gate))
    silu = gate * sigma
    act_ref[...] = (silu * up).astype(jnp.bfloat16)
    gt_ref[...] = (hidden_grad * up * sigma * (1.0 + gate * (1.0 - sigma))).astype(jnp.bfloat16)
    ut_ref[...] = (hidden_grad * silu).astype(jnp.bfloat16)
    for move in moves[4:]:
        move.start()
    slot = jnp.dot(gt_ref[...], wg_ref[...], preferred_element_type=jnp.float32)
    slot += jnp.dot(ut_ref[...], wu_ref[...], preferred_element_type=jnp.float32)
    far_ref[...] = slot[pair_slots:].astype(jnp.bfloat16)
    near_ref[...] = slot[:pair_slots].astype(jnp.bfloat16)
    for move in moves:
        move.wait()


def place_kernel(place_ref, picks_ref, near_ref, far_ref, keep_ref, send_ref):
    own_half, core = place_ref[1], place_ref[2]
    _, rows, width = keep_ref.shape
    pair_slots = near_ref.shape[0]
    backs = []
    for h in range(2):
        cols = pl.ds(pl.multiple_of((own_half if h == 0 else 1 - own_half) * width, width), width)
        slot = jnp.concatenate([near_ref[:, cols], far_ref[:, cols]], axis=0)
        backs.append(lax.dot_general(picks_ref[...], slot, CONTRACT_FIRST, preferred_element_type=jnp.float32))
    keep_ref[0] = backs[0][:rows]
    keep_ref[1] = jnp.where(core == 1, backs[1][:rows], backs[0][rows:])
    send_ref[0] = jnp.where(core == 1, backs[0][rows:], backs[1][:rows]).astype(jnp.bfloat16)
    send_ref[1] = backs[1][rows:].astype(jnp.bfloat16)


def pick_rows(place, shares, top, rows, pair_slots):
    width = shares[0].shape[1]
    vmem = pl.BlockSpec(memory_space=pltpu.VMEM)
    picked = jax.ShapeDtypeStruct((2, pair_slots, 2 * width), jnp.bfloat16)
    return pl.pallas_call(
        functools.partial(pick_kernel, top, rows),
        in_specs=[pl.BlockSpec(memory_space=pltpu.SMEM)] + [vmem] * 4,
        out_specs=[vmem] * 3,
        out_shape=[picked, picked, jax.ShapeDtypeStruct((2 * pair_slots, 2 * rows), jnp.bfloat16)],
        compiler_params=pltpu.CompilerParams(vmem_limit_bytes=VMEM_LIMIT),
        name="pick",
    )(place, *shares)


def run_experts(index, chunks, mine, theirs, weights, kept):
    _, pair_slots, features = mine.shape
    hidden = weights[0].shape[0]
    slots = 2 * pair_slots
    hbm = pl.BlockSpec(memory_space=pltpu.HBM)
    vmem = pl.BlockSpec(memory_space=pltpu.VMEM)
    part = jax.ShapeDtypeStruct((pair_slots, features), jnp.bfloat16)
    wide = jax.ShapeDtypeStruct((chunks * slots, features), jnp.bfloat16)
    narrow = jax.ShapeDtypeStruct((chunks * slots, hidden), jnp.bfloat16)
    return pl.pallas_call(
        functools.partial(expert_kernel, index, kept is not None),
        in_specs=[vmem] * 5 + [hbm] * (0 if kept is None else 5),
        out_specs=[vmem] * 2 + [hbm] * 5,
        out_shape=[part, part, wide, wide, narrow, narrow, narrow],
        scratch_shapes=[pltpu.VMEM((slots, hidden), jnp.bfloat16)] * 3 + [pltpu.SemaphoreType.DMA((7,))],
        input_output_aliases={} if kept is None else {5 + i: 2 + i for i in range(5)},
        compiler_params=pltpu.CompilerParams(vmem_limit_bytes=VMEM_LIMIT),
        name="experts",
    )(mine, theirs, *weights, *(kept or ()))


def place_rows(place, picks, near, far, rows, width):
    vmem = pl.BlockSpec(memory_space=pltpu.VMEM)
    return pl.pallas_call(
        place_kernel,
        in_specs=[pl.BlockSpec(memory_space=pltpu.SMEM)] + [vmem] * 3,
        out_specs=[vmem] * 2,
        out_shape=[
            jax.ShapeDtypeStruct((2, rows, width), jnp.float32),
            jax.ShapeDtypeStruct((2, rows, width), jnp.bfloat16),
        ],
        compiler_params=pltpu.CompilerParams(vmem_limit_bytes=VMEM_LIMIT),
        name="place",
    )(place, picks, near, far)


def ring_order(length):
    return list(range(0, min(1, length))) + list(range(1, length, 2)) + list(range(2, length, 2))[::-1]


def gather_body(tokens, out_grad, routes, combine, w_gate, w_up, w_down):
    experts = lax.axis_size("expert")
    chunks = experts // 4
    rows, width = tokens.shape
    top = routes.shape[1]
    per_pair = rows * top // experts
    capacity = per_pair + per_pair // 8
    pair_slots = -(-2 * capacity // 16) * 16
    order = ring_order(chunks)
    after = {order[i]: order[(i + 1) % chunks] for i in range(chunks)}
    devices = [(e, h) for e in range(experts) for h in range(2)]

    def permute(value, target):
        pairs = [(e * 2 + h, target(e, h)[0] * 2 + target(e, h)[1]) for e, h in devices]
        return lax.ppermute(value, ("expert", "etp"), pairs)

    def to_ring(value):
        return permute(value, lambda e, h: (after[e // 4] * 4 + e % 4, h))

    def to_core(value):
        return permute(value, lambda e, h: (e ^ 1, h))

    def to_first(value):
        return permute(value, lambda e, h: (e, h ^ 1) if e % 2 else (e ^ 2, h))

    def to_second(value):
        return permute(value, lambda e, h: (e ^ 2, h) if e % 2 else (e, h ^ 1))

    me = lax.axis_index("expert")
    place = jnp.stack([me, lax.axis_index("etp"), me % 2]).astype(jnp.int32)
    share = pack_share(tokens, out_grad, routes, combine)
    weights = (w_gate[0], w_up[0], w_down[0])

    def tied(values, mark):
        return lax.optimization_barrier((values, mark))[0]

    def placed(picks, near, far):
        return place_rows(place, picks, near, to_core(far), rows, width)

    def added(keep, came):
        return keep + came.astype(jnp.float32)

    waves = [
        ([("f", 0), ("a", 0)], ("s", 1)),
        ([("b", 0), ("f", 1)], ("s", 2)),
        ([("a", 1), ("b", 1), ("a", 2)], ("s", 3)),
        ([("a", 3), ("f", 3)], ("f", 2)),
        ([("b", 2), ("b", 3)], None),
    ]
    have = {("s", 0): share}
    kept, picked, parts = None, None, None
    late, last, done = [], [], 0
    for plane, ring in waves:
        came = {}
        for kind, c in plane:
            if c < chunks:
                value = have["f" if kind == "b" else "s", c]
                came[kind, c] = to_first(value) if kind == "f" else to_second(value)
        if ring is not None and ring[1] < chunks:
            came[ring] = to_ring(have[ring[0], ring[1] - 1])
        before, parts = parts, None
        if picked is not None:
            mine, theirs, picks = picked
            near, far, *kept = run_experts(done, chunks, mine, to_core(theirs), weights, kept)
            parts, picked = (picks, near, far), None
            done += 1
        if ring is None:
            have.update(came)
            break
        if all((kind, done) in have for kind in "sfab") and done + 1 < chunks:
            picked = pick_rows(place, [have[kind, done] for kind in "sfab"], top, rows, pair_slots)
        listed = sorted(came, reverse=False)
        values, picked, parts, weights = lax.optimization_barrier(
            ([came[key] for key in listed], picked, parts, weights)
        )
        have.update(zip(listed, values))
    mark = []
    if before is not None:
        keep, send = placed(*before)
        late.append((keep, to_second(send)))
        mark.append(send)
    if parts is not None:
        mark.append(parts[1])
    crossed = None
    if parts is not None:
        picks, near, far = parts
        crossed = to_core(far)
    while done < chunks:
        shares = tied([have[kind, done] for kind in "sfab"], [mark, list(came.values())])
        rows_of = pick_rows(place, shares, top, rows, pair_slots)
        last.append(rows_of)
        mark = []
        done += 1
    if crossed is not None:
        keep, send = place_rows(place, picks, near, crossed, rows, width)
        late.append((keep, to_second(send)))
    done -= len(last)
    early = None
    for i, (mine, theirs, picks) in enumerate(last):
        mine = tied(mine, send) if i == 0 else mine
        near, far, *kept = run_experts(done, chunks, mine, to_core(theirs), weights, kept)
        last[i] = picks, near, far
        done += 1
        if i == 0 and len(late) > 1:
            keep, came = late[1]
            pair = added(keep, tied(came, near))
            early = pair[0], to_first(pair[1].astype(jnp.bfloat16))
    nears = [near for _, near, _ in last]
    near, send = nears[-1], nears[0]
    if early is not None:
        came, near = lax.optimization_barrier((early[1], near))
        early = added(early[0], came)
        nears[-1] = near
    for (picks, _, far), first in zip(last, nears):
        keep, send = placed(picks, tied(first, send), far)
        late.append((keep, to_second(send)))
    ties = [nears[0], send]
    marks = [send] * (chunks + 2)
    running = None
    for c in range(1, chunks):
        if c == 1 and early is not None:
            total = early
        else:
            keep, came = late[c]
            pair = added(keep, tied(came, ties[c - 1] if c + 1 < chunks else previous))
            total = added(pair[0], to_first(pair[1].astype(jnp.bfloat16)))
        running = (total if running is None else added(total, running)).astype(jnp.bfloat16)
        previous = running
        if c > 1:
            marks[min(c - 1, 2)] = running
        if c + 1 < chunks:
            running = to_ring(running)
    keep, came = late[0]
    pair = added(keep, tied(came, near))
    came = pair[1].astype(jnp.bfloat16)
    own = added(pair[0], to_first(came if running is None else tied(came, running)))
    grad_tokens = (own if running is None else added(own, to_ring(running))).astype(jnp.bfloat16)
    rows_x, rows_g, acts, gate_term, up_term = kept
    acts, gate_term, up_term = tied(acts, marks[0]), tied(gate_term, marks[1]), tied(up_term, marks[2])
    grad_down = lax.dot_general(acts, rows_g, CONTRACT_FIRST, preferred_element_type=jnp.float32)
    grad_gate = lax.dot_general(gate_term, rows_x, CONTRACT_FIRST, preferred_element_type=jnp.float32)
    grad_up = lax.dot_general(up_term, rows_x, CONTRACT_FIRST, preferred_element_type=jnp.float32)
    return (
        grad_tokens,
        grad_gate.astype(jnp.bfloat16)[None],
        grad_up.astype(jnp.bfloat16)[None],
        grad_down.astype(jnp.bfloat16)[None],
    )


def solution(mesh):
    experts = mesh.shape["expert"]

    def body(tokens, out_grad, routes, combine, w_gate, w_up, w_down):
        rows, width = tokens.shape
        top = routes.shape[1]
        gathers = top * 4 >= experts and experts % 4 == 0 and experts <= 16 and mesh.shape["etp"] == 2
        run = gather_body if gathers and top * rows <= width else exchange_body
        return run(tokens, out_grad, routes, combine, w_gate, w_up, w_down)

    placed = (
        P("expert", "etp"),
        P("expert", "etp"),
        P("expert", None),
        P("expert", None),
        P("expert", "etp", None),
        P("expert", "etp", None),
        P("expert", "etp", None),
    )
    return jax.shard_map(
        body,
        mesh=mesh,
        in_specs=placed,
        out_specs=(
            P("expert", "etp"),
            P("expert", "etp", None),
            P("expert", "etp", None),
            P("expert", "etp", None),
        ),
        check_vma=False,
    )
```

```python
import functools

import jax
import jax.numpy as jnp
from jax import lax
from jax.experimental import pallas as pl
from jax.experimental.pallas import tpu as pltpu
from jax.sharding import PartitionSpec as P

CONTRACT_LAST = (((1,), (1,)), ((), ()))
CONTRACT_FIRST = (((0,), (0,)), ((), ()))
INFO_ROWS = 16
VMEM_LIMIT = 16 * 1024 * 1024


def pack_rows(token_rows, grad_rows, token_of, scale, is_live):
    mask = is_live[:, None].astype(token_rows.dtype)
    inputs_sent = token_rows[token_of] * mask
    grads_sent = (scale[:, None] * grad_rows[token_of].astype(jnp.float32)).astype(jnp.bfloat16)
    return (inputs_sent, grads_sent)


def pair_positions(routed_flat, experts):
    pair_total = routed_flat.shape[0]
    span = 128
    groups = pair_total // span
    labels = jnp.arange(experts, dtype=jnp.int32)
    one_hot = (routed_flat[:, None] == labels[None, :]).astype(jnp.bfloat16)
    grouped = one_hot.reshape(groups, span, experts)
    row_ids = jnp.arange(span, dtype=jnp.int32)
    lower = (row_ids[None, :] < row_ids[:, None]).astype(jnp.bfloat16)
    within = jnp.einsum("ij,bje->bie", lower, grouped, preferred_element_type=jnp.float32)
    group_sums = jnp.sum(grouped.astype(jnp.float32), axis=1)
    group_before = jnp.cumsum(group_sums, axis=0) - group_sums
    earlier = within + group_before[:, None, :]
    counted = jnp.sum(earlier * grouped.astype(jnp.float32), axis=2)
    return counted.reshape(pair_total).astype(jnp.int32)


def exchange_body(tokens, out_grad, routes, combine, w_gate, w_up, w_down):
    experts = lax.axis_size("expert")
    tok_rows = tokens.shape[0]
    col_width = tokens.shape[1]
    choose_count = routes.shape[1]
    per_pair = tok_rows * choose_count // experts
    capacity = per_pair + per_pair // 8
    routed_flat = routes.reshape(-1)
    pair_total = routed_flat.shape[0]
    position = pair_positions(routed_flat, experts)
    target = routed_flat * capacity + position
    anchor = jnp.full((experts * capacity,), pair_total, jnp.int32)
    anchor = anchor.at[target].set(jnp.arange(pair_total, dtype=jnp.int32))
    is_live = anchor < pair_total
    safe_anchor = jnp.minimum(anchor, pair_total - 1)
    token_of = safe_anchor // choose_count
    scale = combine.reshape(-1)[safe_anchor] * is_live.astype(jnp.float32)
    full_tokens, full_grads = (
        lax.all_gather(tokens, "etp", axis=1, tiled=True),
        lax.all_gather(out_grad, "etp", axis=1, tiled=True),
    )
    inputs_sent, grads_sent = pack_rows(full_tokens, full_grads, token_of, scale, is_live)
    rows_x, rows_g = (
        lax.all_to_all(inputs_sent, "expert", split_axis=0, concat_axis=0, tiled=True),
        lax.all_to_all(grads_sent, "expert", split_axis=0, concat_axis=0, tiled=True),
    )
    gate_w = w_gate[0]
    up_w = w_up[0]
    down_w = w_down[0]
    gate = lax.dot_general(rows_x, gate_w, CONTRACT_LAST, preferred_element_type=jnp.float32)
    up = lax.dot_general(rows_x, up_w, CONTRACT_LAST, preferred_element_type=jnp.float32)
    hidden_grad = lax.dot_general(rows_g, down_w, CONTRACT_LAST, preferred_element_type=jnp.float32)
    sigma = jax.nn.sigmoid(gate)
    silu = gate * sigma
    acts = (silu * up).astype(jnp.bfloat16)
    grad_down = lax.dot_general(acts, rows_g, CONTRACT_FIRST, preferred_element_type=jnp.float32)
    gate_term = (hidden_grad * up * sigma * (1.0 + gate * (1.0 - sigma))).astype(jnp.bfloat16)
    up_term = (hidden_grad * silu).astype(jnp.bfloat16)
    grad_gate = lax.dot_general(
        gate_term, rows_x, CONTRACT_FIRST, preferred_element_type=jnp.float32
    )
    grad_up = lax.dot_general(up_term, rows_x, CONTRACT_FIRST, preferred_element_type=jnp.float32)
    swapped_gate, swapped_up = (
        lax.all_to_all(gate_w, "etp", split_axis=1, concat_axis=0, tiled=True),
        lax.all_to_all(up_w, "etp", split_axis=1, concat_axis=0, tiled=True),
    )
    running = jnp.dot(
        lax.all_gather(gate_term, "etp", axis=1, tiled=True),
        swapped_gate,
        preferred_element_type=jnp.float32,
    )
    slot_grads = running + jnp.dot(
        lax.all_gather(up_term, "etp", axis=1, tiled=True),
        swapped_up,
        preferred_element_type=jnp.float32,
    )
    slot_grads = slot_grads.astype(jnp.bfloat16)
    returned = lax.all_to_all(slot_grads, "expert", split_axis=0, concat_axis=0, tiled=True)
    picked = returned[target].astype(jnp.float32).reshape(tok_rows, choose_count, col_width)
    grad_tokens = jnp.sum(picked, axis=1).astype(jnp.bfloat16)
    return (
        grad_tokens,
        grad_gate.astype(jnp.bfloat16)[None],
        grad_up.astype(jnp.bfloat16)[None],
        grad_down.astype(jnp.bfloat16)[None],
    )


def pack_kernel(tokens_ref, grads_ref, routes_ref, combine_ref, out_ref):
    rows = tokens_ref.shape[0]
    out_ref[:rows] = tokens_ref[...]
    out_ref[rows:2 * rows] = grads_ref[...]
    top = routes_ref.shape[0]
    routes = routes_ref[...].astype(jnp.float32)
    weights = combine_ref[...]
    high = weights.astype(jnp.bfloat16).astype(jnp.float32)
    middle = (weights - high).astype(jnp.bfloat16).astype(jnp.float32)
    low = weights - high - middle
    blank = jnp.zeros((INFO_ROWS - 4, rows), jnp.float32)
    for k in range(top):
        own = slice(k, k + 1)
        column = jnp.concatenate([routes[own], high[own], middle[own], low[own], blank], axis=0)
        out_ref[2 * rows:, k * rows:(k + 1) * rows] = column.astype(jnp.bfloat16)


def pack_share(tokens, out_grad, routes, combine):
    rows, width = tokens.shape
    vmem = pl.BlockSpec(memory_space=pltpu.VMEM)
    return pl.pallas_call(
        pack_kernel,
        in_specs=[vmem] * 4,
        out_specs=vmem,
        out_shape=jax.ShapeDtypeStruct((2 * rows + INFO_ROWS, width), jnp.bfloat16),
        name="pack",
    )(tokens, out_grad, routes.T, combine.T)


def pick_kernel(top, rows, place_ref, *refs):
    shares, (mine_ref, theirs_ref, picks_ref) = refs[:4], refs[4:]
    me, own_half, core = place_ref[0], place_ref[1], place_ref[2]
    pair_slots, width = mine_ref.shape[1], shares[0].shape[1]
    earlier = (
        lax.broadcasted_iota(jnp.int32, (2 * rows, 2 * rows), 0)
        < lax.broadcasted_iota(jnp.int32, (2 * rows, 2 * rows), 1)
    ).astype(jnp.bfloat16)
    infos = [
        [share_ref[pl.ds(2 * rows, INFO_ROWS), k * rows:(k + 1) * rows].astype(jnp.float32) for k in range(top)]
        for share_ref in (shares[0], shares[3])
    ]
    picks, scales = [], []
    for expert in (me, me + 1 - 2 * core):
        named, weights = [], []
        for block in infos:
            hits, weight = 0.0, 0.0
            for info in block:
                hit = info[0:1] == expert.astype(jnp.float32)
                hits += hit.astype(jnp.float32)
                weight += jnp.where(hit, info[1:2] + info[2:3] + info[3:4], 0.0)
            named.append(hits)
            weights.append(weight)
        named = jnp.concatenate(named, axis=1)
        weights = jnp.concatenate(weights, axis=1)
        counted = jnp.dot(
            jnp.broadcast_to(named, (16, 2 * rows)).astype(jnp.bfloat16),
            earlier,
            preferred_element_type=jnp.float32,
        )[:1]
        slot_of = jnp.where(named > 0.0, counted.astype(jnp.int32), -1)
        chosen = slot_of == lax.broadcasted_iota(jnp.int32, (pair_slots, 2 * rows), 0)
        picks.append(chosen.astype(jnp.bfloat16))
        scales.append(jnp.sum(jnp.where(chosen, weights, 0.0), axis=1, keepdims=True))
    picks = jnp.concatenate(picks, axis=0)
    scales = jnp.concatenate(scales, axis=0)
    picks_ref[...] = picks
    for h in range(2):
        cols = pl.ds(pl.multiple_of((own_half if h == 0 else 1 - own_half) * width, width), width)
        for part in range(2):
            own, first, second, both = [ref[pl.ds(part * rows, rows)] for ref in shares]
            if h == 0:
                held = jnp.concatenate([own, jnp.where(core == 1, second, first)], axis=0)
            else:
                held = jnp.concatenate([jnp.where(core == 1, first, second), both], axis=0)
            picked = jnp.dot(picks, held, preferred_element_type=jnp.float32)
            if part == 1:
                picked = scales * picked
            picked = picked.astype(jnp.bfloat16)
            mine_ref[part, :, cols] = picked[:pair_slots]
            theirs_ref[part, :, cols] = picked[pair_slots:]


def expert_kernel(index, chained, mine_ref, theirs_ref, wg_ref, wu_ref, wd_ref, *refs):
    near_ref, far_ref, *kept_refs = refs[5 if chained else 0:][:7]
    act_ref, gt_ref, ut_ref, sems = refs[-4:]
    pair_slots = mine_ref.shape[1]
    slots = 2 * pair_slots

    def kept_move(source, target, part, count, i):
        return pltpu.make_async_copy(
            source, kept_refs[target].at[pl.ds(index * slots + part * pair_slots, count)], sems.at[i]
        )

    moves = [
        kept_move(mine_ref.at[0], 0, 0, pair_slots, 0),
        kept_move(theirs_ref.at[0], 0, 1, pair_slots, 1),
        kept_move(mine_ref.at[1], 1, 0, pair_slots, 2),
        kept_move(theirs_ref.at[1], 1, 1, pair_slots, 3),
        kept_move(act_ref, 2, 0, slots, 4),
        kept_move(gt_ref, 3, 0, slots, 5),
        kept_move(ut_ref, 4, 0, slots, 6),
    ]
    for move in moves[:4]:
        move.start()
    rows_x = jnp.concatenate([mine_ref[0], theirs_ref[0]], axis=0)
    rows_g = jnp.concatenate([mine_ref[1], theirs_ref[1]], axis=0)
    gate = lax.dot_general(rows_x, wg_ref[...], CONTRACT_LAST, preferred_element_type=jnp.float32)
    up = lax.dot_general(rows_x, wu_ref[...], CONTRACT_LAST, preferred_element_type=jnp.float32)
    hidden_grad = lax.dot_general(rows_g, wd_ref[...], CONTRACT_LAST, preferred_element_type=jnp.float32)
    sigma = 1.0 / (1.0 + jnp.exp(-gate))
    silu = gate * sigma
    act_ref[...] = (silu * up).astype(jnp.bfloat16)
    gt_ref[...] = (hidden_grad * up * sigma * (1.0 + gate * (1.0 - sigma))).astype(jnp.bfloat16)
    ut_ref[...] = (hidden_grad * silu).astype(jnp.bfloat16)
    for move in moves[4:]:
        move.start()
    slot = jnp.dot(gt_ref[...], wg_ref[...], preferred_element_type=jnp.float32)
    slot += jnp.dot(ut_ref[...], wu_ref[...], preferred_element_type=jnp.float32)
    far_ref[...] = slot[pair_slots:].astype(jnp.bfloat16)
    near_ref[...] = slot[:pair_slots].astype(jnp.bfloat16)
    for move in moves:
        move.wait()


def place_kernel(place_ref, picks_ref, near_ref, far_ref, keep_ref, send_ref):
    own_half, core = place_ref[1], place_ref[2]
    _, rows, width = keep_ref.shape
    pair_slots = near_ref.shape[0]
    backs = []
    for h in range(2):
        cols = pl.ds(pl.multiple_of((own_half if h == 0 else 1 - own_half) * width, width), width)
        slot = jnp.concatenate([near_ref[:, cols], far_ref[:, cols]], axis=0)
        backs.append(lax.dot_general(picks_ref[...], slot, CONTRACT_FIRST, preferred_element_type=jnp.float32))
    keep_ref[0] = backs[0][:rows]
    keep_ref[1] = jnp.where(core == 1, backs[1][:rows], backs[0][rows:])
    send_ref[0] = jnp.where(core == 1, backs[0][rows:], backs[1][:rows]).astype(jnp.bfloat16)
    send_ref[1] = backs[1][rows:].astype(jnp.bfloat16)


def pick_rows(place, shares, top, rows, pair_slots):
    width = shares[0].shape[1]
    vmem = pl.BlockSpec(memory_space=pltpu.VMEM)
    picked = jax.ShapeDtypeStruct((2, pair_slots, 2 * width), jnp.bfloat16)
    return pl.pallas_call(
        functools.partial(pick_kernel, top, rows),
        in_specs=[pl.BlockSpec(memory_space=pltpu.SMEM)] + [vmem] * 4,
        out_specs=[vmem] * 3,
        out_shape=[picked, picked, jax.ShapeDtypeStruct((2 * pair_slots, 2 * rows), jnp.bfloat16)],
        compiler_params=pltpu.CompilerParams(vmem_limit_bytes=VMEM_LIMIT),
        name="pick",
    )(place, *shares)


def run_experts(index, chunks, mine, theirs, weights, kept):
    _, pair_slots, features = mine.shape
    hidden = weights[0].shape[0]
    slots = 2 * pair_slots
    hbm = pl.BlockSpec(memory_space=pltpu.HBM)
    vmem = pl.BlockSpec(memory_space=pltpu.VMEM)
    part = jax.ShapeDtypeStruct((pair_slots, features), jnp.bfloat16)
    wide = jax.ShapeDtypeStruct((chunks * slots, features), jnp.bfloat16)
    narrow = jax.ShapeDtypeStruct((chunks * slots, hidden), jnp.bfloat16)
    return pl.pallas_call(
        functools.partial(expert_kernel, index, kept is not None),
        in_specs=[vmem] * 5 + [hbm] * (0 if kept is None else 5),
        out_specs=[vmem] * 2 + [hbm] * 5,
        out_shape=[part, part, wide, wide, narrow, narrow, narrow],
        scratch_shapes=[pltpu.VMEM((slots, hidden), jnp.bfloat16)] * 3 + [pltpu.SemaphoreType.DMA((7,))],
        input_output_aliases={} if kept is None else {5 + i: 2 + i for i in range(5)},
        compiler_params=pltpu.CompilerParams(vmem_limit_bytes=VMEM_LIMIT),
        name="experts",
    )(mine, theirs, *weights, *(kept or ()))


def place_rows(place, picks, near, far, rows, width):
    vmem = pl.BlockSpec(memory_space=pltpu.VMEM)
    return pl.pallas_call(
        place_kernel,
        in_specs=[pl.BlockSpec(memory_space=pltpu.SMEM)] + [vmem] * 3,
        out_specs=[vmem] * 2,
        out_shape=[
            jax.ShapeDtypeStruct((2, rows, width), jnp.float32),
            jax.ShapeDtypeStruct((2, rows, width), jnp.bfloat16),
        ],
        compiler_params=pltpu.CompilerParams(vmem_limit_bytes=VMEM_LIMIT),
        name="place",
    )(place, picks, near, far)


def ring_order(length):
    return list(range(0, min(1, length))) + list(range(1, length, 2)) + list(range(2, length, 2))[::-1]


def gather_body(tokens, out_grad, routes, combine, w_gate, w_up, w_down):
    experts = lax.axis_size("expert")
    chunks = experts // 4
    rows, width = tokens.shape
    top = routes.shape[1]
    per_pair = rows * top // experts
    capacity = per_pair + per_pair // 8
    pair_slots = -(-2 * capacity // 16) * 16
    order = ring_order(chunks)
    after = {order[i]: order[(i + 1) % chunks] for i in range(chunks)}
    devices = [(e, h) for e in range(experts) for h in range(2)]

    def permute(value, target):
        pairs = [(e * 2 + h, target(e, h)[0] * 2 + target(e, h)[1]) for e, h in devices]
        return lax.ppermute(value, ("expert", "etp"), pairs)

    def to_ring(value):
        return permute(value, lambda e, h: (after[e // 4] * 4 + e % 4, h))

    def to_core(value):
        return permute(value, lambda e, h: (e ^ 1, h))

    def to_first(value):
        return permute(value, lambda e, h: (e, h ^ 1) if e % 2 else (e ^ 2, h))

    def to_second(value):
        return permute(value, lambda e, h: (e ^ 2, h) if e % 2 else (e, h ^ 1))

    me = lax.axis_index("expert")
    place = jnp.stack([me, lax.axis_index("etp"), me % 2]).astype(jnp.int32)
    share = pack_share(tokens, out_grad, routes, combine)
    weights = (w_gate[0], w_up[0], w_down[0])

    def tied(values, mark):
        return lax.optimization_barrier((values, mark))[0]

    def placed(picks, near, far):
        return place_rows(place, picks, near, to_core(far), rows, width)

    def added(keep, came):
        return keep + came.astype(jnp.float32)

    waves = [
        ([("f", 0), ("a", 0)], ("s", 1)),
        ([("b", 0), ("f", 1)], ("s", 2)),
        ([("a", 1), ("b", 1), ("a", 2)], ("s", 3)),
        ([("a", 3), ("f", 3)], ("f", 2)),
        ([("b", 2), ("b", 3)], None),
    ]
    have = {("s", 0): share}
    kept, picked, parts = None, None, None
    late, done = [], 0
    for plane, ring in waves:
        came = {}
        for kind, c in plane:
            if c < chunks:
                value = have["f" if kind == "b" else "s", c]
                came[kind, c] = to_first(value) if kind == "f" else to_second(value)
        if ring is not None and ring[1] < chunks:
            came[ring] = to_ring(have[ring[0], ring[1] - 1])
        before, parts = parts, None
        if picked is not None:
            mine, theirs, picks = picked
            near, far, *kept = run_experts(done, chunks, mine, to_core(theirs), weights, kept)
            parts, picked = (picks, near, far), None
            done += 1
        if ring is None:
            have.update(came)
            break
        if all((kind, done) in have for kind in "sfab") and done + 1 < chunks:
            picked = pick_rows(place, [have[kind, done] for kind in "sfab"], top, rows, pair_slots)
        listed = sorted(came, reverse=False)
        values, picked, parts, weights = lax.optimization_barrier(
            ([came[key] for key in listed], picked, parts, weights)
        )
        have.update(zip(listed, values))
    mark = []
    if before is not None:
        keep, send = placed(*before)
        late.append((keep, to_second(send)))
        mark.append(send)
    if parts is not None:
        mark.append(parts[1])
    while done < chunks:
        shares = tied([have[kind, done] for kind in "sfab"], mark)
        mine, theirs, picks = pick_rows(place, shares, top, rows, pair_slots)
        if parts is not None:
            keep, send = placed(*parts)
            late.append((keep, to_second(send)))
            mine = tied(mine, send)
        near, far, *kept = run_experts(done, chunks, mine, to_core(theirs), weights, kept)
        parts, mark = (picks, near, far), [near]
        done += 1
    keep, send = placed(*parts)
    late.append((keep, to_second(send)))
    marks = [send] * (chunks + 2)
    running, previous = None, send
    for c in range(1, chunks):
        keep, came = late[c]
        came = tied(came, near if c == 1 else send if c + 1 < chunks else previous)
        pair = added(keep, came)
        came = to_first(pair[1].astype(jnp.bfloat16))
        total = added(pair[0], tied(came, send) if c + 2 < chunks else came)
        running = (total if running is None else added(total, running)).astype(jnp.bfloat16)
        previous = running
        if c > 1:
            marks[min(c - 1, 2)] = running
        if c + 1 < chunks:
            running = to_ring(running)
    keep, came = late[0]
    pair = added(keep, tied(came, near))
    came = pair[1].astype(jnp.bfloat16)
    own = added(pair[0], to_first(came if running is None else tied(came, running)))
    grad_tokens = (own if running is None else added(own, to_ring(running))).astype(jnp.bfloat16)
    rows_x, rows_g, acts, gate_term, up_term = kept
    acts, gate_term, up_term = tied(acts, marks[0]), tied(gate_term, marks[1]), tied(up_term, marks[2])
    grad_down = lax.dot_general(acts, rows_g, CONTRACT_FIRST, preferred_element_type=jnp.float32)
    grad_gate = lax.dot_general(gate_term, rows_x, CONTRACT_FIRST, preferred_element_type=jnp.float32)
    grad_up = lax.dot_general(up_term, rows_x, CONTRACT_FIRST, preferred_element_type=jnp.float32)
    return (
        grad_tokens,
        grad_gate.astype(jnp.bfloat16)[None],
        grad_up.astype(jnp.bfloat16)[None],
        grad_down.astype(jnp.bfloat16)[None],
    )


def solution(mesh):
    experts = mesh.shape["expert"]

    def body(tokens, out_grad, routes, combine, w_gate, w_up, w_down):
        rows, width = tokens.shape
        top = routes.shape[1]
        gathers = top * 4 >= experts and experts % 4 == 0 and experts <= 16 and mesh.shape["etp"] == 2
        run = gather_body if gathers and top * rows <= width else exchange_body
        return run(tokens, out_grad, routes, combine, w_gate, w_up, w_down)

    placed = (
        P("expert", "etp"),
        P("expert", "etp"),
        P("expert", None),
        P("expert", None),
        P("expert", "etp", None),
        P("expert", "etp", None),
        P("expert", "etp", None),
    )
    return jax.shard_map(
        body,
        mesh=mesh,
        in_specs=placed,
        out_specs=(
            P("expert", "etp"),
            P("expert", "etp", None),
            P("expert", "etp", None),
            P("expert", "etp", None),
        ),
        check_vma=False,
    )
```

```python
import functools

import jax
import jax.numpy as jnp
from jax import lax
from jax.experimental import pallas as pl
from jax.experimental.pallas import tpu as pltpu
from jax.sharding import PartitionSpec as P

CONTRACT_LAST = (((1,), (1,)), ((), ()))
CONTRACT_FIRST = (((0,), (0,)), ((), ()))
INFO_ROWS = 16
VMEM_LIMIT = 16 * 1024 * 1024


def pack_rows(token_rows, grad_rows, token_of, scale, is_live):
    mask = is_live[:, None].astype(token_rows.dtype)
    inputs_sent = token_rows[token_of] * mask
    grads_sent = (scale[:, None] * grad_rows[token_of].astype(jnp.float32)).astype(jnp.bfloat16)
    return (inputs_sent, grads_sent)


def pair_positions(routed_flat, experts):
    pair_total = routed_flat.shape[0]
    span = 128
    groups = pair_total // span
    labels = jnp.arange(experts, dtype=jnp.int32)
    one_hot = (routed_flat[:, None] == labels[None, :]).astype(jnp.bfloat16)
    grouped = one_hot.reshape(groups, span, experts)
    row_ids = jnp.arange(span, dtype=jnp.int32)
    lower = (row_ids[None, :] < row_ids[:, None]).astype(jnp.bfloat16)
    within = jnp.einsum("ij,bje->bie", lower, grouped, preferred_element_type=jnp.float32)
    group_sums = jnp.sum(grouped.astype(jnp.float32), axis=1)
    group_before = jnp.cumsum(group_sums, axis=0) - group_sums
    earlier = within + group_before[:, None, :]
    counted = jnp.sum(earlier * grouped.astype(jnp.float32), axis=2)
    return counted.reshape(pair_total).astype(jnp.int32)


def exchange_body(tokens, out_grad, routes, combine, w_gate, w_up, w_down):
    experts = lax.axis_size("expert")
    tok_rows = tokens.shape[0]
    col_width = tokens.shape[1]
    choose_count = routes.shape[1]
    per_pair = tok_rows * choose_count // experts
    capacity = per_pair + per_pair // 8
    routed_flat = routes.reshape(-1)
    pair_total = routed_flat.shape[0]
    position = pair_positions(routed_flat, experts)
    target = routed_flat * capacity + position
    anchor = jnp.full((experts * capacity,), pair_total, jnp.int32)
    anchor = anchor.at[target].set(jnp.arange(pair_total, dtype=jnp.int32))
    is_live = anchor < pair_total
    safe_anchor = jnp.minimum(anchor, pair_total - 1)
    token_of = safe_anchor // choose_count
    scale = combine.reshape(-1)[safe_anchor] * is_live.astype(jnp.float32)
    full_tokens, full_grads = (
        lax.all_gather(tokens, "etp", axis=1, tiled=True),
        lax.all_gather(out_grad, "etp", axis=1, tiled=True),
    )
    inputs_sent, grads_sent = pack_rows(full_tokens, full_grads, token_of, scale, is_live)
    rows_x, rows_g = (
        lax.all_to_all(inputs_sent, "expert", split_axis=0, concat_axis=0, tiled=True),
        lax.all_to_all(grads_sent, "expert", split_axis=0, concat_axis=0, tiled=True),
    )
    gate_w = w_gate[0]
    up_w = w_up[0]
    down_w = w_down[0]
    gate = lax.dot_general(rows_x, gate_w, CONTRACT_LAST, preferred_element_type=jnp.float32)
    up = lax.dot_general(rows_x, up_w, CONTRACT_LAST, preferred_element_type=jnp.float32)
    hidden_grad = lax.dot_general(rows_g, down_w, CONTRACT_LAST, preferred_element_type=jnp.float32)
    sigma = jax.nn.sigmoid(gate)
    silu = gate * sigma
    acts = (silu * up).astype(jnp.bfloat16)
    grad_down = lax.dot_general(acts, rows_g, CONTRACT_FIRST, preferred_element_type=jnp.float32)
    gate_term = (hidden_grad * up * sigma * (1.0 + gate * (1.0 - sigma))).astype(jnp.bfloat16)
    up_term = (hidden_grad * silu).astype(jnp.bfloat16)
    grad_gate = lax.dot_general(
        gate_term, rows_x, CONTRACT_FIRST, preferred_element_type=jnp.float32
    )
    grad_up = lax.dot_general(up_term, rows_x, CONTRACT_FIRST, preferred_element_type=jnp.float32)
    swapped_gate, swapped_up = (
        lax.all_to_all(gate_w, "etp", split_axis=1, concat_axis=0, tiled=True),
        lax.all_to_all(up_w, "etp", split_axis=1, concat_axis=0, tiled=True),
    )
    running = jnp.dot(
        lax.all_gather(gate_term, "etp", axis=1, tiled=True),
        swapped_gate,
        preferred_element_type=jnp.float32,
    )
    slot_grads = running + jnp.dot(
        lax.all_gather(up_term, "etp", axis=1, tiled=True),
        swapped_up,
        preferred_element_type=jnp.float32,
    )
    slot_grads = slot_grads.astype(jnp.bfloat16)
    returned = lax.all_to_all(slot_grads, "expert", split_axis=0, concat_axis=0, tiled=True)
    picked = returned[target].astype(jnp.float32).reshape(tok_rows, choose_count, col_width)
    grad_tokens = jnp.sum(picked, axis=1).astype(jnp.bfloat16)
    return (
        grad_tokens,
        grad_gate.astype(jnp.bfloat16)[None],
        grad_up.astype(jnp.bfloat16)[None],
        grad_down.astype(jnp.bfloat16)[None],
    )


def pack_kernel(tokens_ref, grads_ref, routes_ref, combine_ref, out_ref):
    rows = tokens_ref.shape[0]
    out_ref[:rows] = tokens_ref[...]
    out_ref[rows:2 * rows] = grads_ref[...]
    top = routes_ref.shape[0]
    routes = routes_ref[...].astype(jnp.float32)
    weights = combine_ref[...]
    high = weights.astype(jnp.bfloat16).astype(jnp.float32)
    middle = (weights - high).astype(jnp.bfloat16).astype(jnp.float32)
    low = weights - high - middle
    blank = jnp.zeros((INFO_ROWS - 4, rows), jnp.float32)
    for k in range(top):
        own = slice(k, k + 1)
        column = jnp.concatenate([routes[own], high[own], middle[own], low[own], blank], axis=0)
        out_ref[2 * rows:, k * rows:(k + 1) * rows] = column.astype(jnp.bfloat16)


def pack_share(tokens, out_grad, routes, combine):
    rows, width = tokens.shape
    vmem = pl.BlockSpec(memory_space=pltpu.VMEM)
    return pl.pallas_call(
        pack_kernel,
        in_specs=[vmem] * 4,
        out_specs=vmem,
        out_shape=jax.ShapeDtypeStruct((2 * rows + INFO_ROWS, width), jnp.bfloat16),
        name="pack",
    )(tokens, out_grad, routes.T, combine.T)


def pick_kernel(top, rows, place_ref, *refs):
    shares, (mine_ref, theirs_ref, picks_ref) = refs[:4], refs[4:]
    me, own_half, core = place_ref[0], place_ref[1], place_ref[2]
    pair_slots, width = mine_ref.shape[1], shares[0].shape[1]
    earlier = (
        lax.broadcasted_iota(jnp.int32, (2 * rows, 2 * rows), 0)
        < lax.broadcasted_iota(jnp.int32, (2 * rows, 2 * rows), 1)
    ).astype(jnp.bfloat16)
    infos = [
        [share_ref[pl.ds(2 * rows, INFO_ROWS), k * rows:(k + 1) * rows].astype(jnp.float32) for k in range(top)]
        for share_ref in (shares[0], shares[3])
    ]
    picks, scales = [], []
    for expert in (me, me + 1 - 2 * core):
        named, weights = [], []
        for block in infos:
            hits, weight = 0.0, 0.0
            for info in block:
                hit = info[0:1] == expert.astype(jnp.float32)
                hits += hit.astype(jnp.float32)
                weight += jnp.where(hit, info[1:2] + info[2:3] + info[3:4], 0.0)
            named.append(hits)
            weights.append(weight)
        named = jnp.concatenate(named, axis=1)
        weights = jnp.concatenate(weights, axis=1)
        counted = jnp.dot(
            jnp.broadcast_to(named, (16, 2 * rows)).astype(jnp.bfloat16),
            earlier,
            preferred_element_type=jnp.float32,
        )[:1]
        slot_of = jnp.where(named > 0.0, counted.astype(jnp.int32), -1)
        chosen = slot_of == lax.broadcasted_iota(jnp.int32, (pair_slots, 2 * rows), 0)
        picks.append(chosen.astype(jnp.bfloat16))
        scales.append(jnp.sum(jnp.where(chosen, weights, 0.0), axis=1, keepdims=True))
    picks = jnp.concatenate(picks, axis=0)
    scales = jnp.concatenate(scales, axis=0)
    picks_ref[...] = picks
    for h in range(2):
        cols = pl.ds(pl.multiple_of((own_half if h == 0 else 1 - own_half) * width, width), width)
        for part in range(2):
            own, first, second, both = [ref[pl.ds(part * rows, rows)] for ref in shares]
            if h == 0:
                held = jnp.concatenate([own, jnp.where(core == 1, second, first)], axis=0)
            else:
                held = jnp.concatenate([jnp.where(core == 1, first, second), both], axis=0)
            picked = jnp.dot(picks, held, preferred_element_type=jnp.float32)
            if part == 1:
                picked = scales * picked
            picked = picked.astype(jnp.bfloat16)
            mine_ref[part, :, cols] = picked[:pair_slots]
            theirs_ref[part, :, cols] = picked[pair_slots:]


def expert_kernel(index, chained, mine_ref, theirs_ref, wg_ref, wu_ref, wd_ref, *refs):
    near_ref, far_ref, *kept_refs = refs[5 if chained else 0:][:7]
    act_ref, gt_ref, ut_ref, sems = refs[-4:]
    pair_slots = mine_ref.shape[1]
    slots = 2 * pair_slots

    def kept_move(source, target, part, count, i):
        return pltpu.make_async_copy(
            source, kept_refs[target].at[pl.ds(index * slots + part * pair_slots, count)], sems.at[i]
        )

    moves = [
        kept_move(mine_ref.at[0], 0, 0, pair_slots, 0),
        kept_move(theirs_ref.at[0], 0, 1, pair_slots, 1),
        kept_move(mine_ref.at[1], 1, 0, pair_slots, 2),
        kept_move(theirs_ref.at[1], 1, 1, pair_slots, 3),
        kept_move(act_ref, 2, 0, slots, 4),
        kept_move(gt_ref, 3, 0, slots, 5),
        kept_move(ut_ref, 4, 0, slots, 6),
    ]
    for move in moves[:4]:
        move.start()
    rows_x = jnp.concatenate([mine_ref[0], theirs_ref[0]], axis=0)
    rows_g = jnp.concatenate([mine_ref[1], theirs_ref[1]], axis=0)
    gate = lax.dot_general(rows_x, wg_ref[...], CONTRACT_LAST, preferred_element_type=jnp.float32)
    up = lax.dot_general(rows_x, wu_ref[...], CONTRACT_LAST, preferred_element_type=jnp.float32)
    hidden_grad = lax.dot_general(rows_g, wd_ref[...], CONTRACT_LAST, preferred_element_type=jnp.float32)
    sigma = 1.0 / (1.0 + jnp.exp(-gate))
    silu = gate * sigma
    act_ref[...] = (silu * up).astype(jnp.bfloat16)
    gt_ref[...] = (hidden_grad * up * sigma * (1.0 + gate * (1.0 - sigma))).astype(jnp.bfloat16)
    ut_ref[...] = (hidden_grad * silu).astype(jnp.bfloat16)
    for move in moves[4:]:
        move.start()
    slot = jnp.dot(gt_ref[...], wg_ref[...], preferred_element_type=jnp.float32)
    slot += jnp.dot(ut_ref[...], wu_ref[...], preferred_element_type=jnp.float32)
    far_ref[...] = slot[pair_slots:].astype(jnp.bfloat16)
    near_ref[...] = slot[:pair_slots].astype(jnp.bfloat16)
    for move in moves:
        move.wait()


def place_kernel(place_ref, picks_ref, near_ref, far_ref, keep_ref, send_ref):
    own_half, core = place_ref[1], place_ref[2]
    _, rows, width = keep_ref.shape
    pair_slots = near_ref.shape[0]
    backs = []
    for h in range(2):
        cols = pl.ds(pl.multiple_of((own_half if h == 0 else 1 - own_half) * width, width), width)
        slot = jnp.concatenate([near_ref[:, cols], far_ref[:, cols]], axis=0)
        backs.append(lax.dot_general(picks_ref[...], slot, CONTRACT_FIRST, preferred_element_type=jnp.float32))
    keep_ref[0] = backs[0][:rows]
    keep_ref[1] = jnp.where(core == 1, backs[1][:rows], backs[0][rows:])
    send_ref[0] = jnp.where(core == 1, backs[0][rows:], backs[1][:rows]).astype(jnp.bfloat16)
    send_ref[1] = backs[1][rows:].astype(jnp.bfloat16)


def pick_rows(place, shares, top, rows, pair_slots):
    width = shares[0].shape[1]
    vmem = pl.BlockSpec(memory_space=pltpu.VMEM)
    picked = jax.ShapeDtypeStruct((2, pair_slots, 2 * width), jnp.bfloat16)
    return pl.pallas_call(
        functools.partial(pick_kernel, top, rows),
        in_specs=[pl.BlockSpec(memory_space=pltpu.SMEM)] + [vmem] * 4,
        out_specs=[vmem] * 3,
        out_shape=[picked, picked, jax.ShapeDtypeStruct((2 * pair_slots, 2 * rows), jnp.bfloat16)],
        compiler_params=pltpu.CompilerParams(vmem_limit_bytes=VMEM_LIMIT),
        name="pick",
    )(place, *shares)


def run_experts(index, chunks, mine, theirs, weights, kept):
    _, pair_slots, features = mine.shape
    hidden = weights[0].shape[0]
    slots = 2 * pair_slots
    hbm = pl.BlockSpec(memory_space=pltpu.HBM)
    vmem = pl.BlockSpec(memory_space=pltpu.VMEM)
    part = jax.ShapeDtypeStruct((pair_slots, features), jnp.bfloat16)
    wide = jax.ShapeDtypeStruct((chunks * slots, features), jnp.bfloat16)
    narrow = jax.ShapeDtypeStruct((chunks * slots, hidden), jnp.bfloat16)
    return pl.pallas_call(
        functools.partial(expert_kernel, index, kept is not None),
        in_specs=[vmem] * 5 + [hbm] * (0 if kept is None else 5),
        out_specs=[vmem] * 2 + [hbm] * 5,
        out_shape=[part, part, wide, wide, narrow, narrow, narrow],
        scratch_shapes=[pltpu.VMEM((slots, hidden), jnp.bfloat16)] * 3 + [pltpu.SemaphoreType.DMA((7,))],
        input_output_aliases={} if kept is None else {5 + i: 2 + i for i in range(5)},
        compiler_params=pltpu.CompilerParams(vmem_limit_bytes=VMEM_LIMIT),
        name="experts",
    )(mine, theirs, *weights, *(kept or ()))


def place_rows(place, picks, near, far, rows, width):
    vmem = pl.BlockSpec(memory_space=pltpu.VMEM)
    return pl.pallas_call(
        place_kernel,
        in_specs=[pl.BlockSpec(memory_space=pltpu.SMEM)] + [vmem] * 3,
        out_specs=[vmem] * 2,
        out_shape=[
            jax.ShapeDtypeStruct((2, rows, width), jnp.float32),
            jax.ShapeDtypeStruct((2, rows, width), jnp.bfloat16),
        ],
        compiler_params=pltpu.CompilerParams(vmem_limit_bytes=VMEM_LIMIT),
        name="place",
    )(place, picks, near, far)


def ring_order(length):
    return list(range(0, min(1, length))) + list(range(1, length, 2)) + list(range(2, length, 2))[::-1]


def gather_body(tokens, out_grad, routes, combine, w_gate, w_up, w_down):
    experts = lax.axis_size("expert")
    chunks = experts // 4
    rows, width = tokens.shape
    top = routes.shape[1]
    per_pair = rows * top // experts
    capacity = per_pair + per_pair // 8
    pair_slots = -(-2 * capacity // 16) * 16
    order = ring_order(chunks)
    after = {order[i]: order[(i + 1) % chunks] for i in range(chunks)}
    devices = [(e, h) for e in range(experts) for h in range(2)]

    def permute(value, target):
        pairs = [(e * 2 + h, target(e, h)[0] * 2 + target(e, h)[1]) for e, h in devices]
        return lax.ppermute(value, ("expert", "etp"), pairs)

    def to_ring(value):
        return permute(value, lambda e, h: (after[e // 4] * 4 + e % 4, h))

    def to_core(value):
        return permute(value, lambda e, h: (e ^ 1, h))

    def to_first(value):
        return permute(value, lambda e, h: (e, h ^ 1) if e % 2 else (e ^ 2, h))

    def to_second(value):
        return permute(value, lambda e, h: (e ^ 2, h) if e % 2 else (e, h ^ 1))

    me = lax.axis_index("expert")
    place = jnp.stack([me, lax.axis_index("etp"), me % 2]).astype(jnp.int32)
    share = pack_share(tokens, out_grad, routes, combine)
    weights = (w_gate[0], w_up[0], w_down[0])

    def tied(values, mark):
        return lax.optimization_barrier((values, mark))[0]

    def placed(picks, near, far):
        return place_rows(place, picks, near, to_core(far), rows, width)

    def added(keep, came):
        return keep + came.astype(jnp.float32)

    waves = [
        ([("f", 0), ("a", 0)], ("s", 1)),
        ([("b", 0), ("f", 1)], ("s", 2)),
        ([("a", 1), ("b", 1), ("a", 2)], ("s", 3)),
        ([("a", 3), ("f", 3)], ("f", 2)),
        ([("b", 2), ("b", 3)], None),
    ]
    have = {("s", 0): share}
    kept, picked, parts = None, None, None
    late, done = [], 0
    for plane, ring in waves:
        came = {}
        for kind, c in plane:
            if c < chunks:
                value = have["f" if kind == "b" else "s", c]
                came[kind, c] = to_first(value) if kind == "f" else to_second(value)
        if ring is not None and ring[1] < chunks:
            came[ring] = to_ring(have[ring[0], ring[1] - 1])
        before, parts = parts, None
        if picked is not None:
            mine, theirs, picks = picked
            near, far, *kept = run_experts(done, chunks, mine, to_core(theirs), weights, kept)
            parts, picked = (picks, near, far), None
            done += 1
        if ring is None:
            have.update(came)
            break
        if all((kind, done) in have for kind in "sfab") and done + 1 < chunks:
            picked = pick_rows(place, [have[kind, done] for kind in "sfab"], top, rows, pair_slots)
        listed = sorted(came, reverse=False)
        values, picked, parts, weights = lax.optimization_barrier(
            ([came[key] for key in listed], picked, parts, weights)
        )
        have.update(zip(listed, values))
    mark = []
    first_out = None
    if before is not None:
        first_out = placed(*before)
        mark.append(first_out[1])
    if parts is not None:
        mark.append(parts[1])
    while done < chunks:
        shares = tied([have[kind, done] for kind in "sfab"], mark)
        mine, theirs, picks = pick_rows(place, shares, top, rows, pair_slots)
        if parts is not None:
            keep, send = placed(*parts)
            late.append((keep, to_second(send)))
            mine = tied(mine, send)
        near, far, *kept = run_experts(done, chunks, mine, to_core(theirs), weights, kept)
        parts, mark = (picks, near, far), [near]
        done += 1
    keep, send = placed(*parts)
    late.append((keep, to_second(send)))
    if first_out is not None:
        late.insert(0, (first_out[0], to_second(tied(first_out[1], send))))
    marks = [send] * (chunks + 2)
    running, previous = None, send
    for c in range(1, chunks):
        keep, came = late[c]
        came = tied(came, near if c == 1 else send if c + 1 < chunks else previous)
        pair = added(keep, came)
        came = to_first(pair[1].astype(jnp.bfloat16))
        total = added(pair[0], tied(came, send) if c + 2 < chunks else came)
        running = (total if running is None else added(total, running)).astype(jnp.bfloat16)
        previous = running
        if c > 1:
            marks[min(c - 1, 2)] = running
        if c + 1 < chunks:
            running = to_ring(running)
    keep, came = late[0]
    pair = added(keep, came)
    came = pair[1].astype(jnp.bfloat16)
    own = added(pair[0], to_first(came if running is None else tied(came, running)))
    grad_tokens = (own if running is None else added(own, to_ring(running))).astype(jnp.bfloat16)
    rows_x, rows_g, acts, gate_term, up_term = kept
    acts, gate_term, up_term = tied(acts, marks[0]), tied(gate_term, marks[1]), tied(up_term, marks[2])
    grad_down = lax.dot_general(acts, rows_g, CONTRACT_FIRST, preferred_element_type=jnp.float32)
    grad_gate = lax.dot_general(gate_term, rows_x, CONTRACT_FIRST, preferred_element_type=jnp.float32)
    grad_up = lax.dot_general(up_term, rows_x, CONTRACT_FIRST, preferred_element_type=jnp.float32)
    return (
        grad_tokens,
        grad_gate.astype(jnp.bfloat16)[None],
        grad_up.astype(jnp.bfloat16)[None],
        grad_down.astype(jnp.bfloat16)[None],
    )


def solution(mesh):
    experts = mesh.shape["expert"]

    def body(tokens, out_grad, routes, combine, w_gate, w_up, w_down):
        rows, width = tokens.shape
        top = routes.shape[1]
        gathers = top * 4 >= experts and experts % 4 == 0 and experts <= 16 and mesh.shape["etp"] == 2
        run = gather_body if gathers and top * rows <= width else exchange_body
        return run(tokens, out_grad, routes, combine, w_gate, w_up, w_down)

    placed = (
        P("expert", "etp"),
        P("expert", "etp"),
        P("expert", None),
        P("expert", None),
        P("expert", "etp", None),
        P("expert", "etp", None),
        P("expert", "etp", None),
    )
    return jax.shard_map(
        body,
        mesh=mesh,
        in_specs=placed,
        out_specs=(
            P("expert", "etp"),
            P("expert", "etp", None),
            P("expert", "etp", None),
            P("expert", "etp", None),
        ),
        check_vma=False,
    )
```

```python
import functools

import jax
import jax.numpy as jnp
from jax import lax
from jax.experimental import pallas as pl
from jax.experimental.pallas import tpu as pltpu
from jax.sharding import PartitionSpec as P

CONTRACT_LAST = (((1,), (1,)), ((), ()))
CONTRACT_FIRST = (((0,), (0,)), ((), ()))
INFO_ROWS = 16
VMEM_LIMIT = 16 * 1024 * 1024


def pack_rows(token_rows, grad_rows, token_of, scale, is_live):
    mask = is_live[:, None].astype(token_rows.dtype)
    inputs_sent = token_rows[token_of] * mask
    grads_sent = (scale[:, None] * grad_rows[token_of].astype(jnp.float32)).astype(jnp.bfloat16)
    return (inputs_sent, grads_sent)


def pair_positions(routed_flat, experts):
    pair_total = routed_flat.shape[0]
    span = 128
    groups = pair_total // span
    labels = jnp.arange(experts, dtype=jnp.int32)
    one_hot = (routed_flat[:, None] == labels[None, :]).astype(jnp.bfloat16)
    grouped = one_hot.reshape(groups, span, experts)
    row_ids = jnp.arange(span, dtype=jnp.int32)
    lower = (row_ids[None, :] < row_ids[:, None]).astype(jnp.bfloat16)
    within = jnp.einsum("ij,bje->bie", lower, grouped, preferred_element_type=jnp.float32)
    group_sums = jnp.sum(grouped.astype(jnp.float32), axis=1)
    group_before = jnp.cumsum(group_sums, axis=0) - group_sums
    earlier = within + group_before[:, None, :]
    counted = jnp.sum(earlier * grouped.astype(jnp.float32), axis=2)
    return counted.reshape(pair_total).astype(jnp.int32)


def exchange_body(tokens, out_grad, routes, combine, w_gate, w_up, w_down):
    experts = lax.axis_size("expert")
    tok_rows = tokens.shape[0]
    col_width = tokens.shape[1]
    choose_count = routes.shape[1]
    per_pair = tok_rows * choose_count // experts
    capacity = per_pair + per_pair // 8
    routed_flat = routes.reshape(-1)
    pair_total = routed_flat.shape[0]
    position = pair_positions(routed_flat, experts)
    target = routed_flat * capacity + position
    anchor = jnp.full((experts * capacity,), pair_total, jnp.int32)
    anchor = anchor.at[target].set(jnp.arange(pair_total, dtype=jnp.int32))
    is_live = anchor < pair_total
    safe_anchor = jnp.minimum(anchor, pair_total - 1)
    token_of = safe_anchor // choose_count
    scale = combine.reshape(-1)[safe_anchor] * is_live.astype(jnp.float32)
    full_tokens, full_grads = (
        lax.all_gather(tokens, "etp", axis=1, tiled=True),
        lax.all_gather(out_grad, "etp", axis=1, tiled=True),
    )
    inputs_sent, grads_sent = pack_rows(full_tokens, full_grads, token_of, scale, is_live)
    rows_x, rows_g = (
        lax.all_to_all(inputs_sent, "expert", split_axis=0, concat_axis=0, tiled=True),
        lax.all_to_all(grads_sent, "expert", split_axis=0, concat_axis=0, tiled=True),
    )
    gate_w = w_gate[0]
    up_w = w_up[0]
    down_w = w_down[0]
    gate = lax.dot_general(rows_x, gate_w, CONTRACT_LAST, preferred_element_type=jnp.float32)
    up = lax.dot_general(rows_x, up_w, CONTRACT_LAST, preferred_element_type=jnp.float32)
    hidden_grad = lax.dot_general(rows_g, down_w, CONTRACT_LAST, preferred_element_type=jnp.float32)
    sigma = jax.nn.sigmoid(gate)
    silu = gate * sigma
    acts = (silu * up).astype(jnp.bfloat16)
    grad_down = lax.dot_general(acts, rows_g, CONTRACT_FIRST, preferred_element_type=jnp.float32)
    gate_term = (hidden_grad * up * sigma * (1.0 + gate * (1.0 - sigma))).astype(jnp.bfloat16)
    up_term = (hidden_grad * silu).astype(jnp.bfloat16)
    grad_gate = lax.dot_general(
        gate_term, rows_x, CONTRACT_FIRST, preferred_element_type=jnp.float32
    )
    grad_up = lax.dot_general(up_term, rows_x, CONTRACT_FIRST, preferred_element_type=jnp.float32)
    swapped_gate, swapped_up = (
        lax.all_to_all(gate_w, "etp", split_axis=1, concat_axis=0, tiled=True),
        lax.all_to_all(up_w, "etp", split_axis=1, concat_axis=0, tiled=True),
    )
    running = jnp.dot(
        lax.all_gather(gate_term, "etp", axis=1, tiled=True),
        swapped_gate,
        preferred_element_type=jnp.float32,
    )
    slot_grads = running + jnp.dot(
        lax.all_gather(up_term, "etp", axis=1, tiled=True),
        swapped_up,
        preferred_element_type=jnp.float32,
    )
    slot_grads = slot_grads.astype(jnp.bfloat16)
    returned = lax.all_to_all(slot_grads, "expert", split_axis=0, concat_axis=0, tiled=True)
    picked = returned[target].astype(jnp.float32).reshape(tok_rows, choose_count, col_width)
    grad_tokens = jnp.sum(picked, axis=1).astype(jnp.bfloat16)
    return (
        grad_tokens,
        grad_gate.astype(jnp.bfloat16)[None],
        grad_up.astype(jnp.bfloat16)[None],
        grad_down.astype(jnp.bfloat16)[None],
    )


def pack_kernel(tokens_ref, grads_ref, routes_ref, combine_ref, out_ref):
    rows = tokens_ref.shape[0]
    out_ref[:rows] = tokens_ref[...]
    out_ref[rows:2 * rows] = grads_ref[...]
    top = routes_ref.shape[0]
    routes = routes_ref[...].astype(jnp.float32)
    weights = combine_ref[...]
    high = weights.astype(jnp.bfloat16).astype(jnp.float32)
    middle = (weights - high).astype(jnp.bfloat16).astype(jnp.float32)
    low = weights - high - middle
    blank = jnp.zeros((INFO_ROWS - 4, rows), jnp.float32)
    for k in range(top):
        own = slice(k, k + 1)
        column = jnp.concatenate([routes[own], high[own], middle[own], low[own], blank], axis=0)
        out_ref[2 * rows:, k * rows:(k + 1) * rows] = column.astype(jnp.bfloat16)


def pack_share(tokens, out_grad, routes, combine):
    rows, width = tokens.shape
    vmem = pl.BlockSpec(memory_space=pltpu.VMEM)
    return pl.pallas_call(
        pack_kernel,
        in_specs=[vmem] * 4,
        out_specs=vmem,
        out_shape=jax.ShapeDtypeStruct((2 * rows + INFO_ROWS, width), jnp.bfloat16),
        name="pack",
    )(tokens, out_grad, routes.T, combine.T)


def pick_kernel(top, rows, place_ref, *refs):
    shares, (mine_ref, theirs_ref, picks_ref) = refs[:4], refs[4:]
    me, own_half, core = place_ref[0], place_ref[1], place_ref[2]
    pair_slots, width = mine_ref.shape[1], shares[0].shape[1]
    earlier = (
        lax.broadcasted_iota(jnp.int32, (2 * rows, 2 * rows), 0)
        < lax.broadcasted_iota(jnp.int32, (2 * rows, 2 * rows), 1)
    ).astype(jnp.bfloat16)
    infos = [
        [share_ref[pl.ds(2 * rows, INFO_ROWS), k * rows:(k + 1) * rows].astype(jnp.float32) for k in range(top)]
        for share_ref in (shares[0], shares[3])
    ]
    picks, scales = [], []
    for expert in (me, me + 1 - 2 * core):
        named, weights = [], []
        for block in infos:
            hits, weight = 0.0, 0.0
            for info in block:
                hit = info[0:1] == expert.astype(jnp.float32)
                hits += hit.astype(jnp.float32)
                weight += jnp.where(hit, info[1:2] + info[2:3] + info[3:4], 0.0)
            named.append(hits)
            weights.append(weight)
        named = jnp.concatenate(named, axis=1)
        weights = jnp.concatenate(weights, axis=1)
        counted = jnp.dot(
            jnp.broadcast_to(named, (16, 2 * rows)).astype(jnp.bfloat16),
            earlier,
            preferred_element_type=jnp.float32,
        )[:1]
        slot_of = jnp.where(named > 0.0, counted.astype(jnp.int32), -1)
        chosen = slot_of == lax.broadcasted_iota(jnp.int32, (pair_slots, 2 * rows), 0)
        picks.append(chosen.astype(jnp.bfloat16))
        scales.append(jnp.sum(jnp.where(chosen, weights, 0.0), axis=1, keepdims=True))
    picks = jnp.concatenate(picks, axis=0)
    scales = jnp.concatenate(scales, axis=0)
    picks_ref[...] = picks
    for h in range(2):
        cols = pl.ds(pl.multiple_of((own_half if h == 0 else 1 - own_half) * width, width), width)
        for part in range(2):
            own, first, second, both = [ref[pl.ds(part * rows, rows)] for ref in shares]
            if h == 0:
                held = jnp.concatenate([own, jnp.where(core == 1, second, first)], axis=0)
            else:
                held = jnp.concatenate([jnp.where(core == 1, first, second), both], axis=0)
            picked = jnp.dot(picks, held, preferred_element_type=jnp.float32)
            if part == 1:
                picked = scales * picked
            picked = picked.astype(jnp.bfloat16)
            mine_ref[part, :, cols] = picked[:pair_slots]
            theirs_ref[part, :, cols] = picked[pair_slots:]


def expert_kernel(index, chained, mine_ref, theirs_ref, wg_ref, wu_ref, wd_ref, *refs):
    near_ref, far_ref, *kept_refs = refs[5 if chained else 0:][:7]
    act_ref, gt_ref, ut_ref, sems = refs[-4:]
    pair_slots = mine_ref.shape[1]
    slots = 2 * pair_slots

    def kept_move(source, target, part, count, i):
        return pltpu.make_async_copy(
            source, kept_refs[target].at[pl.ds(index * slots + part * pair_slots, count)], sems.at[i]
        )

    moves = [
        kept_move(mine_ref.at[0], 0, 0, pair_slots, 0),
        kept_move(theirs_ref.at[0], 0, 1, pair_slots, 1),
        kept_move(mine_ref.at[1], 1, 0, pair_slots, 2),
        kept_move(theirs_ref.at[1], 1, 1, pair_slots, 3),
        kept_move(act_ref, 2, 0, slots, 4),
        kept_move(gt_ref, 3, 0, slots, 5),
        kept_move(ut_ref, 4, 0, slots, 6),
    ]
    for move in moves[:4]:
        move.start()
    rows_x = jnp.concatenate([mine_ref[0], theirs_ref[0]], axis=0)
    rows_g = jnp.concatenate([mine_ref[1], theirs_ref[1]], axis=0)
    gate = lax.dot_general(rows_x, wg_ref[...], CONTRACT_LAST, preferred_element_type=jnp.float32)
    up = lax.dot_general(rows_x, wu_ref[...], CONTRACT_LAST, preferred_element_type=jnp.float32)
    hidden_grad = lax.dot_general(rows_g, wd_ref[...], CONTRACT_LAST, preferred_element_type=jnp.float32)
    sigma = 1.0 / (1.0 + jnp.exp(-gate))
    silu = gate * sigma
    act_ref[...] = (silu * up).astype(jnp.bfloat16)
    gt_ref[...] = (hidden_grad * up * sigma * (1.0 + gate * (1.0 - sigma))).astype(jnp.bfloat16)
    ut_ref[...] = (hidden_grad * silu).astype(jnp.bfloat16)
    for move in moves[4:]:
        move.start()
    slot = jnp.dot(gt_ref[...], wg_ref[...], preferred_element_type=jnp.float32)
    slot += jnp.dot(ut_ref[...], wu_ref[...], preferred_element_type=jnp.float32)
    far_ref[...] = slot[pair_slots:].astype(jnp.bfloat16)
    near_ref[...] = slot[:pair_slots].astype(jnp.bfloat16)
    for move in moves:
        move.wait()


def place_kernel(place_ref, picks_ref, near_ref, far_ref, keep_ref, send_ref):
    own_half, core = place_ref[1], place_ref[2]
    _, rows, width = keep_ref.shape
    pair_slots = near_ref.shape[0]
    backs = []
    for h in range(2):
        cols = pl.ds(pl.multiple_of((own_half if h == 0 else 1 - own_half) * width, width), width)
        slot = jnp.concatenate([near_ref[:, cols], far_ref[:, cols]], axis=0)
        backs.append(lax.dot_general(picks_ref[...], slot, CONTRACT_FIRST, preferred_element_type=jnp.float32))
    keep_ref[0] = backs[0][:rows]
    keep_ref[1] = jnp.where(core == 1, backs[1][:rows], backs[0][rows:])
    send_ref[0] = jnp.where(core == 1, backs[0][rows:], backs[1][:rows]).astype(jnp.bfloat16)
    send_ref[1] = backs[1][rows:].astype(jnp.bfloat16)


def pick_rows(place, shares, top, rows, pair_slots):
    width = shares[0].shape[1]
    vmem = pl.BlockSpec(memory_space=pltpu.VMEM)
    picked = jax.ShapeDtypeStruct((2, pair_slots, 2 * width), jnp.bfloat16)
    return pl.pallas_call(
        functools.partial(pick_kernel, top, rows),
        in_specs=[pl.BlockSpec(memory_space=pltpu.SMEM)] + [vmem] * 4,
        out_specs=[vmem] * 3,
        out_shape=[picked, picked, jax.ShapeDtypeStruct((2 * pair_slots, 2 * rows), jnp.bfloat16)],
        compiler_params=pltpu.CompilerParams(vmem_limit_bytes=VMEM_LIMIT),
        name="pick",
    )(place, *shares)


def run_experts(index, chunks, mine, theirs, weights, kept):
    _, pair_slots, features = mine.shape
    hidden = weights[0].shape[0]
    slots = 2 * pair_slots
    hbm = pl.BlockSpec(memory_space=pltpu.HBM)
    vmem = pl.BlockSpec(memory_space=pltpu.VMEM)
    part = jax.ShapeDtypeStruct((pair_slots, features), jnp.bfloat16)
    wide = jax.ShapeDtypeStruct((chunks * slots, features), jnp.bfloat16)
    narrow = jax.ShapeDtypeStruct((chunks * slots, hidden), jnp.bfloat16)
    return pl.pallas_call(
        functools.partial(expert_kernel, index, kept is not None),
        in_specs=[vmem] * 5 + [hbm] * (0 if kept is None else 5),
        out_specs=[vmem] * 2 + [hbm] * 5,
        out_shape=[part, part, wide, wide, narrow, narrow, narrow],
        scratch_shapes=[pltpu.VMEM((slots, hidden), jnp.bfloat16)] * 3 + [pltpu.SemaphoreType.DMA((7,))],
        input_output_aliases={} if kept is None else {5 + i: 2 + i for i in range(5)},
        compiler_params=pltpu.CompilerParams(vmem_limit_bytes=VMEM_LIMIT),
        name="experts",
    )(mine, theirs, *weights, *(kept or ()))


def place_rows(place, picks, near, far, rows, width):
    vmem = pl.BlockSpec(memory_space=pltpu.VMEM)
    return pl.pallas_call(
        place_kernel,
        in_specs=[pl.BlockSpec(memory_space=pltpu.SMEM)] + [vmem] * 3,
        out_specs=[vmem] * 2,
        out_shape=[
            jax.ShapeDtypeStruct((2, rows, width), jnp.float32),
            jax.ShapeDtypeStruct((2, rows, width), jnp.bfloat16),
        ],
        compiler_params=pltpu.CompilerParams(vmem_limit_bytes=VMEM_LIMIT),
        name="place",
    )(place, picks, near, far)


def ring_order(length):
    return list(range(0, min(1, length))) + list(range(1, length, 2)) + list(range(2, length, 2))[::-1]


def gather_body(tokens, out_grad, routes, combine, w_gate, w_up, w_down):
    experts = lax.axis_size("expert")
    chunks = experts // 4
    rows, width = tokens.shape
    top = routes.shape[1]
    per_pair = rows * top // experts
    capacity = per_pair + per_pair // 8
    pair_slots = -(-2 * capacity // 16) * 16
    order = ring_order(chunks)
    after = {order[i]: order[(i + 1) % chunks] for i in range(chunks)}
    devices = [(e, h) for e in range(experts) for h in range(2)]

    def permute(value, target):
        pairs = [(e * 2 + h, target(e, h)[0] * 2 + target(e, h)[1]) for e, h in devices]
        return lax.ppermute(value, ("expert", "etp"), pairs)

    def to_ring(value):
        return permute(value, lambda e, h: (after[e // 4] * 4 + e % 4, h))

    def to_core(value):
        return permute(value, lambda e, h: (e ^ 1, h))

    def to_first(value):
        return permute(value, lambda e, h: (e, h ^ 1) if e % 2 else (e ^ 2, h))

    def to_second(value):
        return permute(value, lambda e, h: (e ^ 2, h) if e % 2 else (e, h ^ 1))

    me = lax.axis_index("expert")
    place = jnp.stack([me, lax.axis_index("etp"), me % 2]).astype(jnp.int32)
    share = pack_share(tokens, out_grad, routes, combine)
    weights = (w_gate[0], w_up[0], w_down[0])

    def tied(values, mark):
        return lax.optimization_barrier((values, mark))[0]

    def placed(picks, near, far):
        return place_rows(place, picks, near, to_core(far), rows, width)

    def added(keep, came):
        return keep + came.astype(jnp.float32)

    waves = [
        ([("f", 0), ("a", 0)], ("s", 1)),
        ([("b", 0), ("f", 1)], ("s", 2)),
        ([("a", 1), ("b", 1), ("a", 2)], ("s", 3)),
        ([("a", 3), ("f", 3)], ("f", 2)),
        ([("b", 2), ("b", 3)], None),
    ]
    have = {("s", 0): share}
    kept, picked, parts = None, None, None
    late, done = [], 0
    for plane, ring in waves:
        came = {}
        for kind, c in plane:
            if c < chunks:
                value = have["f" if kind == "b" else "s", c]
                came[kind, c] = to_first(value) if kind == "f" else to_second(value)
        if ring is not None and ring[1] < chunks:
            came[ring] = to_ring(have[ring[0], ring[1] - 1])
        before, parts = parts, None
        if picked is not None:
            mine, theirs, picks = picked
            near, far, *kept = run_experts(done, chunks, mine, to_core(theirs), weights, kept)
            parts, picked = (picks, near, far), None
            done += 1
        if ring is None:
            have.update(came)
            break
        if all((kind, done) in have for kind in "sfab") and done + 1 < chunks:
            picked = pick_rows(place, [have[kind, done] for kind in "sfab"], top, rows, pair_slots)
        listed = sorted(came, reverse=False)
        values, picked, parts, weights = lax.optimization_barrier(
            ([came[key] for key in listed], picked, parts, weights)
        )
        have.update(zip(listed, values))
    mark = []
    first_out = None
    if before is not None:
        first_out = placed(*before)
        mark.append(first_out[1])
    if parts is not None:
        mark.append(parts[1])
    while done < chunks:
        shares = tied([have[kind, done] for kind in "sfab"], mark)
        mine, theirs, picks = pick_rows(place, shares, top, rows, pair_slots)
        if parts is not None:
            keep, send = placed(*parts)
            late.append((keep, to_second(send)))
            mine = tied(mine, send)
        near, far, *kept = run_experts(done, chunks, mine, to_core(theirs), weights, kept)
        parts, mark = (picks, near, far), [near]
        done += 1
    keep, send = placed(*parts)
    late.append((keep, to_second(send)))
    if first_out is not None:
        late.insert(0, (first_out[0], to_second(tied(first_out[1], send))))
    marks = [send] * (chunks + 2)
    running, previous = None, send
    for c in range(1, chunks):
        keep, came = late[c]
        came = tied(came, near if c == 1 else send if c + 1 < chunks else previous)
        pair = added(keep, came)
        leaving = pair[1].astype(jnp.bfloat16)
        came = to_first(leaving)
        total = added(pair[0], tied(came, send) if c + 2 < chunks else came)
        running = (total if running is None else added(total, running)).astype(jnp.bfloat16)
        previous = running
        if c > 1 and c + 1 == chunks:
            marks[1], marks[2] = leaving, running
        if c + 1 < chunks:
            running = to_ring(running)
    keep, came = late[0]
    pair = added(keep, came)
    came = pair[1].astype(jnp.bfloat16)
    own = added(pair[0], to_first(came if running is None else tied(came, running)))
    grad_tokens = (own if running is None else added(own, to_ring(running))).astype(jnp.bfloat16)
    rows_x, rows_g, acts, gate_term, up_term = kept
    acts, gate_term, up_term = tied(acts, marks[0]), tied(gate_term, marks[1]), tied(up_term, marks[2])
    grad_down = lax.dot_general(acts, rows_g, CONTRACT_FIRST, preferred_element_type=jnp.float32)
    grad_gate = lax.dot_general(gate_term, rows_x, CONTRACT_FIRST, preferred_element_type=jnp.float32)
    grad_up = lax.dot_general(up_term, rows_x, CONTRACT_FIRST, preferred_element_type=jnp.float32)
    return (
        grad_tokens,
        grad_gate.astype(jnp.bfloat16)[None],
        grad_up.astype(jnp.bfloat16)[None],
        grad_down.astype(jnp.bfloat16)[None],
    )


def solution(mesh):
    experts = mesh.shape["expert"]

    def body(tokens, out_grad, routes, combine, w_gate, w_up, w_down):
        rows, width = tokens.shape
        top = routes.shape[1]
        gathers = top * 4 >= experts and experts % 4 == 0 and experts <= 16 and mesh.shape["etp"] == 2
        run = gather_body if gathers and top * rows <= width else exchange_body
        return run(tokens, out_grad, routes, combine, w_gate, w_up, w_down)

    placed = (
        P("expert", "etp"),
        P("expert", "etp"),
        P("expert", None),
        P("expert", None),
        P("expert", "etp", None),
        P("expert", "etp", None),
        P("expert", "etp", None),
    )
    return jax.shard_map(
        body,
        mesh=mesh,
        in_specs=placed,
        out_specs=(
            P("expert", "etp"),
            P("expert", "etp", None),
            P("expert", "etp", None),
            P("expert", "etp", None),
        ),
        check_vma=False,
    )
```
